32 devices in a mesh: layer: 2 (over x), expert: 16 (over z, y, core).
Axes of the slice: x: 2, y: 2, z: 4, core: 2. Of those that a mesh axis runs over, the one named last changes fastest.
Arguments:
- grad_hidden: bfloat16 [8192, 384], P(('layer', 'expert')), parts along dimension 0, may hold values from -6 to 6
- grad_out: bfloat16 [8192, 1024], P(('layer', 'expert')), parts along dimension 0, may hold values from -0.41992188 to 0.41992188
- grad_route: int32 [8192, 1], P(('layer', 'expert')), parts along dimension 0, may hold values from 0 to 15; in each aligned block of 256 rows (0 to 255, 256 to 511, ...) at most 32 rows name the same one
- live_rows: int32 [32], P(('layer', 'expert')), parts along dimension 0, may hold values from 1 to 256, 3072 in all
- w_down: bfloat16 [32, 384, 1024], P(('layer', 'expert')), parts along dimension 0, may hold values from -0.3125 to 0.3125
- w_moment: bfloat16 [32, 384, 1024], P(('layer', 'expert')), parts along dimension 0, may hold values from -6 to 6
- perm: int32 [32], P('layer'), parts along dimension 0, may hold values from 0 to 15, each once
- fwd_hidden: bfloat16 [8192, 384], P(('layer', 'expert')), parts along dimension 0, may hold values from -6 to 6
- fwd_route: int32 [8192, 1], P(('layer', 'expert')), parts along dimension 0, may hold values from 0 to 15; in each aligned block of 256 rows (0 to 255, 256 to 511, ...) at most 32 rows name the same one
- fwd_gate: float32 [8192], P(('layer', 'expert')), parts along dimension 0, may hold values from 0.25 to 1
Outputs:
- placed_weight: bfloat16 [32, 384, 1024], P(('layer', 'expert')), parts along dimension 0
- placed_moment: bfloat16 [32, 384, 1024], P(('layer', 'expert')), parts along dimension 0
- fwd_out: bfloat16 [8192, 1024], P(('layer', 'expert')), parts along dimension 0
The draws below stay inside these ranges and needn't reach their ends.
There are 2 independent parts, one for each index of `layer`. The reference program is written for one: setup_inputs(seed, part) draws one part's arguments, and reference() takes and returns one part's arrays. A program takes and returns all parts, laid end to end along the dimension named above; each array names one. Nothing has to cross between parts.
Inputs may be any that keep to these rules, and one draw needn't show every extreme that they name: `grad_route`: among the 256 rows of one device no expert is named more than 32 times, and in some device's rows some expert is named exactly 32 times. `fwd_route`: among the 256 rows of one device no expert is named more than 32 times, and in some device's rows some expert is named exactly 32 times. `live_rows`: within each layer the counts sum to three quarters of 4096, and some device has all 256 rows live. `perm`: each device number appears once.
All inputs are finite; a program needn't handle non-finite values.
Results may differ from the reference program's by a relative error of at most 0.0065.
Values may be sent and summed in bfloat16 or wider, within the bound.
No kernel may reach another device: no remote copies, remote signals or barrier semaphores. Data moves between devices by JAX's collectives and lax.ppermute only.
A program may use at most 64 MiB of HBM per device.

```python
import math
import jax
import jax.numpy as jnp
import numpy as np
from jax import lax

FF = 384
D = 1024
GRAD_DEV = 256
FWD_DEV = 256
EXPERTS = 16
CAP = 32
FCAP = 32
GRAD_ROWS = 4096
FWD_ROWS = 4096


def levels(stream_key, extent, cuts, least, high):
    level = 1.0
    for axis_at, blocks in cuts:
        steps = jax.random.uniform(jax.random.fold_in(jax.random.fold_in(stream_key, 6), axis_at), (blocks,), jnp.float32, least / len(cuts), high / len(cuts))
        level = level * jnp.repeat(jnp.exp(steps), extent[axis_at] // blocks).reshape((-1,) + (1,) * (len(extent) - 1 - axis_at))
    return level


def profile(amount, total, reach, lean):
    loads = [(1 << 20) // math.isqrt(grade ** lean) + 1 for grade in range(2, amount + 1)]
    spare, counts = total - reach - (amount - 1), [1] * (amount - 1)
    while spare > 0:
        candidates = [i for i in range(amount - 1) if counts[i] < reach]
        whole, remaining = sum([loads[i] for i in candidates]), spare
        for i in candidates:
            addition = min(reach - counts[i], max(1, remaining * loads[i] // whole), spare)
            counts[i] = counts[i] + addition
            spare = spare - addition
    return np.array([reach] + counts)


def uneven_parts(key, amount, total, most, slope):
    if amount == 2:
        one = jax.random.randint(key, (), max(1, total - most), min(most, total - 1) + 1)
        return jnp.stack([one, total - one])
    lengths = jnp.asarray(profile(amount, total, most, slope), jnp.int32)
    twos = (amount - 1) // 2
    source_of, sink = lengths[1:1 + 2 * twos:2], lengths[2:2 + 2 * twos:2]
    margin = jnp.minimum(source_of - 1, most - sink)
    moved = jax.random.randint(jax.random.fold_in(key, 1), (twos,), 0, 1 << 20) % (margin + 1)
    lengths = lengths.at[1:1 + 2 * twos:2].set(source_of - moved).at[2:2 + 2 * twos:2].set(sink + moved)
    return lengths[jax.random.permutation(jax.random.fold_in(key, 2), amount)]


def routed_block(stream_key, own, number, rows, amount, top, most, skew):
    ranking = jax.random.permutation(stream_key, amount)
    crowded, usual = load_shares(amount, rows * top, most, skew, True), load_shares(amount, rows * top, most, skew, False)
    places = jnp.arange(amount)

    def named(sizes, turn):
        used = int((sizes > 0).sum())
        fixed = max(1, used // 4)
        moved = fixed + (places - fixed + turn * (used - fixed)) % max(1, amount - fixed)
        return jnp.zeros((amount,), jnp.int32).at[ranking[jnp.where(places < fixed, places, moved)]].set(jnp.asarray(sizes, jnp.int32))

    sizes = jnp.where(number % 4 == 0, named(crowded, number // 4), named(usual, number - number // 4 - 1))
    mixed = jax.random.permutation(jax.random.fold_in(own, 3), amount)
    giver, receiver = mixed[0:amount // 2 * 2:2], mixed[1:amount // 2 * 2:2]
    margin = jnp.minimum(sizes[giver] - 1, most - sizes[receiver]) // 2
    margin = jnp.where((giver == ranking[0]) | (receiver == ranking[0]) | (sizes[receiver] == 0), 0, jnp.maximum(margin, 0))
    moved = jax.random.randint(jax.random.fold_in(own, 4), (amount // 2,), 0, 1 << 20) % (margin + 1)
    sizes = sizes.at[giver].add(-moved).at[receiver].add(moved)
    items = jnp.searchsorted(jnp.cumsum(sizes), jnp.arange(rows * top), side="right").astype(jnp.int32)
    listing = items.reshape(top, rows).T
    listing = listing[jax.random.permutation(jax.random.fold_in(own, 1), rows)]
    turn = jax.random.randint(jax.random.fold_in(own, 2), (rows, 1), 0, top)
    return jnp.take_along_axis(listing, (jnp.arange(top)[None, :] + turn) % top, axis=1)


def load_shares(number_of, total, reach, lean, full):
    weights = [(1 << 20) // math.isqrt(grade ** lean) + 1 for grade in range(1, number_of + 1)]
    largest = reach if full else min(reach, max(-(-total // number_of), total * weights[0] // sum(weights)))
    least = 1 if total - largest >= number_of - 1 else 0
    counts, rest = [largest] + [least] * (number_of - 1), total - largest - least * (number_of - 1)
    while rest > 0:
        free = [i for i in range(1, number_of) if counts[i] < largest] or [i for i in range(1, number_of) if counts[i] < reach]
        whole, budget = sum([weights[i] for i in free]), rest
        for i in free:
            addition = min(reach - counts[i], max(1, budget * weights[i] // whole), rest)
            counts[i] = counts[i] + addition
            rest = rest - addition
    return np.array(counts)


def noise(key, dims, deviation, limit, shards=(), held_as=jnp.bfloat16):
    drawn = jax.random.normal(key, dims, jnp.float32) * deviation
    if len(shards) > 0:
        drawn = levels(key, dims, shards, -0.22, 0.18) * drawn
    return jnp.clip(drawn, min=-limit, max=limit).astype(held_as)


def setup_inputs(seed: int = 0, part: int = 0) -> dict:
    streams_of = jax.random.split(jax.random.key(seed), 11)
    part_keys = jax.random.split(jax.random.fold_in(streams_of[10], part), 11)
    grad_hidden = noise(part_keys[0], (GRAD_ROWS, FF), 1.0, 6.0, ((0, 16),))
    grad_out = noise(part_keys[1], (GRAD_ROWS, D), 0.07, 0.41992188, ((0, 16),))
    grad_route_keys = jax.random.split(jax.random.fold_in(part_keys[2], 1), GRAD_ROWS // GRAD_DEV)
    grad_route_turns = jax.random.permutation(jax.random.fold_in(part_keys[2], 3), GRAD_ROWS // GRAD_DEV)
    grad_route = jax.vmap(lambda own, number: routed_block(jax.random.fold_in(part_keys[2], 2), own, number, GRAD_DEV, EXPERTS, 1, CAP, 2))(grad_route_keys, grad_route_turns).reshape((GRAD_ROWS, 1))
    live_rows = uneven_parts(part_keys[3], EXPERTS, 3 * GRAD_DEV * EXPERTS // 4, GRAD_DEV, 2).astype(jnp.int32)
    w_down = noise(part_keys[4], (EXPERTS, FF, D), FF ** -0.5, 0.3125, ((0, 16),))
    w_moment = noise(part_keys[5], (EXPERTS, FF, D), 1.0, 6.0, ((0, 16),))
    perm = jax.random.permutation(part_keys[6], EXPERTS).astype(jnp.int32)
    fwd_hidden = noise(part_keys[7], (FWD_ROWS, FF), 1.0, 6.0, ((0, 16),))
    fwd_route_keys = jax.random.split(jax.random.fold_in(part_keys[8], 1), FWD_ROWS // FWD_DEV)
    fwd_route_turns = jax.random.permutation(jax.random.fold_in(part_keys[8], 3), FWD_ROWS // FWD_DEV)
    fwd_route = jax.vmap(lambda own, number: routed_block(jax.random.fold_in(part_keys[8], 2), own, number, FWD_DEV, EXPERTS, 1, FCAP, 2))(fwd_route_keys, fwd_route_turns).reshape((FWD_ROWS, 1))
    fwd_gate = jnp.clip(0.25 + 0.75 * jax.random.uniform(part_keys[9], (FWD_ROWS,), jnp.float32) ** levels(part_keys[9], (FWD_ROWS,), ((0, 16),), -0.2, 0.2), 0.25, 1.0)
    return dict(grad_hidden=grad_hidden, grad_out=grad_out, grad_route=grad_route, live_rows=live_rows, w_down=w_down, w_moment=w_moment, perm=perm, fwd_hidden=fwd_hidden, fwd_route=fwd_route, fwd_gate=fwd_gate)


linear_term = 3.4445
cubic_term = -4.775
quintic_term = 2.0315
moment_decay = 0.9
step_scale = 0.25
norm_floor = 1e-07

def build_table(route_ids, is_live, width):
    total_rows = route_ids.shape[0]
    columns = jnp.arange(EXPERTS, dtype=jnp.int32)
    onehot = ((route_ids[:, None] == columns[None, :]) & is_live[:, None]).astype(jnp.int32)
    ranked = lax.optimization_barrier(jnp.sum(jnp.cumsum(onehot, axis=0) * onehot, axis=1)) - 1
    target = jnp.where(is_live, route_ids, EXPERTS).astype(jnp.int32)
    ranked = jnp.where(is_live, ranked, 0).astype(jnp.int32)
    table = jnp.full((EXPERTS, width), total_rows, dtype=jnp.int32)
    return table.at[target, ranked].set(jnp.arange(total_rows, dtype=jnp.int32), mode='drop')

def orthogonalize(moment):
    moment_f = moment.astype(jnp.float32)
    frobenius = jnp.sqrt(jnp.sum(moment_f * moment_f))
    current = (moment_f / (frobenius + norm_floor)).astype(jnp.bfloat16)
    for sweep_index in range(2):
        gramian = lax.dot_general(current, current, (((1,), (1,)), ((), ())), preferred_element_type=jnp.float32).astype(jnp.bfloat16)
        squared = jnp.dot(gramian, gramian, preferred_element_type=jnp.float32)
        poly = (cubic_term * gramian.astype(jnp.float32) + quintic_term * squared).astype(jnp.bfloat16)
        current = (linear_term * current.astype(jnp.float32) + jnp.dot(poly, current, preferred_element_type=jnp.float32)).astype(jnp.bfloat16)
    return current

def reference(grad_hidden, grad_out, grad_route, live_rows, w_down, w_moment, perm, fwd_hidden, fwd_route, fwd_gate):
    is_live = (jnp.arange(GRAD_DEV, dtype=jnp.int32)[None, :] < live_rows[:, None]).reshape(-1)
    table = build_table(grad_route[:, 0], is_live, EXPERTS * CAP)
    hidden_pad = jnp.concatenate([grad_hidden, jnp.zeros((1, FF), jnp.bfloat16)], axis=0)
    out_pad = jnp.concatenate([grad_out, jnp.zeros((1, D), jnp.bfloat16)], axis=0)

    def update_one(packed):
        row_ids, weight, moment = packed
        grad = jnp.dot(hidden_pad[row_ids].T, out_pad[row_ids], preferred_element_type=jnp.float32)
        moment_new = (moment_decay * moment.astype(jnp.float32) + grad).astype(jnp.bfloat16)
        ortho = orthogonalize(moment_new)
        weight_new = (weight.astype(jnp.float32) - step_scale * ortho.astype(jnp.float32)).astype(jnp.bfloat16)
        return (weight_new, moment_new)
    weight_new, moment_new = lax.map(update_one, (table, w_down, w_moment))
    placed_weight = jnp.zeros_like(weight_new).at[perm].set(weight_new)
    placed_moment = jnp.zeros_like(moment_new).at[perm].set(moment_new)
    total_fwd = fwd_hidden.shape[0]
    fwd_table = build_table(fwd_route[:, 0], jnp.ones((total_fwd,), dtype=bool), EXPERTS * FCAP)
    fwd_pad = jnp.concatenate([fwd_hidden, jnp.zeros((1, FF), jnp.bfloat16)], axis=0)

    def forward_one(packed):
        row_ids, weight = packed
        return jnp.dot(fwd_pad[row_ids], weight, preferred_element_type=jnp.float32).astype(jnp.bfloat16)
    expert_out = lax.map(forward_one, (fwd_table, weight_new))
    gathered = jnp.zeros((total_fwd + 1, D), jnp.bfloat16).at[fwd_table.reshape(-1)].set(expert_out.reshape(-1, D))[:total_fwd]
    fwd_out = (gathered.astype(jnp.float32) * fwd_gate[:, None]).astype(jnp.bfloat16)
    return (placed_weight, placed_moment, fwd_out)
```

```python
import functools

import jax
import jax.numpy as jnp
from jax import lax
from jax.experimental import pallas as pl
from jax.experimental.pallas import tpu as pltpu
from jax.sharding import PartitionSpec as P

linear_term = 3.4445
cubic_term = -4.775
quintic_term = 2.0315
moment_decay = 0.9
step_scale = 0.25
norm_floor = 1e-07

F32 = jnp.float32
BF16 = jnp.bfloat16
VMEM = pl.BlockSpec(memory_space=pltpu.VMEM)
SMEM = pl.BlockSpec(memory_space=pltpu.SMEM)
ANY = pl.BlockSpec(memory_space=pl.ANY)
MIB = 1 << 20


def pack_kernel(groups, capacity, live_ref, route_ref, hidden_ref, out_ref, packed_ref):
    rows, ff = hidden_ref.shape
    route = route_ref[...]
    place = lax.broadcasted_iota(jnp.int32, (1, rows), 1)
    live = place < live_ref[0]
    experts = lax.broadcasted_iota(jnp.int32, (groups, rows), 0)
    onehot = jnp.where((experts == route) & live, 1.0, 0.0).astype(BF16)
    before = lax.broadcasted_iota(jnp.int32, (rows, rows), 0)
    after = lax.broadcasted_iota(jnp.int32, (rows, rows), 1)
    upto = jnp.where(before <= after, 1.0, 0.0).astype(BF16)
    ranks = jnp.dot(onehot, upto, preferred_element_type=F32)
    rank = jnp.sum(ranks * onehot.astype(F32), axis=0, keepdims=True).astype(jnp.int32) - 1
    slot_of = jnp.where(live, route * capacity + rank, -1)
    slots = lax.broadcasted_iota(jnp.int32, (groups * capacity, rows), 0)
    selector = jnp.where(slots == slot_of, 1.0, 0.0).astype(BF16)
    packed_ref[:, :ff] = jnp.dot(selector, hidden_ref[...], preferred_element_type=F32).astype(BF16)
    packed_ref[:, ff:] = jnp.dot(selector, out_ref[...], preferred_element_type=F32).astype(BF16)


def pack_rows(live_rows, route, hidden, grad_out, groups, capacity):
    rows, ff = hidden.shape
    width = ff + grad_out.shape[1]
    return pl.pallas_call(
        functools.partial(pack_kernel, groups, capacity),
        out_shape=jax.ShapeDtypeStruct((groups * capacity, width), BF16),
        in_specs=[SMEM, VMEM, VMEM, VMEM],
        out_specs=VMEM,
        compiler_params=pltpu.CompilerParams(vmem_limit_bytes=32 * MIB),
        cost_estimate=pl.CostEstimate(
            flops=2 * groups * capacity * rows * width, bytes_accessed=3 * rows * width * 2, transcendentals=0
        ),
        name="pack_rows",
    )(live_rows, route.reshape(1, rows), hidden, grad_out)


def update_kernel(packed_ref, weight_ref, moment_ref, weight_new_ref, moment_new_ref):
    ff = weight_ref.shape[0]
    grad = lax.dot_general(
        packed_ref[:, :ff], packed_ref[:, ff:], (((0,), (0,)), ((), ())), preferred_element_type=F32
    )
    moment_new = (moment_decay * moment_ref[...].astype(F32) + grad).astype(BF16)
    moment_new_ref[...] = moment_new
    moment_f = moment_new.astype(F32)
    frobenius = jnp.sqrt(jnp.sum(moment_f * moment_f))
    current = (moment_f / (frobenius + norm_floor)).astype(BF16)
    for _ in range(2):
        gramian = lax.dot_general(
            current, current, (((1,), (1,)), ((), ())), preferred_element_type=F32
        ).astype(BF16)
        squared = jnp.dot(gramian, gramian, preferred_element_type=F32)
        poly = (cubic_term * gramian.astype(F32) + quintic_term * squared).astype(BF16)
        current = (
            linear_term * current.astype(F32) + jnp.dot(poly, current, preferred_element_type=F32)
        ).astype(BF16)
    weight_new_ref[...] = (
        weight_ref[...].astype(F32) - step_scale * current.astype(F32)
    ).astype(BF16)


def update(packed, weight, moment):
    ff, d = weight.shape
    shape = jax.ShapeDtypeStruct((ff, d), BF16)
    return pl.pallas_call(
        update_kernel,
        out_shape=(shape, shape),
        in_specs=[VMEM] * 3,
        out_specs=(VMEM, VMEM),
        compiler_params=pltpu.CompilerParams(vmem_limit_bytes=48 * MIB),
        cost_estimate=pl.CostEstimate(
            flops=2 * ff * d * packed.shape[0] + 8 * ff * ff * d + 4 * ff**3,
            bytes_accessed=8 * ff * d + 2 * packed.size,
            transcendentals=1,
        ),
        name="update",
    )(packed, weight, moment)


def reorder_kernel(perm_ref, source_ref, target_ref, sem):
    copies = [
        pltpu.make_async_copy(source_ref.at[e], target_ref.at[perm_ref[e]], sem.at[e])
        for e in range(source_ref.shape[0])
    ]
    for copy in copies:
        copy.start()
    for copy in copies:
        copy.wait()


def reorder(perm, source):
    return pl.pallas_call(
        reorder_kernel,
        out_shape=jax.ShapeDtypeStruct(source.shape, source.dtype),
        in_specs=[SMEM, ANY],
        out_specs=ANY,
        scratch_shapes=[pltpu.SemaphoreType.DMA((source.shape[0],))],
        cost_estimate=pl.CostEstimate(flops=0, bytes_accessed=4 * source.size, transcendentals=0),
        name="reorder",
    )(perm, source)


def forward_kernel(perm_ref, me_ref, route_ref, gate_ref, hidden_ref, weight_ref, out_ref, placed_ref, total):
    e = pl.program_id(0)
    masked = jnp.where(route_ref[...] == e, hidden_ref[...], jnp.zeros_like(hidden_ref))
    product = jnp.dot(masked, weight_ref[0], preferred_element_type=F32)

    @pl.when(e == 0)
    def _():
        total[...] = product

    @pl.when(e > 0)
    def _():
        total[...] += product

    @pl.when(perm_ref[e] == me_ref[0])
    def _():
        placed_ref[...] = weight_ref[0]

    @pl.when(e == pl.num_programs(0) - 1)
    def _():
        expert_out = total[...].astype(BF16).astype(F32)
        out_ref[...] = (gate_ref[...] * expert_out).astype(BF16)


def forward(perm, me, route, gate, hidden, gathered):
    groups, ff, d = gathered.shape
    rows = hidden.shape[0]
    whole = lambda *shape: pl.BlockSpec(shape, lambda e: (0,) * len(shape))
    return pl.pallas_call(
        forward_kernel,
        grid=(groups,),
        out_shape=(jax.ShapeDtypeStruct((rows, d), BF16), jax.ShapeDtypeStruct((ff, d), BF16)),
        in_specs=[
            SMEM,
            SMEM,
            whole(rows, 1),
            whole(rows, 1),
            whole(rows, ff),
            pl.BlockSpec((1, ff, d), lambda e: (e, 0, 0)),
        ],
        out_specs=(whole(rows, d), whole(ff, d)),
        scratch_shapes=[pltpu.VMEM((rows, d), F32)],
        compiler_params=pltpu.CompilerParams(vmem_limit_bytes=32 * MIB),
        cost_estimate=pl.CostEstimate(
            flops=2 * groups * rows * ff * d, bytes_accessed=2 * gathered.size + 8 * rows * d, transcendentals=0
        ),
        name="forward",
    )(perm, me, route, gate.reshape(rows, 1), hidden, gathered)


def exchange(array):
    return lax.all_to_all(array, "expert", split_axis=0, concat_axis=0, tiled=True)


def gathered_plan(
    grad_hidden, grad_out, grad_route, live_rows, w_down, w_moment, perm, fwd_hidden, fwd_route, fwd_gate
):
    groups = lax.axis_size("expert")
    me = lax.axis_index("expert").astype(jnp.int32).reshape(1)
    capacity = max(4, 2 * grad_hidden.shape[0] // groups)
    ff, d = w_down.shape[1:]
    packed = pack_rows(live_rows, grad_route, grad_hidden, grad_out, groups, capacity)
    received = exchange(packed.reshape(groups, capacity, -1)).reshape(groups * capacity, -1)
    weight_new, moment_new = update(received, w_down[0], w_moment[0])
    gathered = lax.all_gather(weight_new, "expert", axis=0, tiled=False)
    spread = exchange(moment_new.reshape(groups, ff // groups, d))
    placed_moment = exchange(reorder(perm, spread)).reshape(1, ff, d)
    fwd_out, placed_weight = forward(perm, me, fwd_route, fwd_gate, fwd_hidden, gathered)
    return placed_weight[None], placed_moment, fwd_out


def lookup(route_ids, mapping):
    columns = jnp.arange(mapping.shape[0], dtype=jnp.int32)
    hits = route_ids[:, None] == columns[None, :]
    return jnp.sum(jnp.where(hits, mapping[None, :], 0), axis=1)


def slot_matrix(target, is_live, groups, capacity):
    columns = jnp.arange(groups, dtype=jnp.int32)
    onehot = ((target[:, None] == columns[None, :]) & is_live[:, None]).astype(jnp.int32)
    ranked = jnp.sum(jnp.cumsum(onehot, axis=0) * onehot, axis=1) - 1
    slot_of = jnp.where(is_live, target * capacity + ranked, -1)
    slots = jnp.arange(groups * capacity, dtype=jnp.int32)
    return (slots[:, None] == slot_of[None, :]).astype(jnp.bfloat16)


def orthogonalize(moment):
    moment_f = moment.astype(jnp.float32)
    frobenius = jnp.sqrt(jnp.sum(moment_f * moment_f))
    current = (moment_f / (frobenius + norm_floor)).astype(jnp.bfloat16)
    for sweep_index in range(2):
        gramian = lax.dot_general(
            current, current, (((1,), (1,)), ((), ())), preferred_element_type=jnp.float32
        ).astype(jnp.bfloat16)
        squared = jnp.dot(gramian, gramian, preferred_element_type=jnp.float32)
        poly = (cubic_term * gramian.astype(jnp.float32) + quintic_term * squared).astype(
            jnp.bfloat16
        )
        current = (
            linear_term * current.astype(jnp.float32)
            + jnp.dot(poly, current, preferred_element_type=jnp.float32)
        ).astype(jnp.bfloat16)
    return current


def relocate(weight, moment, perm):
    groups = lax.axis_size("expert")
    weight_flat = weight.reshape(groups, -1)
    moment_flat = moment.reshape(groups, -1)
    spread_w, spread_m = (
        lax.all_to_all(weight_flat, "expert", split_axis=0, concat_axis=0, tiled=True),
        lax.all_to_all(moment_flat, "expert", split_axis=0, concat_axis=0, tiled=True),
    )
    devices = jnp.arange(groups, dtype=jnp.int32)
    inverse = jnp.sum(jnp.where(perm[None, :] == devices[:, None], devices[None, :], 0), axis=1)
    ordered_w = jnp.take(spread_w, inverse, axis=0)
    ordered_m = jnp.take(spread_m, inverse, axis=0)
    back_w, back_m = (
        lax.all_to_all(ordered_w, "expert", split_axis=0, concat_axis=0, tiled=True),
        lax.all_to_all(ordered_m, "expert", split_axis=0, concat_axis=0, tiled=True),
    )
    return (back_w.reshape(weight.shape), back_m.reshape(moment.shape))


def routed_plan(
    grad_hidden,
    grad_out,
    grad_route,
    live_rows,
    w_down,
    w_moment,
    perm,
    fwd_hidden,
    fwd_route,
    fwd_gate,
):
    groups = lax.axis_size("expert")
    grad_count = grad_hidden.shape[0]
    capacity = max(4, 2 * grad_count // groups)
    is_live = jnp.arange(grad_count, dtype=jnp.int32) < live_rows[0]
    route_ids = grad_route[:, 0]
    weight, moment = relocate(w_down, w_moment, perm)
    target = lookup(route_ids, perm)
    selector = slot_matrix(target, is_live, groups, capacity)
    hidden_buf = (
        jnp.dot(selector, grad_hidden, preferred_element_type=jnp.float32)
        .astype(jnp.bfloat16)
        .reshape(groups, capacity, -1)
    )
    outgrad_buf = (
        jnp.dot(selector, grad_out, preferred_element_type=jnp.float32)
        .astype(jnp.bfloat16)
        .reshape(groups, capacity, -1)
    )
    recv_hidden, recv_outgrad = (
        lax.all_to_all(hidden_buf, "expert", split_axis=0, concat_axis=0, tiled=True),
        lax.all_to_all(outgrad_buf, "expert", split_axis=0, concat_axis=0, tiled=True),
    )
    grad = lax.dot_general(
        recv_hidden.reshape(groups * capacity, -1),
        recv_outgrad.reshape(groups * capacity, -1),
        (((0,), (0,)), ((), ())),
        preferred_element_type=jnp.float32,
    )
    moment_new = (moment_decay * moment[0].astype(jnp.float32) + grad).astype(jnp.bfloat16)
    ortho = orthogonalize(moment_new)
    weight_new = (weight[0].astype(jnp.float32) - step_scale * ortho.astype(jnp.float32)).astype(
        jnp.bfloat16
    )
    weight_new = weight_new[None]
    moment_new = moment_new[None]
    fwd_ids = fwd_route[:, 0]
    placed_weight, placed_moment = (weight_new, moment_new)
    fwd_target = lookup(fwd_ids, perm)
    fwd_weight = weight_new[0]
    fwd_count = fwd_hidden.shape[0]
    fwd_capacity = max(4, 2 * fwd_count // groups)
    fwd_selector = slot_matrix(fwd_target, jnp.ones((fwd_count,), dtype=bool), groups, fwd_capacity)
    fwd_buf = (
        jnp.dot(fwd_selector, fwd_hidden, preferred_element_type=jnp.float32)
        .astype(jnp.bfloat16)
        .reshape(groups, fwd_capacity, -1)
    )
    produced = jnp.einsum(
        "gkf,fd->gkd",
        lax.all_to_all(fwd_buf, "expert", split_axis=0, concat_axis=0, tiled=True),
        fwd_weight,
        preferred_element_type=jnp.float32,
    ).astype(jnp.bfloat16)
    returned = lax.all_to_all(produced, "expert", split_axis=0, concat_axis=0, tiled=True)
    fwd_rows_out = lax.dot_general(
        fwd_selector,
        returned.reshape(groups * fwd_capacity, -1),
        (((0,), (0,)), ((), ())),
        preferred_element_type=jnp.float32,
    )
    fwd_out = (fwd_rows_out * fwd_gate[:, None]).astype(jnp.bfloat16)
    return (placed_weight, placed_moment, fwd_out)


def solution(mesh):
    groups = mesh.shape["expert"]
    in_specs = (
        P(("layer", "expert"), None),
        P(("layer", "expert"), None),
        P(("layer", "expert"), None),
        P(("layer", "expert")),
        P(("layer", "expert"), None, None),
        P(("layer", "expert"), None, None),
        P("layer"),
        P(("layer", "expert"), None),
        P(("layer", "expert"), None),
        P(("layer", "expert")),
    )
    out_specs = (
        P(("layer", "expert"), None, None),
        P(("layer", "expert"), None, None),
        P(("layer", "expert"), None),
    )

    def per_device(*args):
        few = groups <= 2 * args[0].shape[0] // groups
        return (gathered_plan if few else routed_plan)(*args)

    return jax.shard_map(
        per_device, mesh=mesh, in_specs=in_specs, out_specs=out_specs, check_vma=False
    )
```

```python
import functools

import jax
import jax.numpy as jnp
from jax import lax
from jax.experimental import pallas as pl
from jax.experimental.pallas import tpu as pltpu
from jax.sharding import PartitionSpec as P

linear_term = 3.4445
cubic_term = -4.775
quintic_term = 2.0315
moment_decay = 0.9
step_scale = 0.25
norm_floor = 1e-07

F32 = jnp.float32
BF16 = jnp.bfloat16
VMEM = pl.BlockSpec(memory_space=pltpu.VMEM)
SMEM = pl.BlockSpec(memory_space=pltpu.SMEM)
ANY = pl.BlockSpec(memory_space=pl.ANY)
MIB = 1 << 20


def chunk_at(ref, lead, k, rows, columns):
    return ref.at[
        lead,
        pl.ds(pl.multiple_of((k // 2) * rows, rows), rows),
        pl.ds(pl.multiple_of((k % 2) * columns, columns), columns),
    ]


def slot_rows(route, live, groups, capacity, perm_ref):
    rows = route.shape[1]
    experts = lax.broadcasted_iota(jnp.int32, (groups, rows), 0)
    onehot = jnp.where((experts == route) & live, 1.0, 0.0).astype(BF16)
    before = lax.broadcasted_iota(jnp.int32, (rows, rows), 0)
    after = lax.broadcasted_iota(jnp.int32, (rows, rows), 1)
    upto = jnp.where(before <= after, 1.0, 0.0).astype(BF16)
    ranks = jnp.dot(onehot, upto, preferred_element_type=F32)
    rank = jnp.sum(ranks * onehot.astype(F32), axis=0, keepdims=True).astype(jnp.int32) - 1
    target = jnp.zeros_like(route)
    for e in range(groups):
        target = jnp.where(route == e, perm_ref[e], target)
    return jnp.where(live, target * capacity + rank, -1)


def selector_of(slot, slots):
    rows = slot.shape[1]
    places = lax.broadcasted_iota(jnp.int32, (slots, rows), 0)
    return jnp.where(places == slot, 1.0, 0.0).astype(BF16)


def pack_kernel(groups, live_ref, perm_ref, route_ref, fwd_route_ref, hidden_ref, out_ref, fwd_ref, packed_ref, slot_ref):
    rows, ff = hidden_ref.shape
    d = out_ref.shape[1]
    capacity = packed_ref.shape[0] // groups
    place = lax.broadcasted_iota(jnp.int32, (1, rows), 1)
    slot = slot_rows(route_ref[...], place < live_ref[0], groups, capacity, perm_ref)
    selector = selector_of(slot, groups * capacity)
    packed_ref[:, :ff] = jnp.dot(selector, hidden_ref[...], preferred_element_type=F32).astype(BF16)
    packed_ref[:, ff : ff + d] = jnp.dot(selector, out_ref[...], preferred_element_type=F32).astype(BF16)
    fwd_slot = slot_rows(fwd_route_ref[...], place >= 0, groups, capacity, perm_ref)
    slot_ref[...] = fwd_slot
    fwd_selector = selector_of(fwd_slot, groups * capacity)
    packed_ref[:, ff + d :] = jnp.dot(fwd_selector, fwd_ref[...], preferred_element_type=F32).astype(BF16)


def pack_rows(live_rows, perm, route, fwd_route, hidden, grad_out, fwd_hidden, groups, capacity):
    rows, ff = hidden.shape
    width = 2 * ff + grad_out.shape[1]
    return pl.pallas_call(
        functools.partial(pack_kernel, groups),
        out_shape=(
            jax.ShapeDtypeStruct((groups * capacity, width), BF16),
            jax.ShapeDtypeStruct((1, rows), jnp.int32),
        ),
        in_specs=[SMEM, SMEM] + [VMEM] * 5,
        out_specs=(VMEM, VMEM),
        compiler_params=pltpu.CompilerParams(vmem_limit_bytes=32 * MIB),
        cost_estimate=pl.CostEstimate(
            flops=2 * groups * capacity * rows * width, bytes_accessed=6 * rows * width, transcendentals=0
        ),
        name="pack_rows",
    )(live_rows, perm, route.reshape(1, rows), fwd_route.reshape(1, rows), hidden, grad_out, fwd_hidden)


def split_kernel(me_ref, moment_ref, weight_ref, *piece_refs):
    for s, piece in enumerate(piece_refs):
        rows, columns = piece.shape[1:]
        for lead, source in enumerate((moment_ref, weight_ref)):
            piece[lead] = chunk_at(source, 0, me_ref[0] ^ s, rows, columns)[...]


def split(me, moment, weight, groups):
    _, ff, d = weight.shape
    piece = jax.ShapeDtypeStruct((2, ff // (groups // 2), d // 2), BF16)
    return pl.pallas_call(
        split_kernel,
        out_shape=(piece,) * groups,
        in_specs=[SMEM, VMEM, VMEM],
        out_specs=(VMEM,) * groups,
        compiler_params=pltpu.CompilerParams(vmem_limit_bytes=32 * MIB),
        cost_estimate=pl.CostEstimate(flops=0, bytes_accessed=8 * ff * d, transcendentals=0),
        name="split",
    )(me, moment, weight)


def reorder_kernel(me_ref, perm_ref, *refs):
    groups = (len(refs) - 1) // 2
    sources, targets, held = refs[:groups], refs[groups : 2 * groups], refs[-1]
    me = me_ref[0]
    for s, source in enumerate(sources):
        held[me ^ perm_ref[me ^ s]] = source[...]
    for s, target in enumerate(targets):
        target[...] = held[s]


def reorder(me, perm, pieces):
    groups = len(pieces)
    piece = jax.ShapeDtypeStruct(pieces[0].shape, BF16)
    return pl.pallas_call(
        reorder_kernel,
        out_shape=(piece,) * groups,
        in_specs=[SMEM, SMEM] + [VMEM] * groups,
        out_specs=(VMEM,) * groups,
        scratch_shapes=[pltpu.VMEM((groups,) + pieces[0].shape, BF16)],
        compiler_params=pltpu.CompilerParams(vmem_limit_bytes=32 * MIB),
        cost_estimate=pl.CostEstimate(flops=0, bytes_accessed=4 * groups * pieces[0].size, transcendentals=0),
        name="reorder",
    )(me, perm, *pieces)


def update_kernel(groups, me_ref, packed_ref, *refs):
    pieces = refs[:groups]
    weight_new_ref, moment_new_ref, produced_ref, held = refs[groups:]
    _, ff, d = held.shape
    for s, piece in enumerate(pieces):
        rows, columns = piece.shape[1:]
        for lead in range(2):
            chunk_at(held, lead, me_ref[0] ^ s, rows, columns)[...] = piece[lead]
    grad = lax.dot_general(
        packed_ref[:, :ff], packed_ref[:, ff : ff + d], (((0,), (0,)), ((), ())), preferred_element_type=F32
    )
    moment_new = (moment_decay * held[0].astype(F32) + grad).astype(BF16)
    moment_new_ref[...] = moment_new
    moment_f = moment_new.astype(F32)
    frobenius = jnp.sqrt(jnp.sum(moment_f * moment_f))
    current = (moment_f / (frobenius + norm_floor)).astype(BF16)
    for _ in range(2):
        gramian = lax.dot_general(
            current, current, (((1,), (1,)), ((), ())), preferred_element_type=F32
        ).astype(BF16)
        squared = jnp.dot(gramian, gramian, preferred_element_type=F32)
        poly = (cubic_term * gramian.astype(F32) + quintic_term * squared).astype(BF16)
        current = (
            linear_term * current.astype(F32) + jnp.dot(poly, current, preferred_element_type=F32)
        ).astype(BF16)
    weight_new = (held[1].astype(F32) - step_scale * current.astype(F32)).astype(BF16)
    weight_new_ref[...] = weight_new
    produced_ref[...] = jnp.dot(packed_ref[:, ff + d :], weight_new, preferred_element_type=F32).astype(BF16)


def update(me, packed, pieces, ff, d):
    groups = len(pieces)
    slots = packed.shape[0]
    shape = jax.ShapeDtypeStruct((ff, d), BF16)
    return pl.pallas_call(
        functools.partial(update_kernel, groups),
        out_shape=(shape, shape, jax.ShapeDtypeStruct((slots, d), BF16)),
        in_specs=[SMEM] + [VMEM] * (1 + groups),
        out_specs=(VMEM,) * 3,
        scratch_shapes=[pltpu.VMEM((2, ff, d), BF16)],
        compiler_params=pltpu.CompilerParams(vmem_limit_bytes=48 * MIB),
        cost_estimate=pl.CostEstimate(
            flops=4 * ff * d * slots + 8 * ff * ff * d + 4 * ff**3,
            bytes_accessed=8 * ff * d + 2 * packed.size + 2 * slots * d,
            transcendentals=1,
        ),
        name="update",
    )(me, packed, *pieces)


def finish_kernel(slot_ref, gate_ref, returned_ref, out_ref):
    rows = slot_ref.shape[1]
    selector = selector_of(slot_ref[...], returned_ref.shape[0])
    expert_out = lax.dot_general(
        selector, returned_ref[...], (((0,), (0,)), ((), ())), preferred_element_type=F32
    )
    down = lax.broadcasted_iota(jnp.int32, (rows, rows), 0)
    across = lax.broadcasted_iota(jnp.int32, (rows, rows), 1)
    gate = jnp.sum(jnp.where(down == across, gate_ref[...], 0.0), axis=1, keepdims=True)
    out_ref[...] = (gate * expert_out).astype(BF16)


def finish(slot, gate, returned):
    rows = slot.shape[1]
    slots, d = returned.shape
    return pl.pallas_call(
        finish_kernel,
        out_shape=jax.ShapeDtypeStruct((rows, d), BF16),
        in_specs=[VMEM] * 3,
        out_specs=VMEM,
        compiler_params=pltpu.CompilerParams(vmem_limit_bytes=32 * MIB),
        cost_estimate=pl.CostEstimate(
            flops=2 * slots * rows * d, bytes_accessed=2 * d * (slots + rows), transcendentals=0
        ),
        name="finish",
    )(slot, gate.reshape(1, rows), returned)


def exchange(array):
    return lax.all_to_all(array, "expert", split_axis=0, concat_axis=0, tiled=True)


def swap(pieces):
    groups = len(pieces)
    moved = [
        lax.ppermute(pieces[s], "expert", [(i, i ^ s) for i in range(groups)]) for s in range(1, groups)
    ]
    return [pieces[0]] + moved


def partner_plan(
    grad_hidden, grad_out, grad_route, live_rows, w_down, w_moment, perm, fwd_hidden, fwd_route, fwd_gate
):
    groups = lax.axis_size("expert")
    me = lax.axis_index("expert").astype(jnp.int32).reshape(1)
    capacity = max(4, 2 * grad_hidden.shape[0] // groups)
    ff, d = w_down.shape[1:]
    spread = swap(split(me, w_moment, w_down, groups))
    packed, fwd_slot = pack_rows(
        live_rows, perm, grad_route, fwd_route, grad_hidden, grad_out, fwd_hidden, groups, capacity
    )
    received = exchange(packed.reshape(groups, capacity, -1)).reshape(groups * capacity, -1)
    placed = swap(reorder(me, perm, spread))
    weight_new, moment_new, produced = update(me, received, placed, ff, d)
    returned = exchange(produced.reshape(groups, capacity, d)).reshape(groups * capacity, d)
    return weight_new[None], moment_new[None], finish(fwd_slot, fwd_gate, returned)


def lookup(route_ids, mapping):
    columns = jnp.arange(mapping.shape[0], dtype=jnp.int32)
    hits = route_ids[:, None] == columns[None, :]
    return jnp.sum(jnp.where(hits, mapping[None, :], 0), axis=1)


def slot_matrix(target, is_live, groups, capacity):
    columns = jnp.arange(groups, dtype=jnp.int32)
    onehot = ((target[:, None] == columns[None, :]) & is_live[:, None]).astype(jnp.int32)
    ranked = jnp.sum(jnp.cumsum(onehot, axis=0) * onehot, axis=1) - 1
    slot_of = jnp.where(is_live, target * capacity + ranked, -1)
    slots = jnp.arange(groups * capacity, dtype=jnp.int32)
    return (slots[:, None] == slot_of[None, :]).astype(jnp.bfloat16)


def orthogonalize(moment):
    moment_f = moment.astype(jnp.float32)
    frobenius = jnp.sqrt(jnp.sum(moment_f * moment_f))
    current = (moment_f / (frobenius + norm_floor)).astype(jnp.bfloat16)
    for sweep_index in range(2):
        gramian = lax.dot_general(
            current, current, (((1,), (1,)), ((), ())), preferred_element_type=jnp.float32
        ).astype(jnp.bfloat16)
        squared = jnp.dot(gramian, gramian, preferred_element_type=jnp.float32)
        poly = (cubic_term * gramian.astype(jnp.float32) + quintic_term * squared).astype(
            jnp.bfloat16
        )
        current = (
            linear_term * current.astype(jnp.float32)
            + jnp.dot(poly, current, preferred_element_type=jnp.float32)
        ).astype(jnp.bfloat16)
    return current


def relocate(weight, moment, perm):
    groups = lax.axis_size("expert")
    weight_flat = weight.reshape(groups, -1)
    moment_flat = moment.reshape(groups, -1)
    spread_w, spread_m = (
        lax.all_to_all(weight_flat, "expert", split_axis=0, concat_axis=0, tiled=True),
        lax.all_to_all(moment_flat, "expert", split_axis=0, concat_axis=0, tiled=True),
    )
    devices = jnp.arange(groups, dtype=jnp.int32)
    inverse = jnp.sum(jnp.where(perm[None, :] == devices[:, None], devices[None, :], 0), axis=1)
    ordered_w = jnp.take(spread_w, inverse, axis=0)
    ordered_m = jnp.take(spread_m, inverse, axis=0)
    back_w, back_m = (
        lax.all_to_all(ordered_w, "expert", split_axis=0, concat_axis=0, tiled=True),
        lax.all_to_all(ordered_m, "expert", split_axis=0, concat_axis=0, tiled=True),
    )
    return (back_w.reshape(weight.shape), back_m.reshape(moment.shape))


def routed_plan(
    grad_hidden,
    grad_out,
    grad_route,
    live_rows,
    w_down,
    w_moment,
    perm,
    fwd_hidden,
    fwd_route,
    fwd_gate,
):
    groups = lax.axis_size("expert")
    grad_count = grad_hidden.shape[0]
    capacity = max(4, 2 * grad_count // groups)
    is_live = jnp.arange(grad_count, dtype=jnp.int32) < live_rows[0]
    route_ids = grad_route[:, 0]
    weight, moment = relocate(w_down, w_moment, perm)
    target = lookup(route_ids, perm)
    selector = slot_matrix(target, is_live, groups, capacity)
    hidden_buf = (
        jnp.dot(selector, grad_hidden, preferred_element_type=jnp.float32)
        .astype(jnp.bfloat16)
        .reshape(groups, capacity, -1)
    )
    outgrad_buf = (
        jnp.dot(selector, grad_out, preferred_element_type=jnp.float32)
        .astype(jnp.bfloat16)
        .reshape(groups, capacity, -1)
    )
    recv_hidden, recv_outgrad = (
        lax.all_to_all(hidden_buf, "expert", split_axis=0, concat_axis=0, tiled=True),
        lax.all_to_all(outgrad_buf, "expert", split_axis=0, concat_axis=0, tiled=True),
    )
    grad = lax.dot_general(
        recv_hidden.reshape(groups * capacity, -1),
        recv_outgrad.reshape(groups * capacity, -1),
        (((0,), (0,)), ((), ())),
        preferred_element_type=jnp.float32,
    )
    moment_new = (moment_decay * moment[0].astype(jnp.float32) + grad).astype(jnp.bfloat16)
    ortho = orthogonalize(moment_new)
    weight_new = (weight[0].astype(jnp.float32) - step_scale * ortho.astype(jnp.float32)).astype(
        jnp.bfloat16
    )
    weight_new = weight_new[None]
    moment_new = moment_new[None]
    fwd_ids = fwd_route[:, 0]
    placed_weight, placed_moment = (weight_new, moment_new)
    fwd_target = lookup(fwd_ids, perm)
    fwd_weight = weight_new[0]
    fwd_count = fwd_hidden.shape[0]
    fwd_capacity = max(4, 2 * fwd_count // groups)
    fwd_selector = slot_matrix(fwd_target, jnp.ones((fwd_count,), dtype=bool), groups, fwd_capacity)
    fwd_buf = (
        jnp.dot(fwd_selector, fwd_hidden, preferred_element_type=jnp.float32)
        .astype(jnp.bfloat16)
        .reshape(groups, fwd_capacity, -1)
    )
    produced = jnp.einsum(
        "gkf,fd->gkd",
        lax.all_to_all(fwd_buf, "expert", split_axis=0, concat_axis=0, tiled=True),
        fwd_weight,
        preferred_element_type=jnp.float32,
    ).astype(jnp.bfloat16)
    returned = lax.all_to_all(produced, "expert", split_axis=0, concat_axis=0, tiled=True)
    fwd_rows_out = lax.dot_general(
        fwd_selector,
        returned.reshape(groups * fwd_capacity, -1),
        (((0,), (0,)), ((), ())),
        preferred_element_type=jnp.float32,
    )
    fwd_out = (fwd_rows_out * fwd_gate[:, None]).astype(jnp.bfloat16)
    return (placed_weight, placed_moment, fwd_out)


def solution(mesh):
    groups = mesh.shape["expert"]
    in_specs = (
        P(("layer", "expert"), None),
        P(("layer", "expert"), None),
        P(("layer", "expert"), None),
        P(("layer", "expert")),
        P(("layer", "expert"), None, None),
        P(("layer", "expert"), None, None),
        P("layer"),
        P(("layer", "expert"), None),
        P(("layer", "expert"), None),
        P(("layer", "expert")),
    )
    out_specs = (
        P(("layer", "expert"), None, None),
        P(("layer", "expert"), None, None),
        P(("layer", "expert"), None),
    )

    def per_device(*args):
        few = groups & (groups - 1) == 0 and groups <= 2 * args[0].shape[0] // groups
        return (partner_plan if few else routed_plan)(*args)

    return jax.shard_map(
        per_device, mesh=mesh, in_specs=in_specs, out_specs=out_specs, check_vma=False
    )
```

```python
import functools

import jax
import jax.numpy as jnp
from jax import lax
from jax.experimental import pallas as pl
from jax.experimental.pallas import tpu as pltpu
from jax.sharding import PartitionSpec as P

linear_term = 3.4445
cubic_term = -4.775
quintic_term = 2.0315
moment_decay = 0.9
step_scale = 0.25
norm_floor = 1e-07

F32 = jnp.float32
BF16 = jnp.bfloat16
HBM = pl.BlockSpec(memory_space=pltpu.HBM)
VMEM = pl.BlockSpec(memory_space=pltpu.VMEM)
SMEM = pl.BlockSpec(memory_space=pltpu.SMEM)
ANY = pl.BlockSpec(memory_space=pl.ANY)
MIB = 1 << 20


def fetched(refs, held, sem):
    copies = [pltpu.make_async_copy(ref, room, sem.at[n]) for n, (ref, room) in enumerate(zip(refs, held))]
    for copy in copies:
        copy.start()
    for copy in copies:
        copy.wait()


def rooms(arrays):
    return [pltpu.VMEM(a.shape, a.dtype) for a in arrays] + [pltpu.SemaphoreType.DMA((len(arrays),))]


def chunk_at(ref, lead, k, rows, columns):
    return ref.at[
        lead,
        pl.ds(pl.multiple_of((k // 2) * rows, rows), rows),
        pl.ds(pl.multiple_of((k % 2) * columns, columns), columns),
    ]


def slot_rows(route, live, groups, capacity, perm_ref):
    rows = route.shape[1]
    experts = lax.broadcasted_iota(jnp.int32, (groups, rows), 0)
    onehot = jnp.where((experts == route) & live, 1.0, 0.0).astype(BF16)
    before = lax.broadcasted_iota(jnp.int32, (rows, rows), 0)
    after = lax.broadcasted_iota(jnp.int32, (rows, rows), 1)
    upto = jnp.where(before <= after, 1.0, 0.0).astype(BF16)
    ranks = jnp.dot(onehot, upto, preferred_element_type=F32)
    rank = jnp.sum(ranks * onehot.astype(F32), axis=0, keepdims=True).astype(jnp.int32) - 1
    target = jnp.zeros_like(route)
    for e in range(groups):
        target = jnp.where(route == e, perm_ref[e], target)
    return jnp.where(live, target * capacity + rank, -1)


def selector_of(slot, slots):
    rows = slot.shape[1]
    places = lax.broadcasted_iota(jnp.int32, (slots, rows), 0)
    return jnp.where(places == slot, 1.0, 0.0).astype(BF16)


def pack_kernel(groups, live_ref, perm_ref, *refs):
    sources, (packed_ref, slot_ref), held, sem = refs[:5], refs[5:7], refs[7:12], refs[12]
    fetched(sources, held, sem)
    route_ref, fwd_route_ref, hidden_ref, out_ref, fwd_ref = held
    rows, ff = hidden_ref.shape
    d = out_ref.shape[1]
    capacity = packed_ref.shape[0] // groups
    place = lax.broadcasted_iota(jnp.int32, (1, rows), 1)
    slot = slot_rows(route_ref[...], place < live_ref[0], groups, capacity, perm_ref)
    selector = selector_of(slot, groups * capacity)
    packed_ref[:, :ff] = jnp.dot(selector, hidden_ref[...], preferred_element_type=F32).astype(BF16)
    packed_ref[:, ff : ff + d] = jnp.dot(selector, out_ref[...], preferred_element_type=F32).astype(BF16)
    fwd_slot = slot_rows(fwd_route_ref[...], place >= 0, groups, capacity, perm_ref)
    slot_ref[...] = fwd_slot
    fwd_selector = selector_of(fwd_slot, groups * capacity)
    packed_ref[:, ff + d :] = jnp.dot(fwd_selector, fwd_ref[...], preferred_element_type=F32).astype(BF16)


def pack_rows(live_rows, perm, route, fwd_route, hidden, grad_out, fwd_hidden, groups, capacity):
    rows, ff = hidden.shape
    width = 2 * ff + grad_out.shape[1]
    sources = (route.reshape(1, rows), fwd_route.reshape(1, rows), hidden, grad_out, fwd_hidden)
    return pl.pallas_call(
        functools.partial(pack_kernel, groups),
        out_shape=(
            jax.ShapeDtypeStruct((groups * capacity, width), BF16),
            jax.ShapeDtypeStruct((1, rows), jnp.int32),
        ),
        in_specs=[SMEM, SMEM] + [HBM] * 5,
        out_specs=(VMEM, VMEM),
        scratch_shapes=rooms(sources),
        compiler_params=pltpu.CompilerParams(vmem_limit_bytes=32 * MIB),
        cost_estimate=pl.CostEstimate(
            flops=2 * groups * capacity * rows * width, bytes_accessed=6 * rows * width, transcendentals=0
        ),
        name="pack_rows",
    )(live_rows, perm, *sources)


def split_kernel(me_ref, moment_ref, weight_ref, *refs):
    pieces, held, sem = refs[:-3], refs[-3:-1], refs[-1]
    fetched((moment_ref, weight_ref), held, sem)
    for s, piece in enumerate(pieces):
        rows, columns = piece.shape[1:]
        for lead, source in enumerate(held):
            piece[lead] = chunk_at(source, 0, me_ref[0] ^ s, rows, columns)[...]


def split(me, moment, weight, groups):
    _, ff, d = weight.shape
    piece = jax.ShapeDtypeStruct((2, ff // (groups // 2), d // 2), BF16)
    return pl.pallas_call(
        split_kernel,
        out_shape=(piece,) * groups,
        in_specs=[SMEM, HBM, HBM],
        out_specs=(VMEM,) * groups,
        scratch_shapes=rooms((moment, weight)),
        compiler_params=pltpu.CompilerParams(vmem_limit_bytes=32 * MIB),
        cost_estimate=pl.CostEstimate(flops=0, bytes_accessed=8 * ff * d, transcendentals=0),
        name="split",
    )(me, moment, weight)


def reorder_kernel(me_ref, perm_ref, *refs):
    groups = (len(refs) - 1) // 2
    sources, targets, held = refs[:groups], refs[groups : 2 * groups], refs[-1]
    me = me_ref[0]
    for s, source in enumerate(sources):
        held[me ^ perm_ref[me ^ s]] = source[...]
    for s, target in enumerate(targets):
        target[...] = held[s]


def reorder(me, perm, pieces):
    groups = len(pieces)
    piece = jax.ShapeDtypeStruct(pieces[0].shape, BF16)
    return pl.pallas_call(
        reorder_kernel,
        out_shape=(piece,) * groups,
        in_specs=[SMEM, SMEM] + [VMEM] * groups,
        out_specs=(VMEM,) * groups,
        scratch_shapes=[pltpu.VMEM((groups,) + pieces[0].shape, BF16)],
        compiler_params=pltpu.CompilerParams(vmem_limit_bytes=32 * MIB),
        cost_estimate=pl.CostEstimate(flops=0, bytes_accessed=4 * groups * pieces[0].size, transcendentals=0),
        name="reorder",
    )(me, perm, *pieces)


def update_kernel(groups, me_ref, packed_ref, *refs):
    pieces = refs[:groups]
    weight_new_ref, moment_new_ref, produced_ref, held = refs[groups:]
    _, ff, d = held.shape
    for s, piece in enumerate(pieces):
        rows, columns = piece.shape[1:]
        for lead in range(2):
            chunk_at(held, lead, me_ref[0] ^ s, rows, columns)[...] = piece[lead]
    grad = lax.dot_general(
        packed_ref[:, :ff], packed_ref[:, ff : ff + d], (((0,), (0,)), ((), ())), preferred_element_type=F32
    )
    moment_new = (moment_decay * held[0].astype(F32) + grad).astype(BF16)
    moment_new_ref[...] = moment_new
    moment_f = moment_new.astype(F32)
    frobenius = jnp.sqrt(jnp.sum(moment_f * moment_f))
    current = (moment_f / (frobenius + norm_floor)).astype(BF16)
    for _ in range(2):
        gramian = lax.dot_general(
            current, current, (((1,), (1,)), ((), ())), preferred_element_type=F32
        ).astype(BF16)
        squared = jnp.dot(gramian, gramian, preferred_element_type=F32)
        poly = (cubic_term * gramian.astype(F32) + quintic_term * squared).astype(BF16)
        current = (
            linear_term * current.astype(F32) + jnp.dot(poly, current, preferred_element_type=F32)
        ).astype(BF16)
    weight_new = (held[1].astype(F32) - step_scale * current.astype(F32)).astype(BF16)
    weight_new_ref[...] = weight_new
    produced_ref[...] = jnp.dot(packed_ref[:, ff + d :], weight_new, preferred_element_type=F32).astype(BF16)


def update(me, packed, pieces, ff, d):
    groups = len(pieces)
    slots = packed.shape[0]
    shape = jax.ShapeDtypeStruct((ff, d), BF16)
    return pl.pallas_call(
        functools.partial(update_kernel, groups),
        out_shape=(shape, shape, jax.ShapeDtypeStruct((slots, d), BF16)),
        in_specs=[SMEM] + [VMEM] * (1 + groups),
        out_specs=(VMEM,) * 3,
        scratch_shapes=[pltpu.VMEM((2, ff, d), BF16)],
        compiler_params=pltpu.CompilerParams(vmem_limit_bytes=48 * MIB),
        cost_estimate=pl.CostEstimate(
            flops=4 * ff * d * slots + 8 * ff * ff * d + 4 * ff**3,
            bytes_accessed=8 * ff * d + 2 * packed.size + 2 * slots * d,
            transcendentals=1,
        ),
        name="update",
    )(me, packed, *pieces)


def finish_kernel(slot_ref, gate_ref, returned_ref, out_ref):
    rows = slot_ref.shape[1]
    selector = selector_of(slot_ref[...], returned_ref.shape[0])
    expert_out = lax.dot_general(
        selector, returned_ref[...], (((0,), (0,)), ((), ())), preferred_element_type=F32
    )
    down = lax.broadcasted_iota(jnp.int32, (rows, rows), 0)
    across = lax.broadcasted_iota(jnp.int32, (rows, rows), 1)
    gate = jnp.sum(jnp.where(down == across, gate_ref[...], 0.0), axis=1, keepdims=True)
    out_ref[...] = (gate * expert_out).astype(BF16)


def finish(slot, gate, returned):
    rows = slot.shape[1]
    slots, d = returned.shape
    return pl.pallas_call(
        finish_kernel,
        out_shape=jax.ShapeDtypeStruct((rows, d), BF16),
        in_specs=[VMEM] * 3,
        out_specs=VMEM,
        compiler_params=pltpu.CompilerParams(vmem_limit_bytes=32 * MIB),
        cost_estimate=pl.CostEstimate(
            flops=2 * slots * rows * d, bytes_accessed=2 * d * (slots + rows), transcendentals=0
        ),
        name="finish",
    )(slot, gate.reshape(1, rows), returned)


def exchange(array):
    return lax.all_to_all(array, "expert", split_axis=0, concat_axis=0, tiled=True)


def mixed_order(groups):
    far, near = list(range(groups // 2, groups)), list(range(groups // 2 - 1, 0, -1))
    return [s for pair in zip(far, near + [None]) for s in pair if s is not None]


def swap(pieces):
    groups = len(pieces)
    moved = {0: pieces[0]}
    for s in mixed_order(groups):
        moved[s] = lax.ppermute(pieces[s], "expert", [(i, i ^ s) for i in range(groups)])
    return [moved[s] for s in range(groups)]


def partner_plan(
    grad_hidden, grad_out, grad_route, live_rows, w_down, w_moment, perm, fwd_hidden, fwd_route, fwd_gate
):
    groups = lax.axis_size("expert")
    me = lax.axis_index("expert").astype(jnp.int32).reshape(1)
    capacity = max(4, 2 * grad_hidden.shape[0] // groups)
    ff, d = w_down.shape[1:]
    spread = swap(split(me, w_moment, w_down, groups))
    packed, fwd_slot = pack_rows(
        live_rows, perm, grad_route, fwd_route, grad_hidden, grad_out, fwd_hidden, groups, capacity
    )
    received = exchange(packed.reshape(groups, capacity, -1)).reshape(groups * capacity, -1)
    placed = swap(reorder(me, perm, spread))
    weight_new, moment_new, produced = update(me, received, placed, ff, d)
    returned = exchange(produced.reshape(groups, capacity, d)).reshape(groups * capacity, d)
    return weight_new[None], moment_new[None], finish(fwd_slot, fwd_gate, returned)


def lookup(route_ids, mapping):
    columns = jnp.arange(mapping.shape[0], dtype=jnp.int32)
    hits = route_ids[:, None] == columns[None, :]
    return jnp.sum(jnp.where(hits, mapping[None, :], 0), axis=1)


def slot_matrix(target, is_live, groups, capacity):
    columns = jnp.arange(groups, dtype=jnp.int32)
    onehot = ((target[:, None] == columns[None, :]) & is_live[:, None]).astype(jnp.int32)
    ranked = jnp.sum(jnp.cumsum(onehot, axis=0) * onehot, axis=1) - 1
    slot_of = jnp.where(is_live, target * capacity + ranked, -1)
    slots = jnp.arange(groups * capacity, dtype=jnp.int32)
    return (slots[:, None] == slot_of[None, :]).astype(jnp.bfloat16)


def orthogonalize(moment):
    moment_f = moment.astype(jnp.float32)
    frobenius = jnp.sqrt(jnp.sum(moment_f * moment_f))
    current = (moment_f / (frobenius + norm_floor)).astype(jnp.bfloat16)
    for sweep_index in range(2):
        gramian = lax.dot_general(
            current, current, (((1,), (1,)), ((), ())), preferred_element_type=jnp.float32
        ).astype(jnp.bfloat16)
        squared = jnp.dot(gramian, gramian, preferred_element_type=jnp.float32)
        poly = (cubic_term * gramian.astype(jnp.float32) + quintic_term * squared).astype(
            jnp.bfloat16
        )
        current = (
            linear_term * current.astype(jnp.float32)
            + jnp.dot(poly, current, preferred_element_type=jnp.float32)
        ).astype(jnp.bfloat16)
    return current


def relocate(weight, moment, perm):
    groups = lax.axis_size("expert")
    weight_flat = weight.reshape(groups, -1)
    moment_flat = moment.reshape(groups, -1)
    spread_w, spread_m = (
        lax.all_to_all(weight_flat, "expert", split_axis=0, concat_axis=0, tiled=True),
        lax.all_to_all(moment_flat, "expert", split_axis=0, concat_axis=0, tiled=True),
    )
    devices = jnp.arange(groups, dtype=jnp.int32)
    inverse = jnp.sum(jnp.where(perm[None, :] == devices[:, None], devices[None, :], 0), axis=1)
    ordered_w = jnp.take(spread_w, inverse, axis=0)
    ordered_m = jnp.take(spread_m, inverse, axis=0)
    back_w, back_m = (
        lax.all_to_all(ordered_w, "expert", split_axis=0, concat_axis=0, tiled=True),
        lax.all_to_all(ordered_m, "expert", split_axis=0, concat_axis=0, tiled=True),
    )
    return (back_w.reshape(weight.shape), back_m.reshape(moment.shape))


def routed_plan(
    grad_hidden,
    grad_out,
    grad_route,
    live_rows,
    w_down,
    w_moment,
    perm,
    fwd_hidden,
    fwd_route,
    fwd_gate,
):
    groups = lax.axis_size("expert")
    grad_count = grad_hidden.shape[0]
    capacity = max(4, 2 * grad_count // groups)
    is_live = jnp.arange(grad_count, dtype=jnp.int32) < live_rows[0]
    route_ids = grad_route[:, 0]
    weight, moment = relocate(w_down, w_moment, perm)
    target = lookup(route_ids, perm)
    selector = slot_matrix(target, is_live, groups, capacity)
    hidden_buf = (
        jnp.dot(selector, grad_hidden, preferred_element_type=jnp.float32)
        .astype(jnp.bfloat16)
        .reshape(groups, capacity, -1)
    )
    outgrad_buf = (
        jnp.dot(selector, grad_out, preferred_element_type=jnp.float32)
        .astype(jnp.bfloat16)
        .reshape(groups, capacity, -1)
    )
    recv_hidden, recv_outgrad = (
        lax.all_to_all(hidden_buf, "expert", split_axis=0, concat_axis=0, tiled=True),
        lax.all_to_all(outgrad_buf, "expert", split_axis=0, concat_axis=0, tiled=True),
    )
    grad = lax.dot_general(
        recv_hidden.reshape(groups * capacity, -1),
        recv_outgrad.reshape(groups * capacity, -1),
        (((0,), (0,)), ((), ())),
        preferred_element_type=jnp.float32,
    )
    moment_new = (moment_decay * moment[0].astype(jnp.float32) + grad).astype(jnp.bfloat16)
    ortho = orthogonalize(moment_new)
    weight_new = (weight[0].astype(jnp.float32) - step_scale * ortho.astype(jnp.float32)).astype(
        jnp.bfloat16
    )
    weight_new = weight_new[None]
    moment_new = moment_new[None]
    fwd_ids = fwd_route[:, 0]
    placed_weight, placed_moment = (weight_new, moment_new)
    fwd_target = lookup(fwd_ids, perm)
    fwd_weight = weight_new[0]
    fwd_count = fwd_hidden.shape[0]
    fwd_capacity = max(4, 2 * fwd_count // groups)
    fwd_selector = slot_matrix(fwd_target, jnp.ones((fwd_count,), dtype=bool), groups, fwd_capacity)
    fwd_buf = (
        jnp.dot(fwd_selector, fwd_hidden, preferred_element_type=jnp.float32)
        .astype(jnp.bfloat16)
        .reshape(groups, fwd_capacity, -1)
    )
    produced = jnp.einsum(
        "gkf,fd->gkd",
        lax.all_to_all(fwd_buf, "expert", split_axis=0, concat_axis=0, tiled=True),
        fwd_weight,
        preferred_element_type=jnp.float32,
    ).astype(jnp.bfloat16)
    returned = lax.all_to_all(produced, "expert", split_axis=0, concat_axis=0, tiled=True)
    fwd_rows_out = lax.dot_general(
        fwd_selector,
        returned.reshape(groups * fwd_capacity, -1),
        (((0,), (0,)), ((), ())),
        preferred_element_type=jnp.float32,
    )
    fwd_out = (fwd_rows_out * fwd_gate[:, None]).astype(jnp.bfloat16)
    return (placed_weight, placed_moment, fwd_out)


def solution(mesh):
    groups = mesh.shape["expert"]
    in_specs = (
        P(("layer", "expert"), None),
        P(("layer", "expert"), None),
        P(("layer", "expert"), None),
        P(("layer", "expert")),
        P(("layer", "expert"), None, None),
        P(("layer", "expert"), None, None),
        P("layer"),
        P(("layer", "expert"), None),
        P(("layer", "expert"), None),
        P(("layer", "expert")),
    )
    out_specs = (
        P(("layer", "expert"), None, None),
        P(("layer", "expert"), None, None),
        P(("layer", "expert"), None),
    )

    def per_device(*args):
        few = groups & (groups - 1) == 0 and groups <= 2 * args[0].shape[0] // groups
        return (partner_plan if few else routed_plan)(*args)

    return jax.shard_map(
        per_device, mesh=mesh, in_specs=in_specs, out_specs=out_specs, check_vma=False
    )
```

```python
import functools

import jax
import jax.numpy as jnp
from jax import lax
from jax.experimental import pallas as pl
from jax.experimental.pallas import tpu as pltpu
from jax.sharding import PartitionSpec as P

linear_term = 3.4445
cubic_term = -4.775
quintic_term = 2.0315
moment_decay = 0.9
step_scale = 0.25
norm_floor = 1e-07

F32 = jnp.float32
BF16 = jnp.bfloat16
HBM = pl.BlockSpec(memory_space=pltpu.HBM)
VMEM = pl.BlockSpec(memory_space=pltpu.VMEM)
SMEM = pl.BlockSpec(memory_space=pltpu.SMEM)
ANY = pl.BlockSpec(memory_space=pl.ANY)
MIB = 1 << 20


def fetched(refs, held, sem):
    copies = [pltpu.make_async_copy(ref, room, sem.at[n]) for n, (ref, room) in enumerate(zip(refs, held))]
    for copy in copies:
        copy.start()
    for copy in copies:
        copy.wait()


def rooms(arrays):
    return [pltpu.VMEM(a.shape, a.dtype) for a in arrays] + [pltpu.SemaphoreType.DMA((len(arrays),))]


def chunk_at(ref, lead, k, rows, columns):
    return ref.at[
        lead,
        pl.ds(pl.multiple_of((k // 2) * rows, rows), rows),
        pl.ds(pl.multiple_of((k % 2) * columns, columns), columns),
    ]


def slot_rows(route, live, groups, capacity, perm_ref):
    rows = route.shape[1]
    experts = lax.broadcasted_iota(jnp.int32, (groups, rows), 0)
    onehot = jnp.where((experts == route) & live, 1.0, 0.0).astype(BF16)
    before = lax.broadcasted_iota(jnp.int32, (rows, rows), 0)
    after = lax.broadcasted_iota(jnp.int32, (rows, rows), 1)
    upto = jnp.where(before <= after, 1.0, 0.0).astype(BF16)
    ranks = jnp.dot(onehot, upto, preferred_element_type=F32)
    rank = jnp.sum(ranks * onehot.astype(F32), axis=0, keepdims=True).astype(jnp.int32) - 1
    target = jnp.zeros_like(route)
    for e in range(groups):
        target = jnp.where(route == e, perm_ref[e], target)
    return jnp.where(live, target * capacity + rank, -1)


def selector_of(slot, slots):
    rows = slot.shape[1]
    places = lax.broadcasted_iota(jnp.int32, (slots, rows), 0)
    return jnp.where(places == slot, 1.0, 0.0).astype(BF16)


def pack_kernel(groups, live_ref, perm_ref, *refs):
    sources, (packed_ref, slot_ref), held, sem = refs[:5], refs[5:7], refs[7:12], refs[12]
    fetched(sources, held, sem)
    route_ref, fwd_route_ref, hidden_ref, out_ref, fwd_ref = held
    rows, ff = hidden_ref.shape
    d = out_ref.shape[1]
    capacity = packed_ref.shape[0] // groups
    place = lax.broadcasted_iota(jnp.int32, (1, rows), 1)
    slot = slot_rows(route_ref[...], place < live_ref[0], groups, capacity, perm_ref)
    selector = selector_of(slot, groups * capacity)
    packed_ref[:, :ff] = jnp.dot(selector, hidden_ref[...], preferred_element_type=F32).astype(BF16)
    packed_ref[:, ff : ff + d] = jnp.dot(selector, out_ref[...], preferred_element_type=F32).astype(BF16)
    fwd_slot = slot_rows(fwd_route_ref[...], place >= 0, groups, capacity, perm_ref)
    slot_ref[...] = fwd_slot
    fwd_selector = selector_of(fwd_slot, groups * capacity)
    packed_ref[:, ff + d :] = jnp.dot(fwd_selector, fwd_ref[...], preferred_element_type=F32).astype(BF16)


def pack_rows(live_rows, perm, route, fwd_route, hidden, grad_out, fwd_hidden, groups, capacity):
    rows, ff = hidden.shape
    width = 2 * ff + grad_out.shape[1]
    sources = (route.reshape(1, rows), fwd_route.reshape(1, rows), hidden, grad_out, fwd_hidden)
    return pl.pallas_call(
        functools.partial(pack_kernel, groups),
        out_shape=(
            jax.ShapeDtypeStruct((groups * capacity, width), BF16),
            jax.ShapeDtypeStruct((1, rows), jnp.int32),
        ),
        in_specs=[SMEM, SMEM] + [HBM] * 5,
        out_specs=(VMEM, VMEM),
        scratch_shapes=rooms(sources),
        compiler_params=pltpu.CompilerParams(vmem_limit_bytes=60 * MIB),
        cost_estimate=pl.CostEstimate(
            flops=2 * groups * capacity * rows * width, bytes_accessed=6 * rows * width, transcendentals=0
        ),
        name="pack_rows",
    )(live_rows, perm, *sources)


def split_kernel(me_ref, moment_ref, weight_ref, *refs):
    pieces, held, sem = refs[:-3], refs[-3:-1], refs[-1]
    fetched((moment_ref, weight_ref), held, sem)
    for s, piece in zip(mixed_order(len(pieces)), pieces):
        rows, columns = piece.shape[1:]
        for lead, source in enumerate(held):
            piece[lead] = chunk_at(source, 0, me_ref[0] ^ s, rows, columns)[...]


def split(me, moment, weight, groups):
    _, ff, d = weight.shape
    piece = jax.ShapeDtypeStruct((2, ff // (groups // 2), d // 2), BF16)
    return pl.pallas_call(
        split_kernel,
        out_shape=(piece,) * groups,
        in_specs=[SMEM, HBM, HBM],
        out_specs=(VMEM,) * groups,
        scratch_shapes=rooms((moment, weight)),
        compiler_params=pltpu.CompilerParams(vmem_limit_bytes=60 * MIB),
        cost_estimate=pl.CostEstimate(flops=0, bytes_accessed=8 * ff * d, transcendentals=0),
        name="split",
    )(me, moment, weight)


def reorder_kernel(me_ref, perm_ref, *refs):
    groups = (len(refs) - 1) // 2
    sources, targets, held = refs[:groups], refs[groups : 2 * groups], refs[-1]
    me, order = me_ref[0], mixed_order(groups)
    for s, source in zip(order, sources):
        held[me ^ perm_ref[me ^ s]] = source[...]
    for s, target in zip(order, targets):
        target[...] = held[s]


def reorder(me, perm, pieces):
    groups = len(pieces)
    piece = jax.ShapeDtypeStruct(pieces[0].shape, BF16)
    return pl.pallas_call(
        reorder_kernel,
        out_shape=(piece,) * groups,
        in_specs=[SMEM, SMEM] + [VMEM] * groups,
        out_specs=(VMEM,) * groups,
        scratch_shapes=[pltpu.VMEM((groups,) + pieces[0].shape, BF16)],
        compiler_params=pltpu.CompilerParams(vmem_limit_bytes=32 * MIB),
        cost_estimate=pl.CostEstimate(flops=0, bytes_accessed=4 * groups * pieces[0].size, transcendentals=0),
        name="reorder",
    )(me, perm, *pieces)


def update_kernel(groups, me_ref, packed_ref, *refs):
    pieces = refs[:groups]
    weight_new_ref, moment_new_ref, produced_ref, held = refs[groups:]
    _, ff, d = held.shape
    for s, piece in zip(mixed_order(groups), pieces):
        rows, columns = piece.shape[1:]
        for lead in range(2):
            chunk_at(held, lead, me_ref[0] ^ s, rows, columns)[...] = piece[lead]
    grad = lax.dot_general(
        packed_ref[:, :ff], packed_ref[:, ff : ff + d], (((0,), (0,)), ((), ())), preferred_element_type=F32
    )
    moment_new = (moment_decay * held[0].astype(F32) + grad).astype(BF16)
    moment_new_ref[...] = moment_new
    moment_f = moment_new.astype(F32)
    frobenius = jnp.sqrt(jnp.sum(moment_f * moment_f))
    current = (moment_f / (frobenius + norm_floor)).astype(BF16)
    for _ in range(2):
        gramian = lax.dot_general(
            current, current, (((1,), (1,)), ((), ())), preferred_element_type=F32
        ).astype(BF16)
        squared = jnp.dot(gramian, gramian, preferred_element_type=F32)
        poly = (cubic_term * gramian.astype(F32) + quintic_term * squared).astype(BF16)
        current = (
            linear_term * current.astype(F32) + jnp.dot(poly, current, preferred_element_type=F32)
        ).astype(BF16)
    weight_new = (held[1].astype(F32) - step_scale * current.astype(F32)).astype(BF16)
    weight_new_ref[...] = weight_new
    produced_ref[...] = jnp.dot(packed_ref[:, ff + d :], weight_new, preferred_element_type=F32).astype(BF16)


def update(me, packed, pieces, ff, d):
    groups = len(pieces)
    slots = packed.shape[0]
    shape = jax.ShapeDtypeStruct((ff, d), BF16)
    return pl.pallas_call(
        functools.partial(update_kernel, groups),
        out_shape=(shape, shape, jax.ShapeDtypeStruct((slots, d), BF16)),
        in_specs=[SMEM] + [VMEM] * (1 + groups),
        out_specs=(VMEM,) * 3,
        scratch_shapes=[pltpu.VMEM((2, ff, d), BF16)],
        compiler_params=pltpu.CompilerParams(vmem_limit_bytes=48 * MIB),
        cost_estimate=pl.CostEstimate(
            flops=4 * ff * d * slots + 8 * ff * ff * d + 4 * ff**3,
            bytes_accessed=8 * ff * d + 2 * packed.size + 2 * slots * d,
            transcendentals=1,
        ),
        name="update",
    )(me, packed, *pieces)


def finish_kernel(slot_ref, gate_ref, returned_ref, out_ref):
    rows = slot_ref.shape[1]
    selector = selector_of(slot_ref[...], returned_ref.shape[0])
    expert_out = lax.dot_general(
        selector, returned_ref[...], (((0,), (0,)), ((), ())), preferred_element_type=F32
    )
    down = lax.broadcasted_iota(jnp.int32, (rows, rows), 0)
    across = lax.broadcasted_iota(jnp.int32, (rows, rows), 1)
    gate = jnp.sum(jnp.where(down == across, gate_ref[...], 0.0), axis=1, keepdims=True)
    out_ref[...] = (gate * expert_out).astype(BF16)


def finish(slot, gate, returned):
    rows = slot.shape[1]
    slots, d = returned.shape
    return pl.pallas_call(
        finish_kernel,
        out_shape=jax.ShapeDtypeStruct((rows, d), BF16),
        in_specs=[VMEM] * 3,
        out_specs=VMEM,
        compiler_params=pltpu.CompilerParams(vmem_limit_bytes=32 * MIB),
        cost_estimate=pl.CostEstimate(
            flops=2 * slots * rows * d, bytes_accessed=2 * d * (slots + rows), transcendentals=0
        ),
        name="finish",
    )(slot, gate.reshape(1, rows), returned)


def exchange(array):
    return lax.all_to_all(array, "expert", split_axis=0, concat_axis=0, tiled=True)


def mixed_order(groups):
    far, near = list(range(groups // 2, groups)), list(range(groups // 2 - 1, 0, -1))
    return [0] + [s for pair in zip(far, near + [None]) for s in pair if s is not None]


def swap(pieces):
    groups = len(pieces)
    order = mixed_order(groups)
    return [pieces[0]] + [
        lax.ppermute(piece, "expert", [(i, i ^ s) for i in range(groups)]) for s, piece in zip(order[1:], pieces[1:])
    ]


def partner_plan(
    grad_hidden, grad_out, grad_route, live_rows, w_down, w_moment, perm, fwd_hidden, fwd_route, fwd_gate
):
    groups = lax.axis_size("expert")
    me = lax.axis_index("expert").astype(jnp.int32).reshape(1)
    capacity = max(4, 2 * grad_hidden.shape[0] // groups)
    ff, d = w_down.shape[1:]
    spread = swap(split(me, w_moment, w_down, groups))
    packed, fwd_slot = pack_rows(
        live_rows, perm, grad_route, fwd_route, grad_hidden, grad_out, fwd_hidden, groups, capacity
    )
    received = exchange(packed.reshape(groups, capacity, -1)).reshape(groups * capacity, -1)
    placed = swap(reorder(me, perm, spread))
    weight_new, moment_new, produced = update(me, received, placed, ff, d)
    returned = exchange(produced.reshape(groups, capacity, d)).reshape(groups * capacity, d)
    return weight_new[None], moment_new[None], finish(fwd_slot, fwd_gate, returned)


def lookup(route_ids, mapping):
    columns = jnp.arange(mapping.shape[0], dtype=jnp.int32)
    hits = route_ids[:, None] == columns[None, :]
    return jnp.sum(jnp.where(hits, mapping[None, :], 0), axis=1)


def slot_matrix(target, is_live, groups, capacity):
    columns = jnp.arange(groups, dtype=jnp.int32)
    onehot = ((target[:, None] == columns[None, :]) & is_live[:, None]).astype(jnp.int32)
    ranked = jnp.sum(jnp.cumsum(onehot, axis=0) * onehot, axis=1) - 1
    slot_of = jnp.where(is_live, target * capacity + ranked, -1)
    slots = jnp.arange(groups * capacity, dtype=jnp.int32)
    return (slots[:, None] == slot_of[None, :]).astype(jnp.bfloat16)


def orthogonalize(moment):
    moment_f = moment.astype(jnp.float32)
    frobenius = jnp.sqrt(jnp.sum(moment_f * moment_f))
    current = (moment_f / (frobenius + norm_floor)).astype(jnp.bfloat16)
    for sweep_index in range(2):
        gramian = lax.dot_general(
            current, current, (((1,), (1,)), ((), ())), preferred_element_type=jnp.float32
        ).astype(jnp.bfloat16)
        squared = jnp.dot(gramian, gramian, preferred_element_type=jnp.float32)
        poly = (cubic_term * gramian.astype(jnp.float32) + quintic_term * squared).astype(
            jnp.bfloat16
        )
        current = (
            linear_term * current.astype(jnp.float32)
            + jnp.dot(poly, current, preferred_element_type=jnp.float32)
        ).astype(jnp.bfloat16)
    return current


def relocate(weight, moment, perm):
    groups = lax.axis_size("expert")
    weight_flat = weight.reshape(groups, -1)
    moment_flat = moment.reshape(groups, -1)
    spread_w, spread_m = (
        lax.all_to_all(weight_flat, "expert", split_axis=0, concat_axis=0, tiled=True),
        lax.all_to_all(moment_flat, "expert", split_axis=0, concat_axis=0, tiled=True),
    )
    devices = jnp.arange(groups, dtype=jnp.int32)
    inverse = jnp.sum(jnp.where(perm[None, :] == devices[:, None], devices[None, :], 0), axis=1)
    ordered_w = jnp.take(spread_w, inverse, axis=0)
    ordered_m = jnp.take(spread_m, inverse, axis=0)
    back_w, back_m = (
        lax.all_to_all(ordered_w, "expert", split_axis=0, concat_axis=0, tiled=True),
        lax.all_to_all(ordered_m, "expert", split_axis=0, concat_axis=0, tiled=True),
    )
    return (back_w.reshape(weight.shape), back_m.reshape(moment.shape))


def routed_plan(
    grad_hidden,
    grad_out,
    grad_route,
    live_rows,
    w_down,
    w_moment,
    perm,
    fwd_hidden,
    fwd_route,
    fwd_gate,
):
    groups = lax.axis_size("expert")
    grad_count = grad_hidden.shape[0]
    capacity = max(4, 2 * grad_count // groups)
    is_live = jnp.arange(grad_count, dtype=jnp.int32) < live_rows[0]
    route_ids = grad_route[:, 0]
    weight, moment = relocate(w_down, w_moment, perm)
    target = lookup(route_ids, perm)
    selector = slot_matrix(target, is_live, groups, capacity)
    hidden_buf = (
        jnp.dot(selector, grad_hidden, preferred_element_type=jnp.float32)
        .astype(jnp.bfloat16)
        .reshape(groups, capacity, -1)
    )
    outgrad_buf = (
        jnp.dot(selector, grad_out, preferred_element_type=jnp.float32)
        .astype(jnp.bfloat16)
        .reshape(groups, capacity, -1)
    )
    recv_hidden, recv_outgrad = (
        lax.all_to_all(hidden_buf, "expert", split_axis=0, concat_axis=0, tiled=True),
        lax.all_to_all(outgrad_buf, "expert", split_axis=0, concat_axis=0, tiled=True),
    )
    grad = lax.dot_general(
        recv_hidden.reshape(groups * capacity, -1),
        recv_outgrad.reshape(groups * capacity, -1),
        (((0,), (0,)), ((), ())),
        preferred_element_type=jnp.float32,
    )
    moment_new = (moment_decay * moment[0].astype(jnp.float32) + grad).astype(jnp.bfloat16)
    ortho = orthogonalize(moment_new)
    weight_new = (weight[0].astype(jnp.float32) - step_scale * ortho.astype(jnp.float32)).astype(
        jnp.bfloat16
    )
    weight_new = weight_new[None]
    moment_new = moment_new[None]
    fwd_ids = fwd_route[:, 0]
    placed_weight, placed_moment = (weight_new, moment_new)
    fwd_target = lookup(fwd_ids, perm)
    fwd_weight = weight_new[0]
    fwd_count = fwd_hidden.shape[0]
    fwd_capacity = max(4, 2 * fwd_count // groups)
    fwd_selector = slot_matrix(fwd_target, jnp.ones((fwd_count,), dtype=bool), groups, fwd_capacity)
    fwd_buf = (
        jnp.dot(fwd_selector, fwd_hidden, preferred_element_type=jnp.float32)
        .astype(jnp.bfloat16)
        .reshape(groups, fwd_capacity, -1)
    )
    produced = jnp.einsum(
        "gkf,fd->gkd",
        lax.all_to_all(fwd_buf, "expert", split_axis=0, concat_axis=0, tiled=True),
        fwd_weight,
        preferred_element_type=jnp.float32,
    ).astype(jnp.bfloat16)
    returned = lax.all_to_all(produced, "expert", split_axis=0, concat_axis=0, tiled=True)
    fwd_rows_out = lax.dot_general(
        fwd_selector,
        returned.reshape(groups * fwd_capacity, -1),
        (((0,), (0,)), ((), ())),
        preferred_element_type=jnp.float32,
    )
    fwd_out = (fwd_rows_out * fwd_gate[:, None]).astype(jnp.bfloat16)
    return (placed_weight, placed_moment, fwd_out)


def solution(mesh):
    groups = mesh.shape["expert"]
    in_specs = (
        P(("layer", "expert"), None),
        P(("layer", "expert"), None),
        P(("layer", "expert"), None),
        P(("layer", "expert")),
        P(("layer", "expert"), None, None),
        P(("layer", "expert"), None, None),
        P("layer"),
        P(("layer", "expert"), None),
        P(("layer", "expert"), None),
        P(("layer", "expert")),
    )
    out_specs = (
        P(("layer", "expert"), None, None),
        P(("layer", "expert"), None, None),
        P(("layer", "expert"), None),
    )

    def per_device(*args):
        few = groups & (groups - 1) == 0 and groups <= 2 * args[0].shape[0] // groups
        return (partner_plan if few else routed_plan)(*args)

    return jax.shard_map(
        per_device, mesh=mesh, in_specs=in_specs, out_specs=out_specs, check_vma=False
    )
```

```python
import functools

import jax
import jax.numpy as jnp
from jax import lax
from jax.experimental import pallas as pl
from jax.experimental.pallas import tpu as pltpu
from jax.sharding import PartitionSpec as P

linear_term = 3.4445
cubic_term = -4.775
quintic_term = 2.0315
moment_decay = 0.9
step_scale = 0.25
norm_floor = 1e-07

F32 = jnp.float32
BF16 = jnp.bfloat16
HBM = pl.BlockSpec(memory_space=pltpu.HBM)
VMEM = pl.BlockSpec(memory_space=pltpu.VMEM)
SMEM = pl.BlockSpec(memory_space=pltpu.SMEM)
ANY = pl.BlockSpec(memory_space=pl.ANY)
MIB = 1 << 20


def plane_of(groups):
    return 1 << ((groups.bit_length() - 1) // 2)


def line_order(line):
    return [0] + sorted(range(1, line), key=lambda k: (k.bit_length() < line.bit_length() - 1, k))


def along_line(pieces, groups):
    plane = plane_of(groups)
    return [
        lax.ppermute(piece, "expert", [(i, i ^ (k * plane)) for i in range(groups)]) if k else piece
        for k, piece in zip(line_order(groups // plane), pieces)
    ]


def in_plane(stack, groups):
    stacks = [stack]
    for bit in reversed(range(plane_of(groups).bit_length() - 1)):
        stacks += [lax.ppermute(held, "expert", [(i, i ^ (1 << bit)) for i in range(groups)]) for held in stacks]
    return stacks


def plane_offsets(groups):
    offsets = [0]
    for bit in reversed(range(plane_of(groups).bit_length() - 1)):
        offsets += [offset ^ (1 << bit) for offset in offsets]
    return offsets


def block_at(k, rows):
    return pl.ds(pl.multiple_of(k * rows, rows), rows)


def split_kernel(plane, me_ref, moment_ref, weight_ref, *refs):
    pieces, sem = refs[:-1], refs[-1]
    line = len(pieces) // 2
    place = me_ref[0] // plane
    copies = [
        pltpu.make_async_copy(
            source.at[0, block_at(place ^ k, pieces[0].shape[0])], pieces[lead * line + n], sem.at[lead * line + n]
        )
        for lead, source in enumerate((moment_ref, weight_ref))
        for n, k in enumerate(line_order(line))
    ]
    for copy in copies:
        copy.start()
    for copy in copies:
        copy.wait()


def split(me, moment, weight, groups):
    _, ff, d = weight.shape
    plane = plane_of(groups)
    line = groups // plane
    piece = jax.ShapeDtypeStruct((ff // line, d), BF16)
    pieces = pl.pallas_call(
        functools.partial(split_kernel, plane),
        out_shape=(piece,) * (2 * line),
        in_specs=[SMEM, HBM, HBM],
        out_specs=(VMEM,) * (2 * line),
        scratch_shapes=[pltpu.SemaphoreType.DMA((2 * line,))],
        compiler_params=pltpu.CompilerParams(vmem_limit_bytes=60 * MIB),
        cost_estimate=pl.CostEstimate(flops=0, bytes_accessed=8 * ff * d, transcendentals=0),
        name="split",
    )(me, moment, weight)
    return pieces[:line], pieces[line:]


def stack_kernel(order, *refs):
    stack_ref = refs[-1]
    for k, piece in zip(order, refs):
        stack_ref[k] = piece[...]


def stacked(pieces):
    line = len(pieces)
    shape = (line,) + pieces[0].shape
    return pl.pallas_call(
        functools.partial(stack_kernel, line_order(line)),
        out_shape=jax.ShapeDtypeStruct(shape, BF16),
        in_specs=[VMEM] * line,
        out_specs=VMEM,
        compiler_params=pltpu.CompilerParams(vmem_limit_bytes=32 * MIB),
        cost_estimate=pl.CostEstimate(flops=0, bytes_accessed=4 * line * pieces[0].size, transcendentals=0),
        name="stack",
    )(*pieces)


def pick_kernel(groups, me_ref, perm_ref, *refs):
    plane = plane_of(groups)
    line = groups // plane
    stacks, targets = refs[:plane], refs[plane:]
    me = me_ref[0]
    for k, target in zip(line_order(line), targets):
        expert = 0
        for e in range(groups):
            expert = jnp.where(perm_ref[e] == me ^ (k * plane), e, expert)
        offset, place = (expert ^ me) % plane, (expert ^ me) // plane
        for stack, held in zip(plane_offsets(groups), stacks):

            @pl.when(offset == stack)
            def _():
                target[...] = held[place]


def pick(me, perm, stacks, groups):
    line = stacks[0].shape[0]
    piece = jax.ShapeDtypeStruct(stacks[0].shape[1:], BF16)
    return pl.pallas_call(
        functools.partial(pick_kernel, groups),
        out_shape=(piece,) * line,
        in_specs=[SMEM, SMEM] + [VMEM] * len(stacks),
        out_specs=(VMEM,) * line,
        compiler_params=pltpu.CompilerParams(vmem_limit_bytes=32 * MIB),
        cost_estimate=pl.CostEstimate(flops=0, bytes_accessed=4 * stacks[0].size, transcendentals=0),
        name="pick",
    )(me, perm, *stacks)


def relocated(me, perm, pieces, groups):
    stacks = in_plane(stacked(along_line(pieces, groups)), groups)
    return along_line(pick(me, perm, stacks, groups), groups)


def assembled(plane, me_ref, pieces, held):
    rows = pieces[0].shape[0]
    for k, piece in zip(line_order(len(pieces)), pieces):
        held[block_at((me_ref[0] // plane) ^ k, rows)] = piece[...]
    return held[...].astype(F32)


def slot_rows(route, live, groups, capacity, perm_ref):
    rows = route.shape[1]
    experts = lax.broadcasted_iota(jnp.int32, (groups, rows), 0)
    onehot = jnp.where((experts == route) & live, 1.0, 0.0).astype(BF16)
    before = lax.broadcasted_iota(jnp.int32, (rows, rows), 0)
    after = lax.broadcasted_iota(jnp.int32, (rows, rows), 1)
    upto = jnp.where(before <= after, 1.0, 0.0).astype(BF16)
    ranks = jnp.dot(onehot, upto, preferred_element_type=F32)
    rank = jnp.sum(ranks * onehot.astype(F32), axis=0, keepdims=True).astype(jnp.int32) - 1
    target = jnp.zeros_like(route)
    for e in range(groups):
        target = jnp.where(route == e, perm_ref[e], target)
    return jnp.where(live, target * capacity + rank, -1)


def selector_of(slot, slots):
    rows = slot.shape[1]
    places = lax.broadcasted_iota(jnp.int32, (slots, rows), 0)
    return jnp.where(places == slot, 1.0, 0.0).astype(BF16)


def pack_kernel(groups, live_ref, perm_ref, *refs):
    sources, (packed_ref, slot_ref), held, sem = refs[:5], refs[5:7], refs[7:12], refs[12]
    route_ref, fwd_route_ref, hidden_ref, out_ref, fwd_ref = held
    copies = [pltpu.make_async_copy(ref, room, sem.at[n]) for n, (ref, room) in enumerate(zip(sources, held))]
    for copy in copies:
        copy.start()
    rows, ff = hidden_ref.shape
    d = out_ref.shape[1]
    slots = packed_ref.shape[0]
    capacity = slots // groups
    place = lax.broadcasted_iota(jnp.int32, (1, rows), 1)
    copies[0].wait()
    selector = selector_of(slot_rows(route_ref[...], place < live_ref[0], groups, capacity, perm_ref), slots)
    copies[1].wait()
    fwd_slot = slot_rows(fwd_route_ref[...], place >= 0, groups, capacity, perm_ref)
    slot_ref[...] = fwd_slot
    fwd_selector = selector_of(fwd_slot, slots)
    copies[2].wait()
    packed_ref[:, :ff] = jnp.dot(selector, hidden_ref[...], preferred_element_type=F32).astype(BF16)
    copies[3].wait()
    packed_ref[:, ff : ff + d] = jnp.dot(selector, out_ref[...], preferred_element_type=F32).astype(BF16)
    copies[4].wait()
    packed_ref[:, ff + d :] = jnp.dot(fwd_selector, fwd_ref[...], preferred_element_type=F32).astype(BF16)


def pack_rows(live_rows, perm, route, fwd_route, hidden, grad_out, fwd_hidden, groups, capacity):
    rows, ff = hidden.shape
    width = 2 * ff + grad_out.shape[1]
    sources = (route.reshape(1, rows), fwd_route.reshape(1, rows), hidden, grad_out, fwd_hidden)
    return pl.pallas_call(
        functools.partial(pack_kernel, groups),
        out_shape=(
            jax.ShapeDtypeStruct((groups * capacity, width), BF16),
            jax.ShapeDtypeStruct((1, rows), jnp.int32),
        ),
        in_specs=[SMEM, SMEM] + [HBM] * 5,
        out_specs=(VMEM, VMEM),
        scratch_shapes=[pltpu.VMEM(a.shape, a.dtype) for a in sources] + [pltpu.SemaphoreType.DMA((len(sources),))],
        compiler_params=pltpu.CompilerParams(vmem_limit_bytes=60 * MIB),
        cost_estimate=pl.CostEstimate(
            flops=2 * groups * capacity * rows * width, bytes_accessed=6 * rows * width, transcendentals=0
        ),
        name="pack_rows",
    )(live_rows, perm, *sources)


def orthogonal_kernel(plane, me_ref, packed_ref, *refs):
    pieces, (moment_new_ref, ortho_ref, held) = refs[:-3], refs[-3:]
    ff, d = ortho_ref.shape
    grad = lax.dot_general(
        packed_ref[:, :ff], packed_ref[:, ff : ff + d], (((0,), (0,)), ((), ())), preferred_element_type=F32
    )
    moment_new = (moment_decay * assembled(plane, me_ref, pieces, held) + grad).astype(BF16)
    moment_new_ref[...] = moment_new
    moment_f = moment_new.astype(F32)
    frobenius = jnp.sqrt(jnp.sum(moment_f * moment_f))
    current = (moment_f / (frobenius + norm_floor)).astype(BF16)
    for _ in range(2):
        gramian = lax.dot_general(
            current, current, (((1,), (1,)), ((), ())), preferred_element_type=F32
        ).astype(BF16)
        squared = jnp.dot(gramian, gramian, preferred_element_type=F32)
        poly = (cubic_term * gramian.astype(F32) + quintic_term * squared).astype(BF16)
        current = (
            linear_term * current.astype(F32) + jnp.dot(poly, current, preferred_element_type=F32)
        ).astype(BF16)
    ortho_ref[...] = current


def orthogonal(me, packed, pieces, groups):
    line = len(pieces)
    rows, d = pieces[0].shape
    ff = rows * line
    shape = jax.ShapeDtypeStruct((ff, d), BF16)
    return pl.pallas_call(
        functools.partial(orthogonal_kernel, plane_of(groups)),
        out_shape=(shape, shape),
        in_specs=[SMEM] + [VMEM] * (1 + line),
        out_specs=(VMEM, VMEM),
        scratch_shapes=[pltpu.VMEM((ff, d), BF16)],
        compiler_params=pltpu.CompilerParams(vmem_limit_bytes=40 * MIB),
        cost_estimate=pl.CostEstimate(
            flops=2 * ff * d * packed.shape[0] + 8 * ff * ff * d + 4 * ff**3,
            bytes_accessed=6 * ff * d + 2 * packed.size,
            transcendentals=1,
        ),
        name="orthogonal",
    )(me, packed, *pieces)


def produce_kernel(plane, me_ref, packed_ref, ortho_ref, *refs):
    pieces, (weight_new_ref, produced_ref, held) = refs[:-3], refs[-3:]
    ff, d = ortho_ref.shape
    weight = assembled(plane, me_ref, pieces, held)
    weight_new = (weight - step_scale * ortho_ref[...].astype(F32)).astype(BF16)
    weight_new_ref[...] = weight_new
    produced_ref[...] = jnp.dot(packed_ref[:, ff + d :], weight_new, preferred_element_type=F32).astype(BF16)


def produce(me, packed, ortho, pieces, groups):
    slots = packed.shape[0]
    ff, d = ortho.shape
    return pl.pallas_call(
        functools.partial(produce_kernel, plane_of(groups)),
        out_shape=(jax.ShapeDtypeStruct((ff, d), BF16), jax.ShapeDtypeStruct((slots, d), BF16)),
        in_specs=[SMEM] + [VMEM] * (2 + len(pieces)),
        out_specs=(VMEM, VMEM),
        scratch_shapes=[pltpu.VMEM((ff, d), BF16)],
        compiler_params=pltpu.CompilerParams(vmem_limit_bytes=40 * MIB),
        cost_estimate=pl.CostEstimate(
            flops=2 * slots * ff * d, bytes_accessed=8 * ff * d + 2 * slots * (ff + d), transcendentals=0
        ),
        name="produce",
    )(me, packed, ortho, *pieces)


def finish_kernel(slot_ref, gate_ref, returned_ref, out_ref):
    rows = slot_ref.shape[1]
    selector = selector_of(slot_ref[...], returned_ref.shape[0])
    expert_out = lax.dot_general(
        selector, returned_ref[...], (((0,), (0,)), ((), ())), preferred_element_type=F32
    )
    down = lax.broadcasted_iota(jnp.int32, (rows, rows), 0)
    across = lax.broadcasted_iota(jnp.int32, (rows, rows), 1)
    gate = jnp.sum(jnp.where(down == across, gate_ref[...], 0.0), axis=1, keepdims=True)
    out_ref[...] = (gate * expert_out).astype(BF16)


def finish(slot, gate, returned):
    rows = slot.shape[1]
    slots, d = returned.shape
    return pl.pallas_call(
        finish_kernel,
        out_shape=jax.ShapeDtypeStruct((rows, d), BF16),
        in_specs=[VMEM] * 3,
        out_specs=VMEM,
        compiler_params=pltpu.CompilerParams(vmem_limit_bytes=32 * MIB),
        cost_estimate=pl.CostEstimate(
            flops=2 * slots * rows * d, bytes_accessed=2 * d * (slots + rows), transcendentals=0
        ),
        name="finish",
    )(slot, gate.reshape(1, rows), returned)


def exchange(array):
    return lax.all_to_all(array, "expert", split_axis=0, concat_axis=0, tiled=True)


def relocation_plan(
    grad_hidden, grad_out, grad_route, live_rows, w_down, w_moment, perm, fwd_hidden, fwd_route, fwd_gate
):
    groups = lax.axis_size("expert")
    me = lax.axis_index("expert").astype(jnp.int32).reshape(1)
    capacity = max(4, 2 * grad_hidden.shape[0] // groups)
    d = w_down.shape[2]
    moment_pieces, weight_pieces = split(me, w_moment, w_down, groups)
    live_rows, moment_pieces = lax.optimization_barrier((live_rows, moment_pieces))
    packed, fwd_slot = pack_rows(
        live_rows, perm, grad_route, fwd_route, grad_hidden, grad_out, fwd_hidden, groups, capacity
    )
    received = exchange(packed.reshape(groups, capacity, -1)).reshape(groups * capacity, -1)
    moment_placed = relocated(me, perm, moment_pieces, groups)
    weight_placed = relocated(me, perm, weight_pieces, groups)
    moment_new, ortho = orthogonal(me, received, moment_placed, groups)
    weight_new, produced = produce(me, received, ortho, weight_placed, groups)
    returned = exchange(produced.reshape(groups, capacity, d)).reshape(groups * capacity, d)
    return weight_new[None], moment_new[None], finish(fwd_slot, fwd_gate, returned)


def lookup(route_ids, mapping):
    columns = jnp.arange(mapping.shape[0], dtype=jnp.int32)
    hits = route_ids[:, None] == columns[None, :]
    return jnp.sum(jnp.where(hits, mapping[None, :], 0), axis=1)


def slot_matrix(target, is_live, groups, capacity):
    columns = jnp.arange(groups, dtype=jnp.int32)
    onehot = ((target[:, None] == columns[None, :]) & is_live[:, None]).astype(jnp.int32)
    ranked = jnp.sum(jnp.cumsum(onehot, axis=0) * onehot, axis=1) - 1
    slot_of = jnp.where(is_live, target * capacity + ranked, -1)
    slots = jnp.arange(groups * capacity, dtype=jnp.int32)
    return (slots[:, None] == slot_of[None, :]).astype(jnp.bfloat16)


def orthogonalize(moment):
    moment_f = moment.astype(jnp.float32)
    frobenius = jnp.sqrt(jnp.sum(moment_f * moment_f))
    current = (moment_f / (frobenius + norm_floor)).astype(jnp.bfloat16)
    for sweep_index in range(2):
        gramian = lax.dot_general(
            current, current, (((1,), (1,)), ((), ())), preferred_element_type=jnp.float32
        ).astype(jnp.bfloat16)
        squared = jnp.dot(gramian, gramian, preferred_element_type=jnp.float32)
        poly = (cubic_term * gramian.astype(jnp.float32) + quintic_term * squared).astype(
            jnp.bfloat16
        )
        current = (
            linear_term * current.astype(jnp.float32)
            + jnp.dot(poly, current, preferred_element_type=jnp.float32)
        ).astype(jnp.bfloat16)
    return current


def relocate(weight, moment, perm):
    groups = lax.axis_size("expert")
    weight_flat = weight.reshape(groups, -1)
    moment_flat = moment.reshape(groups, -1)
    spread_w, spread_m = (
        lax.all_to_all(weight_flat, "expert", split_axis=0, concat_axis=0, tiled=True),
        lax.all_to_all(moment_flat, "expert", split_axis=0, concat_axis=0, tiled=True),
    )
    devices = jnp.arange(groups, dtype=jnp.int32)
    inverse = jnp.sum(jnp.where(perm[None, :] == devices[:, None], devices[None, :], 0), axis=1)
    ordered_w = jnp.take(spread_w, inverse, axis=0)
    ordered_m = jnp.take(spread_m, inverse, axis=0)
    back_w, back_m = (
        lax.all_to_all(ordered_w, "expert", split_axis=0, concat_axis=0, tiled=True),
        lax.all_to_all(ordered_m, "expert", split_axis=0, concat_axis=0, tiled=True),
    )
    return (back_w.reshape(weight.shape), back_m.reshape(moment.shape))


def routed_plan(
    grad_hidden,
    grad_out,
    grad_route,
    live_rows,
    w_down,
    w_moment,
    perm,
    fwd_hidden,
    fwd_route,
    fwd_gate,
):
    groups = lax.axis_size("expert")
    grad_count = grad_hidden.shape[0]
    capacity = max(4, 2 * grad_count // groups)
    is_live = jnp.arange(grad_count, dtype=jnp.int32) < live_rows[0]
    route_ids = grad_route[:, 0]
    weight, moment = relocate(w_down, w_moment, perm)
    target = lookup(route_ids, perm)
    selector = slot_matrix(target, is_live, groups, capacity)
    hidden_buf = (
        jnp.dot(selector, grad_hidden, preferred_element_type=jnp.float32)
        .astype(jnp.bfloat16)
        .reshape(groups, capacity, -1)
    )
    outgrad_buf = (
        jnp.dot(selector, grad_out, preferred_element_type=jnp.float32)
        .astype(jnp.bfloat16)
        .reshape(groups, capacity, -1)
    )
    recv_hidden, recv_outgrad = (
        lax.all_to_all(hidden_buf, "expert", split_axis=0, concat_axis=0, tiled=True),
        lax.all_to_all(outgrad_buf, "expert", split_axis=0, concat_axis=0, tiled=True),
    )
    grad = lax.dot_general(
        recv_hidden.reshape(groups * capacity, -1),
        recv_outgrad.reshape(groups * capacity, -1),
        (((0,), (0,)), ((), ())),
        preferred_element_type=jnp.float32,
    )
    moment_new = (moment_decay * moment[0].astype(jnp.float32) + grad).astype(jnp.bfloat16)
    ortho = orthogonalize(moment_new)
    weight_new = (weight[0].astype(jnp.float32) - step_scale * ortho.astype(jnp.float32)).astype(
        jnp.bfloat16
    )
    weight_new = weight_new[None]
    moment_new = moment_new[None]
    fwd_ids = fwd_route[:, 0]
    placed_weight, placed_moment = (weight_new, moment_new)
    fwd_target = lookup(fwd_ids, perm)
    fwd_weight = weight_new[0]
    fwd_count = fwd_hidden.shape[0]
    fwd_capacity = max(4, 2 * fwd_count // groups)
    fwd_selector = slot_matrix(fwd_target, jnp.ones((fwd_count,), dtype=bool), groups, fwd_capacity)
    fwd_buf = (
        jnp.dot(fwd_selector, fwd_hidden, preferred_element_type=jnp.float32)
        .astype(jnp.bfloat16)
        .reshape(groups, fwd_capacity, -1)
    )
    produced = jnp.einsum(
        "gkf,fd->gkd",
        lax.all_to_all(fwd_buf, "expert", split_axis=0, concat_axis=0, tiled=True),
        fwd_weight,
        preferred_element_type=jnp.float32,
    ).astype(jnp.bfloat16)
    returned = lax.all_to_all(produced, "expert", split_axis=0, concat_axis=0, tiled=True)
    fwd_rows_out = lax.dot_general(
        fwd_selector,
        returned.reshape(groups * fwd_capacity, -1),
        (((0,), (0,)), ((), ())),
        preferred_element_type=jnp.float32,
    )
    fwd_out = (fwd_rows_out * fwd_gate[:, None]).astype(jnp.bfloat16)
    return (placed_weight, placed_moment, fwd_out)


def solution(mesh):
    groups = mesh.shape["expert"]
    in_specs = (
        P(("layer", "expert"), None),
        P(("layer", "expert"), None),
        P(("layer", "expert"), None),
        P(("layer", "expert")),
        P(("layer", "expert"), None, None),
        P(("layer", "expert"), None, None),
        P("layer"),
        P(("layer", "expert"), None),
        P(("layer", "expert"), None),
        P(("layer", "expert")),
    )
    out_specs = (
        P(("layer", "expert"), None, None),
        P(("layer", "expert"), None, None),
        P(("layer", "expert"), None),
    )

    def per_device(*args):
        few = groups & (groups - 1) == 0 and groups <= 2 * args[0].shape[0] // groups
        return (relocation_plan if few else routed_plan)(*args)

    return jax.shard_map(
        per_device, mesh=mesh, in_specs=in_specs, out_specs=out_specs, check_vma=False
    )
```

```python
import functools

import jax
import jax.numpy as jnp
from jax import lax
from jax.experimental import pallas as pl
from jax.experimental.pallas import tpu as pltpu
from jax.sharding import PartitionSpec as P

linear_term = 3.4445
cubic_term = -4.775
quintic_term = 2.0315
moment_decay = 0.9
step_scale = 0.25
norm_floor = 1e-07

F32 = jnp.float32
BF16 = jnp.bfloat16
HBM = pl.BlockSpec(memory_space=pltpu.HBM)
VMEM = pl.BlockSpec(memory_space=pltpu.VMEM)
SMEM = pl.BlockSpec(memory_space=pltpu.SMEM)
ANY = pl.BlockSpec(memory_space=pl.ANY)
MIB = 1 << 20


def plane_of(groups):
    return 1 << ((groups.bit_length() - 1) // 2)


def line_order(line):
    return [0] + sorted(range(1, line), key=lambda k: (k.bit_length() < line.bit_length() - 1, k))


def along_line(pieces, groups):
    plane = plane_of(groups)
    return [
        lax.ppermute(piece, "expert", [(i, i ^ (k * plane)) for i in range(groups)]) if k else piece
        for k, piece in zip(line_order(groups // plane), pieces)
    ]


def in_plane(stack, groups):
    stacks = [stack]
    for bit in reversed(range(plane_of(groups).bit_length() - 1)):
        stacks += [lax.ppermute(held, "expert", [(i, i ^ (1 << bit)) for i in range(groups)]) for held in stacks]
    return stacks


def plane_offsets(groups):
    offsets = [0]
    for bit in reversed(range(plane_of(groups).bit_length() - 1)):
        offsets += [offset ^ (1 << bit) for offset in offsets]
    return offsets


def block_at(k, rows):
    return pl.ds(pl.multiple_of(k * rows, rows), rows)


def after_kernel(*refs):
    pass


def after(array, *earlier):
    return pl.pallas_call(
        after_kernel,
        out_shape=jax.ShapeDtypeStruct(array.shape, array.dtype),
        in_specs=[ANY] * (1 + len(earlier)),
        out_specs=ANY,
        input_output_aliases={0: 0},
        cost_estimate=pl.CostEstimate(flops=0, bytes_accessed=0, transcendentals=0),
        name="after",
    )(array, *earlier)


def split_kernel(plane, me_ref, moment_ref, weight_ref, *refs):
    pieces, sem = refs[:-1], refs[-1]
    line = len(pieces) // 2
    place = me_ref[0] // plane
    copies = [
        pltpu.make_async_copy(
            source.at[0, block_at(place ^ k, pieces[0].shape[0])], pieces[lead * line + n], sem.at[lead * line + n]
        )
        for lead, source in enumerate((moment_ref, weight_ref))
        for n, k in enumerate(line_order(line))
    ]
    for copy in copies:
        copy.start()
    for copy in copies:
        copy.wait()


def split(me, moment, weight, groups):
    _, ff, d = weight.shape
    plane = plane_of(groups)
    line = groups // plane
    piece = jax.ShapeDtypeStruct((ff // line, d), BF16)
    pieces = pl.pallas_call(
        functools.partial(split_kernel, plane),
        out_shape=(piece,) * (2 * line),
        in_specs=[SMEM, HBM, HBM],
        out_specs=(VMEM,) * (2 * line),
        scratch_shapes=[pltpu.SemaphoreType.DMA((2 * line,))],
        compiler_params=pltpu.CompilerParams(vmem_limit_bytes=60 * MIB),
        cost_estimate=pl.CostEstimate(flops=0, bytes_accessed=8 * ff * d, transcendentals=0),
        name="split",
    )(me, moment, weight)
    return pieces[:line], pieces[line:]


def stack_kernel(order, *refs):
    stack_ref = refs[-1]
    for k, piece in zip(order, refs):
        stack_ref[k] = piece[...]


def stacked(pieces):
    line = len(pieces)
    shape = (line,) + pieces[0].shape
    return pl.pallas_call(
        functools.partial(stack_kernel, line_order(line)),
        out_shape=jax.ShapeDtypeStruct(shape, BF16),
        in_specs=[VMEM] * line,
        out_specs=VMEM,
        compiler_params=pltpu.CompilerParams(vmem_limit_bytes=32 * MIB),
        cost_estimate=pl.CostEstimate(flops=0, bytes_accessed=4 * line * pieces[0].size, transcendentals=0),
        name="stack",
    )(*pieces)


def pick_kernel(groups, me_ref, perm_ref, *refs):
    plane = plane_of(groups)
    line = groups // plane
    stacks, targets = refs[:plane], refs[plane:]
    me = me_ref[0]
    for k, target in zip(line_order(line), targets):
        expert = 0
        for e in range(groups):
            expert = jnp.where(perm_ref[e] == me ^ (k * plane), e, expert)
        offset, place = (expert ^ me) % plane, (expert ^ me) // plane
        for stack, held in zip(plane_offsets(groups), stacks):

            @pl.when(offset == stack)
            def _():
                target[...] = held[place]


def pick(me, perm, stacks, groups):
    line = stacks[0].shape[0]
    piece = jax.ShapeDtypeStruct(stacks[0].shape[1:], BF16)
    return pl.pallas_call(
        functools.partial(pick_kernel, groups),
        out_shape=(piece,) * line,
        in_specs=[SMEM, SMEM] + [VMEM] * len(stacks),
        out_specs=(VMEM,) * line,
        compiler_params=pltpu.CompilerParams(vmem_limit_bytes=32 * MIB),
        cost_estimate=pl.CostEstimate(flops=0, bytes_accessed=4 * stacks[0].size, transcendentals=0),
        name="pick",
    )(me, perm, *stacks)


def relocated(me, perm, stack, groups):
    return along_line(pick(me, perm, in_plane(stack, groups), groups), groups)


def assembled(plane, me_ref, pieces, held):
    rows = pieces[0].shape[0]
    for k, piece in zip(line_order(len(pieces)), pieces):
        held[block_at((me_ref[0] // plane) ^ k, rows)] = piece[...]
    return held[...].astype(F32)


def slot_rows(route, live, groups, capacity, perm_ref):
    rows = route.shape[1]
    experts = lax.broadcasted_iota(jnp.int32, (groups, rows), 0)
    onehot = jnp.where((experts == route) & live, 1.0, 0.0).astype(BF16)
    before = lax.broadcasted_iota(jnp.int32, (rows, rows), 0)
    after = lax.broadcasted_iota(jnp.int32, (rows, rows), 1)
    upto = jnp.where(before <= after, 1.0, 0.0).astype(BF16)
    ranks = jnp.dot(onehot, upto, preferred_element_type=F32)
    rank = jnp.sum(ranks * onehot.astype(F32), axis=0, keepdims=True).astype(jnp.int32) - 1
    target = jnp.zeros_like(route)
    for e in range(groups):
        target = jnp.where(route == e, perm_ref[e], target)
    return jnp.where(live, target * capacity + rank, -1)


def selector_of(slot, slots):
    rows = slot.shape[1]
    places = lax.broadcasted_iota(jnp.int32, (slots, rows), 0)
    return jnp.where(places == slot, 1.0, 0.0).astype(BF16)


def pack_kernel(groups, live_ref, perm_ref, *refs):
    sources, (packed_ref, slot_ref), held, sem = refs[:5], refs[6:8], refs[8:13], refs[13]
    route_ref, fwd_route_ref, hidden_ref, out_ref, fwd_ref = held
    copies = [pltpu.make_async_copy(ref, room, sem.at[n]) for n, (ref, room) in enumerate(zip(sources, held))]
    for copy in copies:
        copy.start()
    rows, ff = hidden_ref.shape
    d = out_ref.shape[1]
    slots = packed_ref.shape[0]
    capacity = slots // groups
    place = lax.broadcasted_iota(jnp.int32, (1, rows), 1)
    copies[0].wait()
    selector = selector_of(slot_rows(route_ref[...], place < live_ref[0], groups, capacity, perm_ref), slots)
    copies[1].wait()
    fwd_slot = slot_rows(fwd_route_ref[...], place >= 0, groups, capacity, perm_ref)
    slot_ref[...] = fwd_slot
    fwd_selector = selector_of(fwd_slot, slots)
    copies[2].wait()
    packed_ref[:, :ff] = jnp.dot(selector, hidden_ref[...], preferred_element_type=F32).astype(BF16)
    copies[3].wait()
    packed_ref[:, ff : ff + d] = jnp.dot(selector, out_ref[...], preferred_element_type=F32).astype(BF16)
    copies[4].wait()
    packed_ref[:, ff + d :] = jnp.dot(fwd_selector, fwd_ref[...], preferred_element_type=F32).astype(BF16)


def pack_rows(live_rows, perm, route, fwd_route, hidden, grad_out, fwd_hidden, earlier, groups, capacity):
    rows, ff = hidden.shape
    width = 2 * ff + grad_out.shape[1]
    sources = (route.reshape(1, rows), fwd_route.reshape(1, rows), hidden, grad_out, fwd_hidden)
    return pl.pallas_call(
        functools.partial(pack_kernel, groups),
        out_shape=(
            jax.ShapeDtypeStruct((groups * capacity, width), BF16),
            jax.ShapeDtypeStruct((1, rows), jnp.int32),
        ),
        in_specs=[SMEM, SMEM] + [HBM] * 5 + [ANY],
        out_specs=(VMEM, VMEM),
        scratch_shapes=[pltpu.VMEM(a.shape, a.dtype) for a in sources] + [pltpu.SemaphoreType.DMA((len(sources),))],
        compiler_params=pltpu.CompilerParams(vmem_limit_bytes=60 * MIB),
        cost_estimate=pl.CostEstimate(
            flops=2 * groups * capacity * rows * width, bytes_accessed=6 * rows * width, transcendentals=0
        ),
        name="pack_rows",
    )(live_rows, perm, *sources, earlier)


def orthogonal_kernel(plane, me_ref, packed_ref, *refs):
    pieces, (moment_new_ref, ortho_ref, held) = refs[:-3], refs[-3:]
    ff, d = ortho_ref.shape
    grad = lax.dot_general(
        packed_ref[:, :ff], packed_ref[:, ff : ff + d], (((0,), (0,)), ((), ())), preferred_element_type=F32
    )
    moment_new = (moment_decay * assembled(plane, me_ref, pieces, held) + grad).astype(BF16)
    moment_new_ref[...] = moment_new
    moment_f = moment_new.astype(F32)
    frobenius = jnp.sqrt(jnp.sum(moment_f * moment_f))
    current = (moment_f / (frobenius + norm_floor)).astype(BF16)
    for _ in range(2):
        gramian = lax.dot_general(
            current, current, (((1,), (1,)), ((), ())), preferred_element_type=F32
        ).astype(BF16)
        squared = jnp.dot(gramian, gramian, preferred_element_type=F32)
        poly = (cubic_term * gramian.astype(F32) + quintic_term * squared).astype(BF16)
        current = (
            linear_term * current.astype(F32) + jnp.dot(poly, current, preferred_element_type=F32)
        ).astype(BF16)
    ortho_ref[...] = current


def orthogonal(me, packed, pieces, groups):
    line = len(pieces)
    rows, d = pieces[0].shape
    ff = rows * line
    shape = jax.ShapeDtypeStruct((ff, d), BF16)
    return pl.pallas_call(
        functools.partial(orthogonal_kernel, plane_of(groups)),
        out_shape=(shape, shape),
        in_specs=[SMEM] + [VMEM] * (1 + line),
        out_specs=(VMEM, VMEM),
        scratch_shapes=[pltpu.VMEM((ff, d), BF16)],
        compiler_params=pltpu.CompilerParams(vmem_limit_bytes=40 * MIB),
        cost_estimate=pl.CostEstimate(
            flops=2 * ff * d * packed.shape[0] + 8 * ff * ff * d + 4 * ff**3,
            bytes_accessed=6 * ff * d + 2 * packed.size,
            transcendentals=1,
        ),
        name="orthogonal",
    )(me, packed, *pieces)


def produce_kernel(plane, me_ref, packed_ref, ortho_ref, *refs):
    pieces, (weight_new_ref, produced_ref, held) = refs[:-3], refs[-3:]
    ff, d = ortho_ref.shape
    weight = assembled(plane, me_ref, pieces, held)
    weight_new = (weight - step_scale * ortho_ref[...].astype(F32)).astype(BF16)
    weight_new_ref[...] = weight_new
    produced_ref[...] = jnp.dot(packed_ref[:, ff + d :], weight_new, preferred_element_type=F32).astype(BF16)


def produce(me, packed, ortho, pieces, groups):
    slots = packed.shape[0]
    ff, d = ortho.shape
    return pl.pallas_call(
        functools.partial(produce_kernel, plane_of(groups)),
        out_shape=(jax.ShapeDtypeStruct((ff, d), BF16), jax.ShapeDtypeStruct((slots, d), BF16)),
        in_specs=[SMEM] + [VMEM] * (2 + len(pieces)),
        out_specs=(VMEM, VMEM),
        scratch_shapes=[pltpu.VMEM((ff, d), BF16)],
        compiler_params=pltpu.CompilerParams(vmem_limit_bytes=40 * MIB),
        cost_estimate=pl.CostEstimate(
            flops=2 * slots * ff * d, bytes_accessed=8 * ff * d + 2 * slots * (ff + d), transcendentals=0
        ),
        name="produce",
    )(me, packed, ortho, *pieces)


def finish_kernel(slot_ref, gate_ref, returned_ref, out_ref):
    rows = slot_ref.shape[1]
    selector = selector_of(slot_ref[...], returned_ref.shape[0])
    expert_out = lax.dot_general(
        selector, returned_ref[...], (((0,), (0,)), ((), ())), preferred_element_type=F32
    )
    down = lax.broadcasted_iota(jnp.int32, (rows, rows), 0)
    across = lax.broadcasted_iota(jnp.int32, (rows, rows), 1)
    gate = jnp.sum(jnp.where(down == across, gate_ref[...], 0.0), axis=1, keepdims=True)
    out_ref[...] = (gate * expert_out).astype(BF16)


def finish(slot, gate, returned):
    rows = slot.shape[1]
    slots, d = returned.shape
    return pl.pallas_call(
        finish_kernel,
        out_shape=jax.ShapeDtypeStruct((rows, d), BF16),
        in_specs=[VMEM] * 3,
        out_specs=VMEM,
        compiler_params=pltpu.CompilerParams(vmem_limit_bytes=32 * MIB),
        cost_estimate=pl.CostEstimate(
            flops=2 * slots * rows * d, bytes_accessed=2 * d * (slots + rows), transcendentals=0
        ),
        name="finish",
    )(slot, gate.reshape(1, rows), returned)


def exchange(array):
    return lax.all_to_all(array, "expert", split_axis=0, concat_axis=0, tiled=True)


def relocation_plan(
    grad_hidden, grad_out, grad_route, live_rows, w_down, w_moment, perm, fwd_hidden, fwd_route, fwd_gate
):
    groups = lax.axis_size("expert")
    me = lax.axis_index("expert").astype(jnp.int32).reshape(1)
    capacity = max(4, 2 * grad_hidden.shape[0] // groups)
    d = w_down.shape[2]
    moment_pieces, weight_pieces = split(me, w_moment, w_down, groups)
    packed, fwd_slot = pack_rows(
        live_rows, perm, grad_route, fwd_route, grad_hidden, grad_out, fwd_hidden, weight_pieces[0], groups, capacity
    )
    moment_stack = stacked(along_line(moment_pieces, groups))
    weight_stack = stacked(along_line(weight_pieces, groups))
    packed = after(packed, moment_stack, weight_stack)
    received = exchange(packed.reshape(groups, capacity, -1)).reshape(groups * capacity, -1)
    moment_placed = relocated(me, perm, moment_stack, groups)
    weight_placed = relocated(me, perm, weight_stack, groups)
    moment_new, ortho = orthogonal(me, received, moment_placed, groups)
    weight_new, produced = produce(me, received, ortho, weight_placed, groups)
    returned = exchange(produced.reshape(groups, capacity, d)).reshape(groups * capacity, d)
    return weight_new[None], moment_new[None], finish(fwd_slot, fwd_gate, returned)


def lookup(route_ids, mapping):
    columns = jnp.arange(mapping.shape[0], dtype=jnp.int32)
    hits = route_ids[:, None] == columns[None, :]
    return jnp.sum(jnp.where(hits, mapping[None, :], 0), axis=1)


def slot_matrix(target, is_live, groups, capacity):
    columns = jnp.arange(groups, dtype=jnp.int32)
    onehot = ((target[:, None] == columns[None, :]) & is_live[:, None]).astype(jnp.int32)
    ranked = jnp.sum(jnp.cumsum(onehot, axis=0) * onehot, axis=1) - 1
    slot_of = jnp.where(is_live, target * capacity + ranked, -1)
    slots = jnp.arange(groups * capacity, dtype=jnp.int32)
    return (slots[:, None] == slot_of[None, :]).astype(jnp.bfloat16)


def orthogonalize(moment):
    moment_f = moment.astype(jnp.float32)
    frobenius = jnp.sqrt(jnp.sum(moment_f * moment_f))
    current = (moment_f / (frobenius + norm_floor)).astype(jnp.bfloat16)
    for sweep_index in range(2):
        gramian = lax.dot_general(
            current, current, (((1,), (1,)), ((), ())), preferred_element_type=jnp.float32
        ).astype(jnp.bfloat16)
        squared = jnp.dot(gramian, gramian, preferred_element_type=jnp.float32)
        poly = (cubic_term * gramian.astype(jnp.float32) + quintic_term * squared).astype(
            jnp.bfloat16
        )
        current = (
            linear_term * current.astype(jnp.float32)
            + jnp.dot(poly, current, preferred_element_type=jnp.float32)
        ).astype(jnp.bfloat16)
    return current


def relocate(weight, moment, perm):
    groups = lax.axis_size("expert")
    weight_flat = weight.reshape(groups, -1)
    moment_flat = moment.reshape(groups, -1)
    spread_w, spread_m = (
        lax.all_to_all(weight_flat, "expert", split_axis=0, concat_axis=0, tiled=True),
        lax.all_to_all(moment_flat, "expert", split_axis=0, concat_axis=0, tiled=True),
    )
    devices = jnp.arange(groups, dtype=jnp.int32)
    inverse = jnp.sum(jnp.where(perm[None, :] == devices[:, None], devices[None, :], 0), axis=1)
    ordered_w = jnp.take(spread_w, inverse, axis=0)
    ordered_m = jnp.take(spread_m, inverse, axis=0)
    back_w, back_m = (
        lax.all_to_all(ordered_w, "expert", split_axis=0, concat_axis=0, tiled=True),
        lax.all_to_all(ordered_m, "expert", split_axis=0, concat_axis=0, tiled=True),
    )
    return (back_w.reshape(weight.shape), back_m.reshape(moment.shape))


def routed_plan(
    grad_hidden,
    grad_out,
    grad_route,
    live_rows,
    w_down,
    w_moment,
    perm,
    fwd_hidden,
    fwd_route,
    fwd_gate,
):
    groups = lax.axis_size("expert")
    grad_count = grad_hidden.shape[0]
    capacity = max(4, 2 * grad_count // groups)
    is_live = jnp.arange(grad_count, dtype=jnp.int32) < live_rows[0]
    route_ids = grad_route[:, 0]
    weight, moment = relocate(w_down, w_moment, perm)
    target = lookup(route_ids, perm)
    selector = slot_matrix(target, is_live, groups, capacity)
    hidden_buf = (
        jnp.dot(selector, grad_hidden, preferred_element_type=jnp.float32)
        .astype(jnp.bfloat16)
        .reshape(groups, capacity, -1)
    )
    outgrad_buf = (
        jnp.dot(selector, grad_out, preferred_element_type=jnp.float32)
        .astype(jnp.bfloat16)
        .reshape(groups, capacity, -1)
    )
    recv_hidden, recv_outgrad = (
        lax.all_to_all(hidden_buf, "expert", split_axis=0, concat_axis=0, tiled=True),
        lax.all_to_all(outgrad_buf, "expert", split_axis=0, concat_axis=0, tiled=True),
    )
    grad = lax.dot_general(
        recv_hidden.reshape(groups * capacity, -1),
        recv_outgrad.reshape(groups * capacity, -1),
        (((0,), (0,)), ((), ())),
        preferred_element_type=jnp.float32,
    )
    moment_new = (moment_decay * moment[0].astype(jnp.float32) + grad).astype(jnp.bfloat16)
    ortho = orthogonalize(moment_new)
    weight_new = (weight[0].astype(jnp.float32) - step_scale * ortho.astype(jnp.float32)).astype(
        jnp.bfloat16
    )
    weight_new = weight_new[None]
    moment_new = moment_new[None]
    fwd_ids = fwd_route[:, 0]
    placed_weight, placed_moment = (weight_new, moment_new)
    fwd_target = lookup(fwd_ids, perm)
    fwd_weight = weight_new[0]
    fwd_count = fwd_hidden.shape[0]
    fwd_capacity = max(4, 2 * fwd_count // groups)
    fwd_selector = slot_matrix(fwd_target, jnp.ones((fwd_count,), dtype=bool), groups, fwd_capacity)
    fwd_buf = (
        jnp.dot(fwd_selector, fwd_hidden, preferred_element_type=jnp.float32)
        .astype(jnp.bfloat16)
        .reshape(groups, fwd_capacity, -1)
    )
    produced = jnp.einsum(
        "gkf,fd->gkd",
        lax.all_to_all(fwd_buf, "expert", split_axis=0, concat_axis=0, tiled=True),
        fwd_weight,
        preferred_element_type=jnp.float32,
    ).astype(jnp.bfloat16)
    returned = lax.all_to_all(produced, "expert", split_axis=0, concat_axis=0, tiled=True)
    fwd_rows_out = lax.dot_general(
        fwd_selector,
        returned.reshape(groups * fwd_capacity, -1),
        (((0,), (0,)), ((), ())),
        preferred_element_type=jnp.float32,
    )
    fwd_out = (fwd_rows_out * fwd_gate[:, None]).astype(jnp.bfloat16)
    return (placed_weight, placed_moment, fwd_out)


def solution(mesh):
    groups = mesh.shape["expert"]
    in_specs = (
        P(("layer", "expert"), None),
        P(("layer", "expert"), None),
        P(("layer", "expert"), None),
        P(("layer", "expert")),
        P(("layer", "expert"), None, None),
        P(("layer", "expert"), None, None),
        P("layer"),
        P(("layer", "expert"), None),
        P(("layer", "expert"), None),
        P(("layer", "expert")),
    )
    out_specs = (
        P(("layer", "expert"), None, None),
        P(("layer", "expert"), None, None),
        P(("layer", "expert"), None),
    )

    def per_device(*args):
        few = groups & (groups - 1) == 0 and groups <= 2 * args[0].shape[0] // groups
        return (relocation_plan if few else routed_plan)(*args)

    return jax.shard_map(
        per_device, mesh=mesh, in_specs=in_specs, out_specs=out_specs, check_vma=False
    )
```

```python
import functools

import jax
import jax.numpy as jnp
from jax import lax
from jax.experimental import pallas as pl
from jax.experimental.pallas import tpu as pltpu
from jax.sharding import PartitionSpec as P

linear_term = 3.4445
cubic_term = -4.775
quintic_term = 2.0315
moment_decay = 0.9
step_scale = 0.25
norm_floor = 1e-07

F32 = jnp.float32
BF16 = jnp.bfloat16
HBM = pl.BlockSpec(memory_space=pltpu.HBM)
VMEM = pl.BlockSpec(memory_space=pltpu.VMEM)
SMEM = pl.BlockSpec(memory_space=pltpu.SMEM)
ANY = pl.BlockSpec(memory_space=pl.ANY)
MIB = 1 << 20


def plane_of(groups):
    return 1 << ((groups.bit_length() - 1) // 2)


def line_order(line):
    return [0] + sorted(range(1, line), key=lambda k: (k.bit_length() < line.bit_length() - 1, k))


def along_line(pieces, groups):
    plane = plane_of(groups)
    return [
        lax.ppermute(piece, "expert", [(i, i ^ (k * plane)) for i in range(groups)]) if k else piece
        for k, piece in zip(line_order(groups // plane), pieces)
    ]


def cross(array, bit, groups):
    return lax.ppermute(array, "expert", [(i, i ^ (1 << bit)) for i in range(groups)])


def in_plane(column, groups):
    bits = list(reversed(range(plane_of(groups).bit_length() - 1)))
    across = [cross(piece, bits[0], groups) for piece in column] if bits else None
    stack, token = stacked(column)
    stacks = [stack] + ([stacked(across)[0]] if bits else [])
    for bit in bits[1:]:
        stacks += [cross(held, bit, groups) for held in stacks]
    return stacks, token


def plane_offsets(groups):
    offsets = [0]
    for bit in reversed(range(plane_of(groups).bit_length() - 1)):
        offsets += [offset ^ (1 << bit) for offset in offsets]
    return offsets


def block_at(k, rows):
    return pl.ds(pl.multiple_of(k * rows, rows), rows)


def after_kernel(*refs):
    pass


def after(array, *earlier):
    return pl.pallas_call(
        after_kernel,
        out_shape=jax.ShapeDtypeStruct(array.shape, array.dtype),
        in_specs=[ANY] * (1 + len(earlier)),
        out_specs=ANY,
        input_output_aliases={0: 0},
        cost_estimate=pl.CostEstimate(flops=0, bytes_accessed=0, transcendentals=0),
        name="after",
    )(array, *earlier)


def split_kernel(plane, me_ref, moment_ref, weight_ref, *refs):
    pieces, sem = refs[:-1], refs[-1]
    line = len(pieces) // 2
    place = me_ref[0] // plane
    copies = [
        pltpu.make_async_copy(
            source.at[0, block_at(place ^ k, pieces[0].shape[0])], pieces[lead * line + n], sem.at[lead * line + n]
        )
        for lead, source in enumerate((moment_ref, weight_ref))
        for n, k in enumerate(line_order(line))
    ]
    for copy in copies:
        copy.start()
    for copy in copies:
        copy.wait()


def split(me, moment, weight, groups):
    _, ff, d = weight.shape
    plane = plane_of(groups)
    line = groups // plane
    piece = jax.ShapeDtypeStruct((ff // line, d), BF16)
    pieces = pl.pallas_call(
        functools.partial(split_kernel, plane),
        out_shape=(piece,) * (2 * line),
        in_specs=[SMEM, HBM, HBM],
        out_specs=(VMEM,) * (2 * line),
        scratch_shapes=[pltpu.SemaphoreType.DMA((2 * line,))],
        compiler_params=pltpu.CompilerParams(vmem_limit_bytes=60 * MIB),
        cost_estimate=pl.CostEstimate(flops=0, bytes_accessed=8 * ff * d, transcendentals=0),
        name="split",
    )(me, moment, weight)
    return pieces[:line], pieces[line:]


def stack_kernel(order, *refs):
    stack_ref, token_ref = refs[-2:]
    for k, piece in zip(order, refs):
        stack_ref[k] = piece[...]
    token_ref[...] = jnp.zeros_like(token_ref)


def stacked(pieces):
    line = len(pieces)
    shape = (line,) + pieces[0].shape
    return pl.pallas_call(
        functools.partial(stack_kernel, line_order(line)),
        out_shape=(jax.ShapeDtypeStruct(shape, BF16), jax.ShapeDtypeStruct((8, 128), F32)),
        in_specs=[VMEM] * line,
        out_specs=(VMEM, VMEM),
        compiler_params=pltpu.CompilerParams(vmem_limit_bytes=32 * MIB),
        cost_estimate=pl.CostEstimate(flops=0, bytes_accessed=4 * line * pieces[0].size, transcendentals=0),
        name="stack",
    )(*pieces)


def pick_kernel(groups, me_ref, perm_ref, *refs):
    plane = plane_of(groups)
    line = groups // plane
    stacks, targets = refs[:plane], refs[plane:]
    me = me_ref[0]
    for k, target in zip(line_order(line), targets):
        expert = 0
        for e in range(groups):
            expert = jnp.where(perm_ref[e] == me ^ (k * plane), e, expert)
        offset, place = (expert ^ me) % plane, (expert ^ me) // plane
        for stack, held in zip(plane_offsets(groups), stacks):

            @pl.when(offset == stack)
            def _():
                target[...] = held[place]


def pick(me, perm, stacks, groups):
    line = stacks[0].shape[0]
    piece = jax.ShapeDtypeStruct(stacks[0].shape[1:], BF16)
    return pl.pallas_call(
        functools.partial(pick_kernel, groups),
        out_shape=(piece,) * line,
        in_specs=[SMEM, SMEM] + [VMEM] * len(stacks),
        out_specs=(VMEM,) * line,
        compiler_params=pltpu.CompilerParams(vmem_limit_bytes=32 * MIB),
        cost_estimate=pl.CostEstimate(flops=0, bytes_accessed=4 * stacks[0].size, transcendentals=0),
        name="pick",
    )(me, perm, *stacks)


def assembled(plane, me_ref, pieces, held):
    rows = pieces[0].shape[0]
    for k, piece in zip(line_order(len(pieces)), pieces):
        held[block_at((me_ref[0] // plane) ^ k, rows)] = piece[...]
    return held[...].astype(F32)


def slot_rows(route, live, groups, capacity, perm_ref):
    rows = route.shape[1]
    experts = lax.broadcasted_iota(jnp.int32, (groups, rows), 0)
    onehot = jnp.where((experts == route) & live, 1.0, 0.0).astype(BF16)
    before = lax.broadcasted_iota(jnp.int32, (rows, rows), 0)
    after = lax.broadcasted_iota(jnp.int32, (rows, rows), 1)
    upto = jnp.where(before <= after, 1.0, 0.0).astype(BF16)
    ranks = jnp.dot(onehot, upto, preferred_element_type=F32)
    rank = jnp.sum(ranks * onehot.astype(F32), axis=0, keepdims=True).astype(jnp.int32) - 1
    target = jnp.zeros_like(route)
    for e in range(groups):
        target = jnp.where(route == e, perm_ref[e], target)
    return jnp.where(live, target * capacity + rank, -1)


def selector_of(slot, slots):
    rows = slot.shape[1]
    places = lax.broadcasted_iota(jnp.int32, (slots, rows), 0)
    return jnp.where(places == slot, 1.0, 0.0).astype(BF16)


def pack_kernel(groups, live_ref, perm_ref, *refs):
    sources, (packed_ref, slot_ref), held, sem = refs[:5], refs[6:8], refs[8:13], refs[13]
    route_ref, fwd_route_ref, hidden_ref, out_ref, fwd_ref = held
    copies = [pltpu.make_async_copy(ref, room, sem.at[n]) for n, (ref, room) in enumerate(zip(sources, held))]
    for copy in copies:
        copy.start()
    rows, ff = hidden_ref.shape
    d = out_ref.shape[1]
    slots = packed_ref.shape[0]
    capacity = slots // groups
    place = lax.broadcasted_iota(jnp.int32, (1, rows), 1)
    copies[0].wait()
    selector = selector_of(slot_rows(route_ref[...], place < live_ref[0], groups, capacity, perm_ref), slots)
    copies[1].wait()
    fwd_slot = slot_rows(fwd_route_ref[...], place >= 0, groups, capacity, perm_ref)
    slot_ref[...] = fwd_slot
    fwd_selector = selector_of(fwd_slot, slots)
    copies[2].wait()
    packed_ref[:, :ff] = jnp.dot(selector, hidden_ref[...], preferred_element_type=F32).astype(BF16)
    copies[3].wait()
    packed_ref[:, ff : ff + d] = jnp.dot(selector, out_ref[...], preferred_element_type=F32).astype(BF16)
    copies[4].wait()
    packed_ref[:, ff + d :] = jnp.dot(fwd_selector, fwd_ref[...], preferred_element_type=F32).astype(BF16)


def pack_rows(live_rows, perm, route, fwd_route, hidden, grad_out, fwd_hidden, earlier, groups, capacity):
    rows, ff = hidden.shape
    width = 2 * ff + grad_out.shape[1]
    sources = (route.reshape(1, rows), fwd_route.reshape(1, rows), hidden, grad_out, fwd_hidden)
    return pl.pallas_call(
        functools.partial(pack_kernel, groups),
        out_shape=(
            jax.ShapeDtypeStruct((groups * capacity, width), BF16),
            jax.ShapeDtypeStruct((1, rows), jnp.int32),
        ),
        in_specs=[SMEM, SMEM] + [HBM] * 5 + [ANY],
        out_specs=(VMEM, VMEM),
        scratch_shapes=[pltpu.VMEM(a.shape, a.dtype) for a in sources] + [pltpu.SemaphoreType.DMA((len(sources),))],
        compiler_params=pltpu.CompilerParams(vmem_limit_bytes=60 * MIB),
        cost_estimate=pl.CostEstimate(
            flops=2 * groups * capacity * rows * width, bytes_accessed=6 * rows * width, transcendentals=0
        ),
        name="pack_rows",
    )(live_rows, perm, *sources, earlier)


def orthogonal_kernel(plane, me_ref, packed_ref, *refs):
    pieces, (moment_new_ref, ortho_ref, held) = refs[:-3], refs[-3:]
    ff, d = ortho_ref.shape
    grad = lax.dot_general(
        packed_ref[:, :ff], packed_ref[:, ff : ff + d], (((0,), (0,)), ((), ())), preferred_element_type=F32
    )
    moment_new = (moment_decay * assembled(plane, me_ref, pieces, held) + grad).astype(BF16)
    moment_new_ref[...] = moment_new
    moment_f = moment_new.astype(F32)
    frobenius = jnp.sqrt(jnp.sum(moment_f * moment_f))
    current = (moment_f / (frobenius + norm_floor)).astype(BF16)
    for _ in range(2):
        gramian = lax.dot_general(
            current, current, (((1,), (1,)), ((), ())), preferred_element_type=F32
        ).astype(BF16)
        squared = jnp.dot(gramian, gramian, preferred_element_type=F32)
        poly = (cubic_term * gramian.astype(F32) + quintic_term * squared).astype(BF16)
        current = (
            linear_term * current.astype(F32) + jnp.dot(poly, current, preferred_element_type=F32)
        ).astype(BF16)
    ortho_ref[...] = current


def orthogonal(me, packed, pieces, groups):
    line = len(pieces)
    rows, d = pieces[0].shape
    ff = rows * line
    shape = jax.ShapeDtypeStruct((ff, d), BF16)
    return pl.pallas_call(
        functools.partial(orthogonal_kernel, plane_of(groups)),
        out_shape=(shape, shape),
        in_specs=[SMEM] + [VMEM] * (1 + line),
        out_specs=(VMEM, VMEM),
        scratch_shapes=[pltpu.VMEM((ff, d), BF16)],
        compiler_params=pltpu.CompilerParams(vmem_limit_bytes=40 * MIB),
        cost_estimate=pl.CostEstimate(
            flops=2 * ff * d * packed.shape[0] + 8 * ff * ff * d + 4 * ff**3,
            bytes_accessed=6 * ff * d + 2 * packed.size,
            transcendentals=1,
        ),
        name="orthogonal",
    )(me, packed, *pieces)


def produce_kernel(plane, me_ref, packed_ref, ortho_ref, *refs):
    pieces, (weight_new_ref, produced_ref, held) = refs[:-3], refs[-3:]
    ff, d = ortho_ref.shape
    weight = assembled(plane, me_ref, pieces, held)
    weight_new = (weight - step_scale * ortho_ref[...].astype(F32)).astype(BF16)
    weight_new_ref[...] = weight_new
    produced_ref[...] = jnp.dot(packed_ref[:, ff + d :], weight_new, preferred_element_type=F32).astype(BF16)


def produce(me, packed, ortho, pieces, groups):
    slots = packed.shape[0]
    ff, d = ortho.shape
    return pl.pallas_call(
        functools.partial(produce_kernel, plane_of(groups)),
        out_shape=(jax.ShapeDtypeStruct((ff, d), BF16), jax.ShapeDtypeStruct((slots, d), BF16)),
        in_specs=[SMEM] + [VMEM] * (2 + len(pieces)),
        out_specs=(VMEM, VMEM),
        scratch_shapes=[pltpu.VMEM((ff, d), BF16)],
        compiler_params=pltpu.CompilerParams(vmem_limit_bytes=40 * MIB),
        cost_estimate=pl.CostEstimate(
            flops=2 * slots * ff * d, bytes_accessed=8 * ff * d + 2 * slots * (ff + d), transcendentals=0
        ),
        name="produce",
    )(me, packed, ortho, *pieces)


def finish_kernel(slot_ref, gate_ref, returned_ref, out_ref):
    rows = slot_ref.shape[1]
    selector = selector_of(slot_ref[...], returned_ref.shape[0])
    expert_out = lax.dot_general(
        selector, returned_ref[...], (((0,), (0,)), ((), ())), preferred_element_type=F32
    )
    down = lax.broadcasted_iota(jnp.int32, (rows, rows), 0)
    across = lax.broadcasted_iota(jnp.int32, (rows, rows), 1)
    gate = jnp.sum(jnp.where(down == across, gate_ref[...], 0.0), axis=1, keepdims=True)
    out_ref[...] = (gate * expert_out).astype(BF16)


def finish(slot, gate, returned):
    rows = slot.shape[1]
    slots, d = returned.shape
    return pl.pallas_call(
        finish_kernel,
        out_shape=jax.ShapeDtypeStruct((rows, d), BF16),
        in_specs=[VMEM] * 3,
        out_specs=VMEM,
        compiler_params=pltpu.CompilerParams(vmem_limit_bytes=32 * MIB),
        cost_estimate=pl.CostEstimate(
            flops=2 * slots * rows * d, bytes_accessed=2 * d * (slots + rows), transcendentals=0
        ),
        name="finish",
    )(slot, gate.reshape(1, rows), returned)


def exchange(array):
    return lax.all_to_all(array, "expert", split_axis=0, concat_axis=0, tiled=True)


def relocation_plan(
    grad_hidden, grad_out, grad_route, live_rows, w_down, w_moment, perm, fwd_hidden, fwd_route, fwd_gate
):
    groups = lax.axis_size("expert")
    me = lax.axis_index("expert").astype(jnp.int32).reshape(1)
    capacity = max(4, 2 * grad_hidden.shape[0] // groups)
    d = w_down.shape[2]
    moment_pieces, weight_pieces = split(me, w_moment, w_down, groups)
    packed, fwd_slot = pack_rows(
        live_rows, perm, grad_route, fwd_route, grad_hidden, grad_out, fwd_hidden, weight_pieces[0], groups, capacity
    )
    moment_stacks, moment_here = in_plane(along_line(moment_pieces, groups), groups)
    weight_stacks, weight_here = in_plane(along_line(weight_pieces, groups), groups)
    packed = after(packed, moment_here, weight_here)
    received = exchange(packed.reshape(groups, capacity, -1)).reshape(groups * capacity, -1)
    moment_placed = along_line(pick(me, perm, moment_stacks, groups), groups)
    weight_placed = along_line(pick(me, perm, weight_stacks, groups), groups)
    moment_new, ortho = orthogonal(me, received, moment_placed, groups)
    weight_new, produced = produce(me, received, ortho, weight_placed, groups)
    returned = exchange(produced.reshape(groups, capacity, d)).reshape(groups * capacity, d)
    return weight_new[None], moment_new[None], finish(fwd_slot, fwd_gate, returned)


def lookup(route_ids, mapping):
    columns = jnp.arange(mapping.shape[0], dtype=jnp.int32)
    hits = route_ids[:, None] == columns[None, :]
    return jnp.sum(jnp.where(hits, mapping[None, :], 0), axis=1)


def slot_matrix(target, is_live, groups, capacity):
    columns = jnp.arange(groups, dtype=jnp.int32)
    onehot = ((target[:, None] == columns[None, :]) & is_live[:, None]).astype(jnp.int32)
    ranked = jnp.sum(jnp.cumsum(onehot, axis=0) * onehot, axis=1) - 1
    slot_of = jnp.where(is_live, target * capacity + ranked, -1)
    slots = jnp.arange(groups * capacity, dtype=jnp.int32)
    return (slots[:, None] == slot_of[None, :]).astype(jnp.bfloat16)


def orthogonalize(moment):
    moment_f = moment.astype(jnp.float32)
    frobenius = jnp.sqrt(jnp.sum(moment_f * moment_f))
    current = (moment_f / (frobenius + norm_floor)).astype(jnp.bfloat16)
    for sweep_index in range(2):
        gramian = lax.dot_general(
            current, current, (((1,), (1,)), ((), ())), preferred_element_type=jnp.float32
        ).astype(jnp.bfloat16)
        squared = jnp.dot(gramian, gramian, preferred_element_type=jnp.float32)
        poly = (cubic_term * gramian.astype(jnp.float32) + quintic_term * squared).astype(
            jnp.bfloat16
        )
        current = (
            linear_term * current.astype(jnp.float32)
            + jnp.dot(poly, current, preferred_element_type=jnp.float32)
        ).astype(jnp.bfloat16)
    return current


def relocate(weight, moment, perm):
    groups = lax.axis_size("expert")
    weight_flat = weight.reshape(groups, -1)
    moment_flat = moment.reshape(groups, -1)
    spread_w, spread_m = (
        lax.all_to_all(weight_flat, "expert", split_axis=0, concat_axis=0, tiled=True),
        lax.all_to_all(moment_flat, "expert", split_axis=0, concat_axis=0, tiled=True),
    )
    devices = jnp.arange(groups, dtype=jnp.int32)
    inverse = jnp.sum(jnp.where(perm[None, :] == devices[:, None], devices[None, :], 0), axis=1)
    ordered_w = jnp.take(spread_w, inverse, axis=0)
    ordered_m = jnp.take(spread_m, inverse, axis=0)
    back_w, back_m = (
        lax.all_to_all(ordered_w, "expert", split_axis=0, concat_axis=0, tiled=True),
        lax.all_to_all(ordered_m, "expert", split_axis=0, concat_axis=0, tiled=True),
    )
    return (back_w.reshape(weight.shape), back_m.reshape(moment.shape))


def routed_plan(
    grad_hidden,
    grad_out,
    grad_route,
    live_rows,
    w_down,
    w_moment,
    perm,
    fwd_hidden,
    fwd_route,
    fwd_gate,
):
    groups = lax.axis_size("expert")
    grad_count = grad_hidden.shape[0]
    capacity = max(4, 2 * grad_count // groups)
    is_live = jnp.arange(grad_count, dtype=jnp.int32) < live_rows[0]
    route_ids = grad_route[:, 0]
    weight, moment = relocate(w_down, w_moment, perm)
    target = lookup(route_ids, perm)
    selector = slot_matrix(target, is_live, groups, capacity)
    hidden_buf = (
        jnp.dot(selector, grad_hidden, preferred_element_type=jnp.float32)
        .astype(jnp.bfloat16)
        .reshape(groups, capacity, -1)
    )
    outgrad_buf = (
        jnp.dot(selector, grad_out, preferred_element_type=jnp.float32)
        .astype(jnp.bfloat16)
        .reshape(groups, capacity, -1)
    )
    recv_hidden, recv_outgrad = (
        lax.all_to_all(hidden_buf, "expert", split_axis=0, concat_axis=0, tiled=True),
        lax.all_to_all(outgrad_buf, "expert", split_axis=0, concat_axis=0, tiled=True),
    )
    grad = lax.dot_general(
        recv_hidden.reshape(groups * capacity, -1),
        recv_outgrad.reshape(groups * capacity, -1),
        (((0,), (0,)), ((), ())),
        preferred_element_type=jnp.float32,
    )
    moment_new = (moment_decay * moment[0].astype(jnp.float32) + grad).astype(jnp.bfloat16)
    ortho = orthogonalize(moment_new)
    weight_new = (weight[0].astype(jnp.float32) - step_scale * ortho.astype(jnp.float32)).astype(
        jnp.bfloat16
    )
    weight_new = weight_new[None]
    moment_new = moment_new[None]
    fwd_ids = fwd_route[:, 0]
    placed_weight, placed_moment = (weight_new, moment_new)
    fwd_target = lookup(fwd_ids, perm)
    fwd_weight = weight_new[0]
    fwd_count = fwd_hidden.shape[0]
    fwd_capacity = max(4, 2 * fwd_count // groups)
    fwd_selector = slot_matrix(fwd_target, jnp.ones((fwd_count,), dtype=bool), groups, fwd_capacity)
    fwd_buf = (
        jnp.dot(fwd_selector, fwd_hidden, preferred_element_type=jnp.float32)
        .astype(jnp.bfloat16)
        .reshape(groups, fwd_capacity, -1)
    )
    produced = jnp.einsum(
        "gkf,fd->gkd",
        lax.all_to_all(fwd_buf, "expert", split_axis=0, concat_axis=0, tiled=True),
        fwd_weight,
        preferred_element_type=jnp.float32,
    ).astype(jnp.bfloat16)
    returned = lax.all_to_all(produced, "expert", split_axis=0, concat_axis=0, tiled=True)
    fwd_rows_out = lax.dot_general(
        fwd_selector,
        returned.reshape(groups * fwd_capacity, -1),
        (((0,), (0,)), ((), ())),
        preferred_element_type=jnp.float32,
    )
    fwd_out = (fwd_rows_out * fwd_gate[:, None]).astype(jnp.bfloat16)
    return (placed_weight, placed_moment, fwd_out)


def solution(mesh):
    groups = mesh.shape["expert"]
    in_specs = (
        P(("layer", "expert"), None),
        P(("layer", "expert"), None),
        P(("layer", "expert"), None),
        P(("layer", "expert")),
        P(("layer", "expert"), None, None),
        P(("layer", "expert"), None, None),
        P("layer"),
        P(("layer", "expert"), None),
        P(("layer", "expert"), None),
        P(("layer", "expert")),
    )
    out_specs = (
        P(("layer", "expert"), None, None),
        P(("layer", "expert"), None, None),
        P(("layer", "expert"), None),
    )

    def per_device(*args):
        few = groups & (groups - 1) == 0 and groups <= 2 * args[0].shape[0] // groups
        return (relocation_plan if few else routed_plan)(*args)

    return jax.shard_map(
        per_device, mesh=mesh, in_specs=in_specs, out_specs=out_specs, check_vma=False
    )
```

```python
import functools

import jax
import jax.numpy as jnp
from jax import lax
from jax.experimental import pallas as pl
from jax.experimental.pallas import tpu as pltpu
from jax.sharding import PartitionSpec as P

linear_term = 3.4445
cubic_term = -4.775
quintic_term = 2.0315
moment_decay = 0.9
step_scale = 0.25
norm_floor = 1e-07

F32 = jnp.float32
BF16 = jnp.bfloat16
HBM = pl.BlockSpec(memory_space=pltpu.HBM)
VMEM = pl.BlockSpec(memory_space=pltpu.VMEM)
SMEM = pl.BlockSpec(memory_space=pltpu.SMEM)
ANY = pl.BlockSpec(memory_space=pl.ANY)
MIB = 1 << 20


def plane_of(groups):
    return 1 << ((groups.bit_length() - 1) // 2)


def line_order(line):
    return [0] + sorted(range(1, line), key=lambda k: (k.bit_length() < line.bit_length() - 1, k))


def along_line(pieces, groups):
    plane = plane_of(groups)
    return [
        lax.ppermute(piece, "expert", [(i, i ^ (k * plane)) for i in range(groups)]) if k else piece
        for k, piece in zip(line_order(groups // plane), pieces)
    ]


def cross(array, bit, groups):
    return lax.ppermute(array, "expert", [(i, i ^ (1 << bit)) for i in range(groups)])


def in_plane(column, groups):
    bits = list(reversed(range(plane_of(groups).bit_length() - 1)))
    across = [cross(piece, bits[0], groups) for piece in column] if bits else None
    stacks, tokens = zip(*[stacked(pieces) for pieces in ([column, across] if bits else [column])])
    for bit in bits[1:]:
        stacks += tuple(cross(held, bit, groups) for held in stacks)
    return stacks, tokens


def plane_offsets(groups):
    offsets = [0]
    for bit in reversed(range(plane_of(groups).bit_length() - 1)):
        offsets += [offset ^ (1 << bit) for offset in offsets]
    return offsets


def block_at(k, rows):
    return pl.ds(pl.multiple_of(k * rows, rows), rows)


def after_kernel(*refs):
    pass


def after(array, *earlier):
    return pl.pallas_call(
        after_kernel,
        out_shape=jax.ShapeDtypeStruct(array.shape, array.dtype),
        in_specs=[ANY] * (1 + len(earlier)),
        out_specs=ANY,
        input_output_aliases={0: 0},
        cost_estimate=pl.CostEstimate(flops=0, bytes_accessed=0, transcendentals=0),
        name="after",
    )(array, *earlier)


def split_kernel(plane, me_ref, moment_ref, weight_ref, *refs):
    pieces, sem = refs[:-1], refs[-1]
    line = len(pieces) // 2
    place = me_ref[0] // plane
    copies = [
        pltpu.make_async_copy(
            source.at[0, block_at(place ^ k, pieces[0].shape[0])], pieces[lead * line + n], sem.at[lead * line + n]
        )
        for lead, source in enumerate((moment_ref, weight_ref))
        for n, k in enumerate(line_order(line))
    ]
    for copy in copies:
        copy.start()
    for copy in copies:
        copy.wait()


def split(me, moment, weight, groups):
    _, ff, d = weight.shape
    plane = plane_of(groups)
    line = groups // plane
    piece = jax.ShapeDtypeStruct((ff // line, d), BF16)
    pieces = pl.pallas_call(
        functools.partial(split_kernel, plane),
        out_shape=(piece,) * (2 * line),
        in_specs=[SMEM, HBM, HBM],
        out_specs=(VMEM,) * (2 * line),
        scratch_shapes=[pltpu.SemaphoreType.DMA((2 * line,))],
        compiler_params=pltpu.CompilerParams(vmem_limit_bytes=60 * MIB),
        cost_estimate=pl.CostEstimate(flops=0, bytes_accessed=8 * ff * d, transcendentals=0),
        name="split",
    )(me, moment, weight)
    return pieces[:line], pieces[line:]


def stack_kernel(order, *refs):
    stack_ref, token_ref = refs[-2:]
    for k, piece in zip(order, refs):
        stack_ref[k] = piece[...]
    token_ref[...] = jnp.zeros_like(token_ref)


def stacked(pieces):
    line = len(pieces)
    shape = (line,) + pieces[0].shape
    return pl.pallas_call(
        functools.partial(stack_kernel, line_order(line)),
        out_shape=(jax.ShapeDtypeStruct(shape, BF16), jax.ShapeDtypeStruct((8, 128), F32)),
        in_specs=[VMEM] * line,
        out_specs=(VMEM, VMEM),
        compiler_params=pltpu.CompilerParams(vmem_limit_bytes=32 * MIB),
        cost_estimate=pl.CostEstimate(flops=0, bytes_accessed=4 * line * pieces[0].size, transcendentals=0),
        name="stack",
    )(*pieces)


def pick_kernel(groups, me_ref, perm_ref, *refs):
    plane = plane_of(groups)
    line = groups // plane
    stacks, targets = refs[:plane], refs[plane:]
    me = me_ref[0]
    for k, target in zip(line_order(line), targets):
        expert = 0
        for e in range(groups):
            expert = jnp.where(perm_ref[e] == me ^ (k * plane), e, expert)
        offset, place = (expert ^ me) % plane, (expert ^ me) // plane
        for stack, held in zip(plane_offsets(groups), stacks):

            @pl.when(offset == stack)
            def _():
                target[...] = held[place]


def pick(me, perm, stacks, groups):
    line = stacks[0].shape[0]
    piece = jax.ShapeDtypeStruct(stacks[0].shape[1:], BF16)
    return pl.pallas_call(
        functools.partial(pick_kernel, groups),
        out_shape=(piece,) * line,
        in_specs=[SMEM, SMEM] + [VMEM] * len(stacks),
        out_specs=(VMEM,) * line,
        compiler_params=pltpu.CompilerParams(vmem_limit_bytes=32 * MIB),
        cost_estimate=pl.CostEstimate(flops=0, bytes_accessed=4 * stacks[0].size, transcendentals=0),
        name="pick",
    )(me, perm, *stacks)


def assembled(plane, me_ref, pieces, held):
    rows = pieces[0].shape[0]
    for k, piece in zip(line_order(len(pieces)), pieces):
        held[block_at((me_ref[0] // plane) ^ k, rows)] = piece[...]
    return held[...].astype(F32)


def slot_rows(route, live, groups, capacity, perm_ref):
    rows = route.shape[1]
    experts = lax.broadcasted_iota(jnp.int32, (groups, rows), 0)
    onehot = jnp.where((experts == route) & live, 1.0, 0.0).astype(BF16)
    before = lax.broadcasted_iota(jnp.int32, (rows, rows), 0)
    after = lax.broadcasted_iota(jnp.int32, (rows, rows), 1)
    upto = jnp.where(before <= after, 1.0, 0.0).astype(BF16)
    ranks = jnp.dot(onehot, upto, preferred_element_type=F32)
    rank = jnp.sum(ranks * onehot.astype(F32), axis=0, keepdims=True).astype(jnp.int32) - 1
    target = jnp.zeros_like(route)
    for e in range(groups):
        target = jnp.where(route == e, perm_ref[e], target)
    return jnp.where(live, target * capacity + rank, -1)


def selector_of(slot, slots):
    rows = slot.shape[1]
    places = lax.broadcasted_iota(jnp.int32, (slots, rows), 0)
    return jnp.where(places == slot, 1.0, 0.0).astype(BF16)


def pack_kernel(groups, live_ref, perm_ref, *refs):
    sources, (packed_ref, slot_ref), held, sem = refs[:5], refs[6:8], refs[8:13], refs[13]
    route_ref, fwd_route_ref, hidden_ref, out_ref, fwd_ref = held
    copies = [pltpu.make_async_copy(ref, room, sem.at[n]) for n, (ref, room) in enumerate(zip(sources, held))]
    for copy in copies:
        copy.start()
    rows, ff = hidden_ref.shape
    d = out_ref.shape[1]
    slots = packed_ref.shape[0]
    capacity = slots // groups
    place = lax.broadcasted_iota(jnp.int32, (1, rows), 1)
    copies[0].wait()
    selector = selector_of(slot_rows(route_ref[...], place < live_ref[0], groups, capacity, perm_ref), slots)
    copies[1].wait()
    fwd_slot = slot_rows(fwd_route_ref[...], place >= 0, groups, capacity, perm_ref)
    slot_ref[...] = fwd_slot
    fwd_selector = selector_of(fwd_slot, slots)
    copies[2].wait()
    packed_ref[:, :ff] = jnp.dot(selector, hidden_ref[...], preferred_element_type=F32).astype(BF16)
    copies[3].wait()
    packed_ref[:, ff : ff + d] = jnp.dot(selector, out_ref[...], preferred_element_type=F32).astype(BF16)
    copies[4].wait()
    packed_ref[:, ff + d :] = jnp.dot(fwd_selector, fwd_ref[...], preferred_element_type=F32).astype(BF16)


def pack_rows(live_rows, perm, route, fwd_route, hidden, grad_out, fwd_hidden, earlier, groups, capacity):
    rows, ff = hidden.shape
    width = 2 * ff + grad_out.shape[1]
    sources = (route.reshape(1, rows), fwd_route.reshape(1, rows), hidden, grad_out, fwd_hidden)
    return pl.pallas_call(
        functools.partial(pack_kernel, groups),
        out_shape=(
            jax.ShapeDtypeStruct((groups * capacity, width), BF16),
            jax.ShapeDtypeStruct((1, rows), jnp.int32),
        ),
        in_specs=[SMEM, SMEM] + [HBM] * 5 + [ANY],
        out_specs=(VMEM, VMEM),
        scratch_shapes=[pltpu.VMEM(a.shape, a.dtype) for a in sources] + [pltpu.SemaphoreType.DMA((len(sources),))],
        compiler_params=pltpu.CompilerParams(vmem_limit_bytes=60 * MIB),
        cost_estimate=pl.CostEstimate(
            flops=2 * groups * capacity * rows * width, bytes_accessed=6 * rows * width, transcendentals=0
        ),
        name="pack_rows",
    )(live_rows, perm, *sources, earlier)


def orthogonal_kernel(plane, me_ref, packed_ref, *refs):
    pieces, (moment_new_ref, ortho_ref, held) = refs[:-3], refs[-3:]
    ff, d = ortho_ref.shape
    grad = lax.dot_general(
        packed_ref[:, :ff], packed_ref[:, ff : ff + d], (((0,), (0,)), ((), ())), preferred_element_type=F32
    )
    moment_new = (moment_decay * assembled(plane, me_ref, pieces, held) + grad).astype(BF16)
    moment_new_ref[...] = moment_new
    moment_f = moment_new.astype(F32)
    frobenius = jnp.sqrt(jnp.sum(moment_f * moment_f))
    current = (moment_f / (frobenius + norm_floor)).astype(BF16)
    for _ in range(2):
        gramian = lax.dot_general(
            current, current, (((1,), (1,)), ((), ())), preferred_element_type=F32
        ).astype(BF16)
        squared = jnp.dot(gramian, gramian, preferred_element_type=F32)
        poly = (cubic_term * gramian.astype(F32) + quintic_term * squared).astype(BF16)
        current = (
            linear_term * current.astype(F32) + jnp.dot(poly, current, preferred_element_type=F32)
        ).astype(BF16)
    ortho_ref[...] = current


def orthogonal(me, packed, pieces, groups):
    line = len(pieces)
    rows, d = pieces[0].shape
    ff = rows * line
    shape = jax.ShapeDtypeStruct((ff, d), BF16)
    return pl.pallas_call(
        functools.partial(orthogonal_kernel, plane_of(groups)),
        out_shape=(shape, shape),
        in_specs=[SMEM] + [VMEM] * (1 + line),
        out_specs=(VMEM, VMEM),
        scratch_shapes=[pltpu.VMEM((ff, d), BF16)],
        compiler_params=pltpu.CompilerParams(vmem_limit_bytes=40 * MIB),
        cost_estimate=pl.CostEstimate(
            flops=2 * ff * d * packed.shape[0] + 8 * ff * ff * d + 4 * ff**3,
            bytes_accessed=6 * ff * d + 2 * packed.size,
            transcendentals=1,
        ),
        name="orthogonal",
    )(me, packed, *pieces)


def produce_kernel(plane, me_ref, packed_ref, ortho_ref, *refs):
    pieces, (weight_new_ref, produced_ref, held) = refs[:-3], refs[-3:]
    ff, d = ortho_ref.shape
    weight = assembled(plane, me_ref, pieces, held)
    weight_new = (weight - step_scale * ortho_ref[...].astype(F32)).astype(BF16)
    weight_new_ref[...] = weight_new
    produced_ref[...] = jnp.dot(packed_ref[:, ff + d :], weight_new, preferred_element_type=F32).astype(BF16)


def produce(me, packed, ortho, pieces, groups):
    slots = packed.shape[0]
    ff, d = ortho.shape
    return pl.pallas_call(
        functools.partial(produce_kernel, plane_of(groups)),
        out_shape=(jax.ShapeDtypeStruct((ff, d), BF16), jax.ShapeDtypeStruct((slots, d), BF16)),
        in_specs=[SMEM] + [VMEM] * (2 + len(pieces)),
        out_specs=(VMEM, VMEM),
        scratch_shapes=[pltpu.VMEM((ff, d), BF16)],
        compiler_params=pltpu.CompilerParams(vmem_limit_bytes=40 * MIB),
        cost_estimate=pl.CostEstimate(
            flops=2 * slots * ff * d, bytes_accessed=8 * ff * d + 2 * slots * (ff + d), transcendentals=0
        ),
        name="produce",
    )(me, packed, ortho, *pieces)


def finish_kernel(slot_ref, gate_ref, returned_ref, out_ref):
    rows = slot_ref.shape[1]
    selector = selector_of(slot_ref[...], returned_ref.shape[0])
    expert_out = lax.dot_general(
        selector, returned_ref[...], (((0,), (0,)), ((), ())), preferred_element_type=F32
    )
    down = lax.broadcasted_iota(jnp.int32, (rows, rows), 0)
    across = lax.broadcasted_iota(jnp.int32, (rows, rows), 1)
    gate = jnp.sum(jnp.where(down == across, gate_ref[...], 0.0), axis=1, keepdims=True)
    out_ref[...] = (gate * expert_out).astype(BF16)


def finish(slot, gate, returned):
    rows = slot.shape[1]
    slots, d = returned.shape
    return pl.pallas_call(
        finish_kernel,
        out_shape=jax.ShapeDtypeStruct((rows, d), BF16),
        in_specs=[VMEM] * 3,
        out_specs=VMEM,
        compiler_params=pltpu.CompilerParams(vmem_limit_bytes=32 * MIB),
        cost_estimate=pl.CostEstimate(
            flops=2 * slots * rows * d, bytes_accessed=2 * d * (slots + rows), transcendentals=0
        ),
        name="finish",
    )(slot, gate.reshape(1, rows), returned)


def exchange(array):
    return lax.all_to_all(array, "expert", split_axis=0, concat_axis=0, tiled=True)


def relocation_plan(
    grad_hidden, grad_out, grad_route, live_rows, w_down, w_moment, perm, fwd_hidden, fwd_route, fwd_gate
):
    groups = lax.axis_size("expert")
    me = lax.axis_index("expert").astype(jnp.int32).reshape(1)
    capacity = max(4, 2 * grad_hidden.shape[0] // groups)
    d = w_down.shape[2]
    moment_pieces, weight_pieces = split(me, w_moment, w_down, groups)
    packed, fwd_slot = pack_rows(
        live_rows, perm, grad_route, fwd_route, grad_hidden, grad_out, fwd_hidden, weight_pieces[0], groups, capacity
    )
    moment_stacks, moment_here = in_plane(along_line(moment_pieces, groups), groups)
    weight_stacks, weight_here = in_plane(along_line(weight_pieces, groups), groups)
    packed = after(packed, *moment_here, *weight_here)
    received = exchange(packed.reshape(groups, capacity, -1)).reshape(groups * capacity, -1)
    moment_placed = along_line(pick(me, perm, moment_stacks, groups), groups)
    weight_placed = along_line(pick(me, perm, weight_stacks, groups), groups)
    moment_new, ortho = orthogonal(me, received, moment_placed, groups)
    weight_new, produced = produce(me, received, ortho, weight_placed, groups)
    returned = exchange(produced.reshape(groups, capacity, d)).reshape(groups * capacity, d)
    return weight_new[None], moment_new[None], finish(fwd_slot, fwd_gate, returned)


def lookup(route_ids, mapping):
    columns = jnp.arange(mapping.shape[0], dtype=jnp.int32)
    hits = route_ids[:, None] == columns[None, :]
    return jnp.sum(jnp.where(hits, mapping[None, :], 0), axis=1)


def slot_matrix(target, is_live, groups, capacity):
    columns = jnp.arange(groups, dtype=jnp.int32)
    onehot = ((target[:, None] == columns[None, :]) & is_live[:, None]).astype(jnp.int32)
    ranked = jnp.sum(jnp.cumsum(onehot, axis=0) * onehot, axis=1) - 1
    slot_of = jnp.where(is_live, target * capacity + ranked, -1)
    slots = jnp.arange(groups * capacity, dtype=jnp.int32)
    return (slots[:, None] == slot_of[None, :]).astype(jnp.bfloat16)


def orthogonalize(moment):
    moment_f = moment.astype(jnp.float32)
    frobenius = jnp.sqrt(jnp.sum(moment_f * moment_f))
    current = (moment_f / (frobenius + norm_floor)).astype(jnp.bfloat16)
    for sweep_index in range(2):
        gramian = lax.dot_general(
            current, current, (((1,), (1,)), ((), ())), preferred_element_type=jnp.float32
        ).astype(jnp.bfloat16)
        squared = jnp.dot(gramian, gramian, preferred_element_type=jnp.float32)
        poly = (cubic_term * gramian.astype(jnp.float32) + quintic_term * squared).astype(
            jnp.bfloat16
        )
        current = (
            linear_term * current.astype(jnp.float32)
            + jnp.dot(poly, current, preferred_element_type=jnp.float32)
        ).astype(jnp.bfloat16)
    return current


def relocate(weight, moment, perm):
    groups = lax.axis_size("expert")
    weight_flat = weight.reshape(groups, -1)
    moment_flat = moment.reshape(groups, -1)
    spread_w, spread_m = (
        lax.all_to_all(weight_flat, "expert", split_axis=0, concat_axis=0, tiled=True),
        lax.all_to_all(moment_flat, "expert", split_axis=0, concat_axis=0, tiled=True),
    )
    devices = jnp.arange(groups, dtype=jnp.int32)
    inverse = jnp.sum(jnp.where(perm[None, :] == devices[:, None], devices[None, :], 0), axis=1)
    ordered_w = jnp.take(spread_w, inverse, axis=0)
    ordered_m = jnp.take(spread_m, inverse, axis=0)
    back_w, back_m = (
        lax.all_to_all(ordered_w, "expert", split_axis=0, concat_axis=0, tiled=True),
        lax.all_to_all(ordered_m, "expert", split_axis=0, concat_axis=0, tiled=True),
    )
    return (back_w.reshape(weight.shape), back_m.reshape(moment.shape))


def routed_plan(
    grad_hidden,
    grad_out,
    grad_route,
    live_rows,
    w_down,
    w_moment,
    perm,
    fwd_hidden,
    fwd_route,
    fwd_gate,
):
    groups = lax.axis_size("expert")
    grad_count = grad_hidden.shape[0]
    capacity = max(4, 2 * grad_count // groups)
    is_live = jnp.arange(grad_count, dtype=jnp.int32) < live_rows[0]
    route_ids = grad_route[:, 0]
    weight, moment = relocate(w_down, w_moment, perm)
    target = lookup(route_ids, perm)
    selector = slot_matrix(target, is_live, groups, capacity)
    hidden_buf = (
        jnp.dot(selector, grad_hidden, preferred_element_type=jnp.float32)
        .astype(jnp.bfloat16)
        .reshape(groups, capacity, -1)
    )
    outgrad_buf = (
        jnp.dot(selector, grad_out, preferred_element_type=jnp.float32)
        .astype(jnp.bfloat16)
        .reshape(groups, capacity, -1)
    )
    recv_hidden, recv_outgrad = (
        lax.all_to_all(hidden_buf, "expert", split_axis=0, concat_axis=0, tiled=True),
        lax.all_to_all(outgrad_buf, "expert", split_axis=0, concat_axis=0, tiled=True),
    )
    grad = lax.dot_general(
        recv_hidden.reshape(groups * capacity, -1),
        recv_outgrad.reshape(groups * capacity, -1),
        (((0,), (0,)), ((), ())),
        preferred_element_type=jnp.float32,
    )
    moment_new = (moment_decay * moment[0].astype(jnp.float32) + grad).astype(jnp.bfloat16)
    ortho = orthogonalize(moment_new)
    weight_new = (weight[0].astype(jnp.float32) - step_scale * ortho.astype(jnp.float32)).astype(
        jnp.bfloat16
    )
    weight_new = weight_new[None]
    moment_new = moment_new[None]
    fwd_ids = fwd_route[:, 0]
    placed_weight, placed_moment = (weight_new, moment_new)
    fwd_target = lookup(fwd_ids, perm)
    fwd_weight = weight_new[0]
    fwd_count = fwd_hidden.shape[0]
    fwd_capacity = max(4, 2 * fwd_count // groups)
    fwd_selector = slot_matrix(fwd_target, jnp.ones((fwd_count,), dtype=bool), groups, fwd_capacity)
    fwd_buf = (
        jnp.dot(fwd_selector, fwd_hidden, preferred_element_type=jnp.float32)
        .astype(jnp.bfloat16)
        .reshape(groups, fwd_capacity, -1)
    )
    produced = jnp.einsum(
        "gkf,fd->gkd",
        lax.all_to_all(fwd_buf, "expert", split_axis=0, concat_axis=0, tiled=True),
        fwd_weight,
        preferred_element_type=jnp.float32,
    ).astype(jnp.bfloat16)
    returned = lax.all_to_all(produced, "expert", split_axis=0, concat_axis=0, tiled=True)
    fwd_rows_out = lax.dot_general(
        fwd_selector,
        returned.reshape(groups * fwd_capacity, -1),
        (((0,), (0,)), ((), ())),
        preferred_element_type=jnp.float32,
    )
    fwd_out = (fwd_rows_out * fwd_gate[:, None]).astype(jnp.bfloat16)
    return (placed_weight, placed_moment, fwd_out)


def solution(mesh):
    groups = mesh.shape["expert"]
    in_specs = (
        P(("layer", "expert"), None),
        P(("layer", "expert"), None),
        P(("layer", "expert"), None),
        P(("layer", "expert")),
        P(("layer", "expert"), None, None),
        P(("layer", "expert"), None, None),
        P("layer"),
        P(("layer", "expert"), None),
        P(("layer", "expert"), None),
        P(("layer", "expert")),
    )
    out_specs = (
        P(("layer", "expert"), None, None),
        P(("layer", "expert"), None, None),
        P(("layer", "expert"), None),
    )

    def per_device(*args):
        few = groups & (groups - 1) == 0 and groups <= 2 * args[0].shape[0] // groups
        return (relocation_plan if few else routed_plan)(*args)

    return jax.shard_map(
        per_device, mesh=mesh, in_specs=in_specs, out_specs=out_specs, check_vma=False
    )
```

```python
import functools

import jax
import jax.numpy as jnp
from jax import lax
from jax.experimental import pallas as pl
from jax.experimental.pallas import tpu as pltpu
from jax.sharding import PartitionSpec as P

linear_term = 3.4445
cubic_term = -4.775
quintic_term = 2.0315
moment_decay = 0.9
step_scale = 0.25
norm_floor = 1e-07

F32 = jnp.float32
BF16 = jnp.bfloat16
HBM = pl.BlockSpec(memory_space=pltpu.HBM)
VMEM = pl.BlockSpec(memory_space=pltpu.VMEM)
SMEM = pl.BlockSpec(memory_space=pltpu.SMEM)
ANY = pl.BlockSpec(memory_space=pl.ANY)
MIB = 1 << 20


def fetched(refs, held, sem):
    copies = [pltpu.make_async_copy(ref, room, sem.at[n]) for n, (ref, room) in enumerate(zip(refs, held))]
    for copy in copies:
        copy.start()
    for copy in copies:
        copy.wait()


def rooms(arrays):
    return [pltpu.VMEM(a.shape, a.dtype) for a in arrays] + [pltpu.SemaphoreType.DMA((len(arrays),))]


def chunk_at(ref, lead, k, rows, columns):
    return ref.at[
        lead,
        pl.ds(pl.multiple_of((k // 2) * rows, rows), rows),
        pl.ds(pl.multiple_of((k % 2) * columns, columns), columns),
    ]


def slot_rows(route, live, groups, capacity, me_ref, perm_ref):
    rows = route.shape[1]
    experts = lax.broadcasted_iota(jnp.int32, (groups, rows), 0)
    onehot = jnp.where((experts == route) & live, 1.0, 0.0).astype(BF16)
    before = lax.broadcasted_iota(jnp.int32, (rows, rows), 0)
    after = lax.broadcasted_iota(jnp.int32, (rows, rows), 1)
    upto = jnp.where(before <= after, 1.0, 0.0).astype(BF16)
    ranks = jnp.dot(onehot, upto, preferred_element_type=F32)
    rank = jnp.sum(ranks * onehot.astype(F32), axis=0, keepdims=True).astype(jnp.int32) - 1
    partner = jnp.zeros_like(route)
    for e in range(groups):
        partner = jnp.where(route == e, perm_ref[e] ^ me_ref[0], partner)
    return jnp.where(live, partner * capacity + rank, -1)


def selector_of(slot, slots):
    rows = slot.shape[1]
    places = lax.broadcasted_iota(jnp.int32, (slots, rows), 0)
    return jnp.where(places == slot, 1.0, 0.0).astype(BF16)


def pack_kernel(groups, live_ref, me_ref, perm_ref, *refs):
    sources, pieces, slot_ref = refs[:5], refs[6 : 6 + groups], refs[6 + groups]
    held, sem = refs[7 + groups : 12 + groups], refs[-1]
    route_ref, fwd_route_ref, hidden_ref, out_ref, fwd_ref = held
    copies = [pltpu.make_async_copy(ref, room, sem.at[n]) for n, (ref, room) in enumerate(zip(sources, held))]
    for copy in copies:
        copy.start()
    rows, ff = hidden_ref.shape
    d = out_ref.shape[1]
    capacity = pieces[0].shape[0]
    slots = groups * capacity
    place = lax.broadcasted_iota(jnp.int32, (1, rows), 1)

    def fill(first, selector, source_ref):
        chosen = jnp.dot(selector, source_ref[...], preferred_element_type=F32).astype(BF16)
        for s, piece in zip(mixed_order(groups), pieces):
            piece[:, first : first + source_ref.shape[1]] = chosen[s * capacity : (s + 1) * capacity]

    copies[0].wait()
    slot = slot_rows(route_ref[...], place < live_ref[0], groups, capacity, me_ref, perm_ref)
    selector = selector_of(slot, slots)
    copies[1].wait()
    fwd_slot = slot_rows(fwd_route_ref[...], place >= 0, groups, capacity, me_ref, perm_ref)
    slot_ref[...] = fwd_slot
    copies[2].wait()
    fill(0, selector, hidden_ref)
    copies[3].wait()
    fill(ff, selector, out_ref)
    copies[4].wait()
    fill(ff + d, selector_of(fwd_slot, slots), fwd_ref)


def pack_rows(live_rows, me, perm, route, fwd_route, hidden, grad_out, fwd_hidden, earlier, groups, capacity):
    rows, ff = hidden.shape
    width = 2 * ff + grad_out.shape[1]
    sources = (route.reshape(1, rows), fwd_route.reshape(1, rows), hidden, grad_out, fwd_hidden)
    *pieces, slot = pl.pallas_call(
        functools.partial(pack_kernel, groups),
        out_shape=(jax.ShapeDtypeStruct((capacity, width), BF16),) * groups
        + (jax.ShapeDtypeStruct((1, rows), jnp.int32),),
        in_specs=[SMEM] * 3 + [HBM] * 5 + [VMEM],
        out_specs=(VMEM,) * (groups + 1),
        scratch_shapes=[pltpu.VMEM(a.shape, a.dtype) for a in sources] + [pltpu.SemaphoreType.DMA((len(sources),))],
        compiler_params=pltpu.CompilerParams(vmem_limit_bytes=32 * MIB),
        cost_estimate=pl.CostEstimate(
            flops=2 * groups * capacity * rows * width, bytes_accessed=6 * rows * width, transcendentals=0
        ),
        name="pack_rows",
    )(live_rows, me, perm, *sources, earlier)
    return pieces, slot


def split_kernel(me_ref, moment_ref, weight_ref, *refs):
    pieces, held, sem = refs[:-3], refs[-3:-1], refs[-1]
    fetched((moment_ref, weight_ref), held, sem)
    for s, piece in zip(mixed_order(len(pieces)), pieces):
        rows, columns = piece.shape[1:]
        for lead, source in enumerate(held):
            piece[lead] = chunk_at(source, 0, me_ref[0] ^ s, rows, columns)[...]


def split(me, moment, weight, groups):
    _, ff, d = weight.shape
    piece = jax.ShapeDtypeStruct((2, ff // (groups // 2), d // 2), BF16)
    return pl.pallas_call(
        split_kernel,
        out_shape=(piece,) * groups,
        in_specs=[SMEM, HBM, HBM],
        out_specs=(VMEM,) * groups,
        scratch_shapes=rooms((moment, weight)),
        compiler_params=pltpu.CompilerParams(vmem_limit_bytes=60 * MIB),
        cost_estimate=pl.CostEstimate(flops=0, bytes_accessed=8 * ff * d, transcendentals=0),
        name="split",
    )(me, moment, weight)


def reorder_kernel(me_ref, perm_ref, *refs):
    groups = len(refs) // 2 - 1
    sources, targets, held = refs[:groups], refs[groups + 1 : 2 * groups + 1], refs[-1]
    me, order = me_ref[0], mixed_order(groups)
    for s, source in zip(order, sources):
        held[me ^ perm_ref[me ^ s]] = source[...]
    for s, target in zip(order, targets):
        target[...] = held[s]


def reorder(me, perm, pieces, earlier):
    groups = len(pieces)
    piece = jax.ShapeDtypeStruct(pieces[0].shape, BF16)
    return pl.pallas_call(
        reorder_kernel,
        out_shape=(piece,) * groups,
        in_specs=[SMEM, SMEM] + [VMEM] * (groups + 1),
        out_specs=(VMEM,) * groups,
        scratch_shapes=[pltpu.VMEM((groups,) + pieces[0].shape, BF16)],
        compiler_params=pltpu.CompilerParams(vmem_limit_bytes=32 * MIB),
        cost_estimate=pl.CostEstimate(flops=0, bytes_accessed=4 * groups * pieces[0].size, transcendentals=0),
        name="reorder",
    )(me, perm, *pieces, earlier)


def update_kernel(groups, me_ref, *refs):
    packed, pieces, produced = refs[:groups], refs[groups : 2 * groups], refs[2 * groups + 2 : 3 * groups + 2]
    weight_new_ref, moment_new_ref = refs[2 * groups : 2 * groups + 2]
    held, rows_ref = refs[-2:]
    _, ff, d = held.shape
    capacity = packed[0].shape[0]
    for n, piece in enumerate(packed):
        rows_ref[n * capacity : (n + 1) * capacity] = piece[...]
    for s, piece in zip(mixed_order(groups), pieces):
        rows, columns = piece.shape[1:]
        for lead in range(2):
            chunk_at(held, lead, me_ref[0] ^ s, rows, columns)[...] = piece[lead]
    grad = lax.dot_general(
        rows_ref[:, :ff], rows_ref[:, ff : ff + d], (((0,), (0,)), ((), ())), preferred_element_type=F32
    )
    moment_new = (moment_decay * held[0].astype(F32) + grad).astype(BF16)
    moment_new_ref[...] = moment_new
    moment_f = moment_new.astype(F32)
    frobenius = jnp.sqrt(jnp.sum(moment_f * moment_f))
    current = (moment_f / (frobenius + norm_floor)).astype(BF16)
    for _ in range(2):
        gramian = lax.dot_general(
            current, current, (((1,), (1,)), ((), ())), preferred_element_type=F32
        ).astype(BF16)
        squared = jnp.dot(gramian, gramian, preferred_element_type=F32)
        poly = (cubic_term * gramian.astype(F32) + quintic_term * squared).astype(BF16)
        current = (
            linear_term * current.astype(F32) + jnp.dot(poly, current, preferred_element_type=F32)
        ).astype(BF16)
    weight_new = (held[1].astype(F32) - step_scale * current.astype(F32)).astype(BF16)
    weight_new_ref[...] = weight_new
    product = jnp.dot(rows_ref[:, ff + d :], weight_new, preferred_element_type=F32).astype(BF16)
    for n, piece in enumerate(produced):
        piece[...] = product[n * capacity : (n + 1) * capacity]


def update(me, packed, pieces, ff, d):
    groups = len(pieces)
    capacity, width = packed[0].shape
    slots = groups * capacity
    shape = jax.ShapeDtypeStruct((ff, d), BF16)
    weight_new, moment_new, *produced = pl.pallas_call(
        functools.partial(update_kernel, groups),
        out_shape=(shape, shape) + (jax.ShapeDtypeStruct((capacity, d), BF16),) * groups,
        in_specs=[SMEM] + [VMEM] * (2 * groups),
        out_specs=(VMEM,) * (groups + 2),
        scratch_shapes=[pltpu.VMEM((2, ff, d), BF16), pltpu.VMEM((slots, width), BF16)],
        compiler_params=pltpu.CompilerParams(vmem_limit_bytes=40 * MIB),
        cost_estimate=pl.CostEstimate(
            flops=4 * ff * d * slots + 8 * ff * ff * d + 4 * ff**3,
            bytes_accessed=8 * ff * d + 2 * slots * (width + d),
            transcendentals=1,
        ),
        name="update",
    )(me, *packed, *pieces)
    return weight_new, moment_new, produced


def finish_kernel(groups, slot_ref, gate_ref, *refs):
    pieces, (out_ref, returned_ref) = refs[:groups], refs[groups:]
    capacity = pieces[0].shape[0]
    for s, piece in zip(mixed_order(groups), pieces):
        returned_ref[s * capacity : (s + 1) * capacity] = piece[...]
    rows = slot_ref.shape[1]
    selector = selector_of(slot_ref[...], groups * capacity)
    expert_out = lax.dot_general(
        selector, returned_ref[...], (((0,), (0,)), ((), ())), preferred_element_type=F32
    )
    down = lax.broadcasted_iota(jnp.int32, (rows, rows), 0)
    across = lax.broadcasted_iota(jnp.int32, (rows, rows), 1)
    gate = jnp.sum(jnp.where(down == across, gate_ref[...], 0.0), axis=1, keepdims=True)
    out_ref[...] = (gate * expert_out).astype(BF16)


def finish(slot, gate, returned):
    groups = len(returned)
    rows = slot.shape[1]
    capacity, d = returned[0].shape
    slots = groups * capacity
    return pl.pallas_call(
        functools.partial(finish_kernel, groups),
        out_shape=jax.ShapeDtypeStruct((rows, d), BF16),
        in_specs=[VMEM] * (2 + groups),
        out_specs=VMEM,
        scratch_shapes=[pltpu.VMEM((slots, d), BF16)],
        compiler_params=pltpu.CompilerParams(vmem_limit_bytes=32 * MIB),
        cost_estimate=pl.CostEstimate(
            flops=2 * slots * rows * d, bytes_accessed=2 * d * (slots + rows), transcendentals=0
        ),
        name="finish",
    )(slot, gate.reshape(1, rows), *returned)


def mixed_order(groups):
    far, near = list(range(groups // 2, groups)), list(range(groups // 2 - 1, 0, -1))
    return [0] + [s for pair in zip(far, near + [None]) for s in pair if s is not None]


def swap(pieces):
    groups = len(pieces)
    order = mixed_order(groups)
    return [pieces[0]] + [
        lax.ppermute(piece, "expert", [(i, i ^ s) for i in range(groups)]) for s, piece in zip(order[1:], pieces[1:])
    ]


def partner_plan(
    grad_hidden, grad_out, grad_route, live_rows, w_down, w_moment, perm, fwd_hidden, fwd_route, fwd_gate
):
    groups = lax.axis_size("expert")
    me = lax.axis_index("expert").astype(jnp.int32).reshape(1)
    capacity = max(4, 2 * grad_hidden.shape[0] // groups)
    ff, d = w_down.shape[1:]
    spread = swap(split(me, w_moment, w_down, groups))
    packed, fwd_slot = pack_rows(
        live_rows, me, perm, grad_route, fwd_route, grad_hidden, grad_out, fwd_hidden,
        spread[2 * groups // 3], groups, capacity,
    )
    received = swap(packed)
    placed = swap(reorder(me, perm, spread, received[groups // 3]))
    weight_new, moment_new, produced = update(me, received, placed, ff, d)
    return weight_new[None], moment_new[None], finish(fwd_slot, fwd_gate, swap(produced))


def lookup(route_ids, mapping):
    columns = jnp.arange(mapping.shape[0], dtype=jnp.int32)
    hits = route_ids[:, None] == columns[None, :]
    return jnp.sum(jnp.where(hits, mapping[None, :], 0), axis=1)


def slot_matrix(target, is_live, groups, capacity):
    columns = jnp.arange(groups, dtype=jnp.int32)
    onehot = ((target[:, None] == columns[None, :]) & is_live[:, None]).astype(jnp.int32)
    ranked = jnp.sum(jnp.cumsum(onehot, axis=0) * onehot, axis=1) - 1
    slot_of = jnp.where(is_live, target * capacity + ranked, -1)
    slots = jnp.arange(groups * capacity, dtype=jnp.int32)
    return (slots[:, None] == slot_of[None, :]).astype(jnp.bfloat16)


def orthogonalize(moment):
    moment_f = moment.astype(jnp.float32)
    frobenius = jnp.sqrt(jnp.sum(moment_f * moment_f))
    current = (moment_f / (frobenius + norm_floor)).astype(jnp.bfloat16)
    for sweep_index in range(2):
        gramian = lax.dot_general(
            current, current, (((1,), (1,)), ((), ())), preferred_element_type=jnp.float32
        ).astype(jnp.bfloat16)
        squared = jnp.dot(gramian, gramian, preferred_element_type=jnp.float32)
        poly = (cubic_term * gramian.astype(jnp.float32) + quintic_term * squared).astype(
            jnp.bfloat16
        )
        current = (
            linear_term * current.astype(jnp.float32)
            + jnp.dot(poly, current, preferred_element_type=jnp.float32)
        ).astype(jnp.bfloat16)
    return current


def relocate(weight, moment, perm):
    groups = lax.axis_size("expert")
    weight_flat = weight.reshape(groups, -1)
    moment_flat = moment.reshape(groups, -1)
    spread_w, spread_m = (
        lax.all_to_all(weight_flat, "expert", split_axis=0, concat_axis=0, tiled=True),
        lax.all_to_all(moment_flat, "expert", split_axis=0, concat_axis=0, tiled=True),
    )
    devices = jnp.arange(groups, dtype=jnp.int32)
    inverse = jnp.sum(jnp.where(perm[None, :] == devices[:, None], devices[None, :], 0), axis=1)
    ordered_w = jnp.take(spread_w, inverse, axis=0)
    ordered_m = jnp.take(spread_m, inverse, axis=0)
    back_w, back_m = (
        lax.all_to_all(ordered_w, "expert", split_axis=0, concat_axis=0, tiled=True),
        lax.all_to_all(ordered_m, "expert", split_axis=0, concat_axis=0, tiled=True),
    )
    return (back_w.reshape(weight.shape), back_m.reshape(moment.shape))


def routed_plan(
    grad_hidden,
    grad_out,
    grad_route,
    live_rows,
    w_down,
    w_moment,
    perm,
    fwd_hidden,
    fwd_route,
    fwd_gate,
):
    groups = lax.axis_size("expert")
    grad_count = grad_hidden.shape[0]
    capacity = max(4, 2 * grad_count // groups)
    is_live = jnp.arange(grad_count, dtype=jnp.int32) < live_rows[0]
    route_ids = grad_route[:, 0]
    weight, moment = relocate(w_down, w_moment, perm)
    target = lookup(route_ids, perm)
    selector = slot_matrix(target, is_live, groups, capacity)
    hidden_buf = (
        jnp.dot(selector, grad_hidden, preferred_element_type=jnp.float32)
        .astype(jnp.bfloat16)
        .reshape(groups, capacity, -1)
    )
    outgrad_buf = (
        jnp.dot(selector, grad_out, preferred_element_type=jnp.float32)
        .astype(jnp.bfloat16)
        .reshape(groups, capacity, -1)
    )
    recv_hidden, recv_outgrad = (
        lax.all_to_all(hidden_buf, "expert", split_axis=0, concat_axis=0, tiled=True),
        lax.all_to_all(outgrad_buf, "expert", split_axis=0, concat_axis=0, tiled=True),
    )
    grad = lax.dot_general(
        recv_hidden.reshape(groups * capacity, -1),
        recv_outgrad.reshape(groups * capacity, -1),
        (((0,), (0,)), ((), ())),
        preferred_element_type=jnp.float32,
    )
    moment_new = (moment_decay * moment[0].astype(jnp.float32) + grad).astype(jnp.bfloat16)
    ortho = orthogonalize(moment_new)
    weight_new = (weight[0].astype(jnp.float32) - step_scale * ortho.astype(jnp.float32)).astype(
        jnp.bfloat16
    )
    weight_new = weight_new[None]
    moment_new = moment_new[None]
    fwd_ids = fwd_route[:, 0]
    placed_weight, placed_moment = (weight_new, moment_new)
    fwd_target = lookup(fwd_ids, perm)
    fwd_weight = weight_new[0]
    fwd_count = fwd_hidden.shape[0]
    fwd_capacity = max(4, 2 * fwd_count // groups)
    fwd_selector = slot_matrix(fwd_target, jnp.ones((fwd_count,), dtype=bool), groups, fwd_capacity)
    fwd_buf = (
        jnp.dot(fwd_selector, fwd_hidden, preferred_element_type=jnp.float32)
        .astype(jnp.bfloat16)
        .reshape(groups, fwd_capacity, -1)
    )
    produced = jnp.einsum(
        "gkf,fd->gkd",
        lax.all_to_all(fwd_buf, "expert", split_axis=0, concat_axis=0, tiled=True),
        fwd_weight,
        preferred_element_type=jnp.float32,
    ).astype(jnp.bfloat16)
    returned = lax.all_to_all(produced, "expert", split_axis=0, concat_axis=0, tiled=True)
    fwd_rows_out = lax.dot_general(
        fwd_selector,
        returned.reshape(groups * fwd_capacity, -1),
        (((0,), (0,)), ((), ())),
        preferred_element_type=jnp.float32,
    )
    fwd_out = (fwd_rows_out * fwd_gate[:, None]).astype(jnp.bfloat16)
    return (placed_weight, placed_moment, fwd_out)


def solution(mesh):
    groups = mesh.shape["expert"]
    in_specs = (
        P(("layer", "expert"), None),
        P(("layer", "expert"), None),
        P(("layer", "expert"), None),
        P(("layer", "expert")),
        P(("layer", "expert"), None, None),
        P(("layer", "expert"), None, None),
        P("layer"),
        P(("layer", "expert"), None),
        P(("layer", "expert"), None),
        P(("layer", "expert")),
    )
    out_specs = (
        P(("layer", "expert"), None, None),
        P(("layer", "expert"), None, None),
        P(("layer", "expert"), None),
    )

    def per_device(*args):
        few = groups & (groups - 1) == 0 and groups <= 2 * args[0].shape[0] // groups
        return (partner_plan if few else routed_plan)(*args)

    return jax.shard_map(
        per_device, mesh=mesh, in_specs=in_specs, out_specs=out_specs, check_vma=False
    )
```

```python
import functools

import jax
import jax.numpy as jnp
from jax import lax
from jax.experimental import pallas as pl
from jax.experimental.pallas import tpu as pltpu
from jax.sharding import PartitionSpec as P

linear_term = 3.4445
cubic_term = -4.775
quintic_term = 2.0315
moment_decay = 0.9
step_scale = 0.25
norm_floor = 1e-07

F32 = jnp.float32
BF16 = jnp.bfloat16
HBM = pl.BlockSpec(memory_space=pltpu.HBM)
VMEM = pl.BlockSpec(memory_space=pltpu.VMEM)
SMEM = pl.BlockSpec(memory_space=pltpu.SMEM)
ANY = pl.BlockSpec(memory_space=pl.ANY)
MIB = 1 << 20


def row_block(k, rows):
    return pl.ds(pl.multiple_of(k * rows, rows), rows)


def crossing_ranks(half, base, perm_ref):
    flags = [(perm_ref[base + q] // half != base // half).astype(jnp.int32) for q in range(half)]
    ranks, count = [], 0
    for flag in flags:
        ranks.append(count)
        count = count + flag
    return flags, ranks


def slots_of(half):
    return half // 2, 1, half - half // 2 - 1


def slot_rows(route, live, groups, capacity, me_ref, perm_ref):
    rows = route.shape[1]
    experts = lax.broadcasted_iota(jnp.int32, (groups, rows), 0)
    onehot = jnp.where((experts == route) & live, 1.0, 0.0).astype(BF16)
    before = lax.broadcasted_iota(jnp.int32, (rows, rows), 0)
    after = lax.broadcasted_iota(jnp.int32, (rows, rows), 1)
    upto = jnp.where(before <= after, 1.0, 0.0).astype(BF16)
    ranks = jnp.dot(onehot, upto, preferred_element_type=F32)
    rank = jnp.sum(ranks * onehot.astype(F32), axis=0, keepdims=True).astype(jnp.int32) - 1
    partner = jnp.zeros_like(route)
    for e in range(groups):
        partner = jnp.where(route == e, perm_ref[e] ^ me_ref[0], partner)
    return jnp.where(live, partner * capacity + rank, -1)


def selector_of(slot, slots):
    rows = slot.shape[1]
    places = lax.broadcasted_iota(jnp.int32, (slots, rows), 0)
    return jnp.where(places == slot, 1.0, 0.0).astype(BF16)


def pack_kernel(groups, live_ref, me_ref, perm_ref, *refs):
    sources, pieces, (slot_ref, gates_ref) = refs[:6], refs[7 : 7 + groups], refs[7 + groups : 9 + groups]
    held, sem = refs[9 + groups : 15 + groups], refs[-1]
    route_ref, fwd_route_ref, hidden_ref, out_ref, fwd_ref, gate_ref = held
    copies = [pltpu.make_async_copy(ref, room, sem.at[n]) for n, (ref, room) in enumerate(zip(sources, held))]
    for copy in copies:
        copy.start()
    rows, ff = hidden_ref.shape
    d = out_ref.shape[1]
    capacity = pieces[0].shape[0]
    slots = groups * capacity
    place = lax.broadcasted_iota(jnp.int32, (1, rows), 1)

    def fill(first, selector, source_ref):
        chosen = jnp.dot(selector, source_ref[...], preferred_element_type=F32).astype(BF16)
        for s, piece in zip(mixed_order(groups), pieces):
            piece[:, first : first + source_ref.shape[1]] = chosen[s * capacity : (s + 1) * capacity]

    copies[0].wait()
    slot = slot_rows(route_ref[...], place < live_ref[0], groups, capacity, me_ref, perm_ref)
    selector = selector_of(slot, slots)
    copies[1].wait()
    fwd_slot = slot_rows(fwd_route_ref[...], place >= 0, groups, capacity, me_ref, perm_ref)
    slot_ref[...] = fwd_slot
    copies[2].wait()
    fill(0, selector, hidden_ref)
    copies[3].wait()
    fill(ff, selector, out_ref)
    copies[4].wait()
    fill(ff + d, selector_of(fwd_slot, slots), fwd_ref)
    copies[5].wait()
    down = lax.broadcasted_iota(jnp.int32, (rows, rows), 0)
    across = lax.broadcasted_iota(jnp.int32, (rows, rows), 1)
    gates_ref[...] = jnp.sum(jnp.where(down == across, gate_ref[...], 0.0), axis=1, keepdims=True)


def pack_rows(live_rows, me, perm, route, fwd_route, hidden, grad_out, fwd_hidden, gate, earlier, groups, capacity):
    rows, ff = hidden.shape
    width = 2 * ff + grad_out.shape[1]
    sources = (route.reshape(1, rows), fwd_route.reshape(1, rows), hidden, grad_out, fwd_hidden, gate.reshape(1, rows))
    *pieces, slot, gates = pl.pallas_call(
        functools.partial(pack_kernel, groups),
        out_shape=(jax.ShapeDtypeStruct((capacity, width), BF16),) * groups
        + (jax.ShapeDtypeStruct((1, rows), jnp.int32), jax.ShapeDtypeStruct((rows, 1), F32)),
        in_specs=[SMEM] * 3 + [HBM] * 6 + [VMEM],
        out_specs=(VMEM,) * (groups + 2),
        scratch_shapes=[pltpu.VMEM(a.shape, a.dtype) for a in sources] + [pltpu.SemaphoreType.DMA((len(sources),))],
        compiler_params=pltpu.CompilerParams(vmem_limit_bytes=32 * MIB),
        cost_estimate=pl.CostEstimate(
            flops=2 * groups * capacity * rows * width, bytes_accessed=6 * rows * width, transcendentals=0
        ),
        name="pack_rows",
    )(live_rows, me, perm, *sources, earlier)
    return pieces, slot, gates


def split_kernel(me_ref, moment_ref, weight_ref, *refs):
    pieces, sem = refs[:-1], refs[-1]
    half, rows = len(pieces), pieces[0].shape[1]
    copies = [
        pltpu.make_async_copy(
            source.at[0, row_block((me_ref[0] ^ s) % half, rows)], piece.at[lead], sem.at[lead * half + s]
        )
        for s, piece in enumerate(pieces)
        for lead, source in enumerate((moment_ref, weight_ref))
    ]
    for copy in copies:
        copy.start()
    for copy in copies:
        copy.wait()


def split(me, moment, weight, half):
    _, ff, d = weight.shape
    piece = jax.ShapeDtypeStruct((2, ff // half, d), BF16)
    return pl.pallas_call(
        split_kernel,
        out_shape=(piece,) * half,
        in_specs=[SMEM, HBM, HBM],
        out_specs=(VMEM,) * half,
        scratch_shapes=[pltpu.SemaphoreType.DMA((2 * half,))],
        compiler_params=pltpu.CompilerParams(vmem_limit_bytes=60 * MIB),
        cost_estimate=pl.CostEstimate(flops=0, bytes_accessed=8 * ff * d, transcendentals=0),
        name="split",
    )(me, moment, weight)


def sort_kernel(me_ref, perm_ref, *refs):
    pieces, (near_ref, *slot_refs) = refs[:-4], refs[-4:]
    half = len(pieces)
    me = me_ref[0]
    base = me // half * half
    flags, ranks = crossing_ranks(half, base, perm_ref)
    for s, piece in enumerate(pieces):
        place = (me ^ s) % half
        crosses, rank = 0, 0
        for q in range(half):
            crosses = jnp.where(place == q, flags[q], crosses)
            rank = jnp.where(place == q, ranks[q], rank)
        near = (perm_ref[base + place] ^ me) % half

        @pl.when(crosses == 0)
        def _():
            near_ref[near] = piece[...]

        first = 0
        for slots in slot_refs:
            count = slots.shape[0]

            @pl.when((crosses == 1) & (rank >= first) & (rank < first + count))
            def _():
                slots[rank - first] = piece[...]

            first += count


def sort_pieces(me, perm, pieces):
    half = len(pieces)
    shape = pieces[0].shape
    counts = (half,) + slots_of(half)
    return pl.pallas_call(
        sort_kernel,
        out_shape=tuple(jax.ShapeDtypeStruct((count,) + shape, BF16) for count in counts),
        in_specs=[SMEM, SMEM] + [VMEM] * half,
        out_specs=(VMEM,) * len(counts),
        compiler_params=pltpu.CompilerParams(vmem_limit_bytes=32 * MIB),
        cost_estimate=pl.CostEstimate(flops=0, bytes_accessed=4 * half * pieces[0].size, transcendentals=0),
        name="sort_pieces",
    )(me, perm, *pieces)


def join_kernel(half, me_ref, perm_ref, near_ref, *refs):
    slot_refs, targets = refs[:3], refs[3:]
    me = me_ref[0]
    base = me // half * half
    flags, ranks = crossing_ranks(half, half - base, perm_ref)
    for s, target in enumerate(targets):
        crosses, rank = 0, 0
        for q in range(half):
            here = perm_ref[half - base + q] == me ^ s
            crosses = jnp.where(here, 1, crosses)
            rank = jnp.where(here, ranks[q], rank)

        @pl.when(crosses == 0)
        def _():
            target[...] = near_ref[s]

        first = 0
        for slots in slot_refs:
            count = slots.shape[0]

            @pl.when((crosses == 1) & (rank >= first) & (rank < first + count))
            def _():
                target[...] = slots[rank - first]

            first += count


def join_pieces(me, perm, near, slots):
    half = near.shape[0]
    piece = jax.ShapeDtypeStruct(near.shape[1:], BF16)
    return pl.pallas_call(
        functools.partial(join_kernel, half),
        out_shape=(piece,) * half,
        in_specs=[SMEM, SMEM] + [VMEM] * 4,
        out_specs=(VMEM,) * half,
        compiler_params=pltpu.CompilerParams(vmem_limit_bytes=32 * MIB),
        cost_estimate=pl.CostEstimate(flops=0, bytes_accessed=4 * near.size, transcendentals=0),
        name="join_pieces",
    )(me, perm, near, *slots)


def gradient_kernel(groups, *refs):
    pieces, (grad_ref, fwd_ref, rows_ref) = refs[:groups], refs[groups:]
    ff, d = grad_ref.shape
    capacity = pieces[0].shape[0]
    for n, piece in enumerate(pieces):
        span = slice(n * capacity, (n + 1) * capacity)
        rows_ref[span] = piece[:, : ff + d]
        fwd_ref[span] = piece[:, ff + d :]
    grad_ref[...] = lax.dot_general(
        rows_ref[:, :ff], rows_ref[:, ff:], (((0,), (0,)), ((), ())), preferred_element_type=F32
    )


def gradient(pieces, ff, d):
    groups = len(pieces)
    slots = groups * pieces[0].shape[0]
    return pl.pallas_call(
        functools.partial(gradient_kernel, groups),
        out_shape=(jax.ShapeDtypeStruct((ff, d), F32), jax.ShapeDtypeStruct((slots, ff), BF16)),
        in_specs=[VMEM] * groups,
        out_specs=(VMEM, VMEM),
        scratch_shapes=[pltpu.VMEM((slots, ff + d), BF16)],
        compiler_params=pltpu.CompilerParams(vmem_limit_bytes=32 * MIB),
        cost_estimate=pl.CostEstimate(
            flops=2 * ff * d * slots, bytes_accessed=4 * ff * d + 4 * slots * (ff + d), transcendentals=0
        ),
        name="gradient",
    )(*pieces)


def update_kernel(half, me_ref, grad_ref, fwd_ref, *refs):
    pieces, (weight_new_ref, moment_new_ref, *produced), held = refs[:half], refs[half:-1], refs[-1]
    rows = pieces[0].shape[1]
    for s, piece in enumerate(pieces):
        for lead in range(2):
            held[lead, row_block((me_ref[0] ^ s) % half, rows)] = piece[lead]
    moment_new = (moment_decay * held[0].astype(F32) + grad_ref[...]).astype(BF16)
    moment_new_ref[...] = moment_new
    moment_f = moment_new.astype(F32)
    frobenius = jnp.sqrt(jnp.sum(moment_f * moment_f))
    current = (moment_f / (frobenius + norm_floor)).astype(BF16)
    for _ in range(2):
        gramian = lax.dot_general(
            current, current, (((1,), (1,)), ((), ())), preferred_element_type=F32
        ).astype(BF16)
        squared = jnp.dot(gramian, gramian, preferred_element_type=F32)
        poly = (cubic_term * gramian.astype(F32) + quintic_term * squared).astype(BF16)
        current = (
            linear_term * current.astype(F32) + jnp.dot(poly, current, preferred_element_type=F32)
        ).astype(BF16)
    weight_new = (held[1].astype(F32) - step_scale * current.astype(F32)).astype(BF16)
    weight_new_ref[...] = weight_new
    product = jnp.dot(fwd_ref[...], weight_new, preferred_element_type=F32).astype(BF16)
    groups, capacity = len(produced), produced[0].shape[0]
    came = mixed_order(groups)
    for s, piece in zip(return_order(groups), produced):
        n = came.index(s)
        piece[...] = product[n * capacity : (n + 1) * capacity]


def update(me, grad, fwd_rows, pieces, groups):
    half = len(pieces)
    ff, d = grad.shape
    slots = fwd_rows.shape[0]
    shape = jax.ShapeDtypeStruct((ff, d), BF16)
    weight_new, moment_new, *produced = pl.pallas_call(
        functools.partial(update_kernel, half),
        out_shape=(shape, shape) + (jax.ShapeDtypeStruct((slots // groups, d), BF16),) * groups,
        in_specs=[SMEM] + [VMEM] * (2 + half),
        out_specs=(VMEM,) * (groups + 2),
        scratch_shapes=[pltpu.VMEM((2, ff, d), BF16)],
        compiler_params=pltpu.CompilerParams(vmem_limit_bytes=40 * MIB),
        cost_estimate=pl.CostEstimate(
            flops=2 * ff * d * slots + 8 * ff * ff * d + 4 * ff**3,
            bytes_accessed=12 * ff * d + 2 * slots * (ff + d),
            transcendentals=1,
        ),
        name="update",
    )(me, grad, fwd_rows, *pieces)
    return weight_new, moment_new, produced


def finish_kernel(groups, slot_ref, gates_ref, *refs):
    pieces, (out_ref, returned_ref) = refs[:groups], refs[groups:]
    capacity = pieces[0].shape[0]
    for s, piece in zip(return_order(groups), pieces):
        returned_ref[s * capacity : (s + 1) * capacity] = piece[...]
    selector = selector_of(slot_ref[...], groups * capacity)
    expert_out = lax.dot_general(
        selector, returned_ref[...], (((0,), (0,)), ((), ())), preferred_element_type=F32
    )
    out_ref[...] = (gates_ref[...] * expert_out).astype(BF16)


def finish(slot, gates, returned):
    groups = len(returned)
    rows = slot.shape[1]
    capacity, d = returned[0].shape
    slots = groups * capacity
    return pl.pallas_call(
        functools.partial(finish_kernel, groups),
        out_shape=jax.ShapeDtypeStruct((rows, d), BF16),
        in_specs=[VMEM] * (2 + groups),
        out_specs=VMEM,
        scratch_shapes=[pltpu.VMEM((slots, d), BF16)],
        compiler_params=pltpu.CompilerParams(vmem_limit_bytes=32 * MIB),
        cost_estimate=pl.CostEstimate(
            flops=2 * slots * rows * d, bytes_accessed=2 * d * (slots + rows), transcendentals=0
        ),
        name="finish",
    )(slot, gates, *returned)


def mixed_order(groups):
    far, near = list(range(groups // 2, groups)), list(range(groups // 2 - 1, 0, -1))
    return [0] + [s for pair in zip(far, near + [None]) for s in pair if s is not None]


def return_order(groups):
    far, near = list(range(groups // 2, groups)), list(range(groups // 2 - 1, 0, -1))
    order = [0]
    while far or near:
        order += far[:2] + near[:1]
        far, near = far[2:], near[1:]
    return order


def swap(pieces, order):
    groups = lax.axis_size("expert")
    return [
        lax.ppermute(piece, "expert", [(i, i ^ s) for i in range(groups)]) if s else piece
        for s, piece in zip(order, pieces)
    ]


def halves_plan(
    grad_hidden, grad_out, grad_route, live_rows, w_down, w_moment, perm, fwd_hidden, fwd_route, fwd_gate
):
    groups = lax.axis_size("expert")
    layers = lax.axis_size("layer")
    half = groups // 2
    me = lax.axis_index("expert").astype(jnp.int32).reshape(1)
    capacity = max(4, 2 * grad_hidden.shape[0] // groups)
    ff, d = w_down.shape[1:]
    crossing = jnp.sum((perm[:half] >= half).astype(jnp.int32)).reshape(1)
    most = crossing
    for turn in range(1, layers):
        other = lax.ppermute(crossing, "layer", [(i, (i + turn) % layers) for i in range(layers)])
        most = jnp.maximum(most, other)
    most = most[0]

    spread = swap(split(me, w_moment, w_down, half), range(half))
    packed, fwd_slot, gates = pack_rows(
        live_rows, me, perm, grad_route, fwd_route, grad_hidden, grad_out, fwd_hidden, fwd_gate,
        spread[1], groups, capacity,
    )
    received = swap(packed, mixed_order(groups))
    near, *slots = sort_pieces(me, perm, spread)

    def mirror(array):
        return swap([array], [half])[0]

    always, following, rest = slots_of(half)
    crossed = [
        mirror(slots[0]),
        lax.cond(most > always, mirror, lambda array: array, slots[1]),
        lax.cond(most > always + following, mirror, lambda array: array, slots[2]),
    ]
    placed = swap(join_pieces(me, perm, near, crossed), range(half))
    grad, fwd_rows = gradient(received, ff, d)
    weight_new, moment_new, produced = update(me, grad, fwd_rows, placed, groups)
    returned = swap(produced, return_order(groups))
    return weight_new[None], moment_new[None], finish(fwd_slot, gates, returned)


def lookup(route_ids, mapping):
    columns = jnp.arange(mapping.shape[0], dtype=jnp.int32)
    hits = route_ids[:, None] == columns[None, :]
    return jnp.sum(jnp.where(hits, mapping[None, :], 0), axis=1)


def slot_matrix(target, is_live, groups, capacity):
    columns = jnp.arange(groups, dtype=jnp.int32)
    onehot = ((target[:, None] == columns[None, :]) & is_live[:, None]).astype(jnp.int32)
    ranked = jnp.sum(jnp.cumsum(onehot, axis=0) * onehot, axis=1) - 1
    slot_of = jnp.where(is_live, target * capacity + ranked, -1)
    slots = jnp.arange(groups * capacity, dtype=jnp.int32)
    return (slots[:, None] == slot_of[None, :]).astype(jnp.bfloat16)


def orthogonalize(moment):
    moment_f = moment.astype(jnp.float32)
    frobenius = jnp.sqrt(jnp.sum(moment_f * moment_f))
    current = (moment_f / (frobenius + norm_floor)).astype(jnp.bfloat16)
    for sweep_index in range(2):
        gramian = lax.dot_general(
            current, current, (((1,), (1,)), ((), ())), preferred_element_type=jnp.float32
        ).astype(jnp.bfloat16)
        squared = jnp.dot(gramian, gramian, preferred_element_type=jnp.float32)
        poly = (cubic_term * gramian.astype(jnp.float32) + quintic_term * squared).astype(
            jnp.bfloat16
        )
        current = (
            linear_term * current.astype(jnp.float32)
            + jnp.dot(poly, current, preferred_element_type=jnp.float32)
        ).astype(jnp.bfloat16)
    return current


def relocate(weight, moment, perm):
    groups = lax.axis_size("expert")
    weight_flat = weight.reshape(groups, -1)
    moment_flat = moment.reshape(groups, -1)
    spread_w, spread_m = (
        lax.all_to_all(weight_flat, "expert", split_axis=0, concat_axis=0, tiled=True),
        lax.all_to_all(moment_flat, "expert", split_axis=0, concat_axis=0, tiled=True),
    )
    devices = jnp.arange(groups, dtype=jnp.int32)
    inverse = jnp.sum(jnp.where(perm[None, :] == devices[:, None], devices[None, :], 0), axis=1)
    ordered_w = jnp.take(spread_w, inverse, axis=0)
    ordered_m = jnp.take(spread_m, inverse, axis=0)
    back_w, back_m = (
        lax.all_to_all(ordered_w, "expert", split_axis=0, concat_axis=0, tiled=True),
        lax.all_to_all(ordered_m, "expert", split_axis=0, concat_axis=0, tiled=True),
    )
    return (back_w.reshape(weight.shape), back_m.reshape(moment.shape))


def routed_plan(
    grad_hidden,
    grad_out,
    grad_route,
    live_rows,
    w_down,
    w_moment,
    perm,
    fwd_hidden,
    fwd_route,
    fwd_gate,
):
    groups = lax.axis_size("expert")
    grad_count = grad_hidden.shape[0]
    capacity = max(4, 2 * grad_count // groups)
    is_live = jnp.arange(grad_count, dtype=jnp.int32) < live_rows[0]
    route_ids = grad_route[:, 0]
    weight, moment = relocate(w_down, w_moment, perm)
    target = lookup(route_ids, perm)
    selector = slot_matrix(target, is_live, groups, capacity)
    hidden_buf = (
        jnp.dot(selector, grad_hidden, preferred_element_type=jnp.float32)
        .astype(jnp.bfloat16)
        .reshape(groups, capacity, -1)
    )
    outgrad_buf = (
        jnp.dot(selector, grad_out, preferred_element_type=jnp.float32)
        .astype(jnp.bfloat16)
        .reshape(groups, capacity, -1)
    )
    recv_hidden, recv_outgrad = (
        lax.all_to_all(hidden_buf, "expert", split_axis=0, concat_axis=0, tiled=True),
        lax.all_to_all(outgrad_buf, "expert", split_axis=0, concat_axis=0, tiled=True),
    )
    grad = lax.dot_general(
        recv_hidden.reshape(groups * capacity, -1),
        recv_outgrad.reshape(groups * capacity, -1),
        (((0,), (0,)), ((), ())),
        preferred_element_type=jnp.float32,
    )
    moment_new = (moment_decay * moment[0].astype(jnp.float32) + grad).astype(jnp.bfloat16)
    ortho = orthogonalize(moment_new)
    weight_new = (weight[0].astype(jnp.float32) - step_scale * ortho.astype(jnp.float32)).astype(
        jnp.bfloat16
    )
    weight_new = weight_new[None]
    moment_new = moment_new[None]
    fwd_ids = fwd_route[:, 0]
    placed_weight, placed_moment = (weight_new, moment_new)
    fwd_target = lookup(fwd_ids, perm)
    fwd_weight = weight_new[0]
    fwd_count = fwd_hidden.shape[0]
    fwd_capacity = max(4, 2 * fwd_count // groups)
    fwd_selector = slot_matrix(fwd_target, jnp.ones((fwd_count,), dtype=bool), groups, fwd_capacity)
    fwd_buf = (
        jnp.dot(fwd_selector, fwd_hidden, preferred_element_type=jnp.float32)
        .astype(jnp.bfloat16)
        .reshape(groups, fwd_capacity, -1)
    )
    produced = jnp.einsum(
        "gkf,fd->gkd",
        lax.all_to_all(fwd_buf, "expert", split_axis=0, concat_axis=0, tiled=True),
        fwd_weight,
        preferred_element_type=jnp.float32,
    ).astype(jnp.bfloat16)
    returned = lax.all_to_all(produced, "expert", split_axis=0, concat_axis=0, tiled=True)
    fwd_rows_out = lax.dot_general(
        fwd_selector,
        returned.reshape(groups * fwd_capacity, -1),
        (((0,), (0,)), ((), ())),
        preferred_element_type=jnp.float32,
    )
    fwd_out = (fwd_rows_out * fwd_gate[:, None]).astype(jnp.bfloat16)
    return (placed_weight, placed_moment, fwd_out)


def solution(mesh):
    groups = mesh.shape["expert"]
    in_specs = (
        P(("layer", "expert"), None),
        P(("layer", "expert"), None),
        P(("layer", "expert"), None),
        P(("layer", "expert")),
        P(("layer", "expert"), None, None),
        P(("layer", "expert"), None, None),
        P("layer"),
        P(("layer", "expert"), None),
        P(("layer", "expert"), None),
        P(("layer", "expert")),
    )
    out_specs = (
        P(("layer", "expert"), None, None),
        P(("layer", "expert"), None, None),
        P(("layer", "expert"), None),
    )

    def per_device(*args):
        few = groups >= 8 and groups & (groups - 1) == 0 and groups <= 2 * args[0].shape[0] // groups
        return (halves_plan if few else routed_plan)(*args)

    return jax.shard_map(
        per_device, mesh=mesh, in_specs=in_specs, out_specs=out_specs, check_vma=False
    )
```

```python
import functools

import jax
import jax.numpy as jnp
from jax import lax
from jax.experimental import pallas as pl
from jax.experimental.pallas import tpu as pltpu
from jax.sharding import PartitionSpec as P

linear_term = 3.4445
cubic_term = -4.775
quintic_term = 2.0315
moment_decay = 0.9
step_scale = 0.25
norm_floor = 1e-07

F32 = jnp.float32
BF16 = jnp.bfloat16
HBM = pl.BlockSpec(memory_space=pltpu.HBM)
VMEM = pl.BlockSpec(memory_space=pltpu.VMEM)
SMEM = pl.BlockSpec(memory_space=pltpu.SMEM)
ANY = pl.BlockSpec(memory_space=pl.ANY)
MIB = 1 << 20


def row_block(k, rows):
    return pl.ds(pl.multiple_of(k * rows, rows), rows)


def crossing_ranks(half, base, perm_ref):
    flags = [(perm_ref[base + q] // half != base // half).astype(jnp.int32) for q in range(half)]
    ranks, count = [], 0
    for flag in flags:
        ranks.append(count)
        count = count + flag
    return flags, ranks


def slots_of(half):
    return half // 2, 1, half - half // 2 - 1


def slot_rows(route, live, groups, capacity, me_ref, perm_ref):
    rows = route.shape[1]
    experts = lax.broadcasted_iota(jnp.int32, (groups, rows), 0)
    onehot = jnp.where((experts == route) & live, 1.0, 0.0).astype(BF16)
    before = lax.broadcasted_iota(jnp.int32, (rows, rows), 0)
    after = lax.broadcasted_iota(jnp.int32, (rows, rows), 1)
    upto = jnp.where(before <= after, 1.0, 0.0).astype(BF16)
    ranks = jnp.dot(onehot, upto, preferred_element_type=F32)
    rank = jnp.sum(ranks * onehot.astype(F32), axis=0, keepdims=True).astype(jnp.int32) - 1
    partner = jnp.zeros_like(route)
    for e in range(groups):
        partner = jnp.where(route == e, perm_ref[e] ^ me_ref[0], partner)
    return jnp.where(live, partner * capacity + rank, -1)


def selector_of(slot, slots):
    rows = slot.shape[1]
    places = lax.broadcasted_iota(jnp.int32, (slots, rows), 0)
    return jnp.where(places == slot, 1.0, 0.0).astype(BF16)


def pack_kernel(groups, live_ref, me_ref, perm_ref, *refs):
    sources, pieces, (slot_ref, gates_ref) = refs[:6], refs[7 : 7 + groups], refs[7 + groups : 9 + groups]
    held, sem = refs[9 + groups : 15 + groups], refs[-1]
    route_ref, fwd_route_ref, hidden_ref, out_ref, fwd_ref, gate_ref = held
    copies = [pltpu.make_async_copy(ref, room, sem.at[n]) for n, (ref, room) in enumerate(zip(sources, held))]
    for copy in copies:
        copy.start()
    rows, ff = hidden_ref.shape
    d = out_ref.shape[1]
    capacity = pieces[0].shape[0]
    slots = groups * capacity
    place = lax.broadcasted_iota(jnp.int32, (1, rows), 1)

    def fill(first, selector, source_ref):
        chosen = jnp.dot(selector, source_ref[...], preferred_element_type=F32).astype(BF16)
        for s, piece in zip(mixed_order(groups), pieces):
            piece[:, first : first + source_ref.shape[1]] = chosen[s * capacity : (s + 1) * capacity]

    copies[0].wait()
    slot = slot_rows(route_ref[...], place < live_ref[0], groups, capacity, me_ref, perm_ref)
    selector = selector_of(slot, slots)
    copies[1].wait()
    fwd_slot = slot_rows(fwd_route_ref[...], place >= 0, groups, capacity, me_ref, perm_ref)
    slot_ref[...] = fwd_slot
    copies[2].wait()
    fill(0, selector, hidden_ref)
    copies[3].wait()
    fill(ff, selector, out_ref)
    copies[4].wait()
    fill(ff + d, selector_of(fwd_slot, slots), fwd_ref)
    copies[5].wait()
    down = lax.broadcasted_iota(jnp.int32, (rows, rows), 0)
    across = lax.broadcasted_iota(jnp.int32, (rows, rows), 1)
    gates_ref[...] = jnp.sum(jnp.where(down == across, gate_ref[...], 0.0), axis=1, keepdims=True)


def pack_rows(live_rows, me, perm, route, fwd_route, hidden, grad_out, fwd_hidden, gate, earlier, groups, capacity):
    rows, ff = hidden.shape
    width = 2 * ff + grad_out.shape[1]
    sources = (route.reshape(1, rows), fwd_route.reshape(1, rows), hidden, grad_out, fwd_hidden, gate.reshape(1, rows))
    *pieces, slot, gates = pl.pallas_call(
        functools.partial(pack_kernel, groups),
        out_shape=(jax.ShapeDtypeStruct((capacity, width), BF16),) * groups
        + (jax.ShapeDtypeStruct((1, rows), jnp.int32), jax.ShapeDtypeStruct((rows, 1), F32)),
        in_specs=[SMEM] * 3 + [HBM] * 6 + [VMEM],
        out_specs=(VMEM,) * (groups + 2),
        scratch_shapes=[pltpu.VMEM(a.shape, a.dtype) for a in sources] + [pltpu.SemaphoreType.DMA((len(sources),))],
        compiler_params=pltpu.CompilerParams(vmem_limit_bytes=32 * MIB),
        cost_estimate=pl.CostEstimate(
            flops=2 * groups * capacity * rows * width, bytes_accessed=6 * rows * width, transcendentals=0
        ),
        name="pack_rows",
    )(live_rows, me, perm, *sources, earlier)
    return pieces, slot, gates


def split_kernel(me_ref, matrix_ref, *refs):
    pieces, sem = refs[1:-1], refs[-1]
    half, rows = len(pieces), pieces[0].shape[0]
    copies = [
        pltpu.make_async_copy(matrix_ref.at[0, row_block((me_ref[0] ^ s) % half, rows)], piece, sem.at[s])
        for s, piece in zip(return_order(half), pieces)
    ]
    for copy in copies:
        copy.start()
    for copy in copies:
        copy.wait()


def split(me, matrix, earlier, half):
    _, ff, d = matrix.shape
    piece = jax.ShapeDtypeStruct((ff // half, d), BF16)
    return pl.pallas_call(
        split_kernel,
        out_shape=(piece,) * half,
        in_specs=[SMEM, HBM, VMEM],
        out_specs=(VMEM,) * half,
        scratch_shapes=[pltpu.SemaphoreType.DMA((half,))],
        compiler_params=pltpu.CompilerParams(vmem_limit_bytes=60 * MIB),
        cost_estimate=pl.CostEstimate(flops=0, bytes_accessed=4 * ff * d, transcendentals=0),
        name="split",
    )(me, matrix, earlier)


def sort_kernel(me_ref, perm_ref, *refs):
    pieces, (near_ref, *slot_refs) = refs[:-4], refs[-4:]
    half = len(pieces)
    me = me_ref[0]
    base = me // half * half
    flags, ranks = crossing_ranks(half, base, perm_ref)
    for s, piece in zip(return_order(half), pieces):
        place = (me ^ s) % half
        crosses, rank = 0, 0
        for q in range(half):
            crosses = jnp.where(place == q, flags[q], crosses)
            rank = jnp.where(place == q, ranks[q], rank)
        near = (perm_ref[base + place] ^ me) % half

        @pl.when(crosses == 0)
        def _():
            near_ref[near] = piece[...]

        first = 0
        for slots in slot_refs:
            count = slots.shape[0]

            @pl.when((crosses == 1) & (rank >= first) & (rank < first + count))
            def _():
                slots[rank - first] = piece[...]

            first += count


def sort_pieces(me, perm, pieces):
    half = len(pieces)
    shape = pieces[0].shape
    counts = (half,) + slots_of(half)
    return pl.pallas_call(
        sort_kernel,
        out_shape=tuple(jax.ShapeDtypeStruct((count,) + shape, BF16) for count in counts),
        in_specs=[SMEM, SMEM] + [VMEM] * half,
        out_specs=(VMEM,) * len(counts),
        compiler_params=pltpu.CompilerParams(vmem_limit_bytes=32 * MIB),
        cost_estimate=pl.CostEstimate(flops=0, bytes_accessed=4 * half * pieces[0].size, transcendentals=0),
        name="sort_pieces",
    )(me, perm, *pieces)


def join_kernel(half, me_ref, perm_ref, near_ref, *refs):
    slot_refs, targets = refs[:3], refs[3:]
    me = me_ref[0]
    base = me // half * half
    flags, ranks = crossing_ranks(half, half - base, perm_ref)
    for s, target in zip(return_order(half), targets):
        crosses, rank = 0, 0
        for q in range(half):
            here = perm_ref[half - base + q] == me ^ s
            crosses = jnp.where(here, 1, crosses)
            rank = jnp.where(here, ranks[q], rank)

        @pl.when(crosses == 0)
        def _():
            target[...] = near_ref[s]

        first = 0
        for slots in slot_refs:
            count = slots.shape[0]

            @pl.when((crosses == 1) & (rank >= first) & (rank < first + count))
            def _():
                target[...] = slots[rank - first]

            first += count


def join_pieces(me, perm, near, slots):
    half = near.shape[0]
    piece = jax.ShapeDtypeStruct(near.shape[1:], BF16)
    return pl.pallas_call(
        functools.partial(join_kernel, half),
        out_shape=(piece,) * half,
        in_specs=[SMEM, SMEM] + [VMEM] * 4,
        out_specs=(VMEM,) * half,
        compiler_params=pltpu.CompilerParams(vmem_limit_bytes=32 * MIB),
        cost_estimate=pl.CostEstimate(flops=0, bytes_accessed=4 * near.size, transcendentals=0),
        name="join_pieces",
    )(me, perm, near, *slots)


def gradient_kernel(groups, *refs):
    pieces, (grad_ref, fwd_ref, rows_ref) = refs[:groups], refs[groups:]
    ff, d = grad_ref.shape
    capacity = pieces[0].shape[0]
    for n, piece in enumerate(pieces):
        span = slice(n * capacity, (n + 1) * capacity)
        rows_ref[span] = piece[:, : ff + d]
        fwd_ref[span] = piece[:, ff + d :]
    grad_ref[...] = lax.dot_general(
        rows_ref[:, :ff], rows_ref[:, ff:], (((0,), (0,)), ((), ())), preferred_element_type=F32
    )


def gradient(pieces, ff, d):
    groups = len(pieces)
    slots = groups * pieces[0].shape[0]
    return pl.pallas_call(
        functools.partial(gradient_kernel, groups),
        out_shape=(jax.ShapeDtypeStruct((ff, d), F32), jax.ShapeDtypeStruct((slots, ff), BF16)),
        in_specs=[VMEM] * groups,
        out_specs=(VMEM, VMEM),
        scratch_shapes=[pltpu.VMEM((slots, ff + d), BF16)],
        compiler_params=pltpu.CompilerParams(vmem_limit_bytes=32 * MIB),
        cost_estimate=pl.CostEstimate(
            flops=2 * ff * d * slots, bytes_accessed=4 * ff * d + 4 * slots * (ff + d), transcendentals=0
        ),
        name="gradient",
    )(*pieces)


def assembled(me_ref, pieces, held):
    half, rows = len(pieces), pieces[0].shape[0]
    for s, piece in zip(return_order(half), pieces):
        held[row_block((me_ref[0] ^ s) % half, rows)] = piece[...]
    return held[...].astype(F32)


def orthogonal_kernel(me_ref, grad_ref, *refs):
    pieces, (moment_new_ref, ortho_ref, held) = refs[:-3], refs[-3:]
    moment_new = (moment_decay * assembled(me_ref, pieces, held) + grad_ref[...]).astype(BF16)
    moment_new_ref[...] = moment_new
    moment_f = moment_new.astype(F32)
    frobenius = jnp.sqrt(jnp.sum(moment_f * moment_f))
    current = (moment_f / (frobenius + norm_floor)).astype(BF16)
    for _ in range(2):
        gramian = lax.dot_general(
            current, current, (((1,), (1,)), ((), ())), preferred_element_type=F32
        ).astype(BF16)
        squared = jnp.dot(gramian, gramian, preferred_element_type=F32)
        poly = (cubic_term * gramian.astype(F32) + quintic_term * squared).astype(BF16)
        current = (
            linear_term * current.astype(F32) + jnp.dot(poly, current, preferred_element_type=F32)
        ).astype(BF16)
    ortho_ref[...] = current


def orthogonal(me, grad, pieces):
    ff, d = grad.shape
    shape = jax.ShapeDtypeStruct((ff, d), BF16)
    return pl.pallas_call(
        orthogonal_kernel,
        out_shape=(shape, shape),
        in_specs=[SMEM, VMEM] + [VMEM] * len(pieces),
        out_specs=(VMEM, VMEM),
        scratch_shapes=[pltpu.VMEM((ff, d), BF16)],
        compiler_params=pltpu.CompilerParams(vmem_limit_bytes=32 * MIB),
        cost_estimate=pl.CostEstimate(
            flops=8 * ff * ff * d + 4 * ff**3, bytes_accessed=10 * ff * d, transcendentals=1
        ),
        name="orthogonal",
    )(me, grad, *pieces)


def produce_kernel(half, me_ref, ortho_ref, fwd_ref, *refs):
    pieces, (weight_new_ref, *produced), held = refs[:half], refs[half:-1], refs[-1]
    weight = assembled(me_ref, pieces, held)
    weight_new = (weight - step_scale * ortho_ref[...].astype(F32)).astype(BF16)
    weight_new_ref[...] = weight_new
    product = jnp.dot(fwd_ref[...], weight_new, preferred_element_type=F32).astype(BF16)
    groups, capacity = len(produced), produced[0].shape[0]
    came = mixed_order(groups)
    for s, piece in zip(return_order(groups), produced):
        n = came.index(s)
        piece[...] = product[n * capacity : (n + 1) * capacity]


def produce(me, ortho, fwd_rows, pieces, groups):
    half = len(pieces)
    ff, d = ortho.shape
    slots = fwd_rows.shape[0]
    weight_new, *produced = pl.pallas_call(
        functools.partial(produce_kernel, half),
        out_shape=(jax.ShapeDtypeStruct((ff, d), BF16),)
        + (jax.ShapeDtypeStruct((slots // groups, d), BF16),) * groups,
        in_specs=[SMEM] + [VMEM] * (2 + half),
        out_specs=(VMEM,) * (groups + 1),
        scratch_shapes=[pltpu.VMEM((ff, d), BF16)],
        compiler_params=pltpu.CompilerParams(vmem_limit_bytes=32 * MIB),
        cost_estimate=pl.CostEstimate(
            flops=2 * ff * d * slots, bytes_accessed=8 * ff * d + 2 * slots * (ff + d), transcendentals=0
        ),
        name="produce",
    )(me, ortho, fwd_rows, *pieces)
    return weight_new, produced


def finish_kernel(groups, slot_ref, gates_ref, *refs):
    pieces, (out_ref, returned_ref) = refs[:groups], refs[groups:]
    capacity = pieces[0].shape[0]
    for s, piece in zip(return_order(groups), pieces):
        returned_ref[s * capacity : (s + 1) * capacity] = piece[...]
    selector = selector_of(slot_ref[...], groups * capacity)
    expert_out = lax.dot_general(
        selector, returned_ref[...], (((0,), (0,)), ((), ())), preferred_element_type=F32
    )
    out_ref[...] = (gates_ref[...] * expert_out).astype(BF16)


def finish(slot, gates, returned):
    groups = len(returned)
    rows = slot.shape[1]
    capacity, d = returned[0].shape
    slots = groups * capacity
    return pl.pallas_call(
        functools.partial(finish_kernel, groups),
        out_shape=jax.ShapeDtypeStruct((rows, d), BF16),
        in_specs=[VMEM] * (2 + groups),
        out_specs=VMEM,
        scratch_shapes=[pltpu.VMEM((slots, d), BF16)],
        compiler_params=pltpu.CompilerParams(vmem_limit_bytes=32 * MIB),
        cost_estimate=pl.CostEstimate(
            flops=2 * slots * rows * d, bytes_accessed=2 * d * (slots + rows), transcendentals=0
        ),
        name="finish",
    )(slot, gates, *returned)


def mixed_order(groups):
    far, near = list(range(groups // 2, groups)), list(range(groups // 2 - 1, 0, -1))
    return [0] + [s for pair in zip(far, near + [None]) for s in pair if s is not None]


def return_order(groups):
    far, near = list(range(groups // 2, groups)), list(range(groups // 2 - 1, 0, -1))
    order = [0]
    while far or near:
        order += far[:2] + near[:1]
        far, near = far[2:], near[1:]
    return order


def swap(pieces, order):
    groups = lax.axis_size("expert")
    return [
        lax.ppermute(piece, "expert", [(i, i ^ s) for i in range(groups)]) if s else piece
        for s, piece in zip(order, pieces)
    ]


def halves_plan(
    grad_hidden, grad_out, grad_route, live_rows, w_down, w_moment, perm, fwd_hidden, fwd_route, fwd_gate
):
    groups = lax.axis_size("expert")
    layers = lax.axis_size("layer")
    half = groups // 2
    me = lax.axis_index("expert").astype(jnp.int32).reshape(1)
    capacity = max(4, 2 * grad_hidden.shape[0] // groups)
    ff, d = w_down.shape[1:]
    crossing = jnp.sum((perm[:half] >= half).astype(jnp.int32)).reshape(1)
    most = crossing
    for turn in range(1, layers):
        other = lax.ppermute(crossing, "layer", [(i, (i + turn) % layers) for i in range(layers)])
        most = jnp.maximum(most, other)
    most = most[0]

    near_order, slot_counts = return_order(half), slots_of(half)

    def mirror(array):
        return swap([array], [half])[0]

    def gathered(spread):
        near, first, following, rest = sort_pieces(me, perm, spread)
        crossed = [
            mirror(first),
            lax.cond(most > slot_counts[0], mirror, lambda array: array, following),
            lax.cond(most > slot_counts[0] + slot_counts[1], mirror, lambda array: array, rest),
        ]
        return swap(join_pieces(me, perm, near, crossed), near_order)

    moment_pieces = split(me, w_moment, live_rows, half)
    packed, fwd_slot, gates = pack_rows(
        live_rows, me, perm, grad_route, fwd_route, grad_hidden, grad_out, fwd_hidden, fwd_gate,
        moment_pieces[0], groups, capacity,
    )
    weight_pieces = split(me, w_down, fwd_slot, half)
    received = swap(packed, mixed_order(groups))
    moment_placed = gathered(swap(moment_pieces, near_order))
    weight_placed = gathered(swap(weight_pieces, near_order))
    grad, fwd_rows = gradient(received, ff, d)
    moment_new, ortho = orthogonal(me, grad, moment_placed)
    weight_new, produced = produce(me, ortho, fwd_rows, weight_placed, groups)
    returned = swap(produced, return_order(groups))
    return weight_new[None], moment_new[None], finish(fwd_slot, gates, returned)


def lookup(route_ids, mapping):
    columns = jnp.arange(mapping.shape[0], dtype=jnp.int32)
    hits = route_ids[:, None] == columns[None, :]
    return jnp.sum(jnp.where(hits, mapping[None, :], 0), axis=1)


def slot_matrix(target, is_live, groups, capacity):
    columns = jnp.arange(groups, dtype=jnp.int32)
    onehot = ((target[:, None] == columns[None, :]) & is_live[:, None]).astype(jnp.int32)
    ranked = jnp.sum(jnp.cumsum(onehot, axis=0) * onehot, axis=1) - 1
    slot_of = jnp.where(is_live, target * capacity + ranked, -1)
    slots = jnp.arange(groups * capacity, dtype=jnp.int32)
    return (slots[:, None] == slot_of[None, :]).astype(jnp.bfloat16)


def orthogonalize(moment):
    moment_f = moment.astype(jnp.float32)
    frobenius = jnp.sqrt(jnp.sum(moment_f * moment_f))
    current = (moment_f / (frobenius + norm_floor)).astype(jnp.bfloat16)
    for sweep_index in range(2):
        gramian = lax.dot_general(
            current, current, (((1,), (1,)), ((), ())), preferred_element_type=jnp.float32
        ).astype(jnp.bfloat16)
        squared = jnp.dot(gramian, gramian, preferred_element_type=jnp.float32)
        poly = (cubic_term * gramian.astype(jnp.float32) + quintic_term * squared).astype(
            jnp.bfloat16
        )
        current = (
            linear_term * current.astype(jnp.float32)
            + jnp.dot(poly, current, preferred_element_type=jnp.float32)
        ).astype(jnp.bfloat16)
    return current


def relocate(weight, moment, perm):
    groups = lax.axis_size("expert")
    weight_flat = weight.reshape(groups, -1)
    moment_flat = moment.reshape(groups, -1)
    spread_w, spread_m = (
        lax.all_to_all(weight_flat, "expert", split_axis=0, concat_axis=0, tiled=True),
        lax.all_to_all(moment_flat, "expert", split_axis=0, concat_axis=0, tiled=True),
    )
    devices = jnp.arange(groups, dtype=jnp.int32)
    inverse = jnp.sum(jnp.where(perm[None, :] == devices[:, None], devices[None, :], 0), axis=1)
    ordered_w = jnp.take(spread_w, inverse, axis=0)
    ordered_m = jnp.take(spread_m, inverse, axis=0)
    back_w, back_m = (
        lax.all_to_all(ordered_w, "expert", split_axis=0, concat_axis=0, tiled=True),
        lax.all_to_all(ordered_m, "expert", split_axis=0, concat_axis=0, tiled=True),
    )
    return (back_w.reshape(weight.shape), back_m.reshape(moment.shape))


def routed_plan(
    grad_hidden,
    grad_out,
    grad_route,
    live_rows,
    w_down,
    w_moment,
    perm,
    fwd_hidden,
    fwd_route,
    fwd_gate,
):
    groups = lax.axis_size("expert")
    grad_count = grad_hidden.shape[0]
    capacity = max(4, 2 * grad_count // groups)
    is_live = jnp.arange(grad_count, dtype=jnp.int32) < live_rows[0]
    route_ids = grad_route[:, 0]
    weight, moment = relocate(w_down, w_moment, perm)
    target = lookup(route_ids, perm)
    selector = slot_matrix(target, is_live, groups, capacity)
    hidden_buf = (
        jnp.dot(selector, grad_hidden, preferred_element_type=jnp.float32)
        .astype(jnp.bfloat16)
        .reshape(groups, capacity, -1)
    )
    outgrad_buf = (
        jnp.dot(selector, grad_out, preferred_element_type=jnp.float32)
        .astype(jnp.bfloat16)
        .reshape(groups, capacity, -1)
    )
    recv_hidden, recv_outgrad = (
        lax.all_to_all(hidden_buf, "expert", split_axis=0, concat_axis=0, tiled=True),
        lax.all_to_all(outgrad_buf, "expert", split_axis=0, concat_axis=0, tiled=True),
    )
    grad = lax.dot_general(
        recv_hidden.reshape(groups * capacity, -1),
        recv_outgrad.reshape(groups * capacity, -1),
        (((0,), (0,)), ((), ())),
        preferred_element_type=jnp.float32,
    )
    moment_new = (moment_decay * moment[0].astype(jnp.float32) + grad).astype(jnp.bfloat16)
    ortho = orthogonalize(moment_new)
    weight_new = (weight[0].astype(jnp.float32) - step_scale * ortho.astype(jnp.float32)).astype(
        jnp.bfloat16
    )
    weight_new = weight_new[None]
    moment_new = moment_new[None]
    fwd_ids = fwd_route[:, 0]
    placed_weight, placed_moment = (weight_new, moment_new)
    fwd_target = lookup(fwd_ids, perm)
    fwd_weight = weight_new[0]
    fwd_count = fwd_hidden.shape[0]
    fwd_capacity = max(4, 2 * fwd_count // groups)
    fwd_selector = slot_matrix(fwd_target, jnp.ones((fwd_count,), dtype=bool), groups, fwd_capacity)
    fwd_buf = (
        jnp.dot(fwd_selector, fwd_hidden, preferred_element_type=jnp.float32)
        .astype(jnp.bfloat16)
        .reshape(groups, fwd_capacity, -1)
    )
    produced = jnp.einsum(
        "gkf,fd->gkd",
        lax.all_to_all(fwd_buf, "expert", split_axis=0, concat_axis=0, tiled=True),
        fwd_weight,
        preferred_element_type=jnp.float32,
    ).astype(jnp.bfloat16)
    returned = lax.all_to_all(produced, "expert", split_axis=0, concat_axis=0, tiled=True)
    fwd_rows_out = lax.dot_general(
        fwd_selector,
        returned.reshape(groups * fwd_capacity, -1),
        (((0,), (0,)), ((), ())),
        preferred_element_type=jnp.float32,
    )
    fwd_out = (fwd_rows_out * fwd_gate[:, None]).astype(jnp.bfloat16)
    return (placed_weight, placed_moment, fwd_out)


def solution(mesh):
    groups = mesh.shape["expert"]
    in_specs = (
        P(("layer", "expert"), None),
        P(("layer", "expert"), None),
        P(("layer", "expert"), None),
        P(("layer", "expert")),
        P(("layer", "expert"), None, None),
        P(("layer", "expert"), None, None),
        P("layer"),
        P(("layer", "expert"), None),
        P(("layer", "expert"), None),
        P(("layer", "expert")),
    )
    out_specs = (
        P(("layer", "expert"), None, None),
        P(("layer", "expert"), None, None),
        P(("layer", "expert"), None),
    )

    def per_device(*args):
        few = groups >= 8 and groups & (groups - 1) == 0 and groups <= 2 * args[0].shape[0] // groups
        return (halves_plan if few else routed_plan)(*args)

    return jax.shard_map(
        per_device, mesh=mesh, in_specs=in_specs, out_specs=out_specs, check_vma=False
    )
```

```python
import functools

import jax
import jax.numpy as jnp
from jax import lax
from jax.experimental import pallas as pl
from jax.experimental.pallas import tpu as pltpu
from jax.sharding import PartitionSpec as P

linear_term = 3.4445
cubic_term = -4.775
quintic_term = 2.0315
moment_decay = 0.9
step_scale = 0.25
norm_floor = 1e-07

F32 = jnp.float32
BF16 = jnp.bfloat16
HBM = pl.BlockSpec(memory_space=pltpu.HBM)
VMEM = pl.BlockSpec(memory_space=pltpu.VMEM)
SMEM = pl.BlockSpec(memory_space=pltpu.SMEM)
ANY = pl.BlockSpec(memory_space=pl.ANY)
MIB = 1 << 20


def row_block(k, rows):
    return pl.ds(pl.multiple_of(k * rows, rows), rows)


def crossing_ranks(half, base, perm_ref):
    flags = [(perm_ref[base + q] // half != base // half).astype(jnp.int32) for q in range(half)]
    ranks, count = [], 0
    for flag in flags:
        ranks.append(count)
        count = count + flag
    return flags, ranks


def slots_of(half):
    return half // 2, 1, half - half // 2 - 1


def slot_rows(route, live, groups, capacity, me_ref, perm_ref):
    rows = route.shape[1]
    experts = lax.broadcasted_iota(jnp.int32, (groups, rows), 0)
    onehot = jnp.where((experts == route) & live, 1.0, 0.0).astype(BF16)
    before = lax.broadcasted_iota(jnp.int32, (rows, rows), 0)
    after = lax.broadcasted_iota(jnp.int32, (rows, rows), 1)
    upto = jnp.where(before <= after, 1.0, 0.0).astype(BF16)
    ranks = jnp.dot(onehot, upto, preferred_element_type=F32)
    rank = jnp.sum(ranks * onehot.astype(F32), axis=0, keepdims=True).astype(jnp.int32) - 1
    partner = jnp.zeros_like(route)
    for e in range(groups):
        partner = jnp.where(route == e, perm_ref[e] ^ me_ref[0], partner)
    return jnp.where(live, partner * capacity + rank, -1)


def selector_of(slot, slots):
    rows = slot.shape[1]
    places = lax.broadcasted_iota(jnp.int32, (slots, rows), 0)
    return jnp.where(places == slot, 1.0, 0.0).astype(BF16)


def prepare_kernel(groups, half, live_ref, me_ref, perm_ref, *refs):
    sources, refs = refs[:8], refs[8:]
    moment_pieces, weight_pieces, packed_pieces = refs[:half], refs[half : 2 * half], refs[2 * half : 2 * half + groups]
    slot_ref, gates_ref = refs[2 * half + groups : 2 * half + groups + 2]
    *held, packed, in_sem, out_sem = refs[2 * half + groups + 2 :]
    moment_ref, route_ref, fwd_route_ref, hidden_ref, out_ref, fwd_ref, gate_ref, weight_ref = held
    copies = [pltpu.make_async_copy(ref, room, in_sem.at[n]) for n, (ref, room) in enumerate(zip(sources, held))]
    for copy in copies:
        copy.start()
    rows, ff = hidden_ref.shape
    d = out_ref.shape[1]
    capacity = packed_pieces[0].shape[0]
    slots = groups * capacity
    place = lax.broadcasted_iota(jnp.int32, (1, rows), 1)
    leaving = []

    def leave(source, piece):
        copy = pltpu.make_async_copy(source, piece, out_sem.at[len(leaving)])
        copy.start()
        leaving.append(copy)

    def leave_blocks(matrix, pieces):
        for s, piece in zip(return_order(half), pieces):
            leave(matrix.at[0, row_block((me_ref[0] ^ s) % half, piece.shape[0])], piece)

    copies[0].wait()
    leave_blocks(moment_ref, moment_pieces)
    copies[1].wait()
    slot = slot_rows(route_ref[...], place < live_ref[0], groups, capacity, me_ref, perm_ref)
    selector = selector_of(slot, slots)
    copies[2].wait()
    fwd_slot = slot_rows(fwd_route_ref[...], place >= 0, groups, capacity, me_ref, perm_ref)
    slot_ref[...] = fwd_slot
    copies[3].wait()
    packed[:, :ff] = jnp.dot(selector, hidden_ref[...], preferred_element_type=F32).astype(BF16)
    copies[4].wait()
    packed[:, ff : ff + d] = jnp.dot(selector, out_ref[...], preferred_element_type=F32).astype(BF16)
    copies[5].wait()
    fwd_selector = selector_of(fwd_slot, slots)
    packed[:, ff + d :] = jnp.dot(fwd_selector, fwd_ref[...], preferred_element_type=F32).astype(BF16)
    for s, piece in zip(mixed_order(groups), packed_pieces):
        leave(packed.at[pl.ds(s * capacity, capacity)], piece)
    copies[7].wait()
    leave_blocks(weight_ref, weight_pieces)
    copies[6].wait()
    down = lax.broadcasted_iota(jnp.int32, (rows, rows), 0)
    across = lax.broadcasted_iota(jnp.int32, (rows, rows), 1)
    gates_ref[...] = jnp.sum(jnp.where(down == across, gate_ref[...], 0.0), axis=1, keepdims=True)
    for copy in leaving:
        copy.wait()


def prepare(live_rows, me, perm, route, fwd_route, hidden, grad_out, fwd_hidden, gate, moment, weight, groups, capacity):
    rows, ff = hidden.shape
    d = grad_out.shape[1]
    half = groups // 2
    width = 2 * ff + d
    sources = (
        moment, route.reshape(1, rows), fwd_route.reshape(1, rows), hidden, grad_out, fwd_hidden,
        gate.reshape(1, rows), weight,
    )
    block = jax.ShapeDtypeStruct((ff // half, d), BF16)
    outputs = pl.pallas_call(
        functools.partial(prepare_kernel, groups, half),
        out_shape=(block,) * (2 * half)
        + (jax.ShapeDtypeStruct((capacity, width), BF16),) * groups
        + (jax.ShapeDtypeStruct((1, rows), jnp.int32), jax.ShapeDtypeStruct((rows, 1), F32)),
        in_specs=[SMEM] * 3 + [HBM] * len(sources),
        out_specs=(HBM,) * (2 * half + groups) + (VMEM, VMEM),
        scratch_shapes=[pltpu.VMEM(a.shape, a.dtype) for a in sources]
        + [
            pltpu.VMEM((groups * capacity, width), BF16),
            pltpu.SemaphoreType.DMA((len(sources),)),
            pltpu.SemaphoreType.DMA((2 * half + groups,)),
        ],
        compiler_params=pltpu.CompilerParams(vmem_limit_bytes=60 * MIB),
        cost_estimate=pl.CostEstimate(
            flops=2 * groups * capacity * rows * width,
            bytes_accessed=8 * ff * d + 6 * rows * width,
            transcendentals=0,
        ),
        name="prepare",
    )(live_rows, me, perm, *sources)
    *pieces, slot, gates = outputs
    return pieces[:half], pieces[half : 2 * half], pieces[2 * half :], slot, gates


def sort_kernel(me_ref, perm_ref, *refs):
    pieces, (near_ref, *slot_refs) = refs[:-4], refs[-4:]
    half = len(pieces)
    me = me_ref[0]
    base = me // half * half
    flags, ranks = crossing_ranks(half, base, perm_ref)
    for s, piece in zip(return_order(half), pieces):
        place = (me ^ s) % half
        crosses, rank = 0, 0
        for q in range(half):
            crosses = jnp.where(place == q, flags[q], crosses)
            rank = jnp.where(place == q, ranks[q], rank)
        near = (perm_ref[base + place] ^ me) % half

        @pl.when(crosses == 0)
        def _():
            near_ref[near] = piece[...]

        first = 0
        for slots in slot_refs:
            count = slots.shape[0]

            @pl.when((crosses == 1) & (rank >= first) & (rank < first + count))
            def _():
                slots[rank - first] = piece[...]

            first += count


def sort_pieces(me, perm, pieces):
    half = len(pieces)
    shape = pieces[0].shape
    counts = (half,) + slots_of(half)
    return pl.pallas_call(
        sort_kernel,
        out_shape=tuple(jax.ShapeDtypeStruct((count,) + shape, BF16) for count in counts),
        in_specs=[SMEM, SMEM] + [VMEM] * half,
        out_specs=(VMEM,) * len(counts),
        compiler_params=pltpu.CompilerParams(vmem_limit_bytes=60 * MIB),
        cost_estimate=pl.CostEstimate(flops=0, bytes_accessed=4 * half * pieces[0].size, transcendentals=0),
        name="sort_pieces",
    )(me, perm, *pieces)


def join_kernel(half, me_ref, perm_ref, near_ref, *refs):
    slot_refs, targets = refs[:3], refs[4:]
    me = me_ref[0]
    base = me // half * half
    flags, ranks = crossing_ranks(half, half - base, perm_ref)
    for s, target in zip(return_order(half), targets):
        crosses, rank = 0, 0
        for q in range(half):
            here = perm_ref[half - base + q] == me ^ s
            crosses = jnp.where(here, 1, crosses)
            rank = jnp.where(here, ranks[q], rank)

        @pl.when(crosses == 0)
        def _():
            target[...] = near_ref[s]

        first = 0
        for slots in slot_refs:
            count = slots.shape[0]

            @pl.when((crosses == 1) & (rank >= first) & (rank < first + count))
            def _():
                target[...] = slots[rank - first]

            first += count


def join_pieces(me, perm, near, slots, earlier):
    half = near.shape[0]
    piece = jax.ShapeDtypeStruct(near.shape[1:], BF16)
    return pl.pallas_call(
        functools.partial(join_kernel, half),
        out_shape=(piece,) * half,
        in_specs=[SMEM, SMEM] + [VMEM] * 5,
        out_specs=(VMEM,) * half,
        compiler_params=pltpu.CompilerParams(vmem_limit_bytes=60 * MIB),
        cost_estimate=pl.CostEstimate(flops=0, bytes_accessed=4 * near.size, transcendentals=0),
        name="join_pieces",
    )(me, perm, near, *slots, earlier)


def gradient_kernel(first, *refs):
    count = len(refs) - 4 if first else len(refs) - 5
    pieces, (grad_ref, fwd_ref, token_ref, rows_ref) = refs[:count], refs[-4:]
    ff, d = grad_ref.shape
    capacity = pieces[0].shape[0]
    for n, piece in enumerate(pieces):
        span = slice(n * capacity, (n + 1) * capacity)
        rows_ref[span] = piece[:, : ff + d]
        fwd_ref[span] = piece[:, ff + d :]
    grad = lax.dot_general(
        rows_ref[:, :ff], rows_ref[:, ff:], (((0,), (0,)), ((), ())), preferred_element_type=F32
    )
    grad_ref[...] = grad if first else refs[count][...] + grad
    token_ref[...] = jnp.zeros_like(token_ref)


def gradient(pieces, ff, d, *sofar):
    slots = len(pieces) * pieces[0].shape[0]
    return pl.pallas_call(
        functools.partial(gradient_kernel, not sofar),
        out_shape=(
            jax.ShapeDtypeStruct((ff, d), F32),
            jax.ShapeDtypeStruct((slots, ff), BF16),
            jax.ShapeDtypeStruct((8, 128), F32),
        ),
        in_specs=[VMEM] * (len(pieces) + len(sofar)),
        out_specs=(VMEM,) * 3,
        scratch_shapes=[pltpu.VMEM((slots, ff + d), BF16)],
        compiler_params=pltpu.CompilerParams(vmem_limit_bytes=32 * MIB),
        cost_estimate=pl.CostEstimate(
            flops=2 * ff * d * slots, bytes_accessed=4 * ff * d + 4 * slots * (ff + d), transcendentals=0
        ),
        name="gradient",
    )(*pieces, *sofar)


def assembled(me_ref, pieces, held):
    half, rows = len(pieces), pieces[0].shape[0]
    for s, piece in zip(return_order(half), pieces):
        held[row_block((me_ref[0] ^ s) % half, rows)] = piece[...]
    return held[...].astype(F32)


def orthogonal_kernel(me_ref, grad_ref, *refs):
    pieces, (moment_new_ref, ortho_ref, held) = refs[:-3], refs[-3:]
    moment_new = (moment_decay * assembled(me_ref, pieces, held) + grad_ref[...]).astype(BF16)
    moment_new_ref[...] = moment_new
    moment_f = moment_new.astype(F32)
    frobenius = jnp.sqrt(jnp.sum(moment_f * moment_f))
    current = (moment_f / (frobenius + norm_floor)).astype(BF16)
    for _ in range(2):
        gramian = lax.dot_general(
            current, current, (((1,), (1,)), ((), ())), preferred_element_type=F32
        ).astype(BF16)
        squared = jnp.dot(gramian, gramian, preferred_element_type=F32)
        poly = (cubic_term * gramian.astype(F32) + quintic_term * squared).astype(BF16)
        current = (
            linear_term * current.astype(F32) + jnp.dot(poly, current, preferred_element_type=F32)
        ).astype(BF16)
    ortho_ref[...] = current


def orthogonal(me, grad, pieces):
    ff, d = grad.shape
    shape = jax.ShapeDtypeStruct((ff, d), BF16)
    return pl.pallas_call(
        orthogonal_kernel,
        out_shape=(shape, shape),
        in_specs=[SMEM, VMEM] + [VMEM] * len(pieces),
        out_specs=(VMEM, VMEM),
        scratch_shapes=[pltpu.VMEM((ff, d), BF16)],
        compiler_params=pltpu.CompilerParams(vmem_limit_bytes=32 * MIB),
        cost_estimate=pl.CostEstimate(
            flops=8 * ff * ff * d + 4 * ff**3, bytes_accessed=10 * ff * d, transcendentals=1
        ),
        name="orthogonal",
    )(me, grad, *pieces)


def produce_kernel(half, me_ref, ortho_ref, early_ref, late_ref, *refs):
    pieces, (weight_new_ref, *produced), held = refs[:half], refs[half:-1], refs[-1]
    weight = assembled(me_ref, pieces, held)
    weight_new = (weight - step_scale * ortho_ref[...].astype(F32)).astype(BF16)
    weight_new_ref[...] = weight_new
    products = [
        jnp.dot(ref[...], weight_new, preferred_element_type=F32).astype(BF16) for ref in (early_ref, late_ref)
    ]
    groups, capacity = len(produced), produced[0].shape[0]
    came = mixed_order(groups)
    for s, piece in zip(return_order(groups), produced):
        part, n = divmod(came.index(s), groups // 2)
        piece[...] = products[part][n * capacity : (n + 1) * capacity]


def produce(me, ortho, fwd_rows, pieces, groups):
    half = len(pieces)
    ff, d = ortho.shape
    slots = 2 * fwd_rows[0].shape[0]
    weight_new, *produced = pl.pallas_call(
        functools.partial(produce_kernel, half),
        out_shape=(jax.ShapeDtypeStruct((ff, d), BF16),)
        + (jax.ShapeDtypeStruct((slots // groups, d), BF16),) * groups,
        in_specs=[SMEM] + [VMEM] * (3 + half),
        out_specs=(VMEM,) * (groups + 1),
        scratch_shapes=[pltpu.VMEM((ff, d), BF16)],
        compiler_params=pltpu.CompilerParams(vmem_limit_bytes=32 * MIB),
        cost_estimate=pl.CostEstimate(
            flops=2 * ff * d * slots, bytes_accessed=8 * ff * d + 2 * slots * (ff + d), transcendentals=0
        ),
        name="produce",
    )(me, ortho, *fwd_rows, *pieces)
    return weight_new, produced


def finish_kernel(groups, slot_ref, gates_ref, *refs):
    pieces, (out_ref, returned_ref) = refs[:groups], refs[groups:]
    capacity = pieces[0].shape[0]
    for s, piece in zip(return_order(groups), pieces):
        returned_ref[s * capacity : (s + 1) * capacity] = piece[...]
    selector = selector_of(slot_ref[...], groups * capacity)
    expert_out = lax.dot_general(
        selector, returned_ref[...], (((0,), (0,)), ((), ())), preferred_element_type=F32
    )
    out_ref[...] = (gates_ref[...] * expert_out).astype(BF16)


def finish(slot, gates, returned):
    groups = len(returned)
    rows = slot.shape[1]
    capacity, d = returned[0].shape
    slots = groups * capacity
    return pl.pallas_call(
        functools.partial(finish_kernel, groups),
        out_shape=jax.ShapeDtypeStruct((rows, d), BF16),
        in_specs=[VMEM] * (2 + groups),
        out_specs=VMEM,
        scratch_shapes=[pltpu.VMEM((slots, d), BF16)],
        compiler_params=pltpu.CompilerParams(vmem_limit_bytes=32 * MIB),
        cost_estimate=pl.CostEstimate(
            flops=2 * slots * rows * d, bytes_accessed=2 * d * (slots + rows), transcendentals=0
        ),
        name="finish",
    )(slot, gates, *returned)


def mixed_order(groups):
    far, near = list(range(groups // 2, groups)), list(range(groups // 2 - 1, 0, -1))
    return [0] + [s for pair in zip(far, near + [None]) for s in pair if s is not None]


def return_order(groups):
    far, near = list(range(groups // 2, groups)), list(range(groups // 2 - 1, 0, -1))
    order = [0]
    while far or near:
        order += far[:2] + near[:1]
        far, near = far[2:], near[1:]
    return order


def swap(pieces, order):
    groups = lax.axis_size("expert")
    return [
        lax.ppermute(piece, "expert", [(i, i ^ s) for i in range(groups)]) if s else piece
        for s, piece in zip(order, pieces)
    ]


def halves_plan(
    grad_hidden, grad_out, grad_route, live_rows, w_down, w_moment, perm, fwd_hidden, fwd_route, fwd_gate
):
    groups = lax.axis_size("expert")
    layers = lax.axis_size("layer")
    half = groups // 2
    me = lax.axis_index("expert").astype(jnp.int32).reshape(1)
    capacity = max(4, 2 * grad_hidden.shape[0] // groups)
    ff, d = w_down.shape[1:]
    crossing = jnp.sum((perm[:half] >= half).astype(jnp.int32)).reshape(1)
    most = crossing
    for turn in range(1, layers):
        other = lax.ppermute(crossing, "layer", [(i, (i + turn) % layers) for i in range(layers)])
        most = jnp.maximum(most, other)
    most = most[0]

    near_order, slot_counts = return_order(half), slots_of(half)

    def mirror(array):
        return swap([array], [half])[0]

    def gathered(spread, earlier):
        near, first, following, rest = sort_pieces(me, perm, spread)
        crossed = [
            mirror(first),
            lax.cond(most > slot_counts[0], mirror, lambda array: array, following),
            lax.cond(most > slot_counts[0] + slot_counts[1], mirror, lambda array: array, rest),
        ]
        return swap(join_pieces(me, perm, near, crossed, earlier), near_order)

    moment_pieces, weight_pieces, packed, fwd_slot, gates = prepare(
        live_rows, me, perm, grad_route, fwd_route, grad_hidden, grad_out, fwd_hidden, fwd_gate, w_moment, w_down,
        groups, capacity,
    )
    received = swap(packed, mixed_order(groups))
    early_grad, early_rows, token = gradient(received[:half], ff, d)
    moment_placed = gathered(swap(moment_pieces, near_order), token)
    weight_placed = gathered(swap(weight_pieces, near_order), token)
    grad, late_rows, _ = gradient(received[half:], ff, d, early_grad)
    moment_new, ortho = orthogonal(me, grad, moment_placed)
    weight_new, produced = produce(me, ortho, (early_rows, late_rows), weight_placed, groups)
    returned = swap(produced, return_order(groups))
    return weight_new[None], moment_new[None], finish(fwd_slot, gates, returned)


def lookup(route_ids, mapping):
    columns = jnp.arange(mapping.shape[0], dtype=jnp.int32)
    hits = route_ids[:, None] == columns[None, :]
    return jnp.sum(jnp.where(hits, mapping[None, :], 0), axis=1)


def slot_matrix(target, is_live, groups, capacity):
    columns = jnp.arange(groups, dtype=jnp.int32)
    onehot = ((target[:, None] == columns[None, :]) & is_live[:, None]).astype(jnp.int32)
    ranked = jnp.sum(jnp.cumsum(onehot, axis=0) * onehot, axis=1) - 1
    slot_of = jnp.where(is_live, target * capacity + ranked, -1)
    slots = jnp.arange(groups * capacity, dtype=jnp.int32)
    return (slots[:, None] == slot_of[None, :]).astype(jnp.bfloat16)


def orthogonalize(moment):
    moment_f = moment.astype(jnp.float32)
    frobenius = jnp.sqrt(jnp.sum(moment_f * moment_f))
    current = (moment_f / (frobenius + norm_floor)).astype(jnp.bfloat16)
    for sweep_index in range(2):
        gramian = lax.dot_general(
            current, current, (((1,), (1,)), ((), ())), preferred_element_type=jnp.float32
        ).astype(jnp.bfloat16)
        squared = jnp.dot(gramian, gramian, preferred_element_type=jnp.float32)
        poly = (cubic_term * gramian.astype(jnp.float32) + quintic_term * squared).astype(
            jnp.bfloat16
        )
        current = (
            linear_term * current.astype(jnp.float32)
            + jnp.dot(poly, current, preferred_element_type=jnp.float32)
        ).astype(jnp.bfloat16)
    return current


def relocate(weight, moment, perm):
    groups = lax.axis_size("expert")
    weight_flat = weight.reshape(groups, -1)
    moment_flat = moment.reshape(groups, -1)
    spread_w, spread_m = (
        lax.all_to_all(weight_flat, "expert", split_axis=0, concat_axis=0, tiled=True),
        lax.all_to_all(moment_flat, "expert", split_axis=0, concat_axis=0, tiled=True),
    )
    devices = jnp.arange(groups, dtype=jnp.int32)
    inverse = jnp.sum(jnp.where(perm[None, :] == devices[:, None], devices[None, :], 0), axis=1)
    ordered_w = jnp.take(spread_w, inverse, axis=0)
    ordered_m = jnp.take(spread_m, inverse, axis=0)
    back_w, back_m = (
        lax.all_to_all(ordered_w, "expert", split_axis=0, concat_axis=0, tiled=True),
        lax.all_to_all(ordered_m, "expert", split_axis=0, concat_axis=0, tiled=True),
    )
    return (back_w.reshape(weight.shape), back_m.reshape(moment.shape))


def routed_plan(
    grad_hidden,
    grad_out,
    grad_route,
    live_rows,
    w_down,
    w_moment,
    perm,
    fwd_hidden,
    fwd_route,
    fwd_gate,
):
    groups = lax.axis_size("expert")
    grad_count = grad_hidden.shape[0]
    capacity = max(4, 2 * grad_count // groups)
    is_live = jnp.arange(grad_count, dtype=jnp.int32) < live_rows[0]
    route_ids = grad_route[:, 0]
    weight, moment = relocate(w_down, w_moment, perm)
    target = lookup(route_ids, perm)
    selector = slot_matrix(target, is_live, groups, capacity)
    hidden_buf = (
        jnp.dot(selector, grad_hidden, preferred_element_type=jnp.float32)
        .astype(jnp.bfloat16)
        .reshape(groups, capacity, -1)
    )
    outgrad_buf = (
        jnp.dot(selector, grad_out, preferred_element_type=jnp.float32)
        .astype(jnp.bfloat16)
        .reshape(groups, capacity, -1)
    )
    recv_hidden, recv_outgrad = (
        lax.all_to_all(hidden_buf, "expert", split_axis=0, concat_axis=0, tiled=True),
        lax.all_to_all(outgrad_buf, "expert", split_axis=0, concat_axis=0, tiled=True),
    )
    grad = lax.dot_general(
        recv_hidden.reshape(groups * capacity, -1),
        recv_outgrad.reshape(groups * capacity, -1),
        (((0,), (0,)), ((), ())),
        preferred_element_type=jnp.float32,
    )
    moment_new = (moment_decay * moment[0].astype(jnp.float32) + grad).astype(jnp.bfloat16)
    ortho = orthogonalize(moment_new)
    weight_new = (weight[0].astype(jnp.float32) - step_scale * ortho.astype(jnp.float32)).astype(
        jnp.bfloat16
    )
    weight_new = weight_new[None]
    moment_new = moment_new[None]
    fwd_ids = fwd_route[:, 0]
    placed_weight, placed_moment = (weight_new, moment_new)
    fwd_target = lookup(fwd_ids, perm)
    fwd_weight = weight_new[0]
    fwd_count = fwd_hidden.shape[0]
    fwd_capacity = max(4, 2 * fwd_count // groups)
    fwd_selector = slot_matrix(fwd_target, jnp.ones((fwd_count,), dtype=bool), groups, fwd_capacity)
    fwd_buf = (
        jnp.dot(fwd_selector, fwd_hidden, preferred_element_type=jnp.float32)
        .astype(jnp.bfloat16)
        .reshape(groups, fwd_capacity, -1)
    )
    produced = jnp.einsum(
        "gkf,fd->gkd",
        lax.all_to_all(fwd_buf, "expert", split_axis=0, concat_axis=0, tiled=True),
        fwd_weight,
        preferred_element_type=jnp.float32,
    ).astype(jnp.bfloat16)
    returned = lax.all_to_all(produced, "expert", split_axis=0, concat_axis=0, tiled=True)
    fwd_rows_out = lax.dot_general(
        fwd_selector,
        returned.reshape(groups * fwd_capacity, -1),
        (((0,), (0,)), ((), ())),
        preferred_element_type=jnp.float32,
    )
    fwd_out = (fwd_rows_out * fwd_gate[:, None]).astype(jnp.bfloat16)
    return (placed_weight, placed_moment, fwd_out)


def solution(mesh):
    groups = mesh.shape["expert"]
    in_specs = (
        P(("layer", "expert"), None),
        P(("layer", "expert"), None),
        P(("layer", "expert"), None),
        P(("layer", "expert")),
        P(("layer", "expert"), None, None),
        P(("layer", "expert"), None, None),
        P("layer"),
        P(("layer", "expert"), None),
        P(("layer", "expert"), None),
        P(("layer", "expert")),
    )
    out_specs = (
        P(("layer", "expert"), None, None),
        P(("layer", "expert"), None, None),
        P(("layer", "expert"), None),
    )

    def per_device(*args):
        few = groups >= 8 and groups & (groups - 1) == 0 and groups <= 2 * args[0].shape[0] // groups
        return (halves_plan if few else routed_plan)(*args)

    return jax.shard_map(
        per_device, mesh=mesh, in_specs=in_specs, out_specs=out_specs, check_vma=False
    )
```

```python
import functools

import jax
import jax.numpy as jnp
from jax import lax
from jax.experimental import pallas as pl
from jax.experimental.pallas import tpu as pltpu
from jax.sharding import PartitionSpec as P

linear_term = 3.4445
cubic_term = -4.775
quintic_term = 2.0315
moment_decay = 0.9
step_scale = 0.25
norm_floor = 1e-07

F32 = jnp.float32
BF16 = jnp.bfloat16
HBM = pl.BlockSpec(memory_space=pltpu.HBM)
VMEM = pl.BlockSpec(memory_space=pltpu.VMEM)
SMEM = pl.BlockSpec(memory_space=pltpu.SMEM)
ANY = pl.BlockSpec(memory_space=pl.ANY)
MIB = 1 << 20


def fetched(refs, held, sem):
    copies = [pltpu.make_async_copy(ref, room, sem.at[n]) for n, (ref, room) in enumerate(zip(refs, held))]
    for copy in copies:
        copy.start()
    for copy in copies:
        copy.wait()


def rooms(arrays):
    return [pltpu.VMEM(a.shape, a.dtype) for a in arrays] + [pltpu.SemaphoreType.DMA((len(arrays),))]


def chunk_at(ref, lead, k, rows, columns):
    return ref.at[
        lead,
        pl.ds(pl.multiple_of((k // 2) * rows, rows), rows),
        pl.ds(pl.multiple_of((k % 2) * columns, columns), columns),
    ]


def slot_rows(route, live, groups, capacity, me_ref, perm_ref):
    rows = route.shape[1]
    experts = lax.broadcasted_iota(jnp.int32, (groups, rows), 0)
    onehot = jnp.where((experts == route) & live, 1.0, 0.0).astype(BF16)
    before = lax.broadcasted_iota(jnp.int32, (rows, rows), 0)
    after = lax.broadcasted_iota(jnp.int32, (rows, rows), 1)
    upto = jnp.where(before <= after, 1.0, 0.0).astype(BF16)
    ranks = jnp.dot(onehot, upto, preferred_element_type=F32)
    rank = jnp.sum(ranks * onehot.astype(F32), axis=0, keepdims=True).astype(jnp.int32) - 1
    partner = jnp.zeros_like(route)
    for e in range(groups):
        partner = jnp.where(route == e, perm_ref[e] ^ me_ref[0], partner)
    return jnp.where(live, partner * capacity + rank, -1)


def selector_of(slot, slots):
    rows = slot.shape[1]
    places = lax.broadcasted_iota(jnp.int32, (slots, rows), 0)
    return jnp.where(places == slot, 1.0, 0.0).astype(BF16)


def pack_kernel(groups, live_ref, me_ref, perm_ref, *refs):
    sources, pieces, (slot_ref, gates_ref) = refs[:6], refs[7 : 7 + groups], refs[7 + groups : 9 + groups]
    held, sem = refs[9 + groups : 15 + groups], refs[-1]
    route_ref, fwd_route_ref, hidden_ref, out_ref, fwd_ref, gate_ref = held
    copies = [pltpu.make_async_copy(ref, room, sem.at[n]) for n, (ref, room) in enumerate(zip(sources, held))]
    for copy in copies:
        copy.start()
    rows, ff = hidden_ref.shape
    d = out_ref.shape[1]
    capacity = pieces[0].shape[0]
    slots = groups * capacity
    place = lax.broadcasted_iota(jnp.int32, (1, rows), 1)

    def fill(first, selector, source_ref):
        chosen = jnp.dot(selector, source_ref[...], preferred_element_type=F32).astype(BF16)
        for s, piece in zip(mixed_order(groups), pieces):
            piece[:, first : first + source_ref.shape[1]] = chosen[s * capacity : (s + 1) * capacity]

    copies[0].wait()
    slot = slot_rows(route_ref[...], place < live_ref[0], groups, capacity, me_ref, perm_ref)
    selector = selector_of(slot, slots)
    copies[1].wait()
    fwd_slot = slot_rows(fwd_route_ref[...], place >= 0, groups, capacity, me_ref, perm_ref)
    slot_ref[...] = fwd_slot
    copies[2].wait()
    fill(0, selector, hidden_ref)
    copies[3].wait()
    fill(ff, selector, out_ref)
    copies[4].wait()
    fill(ff + d, selector_of(fwd_slot, slots), fwd_ref)
    copies[5].wait()
    down = lax.broadcasted_iota(jnp.int32, (rows, rows), 0)
    across = lax.broadcasted_iota(jnp.int32, (rows, rows), 1)
    gates_ref[...] = jnp.sum(jnp.where(down == across, gate_ref[...], 0.0), axis=1, keepdims=True)


def pack_rows(live_rows, me, perm, route, fwd_route, hidden, grad_out, fwd_hidden, gate, earlier, groups, capacity):
    rows, ff = hidden.shape
    width = 2 * ff + grad_out.shape[1]
    sources = (route.reshape(1, rows), fwd_route.reshape(1, rows), hidden, grad_out, fwd_hidden, gate.reshape(1, rows))
    *pieces, slot, gates = pl.pallas_call(
        functools.partial(pack_kernel, groups),
        out_shape=(jax.ShapeDtypeStruct((capacity, width), BF16),) * groups
        + (jax.ShapeDtypeStruct((1, rows), jnp.int32), jax.ShapeDtypeStruct((rows, 1), F32)),
        in_specs=[SMEM] * 3 + [HBM] * 6 + [VMEM],
        out_specs=(VMEM,) * (groups + 2),
        scratch_shapes=[pltpu.VMEM(a.shape, a.dtype) for a in sources] + [pltpu.SemaphoreType.DMA((len(sources),))],
        compiler_params=pltpu.CompilerParams(vmem_limit_bytes=32 * MIB),
        cost_estimate=pl.CostEstimate(
            flops=2 * groups * capacity * rows * width, bytes_accessed=6 * rows * width, transcendentals=0
        ),
        name="pack_rows",
    )(live_rows, me, perm, *sources, earlier)
    return pieces, slot, gates


def split_kernel(me_ref, moment_ref, weight_ref, *refs):
    pieces, held, sem = refs[:-3], refs[-3:-1], refs[-1]
    fetched((moment_ref, weight_ref), held, sem)
    for s, piece in zip(mixed_order(len(pieces)), pieces):
        rows, columns = piece.shape[1:]
        for lead, source in enumerate(held):
            piece[lead] = chunk_at(source, 0, me_ref[0] ^ s, rows, columns)[...]


def split(me, moment, weight, groups):
    _, ff, d = weight.shape
    piece = jax.ShapeDtypeStruct((2, ff // (groups // 2), d // 2), BF16)
    return pl.pallas_call(
        split_kernel,
        out_shape=(piece,) * groups,
        in_specs=[SMEM, HBM, HBM],
        out_specs=(VMEM,) * groups,
        scratch_shapes=rooms((moment, weight)),
        compiler_params=pltpu.CompilerParams(vmem_limit_bytes=60 * MIB),
        cost_estimate=pl.CostEstimate(flops=0, bytes_accessed=8 * ff * d, transcendentals=0),
        name="split",
    )(me, moment, weight)


def reorder_kernel(me_ref, perm_ref, *refs):
    groups = len(refs) // 2 - 1
    sources, targets, held = refs[:groups], refs[groups + 1 : 2 * groups + 1], refs[-1]
    me, order = me_ref[0], mixed_order(groups)
    for s, source in zip(order, sources):
        held[me ^ perm_ref[me ^ s]] = source[...]
    for s, target in zip(return_order(groups), targets):
        target[...] = held[s]


def reorder(me, perm, pieces, earlier):
    groups = len(pieces)
    piece = jax.ShapeDtypeStruct(pieces[0].shape, BF16)
    return pl.pallas_call(
        reorder_kernel,
        out_shape=(piece,) * groups,
        in_specs=[SMEM, SMEM] + [VMEM] * (groups + 1),
        out_specs=(VMEM,) * groups,
        scratch_shapes=[pltpu.VMEM((groups,) + pieces[0].shape, BF16)],
        compiler_params=pltpu.CompilerParams(vmem_limit_bytes=32 * MIB),
        cost_estimate=pl.CostEstimate(flops=0, bytes_accessed=4 * groups * pieces[0].size, transcendentals=0),
        name="reorder",
    )(me, perm, *pieces, earlier)


def gradient_kernel(groups, *refs):
    pieces, (grad_ref, fwd_ref, rows_ref) = refs[:groups], refs[groups:]
    ff, d = grad_ref.shape
    capacity = pieces[0].shape[0]
    for n, piece in enumerate(pieces):
        span = slice(n * capacity, (n + 1) * capacity)
        rows_ref[span] = piece[:, : ff + d]
        fwd_ref[span] = piece[:, ff + d :]
    grad_ref[...] = lax.dot_general(
        rows_ref[:, :ff], rows_ref[:, ff:], (((0,), (0,)), ((), ())), preferred_element_type=F32
    )


def gradient(pieces, ff, d):
    groups = len(pieces)
    slots = groups * pieces[0].shape[0]
    return pl.pallas_call(
        functools.partial(gradient_kernel, groups),
        out_shape=(jax.ShapeDtypeStruct((ff, d), F32), jax.ShapeDtypeStruct((slots, ff), BF16)),
        in_specs=[VMEM] * groups,
        out_specs=(VMEM, VMEM),
        scratch_shapes=[pltpu.VMEM((slots, ff + d), BF16)],
        compiler_params=pltpu.CompilerParams(vmem_limit_bytes=32 * MIB),
        cost_estimate=pl.CostEstimate(
            flops=2 * ff * d * slots, bytes_accessed=4 * ff * d + 4 * slots * (ff + d), transcendentals=0
        ),
        name="gradient",
    )(*pieces)


def update_kernel(groups, me_ref, grad_ref, fwd_ref, *refs):
    pieces, (weight_new_ref, moment_new_ref, *produced), held = refs[:groups], refs[groups:-1], refs[-1]
    for s, piece in zip(return_order(groups), pieces):
        rows, columns = piece.shape[1:]
        for lead in range(2):
            chunk_at(held, lead, me_ref[0] ^ s, rows, columns)[...] = piece[lead]
    moment_new = (moment_decay * held[0].astype(F32) + grad_ref[...]).astype(BF16)
    moment_new_ref[...] = moment_new
    moment_f = moment_new.astype(F32)
    frobenius = jnp.sqrt(jnp.sum(moment_f * moment_f))
    current = (moment_f / (frobenius + norm_floor)).astype(BF16)
    for _ in range(2):
        gramian = lax.dot_general(
            current, current, (((1,), (1,)), ((), ())), preferred_element_type=F32
        ).astype(BF16)
        squared = jnp.dot(gramian, gramian, preferred_element_type=F32)
        poly = (cubic_term * gramian.astype(F32) + quintic_term * squared).astype(BF16)
        current = (
            linear_term * current.astype(F32) + jnp.dot(poly, current, preferred_element_type=F32)
        ).astype(BF16)
    weight_new = (held[1].astype(F32) - step_scale * current.astype(F32)).astype(BF16)
    weight_new_ref[...] = weight_new
    product = jnp.dot(fwd_ref[...], weight_new, preferred_element_type=F32).astype(BF16)
    capacity, came = produced[0].shape[0], mixed_order(groups)
    for s, piece in zip(return_order(groups), produced):
        n = came.index(s)
        piece[...] = product[n * capacity : (n + 1) * capacity]


def update(me, grad, fwd_rows, pieces):
    groups = len(pieces)
    ff, d = grad.shape
    slots = fwd_rows.shape[0]
    shape = jax.ShapeDtypeStruct((ff, d), BF16)
    weight_new, moment_new, *produced = pl.pallas_call(
        functools.partial(update_kernel, groups),
        out_shape=(shape, shape) + (jax.ShapeDtypeStruct((slots // groups, d), BF16),) * groups,
        in_specs=[SMEM] + [VMEM] * (2 + groups),
        out_specs=(VMEM,) * (groups + 2),
        scratch_shapes=[pltpu.VMEM((2, ff, d), BF16)],
        compiler_params=pltpu.CompilerParams(vmem_limit_bytes=40 * MIB),
        cost_estimate=pl.CostEstimate(
            flops=2 * ff * d * slots + 8 * ff * ff * d + 4 * ff**3,
            bytes_accessed=12 * ff * d + 2 * slots * (ff + d),
            transcendentals=1,
        ),
        name="update",
    )(me, grad, fwd_rows, *pieces)
    return weight_new, moment_new, produced


def finish_kernel(groups, slot_ref, gates_ref, *refs):
    pieces, (out_ref, returned_ref) = refs[:groups], refs[groups:]
    capacity = pieces[0].shape[0]
    for s, piece in zip(return_order(groups), pieces):
        returned_ref[s * capacity : (s + 1) * capacity] = piece[...]
    selector = selector_of(slot_ref[...], groups * capacity)
    expert_out = lax.dot_general(
        selector, returned_ref[...], (((0,), (0,)), ((), ())), preferred_element_type=F32
    )
    out_ref[...] = (gates_ref[...] * expert_out).astype(BF16)


def finish(slot, gates, returned):
    groups = len(returned)
    rows = slot.shape[1]
    capacity, d = returned[0].shape
    slots = groups * capacity
    return pl.pallas_call(
        functools.partial(finish_kernel, groups),
        out_shape=jax.ShapeDtypeStruct((rows, d), BF16),
        in_specs=[VMEM] * (2 + groups),
        out_specs=VMEM,
        scratch_shapes=[pltpu.VMEM((slots, d), BF16)],
        compiler_params=pltpu.CompilerParams(vmem_limit_bytes=32 * MIB),
        cost_estimate=pl.CostEstimate(
            flops=2 * slots * rows * d, bytes_accessed=2 * d * (slots + rows), transcendentals=0
        ),
        name="finish",
    )(slot, gates, *returned)


def mixed_order(groups):
    far, near = list(range(groups // 2, groups)), list(range(groups // 2 - 1, 0, -1))
    return [0] + [s for pair in zip(far, near + [None]) for s in pair if s is not None]


def return_order(groups):
    far, near = list(range(groups // 2, groups)), list(range(groups // 2 - 1, 0, -1))
    order = [0]
    while far or near:
        order += far[:2] + near[:1]
        far, near = far[2:], near[1:]
    return order


def swap(pieces, order):
    groups = lax.axis_size("expert")
    return [
        lax.ppermute(piece, "expert", [(i, i ^ s) for i in range(groups)]) if s else piece
        for s, piece in zip(order, pieces)
    ]


def partner_plan(
    grad_hidden, grad_out, grad_route, live_rows, w_down, w_moment, perm, fwd_hidden, fwd_route, fwd_gate
):
    groups = lax.axis_size("expert")
    me = lax.axis_index("expert").astype(jnp.int32).reshape(1)
    capacity = max(4, 2 * grad_hidden.shape[0] // groups)
    ff, d = w_down.shape[1:]
    spread = swap(split(me, w_moment, w_down, groups), mixed_order(groups))
    packed, fwd_slot, gates = pack_rows(
        live_rows, me, perm, grad_route, fwd_route, grad_hidden, grad_out, fwd_hidden, fwd_gate,
        spread[2 * groups // 3], groups, capacity,
    )
    received = swap(packed, mixed_order(groups))
    placed = swap(reorder(me, perm, spread, received[groups // 3]), return_order(groups))
    grad, fwd_rows = gradient(received, ff, d)
    weight_new, moment_new, produced = update(me, grad, fwd_rows, placed)
    returned = swap(produced, return_order(groups))
    return weight_new[None], moment_new[None], finish(fwd_slot, gates, returned)


def lookup(route_ids, mapping):
    columns = jnp.arange(mapping.shape[0], dtype=jnp.int32)
    hits = route_ids[:, None] == columns[None, :]
    return jnp.sum(jnp.where(hits, mapping[None, :], 0), axis=1)


def slot_matrix(target, is_live, groups, capacity):
    columns = jnp.arange(groups, dtype=jnp.int32)
    onehot = ((target[:, None] == columns[None, :]) & is_live[:, None]).astype(jnp.int32)
    ranked = jnp.sum(jnp.cumsum(onehot, axis=0) * onehot, axis=1) - 1
    slot_of = jnp.where(is_live, target * capacity + ranked, -1)
    slots = jnp.arange(groups * capacity, dtype=jnp.int32)
    return (slots[:, None] == slot_of[None, :]).astype(jnp.bfloat16)


def orthogonalize(moment):
    moment_f = moment.astype(jnp.float32)
    frobenius = jnp.sqrt(jnp.sum(moment_f * moment_f))
    current = (moment_f / (frobenius + norm_floor)).astype(jnp.bfloat16)
    for sweep_index in range(2):
        gramian = lax.dot_general(
            current, current, (((1,), (1,)), ((), ())), preferred_element_type=jnp.float32
        ).astype(jnp.bfloat16)
        squared = jnp.dot(gramian, gramian, preferred_element_type=jnp.float32)
        poly = (cubic_term * gramian.astype(jnp.float32) + quintic_term * squared).astype(
            jnp.bfloat16
        )
        current = (
            linear_term * current.astype(jnp.float32)
            + jnp.dot(poly, current, preferred_element_type=jnp.float32)
        ).astype(jnp.bfloat16)
    return current


def relocate(weight, moment, perm):
    groups = lax.axis_size("expert")
    weight_flat = weight.reshape(groups, -1)
    moment_flat = moment.reshape(groups, -1)
    spread_w, spread_m = (
        lax.all_to_all(weight_flat, "expert", split_axis=0, concat_axis=0, tiled=True),
        lax.all_to_all(moment_flat, "expert", split_axis=0, concat_axis=0, tiled=True),
    )
    devices = jnp.arange(groups, dtype=jnp.int32)
    inverse = jnp.sum(jnp.where(perm[None, :] == devices[:, None], devices[None, :], 0), axis=1)
    ordered_w = jnp.take(spread_w, inverse, axis=0)
    ordered_m = jnp.take(spread_m, inverse, axis=0)
    back_w, back_m = (
        lax.all_to_all(ordered_w, "expert", split_axis=0, concat_axis=0, tiled=True),
        lax.all_to_all(ordered_m, "expert", split_axis=0, concat_axis=0, tiled=True),
    )
    return (back_w.reshape(weight.shape), back_m.reshape(moment.shape))


def routed_plan(
    grad_hidden,
    grad_out,
    grad_route,
    live_rows,
    w_down,
    w_moment,
    perm,
    fwd_hidden,
    fwd_route,
    fwd_gate,
):
    groups = lax.axis_size("expert")
    grad_count = grad_hidden.shape[0]
    capacity = max(4, 2 * grad_count // groups)
    is_live = jnp.arange(grad_count, dtype=jnp.int32) < live_rows[0]
    route_ids = grad_route[:, 0]
    weight, moment = relocate(w_down, w_moment, perm)
    target = lookup(route_ids, perm)
    selector = slot_matrix(target, is_live, groups, capacity)
    hidden_buf = (
        jnp.dot(selector, grad_hidden, preferred_element_type=jnp.float32)
        .astype(jnp.bfloat16)
        .reshape(groups, capacity, -1)
    )
    outgrad_buf = (
        jnp.dot(selector, grad_out, preferred_element_type=jnp.float32)
        .astype(jnp.bfloat16)
        .reshape(groups, capacity, -1)
    )
    recv_hidden, recv_outgrad = (
        lax.all_to_all(hidden_buf, "expert", split_axis=0, concat_axis=0, tiled=True),
        lax.all_to_all(outgrad_buf, "expert", split_axis=0, concat_axis=0, tiled=True),
    )
    grad = lax.dot_general(
        recv_hidden.reshape(groups * capacity, -1),
        recv_outgrad.reshape(groups * capacity, -1),
        (((0,), (0,)), ((), ())),
        preferred_element_type=jnp.float32,
    )
    moment_new = (moment_decay * moment[0].astype(jnp.float32) + grad).astype(jnp.bfloat16)
    ortho = orthogonalize(moment_new)
    weight_new = (weight[0].astype(jnp.float32) - step_scale * ortho.astype(jnp.float32)).astype(
        jnp.bfloat16
    )
    weight_new = weight_new[None]
    moment_new = moment_new[None]
    fwd_ids = fwd_route[:, 0]
    placed_weight, placed_moment = (weight_new, moment_new)
    fwd_target = lookup(fwd_ids, perm)
    fwd_weight = weight_new[0]
    fwd_count = fwd_hidden.shape[0]
    fwd_capacity = max(4, 2 * fwd_count // groups)
    fwd_selector = slot_matrix(fwd_target, jnp.ones((fwd_count,), dtype=bool), groups, fwd_capacity)
    fwd_buf = (
        jnp.dot(fwd_selector, fwd_hidden, preferred_element_type=jnp.float32)
        .astype(jnp.bfloat16)
        .reshape(groups, fwd_capacity, -1)
    )
    produced = jnp.einsum(
        "gkf,fd->gkd",
        lax.all_to_all(fwd_buf, "expert", split_axis=0, concat_axis=0, tiled=True),
        fwd_weight,
        preferred_element_type=jnp.float32,
    ).astype(jnp.bfloat16)
    returned = lax.all_to_all(produced, "expert", split_axis=0, concat_axis=0, tiled=True)
    fwd_rows_out = lax.dot_general(
        fwd_selector,
        returned.reshape(groups * fwd_capacity, -1),
        (((0,), (0,)), ((), ())),
        preferred_element_type=jnp.float32,
    )
    fwd_out = (fwd_rows_out * fwd_gate[:, None]).astype(jnp.bfloat16)
    return (placed_weight, placed_moment, fwd_out)


def solution(mesh):
    groups = mesh.shape["expert"]
    in_specs = (
        P(("layer", "expert"), None),
        P(("layer", "expert"), None),
        P(("layer", "expert"), None),
        P(("layer", "expert")),
        P(("layer", "expert"), None, None),
        P(("layer", "expert"), None, None),
        P("layer"),
        P(("layer", "expert"), None),
        P(("layer", "expert"), None),
        P(("layer", "expert")),
    )
    out_specs = (
        P(("layer", "expert"), None, None),
        P(("layer", "expert"), None, None),
        P(("layer", "expert"), None),
    )

    def per_device(*args):
        few = groups & (groups - 1) == 0 and groups <= 2 * args[0].shape[0] // groups
        return (partner_plan if few else routed_plan)(*args)

    return jax.shard_map(
        per_device, mesh=mesh, in_specs=in_specs, out_specs=out_specs, check_vma=False
    )
```

```python
import functools

import jax
import jax.numpy as jnp
from jax import lax
from jax.experimental import pallas as pl
from jax.experimental.pallas import tpu as pltpu
from jax.sharding import PartitionSpec as P

linear_term = 3.4445
cubic_term = -4.775
quintic_term = 2.0315
moment_decay = 0.9
step_scale = 0.25
norm_floor = 1e-07

F32 = jnp.float32
BF16 = jnp.bfloat16
HBM = pl.BlockSpec(memory_space=pltpu.HBM)
VMEM = pl.BlockSpec(memory_space=pltpu.VMEM)
SMEM = pl.BlockSpec(memory_space=pltpu.SMEM)
ANY = pl.BlockSpec(memory_space=pl.ANY)
MIB = 1 << 20


def row_block(k, rows):
    return pl.ds(pl.multiple_of(k * rows, rows), rows)


def crossing_ranks(half, base, perm_ref):
    flags = [(perm_ref[base + q] // half != base // half).astype(jnp.int32) for q in range(half)]
    ranks, count = [], 0
    for flag in flags:
        ranks.append(count)
        count = count + flag
    return flags, ranks


def slots_of(half):
    return half // 2, 1, half - half // 2 - 1


def slot_rows(route, live, groups, capacity, me_ref, perm_ref):
    rows = route.shape[1]
    experts = lax.broadcasted_iota(jnp.int32, (groups, rows), 0)
    onehot = jnp.where((experts == route) & live, 1.0, 0.0).astype(BF16)
    before = lax.broadcasted_iota(jnp.int32, (rows, rows), 0)
    after = lax.broadcasted_iota(jnp.int32, (rows, rows), 1)
    upto = jnp.where(before <= after, 1.0, 0.0).astype(BF16)
    ranks = jnp.dot(onehot, upto, preferred_element_type=F32)
    rank = jnp.sum(ranks * onehot.astype(F32), axis=0, keepdims=True).astype(jnp.int32) - 1
    partner = jnp.zeros_like(route)
    for e in range(groups):
        partner = jnp.where(route == e, perm_ref[e] ^ me_ref[0], partner)
    return jnp.where(live, partner * capacity + rank, -1)


def selector_of(slot, slots):
    rows = slot.shape[1]
    places = lax.broadcasted_iota(jnp.int32, (slots, rows), 0)
    return jnp.where(places == slot, 1.0, 0.0).astype(BF16)


def pack_kernel(groups, live_ref, me_ref, perm_ref, *refs):
    early = 1 + len(dispatch_sets(groups)[0])
    sources, pieces, (later_ref, slot_ref, gates_ref) = refs[:6], refs[7 : 7 + early], refs[7 + early : 10 + early]
    held, sem = refs[10 + early : 16 + early], refs[-1]
    route_ref, fwd_route_ref, hidden_ref, out_ref, fwd_ref, gate_ref = held
    copies = [pltpu.make_async_copy(ref, room, sem.at[n]) for n, (ref, room) in enumerate(zip(sources, held))]
    for copy in copies:
        copy.start()
    rows, ff = hidden_ref.shape
    d = out_ref.shape[1]
    capacity = pieces[0].shape[0]
    slots = groups * capacity
    place = lax.broadcasted_iota(jnp.int32, (1, rows), 1)
    order = dispatch_order(groups)

    def fill(first, selector, source_ref):
        chosen = jnp.dot(selector, source_ref[...], preferred_element_type=F32).astype(BF16)
        columns = slice(first, first + source_ref.shape[1])
        for n, s in enumerate(order):
            block = chosen[s * capacity : (s + 1) * capacity]
            if n < early:
                pieces[n][:, columns] = block
            else:
                later_ref[n - early, :, columns] = block

    copies[0].wait()
    slot = slot_rows(route_ref[...], place < live_ref[0], groups, capacity, me_ref, perm_ref)
    selector = selector_of(slot, slots)
    copies[1].wait()
    fwd_slot = slot_rows(fwd_route_ref[...], place >= 0, groups, capacity, me_ref, perm_ref)
    slot_ref[...] = fwd_slot
    copies[2].wait()
    fill(0, selector, hidden_ref)
    copies[3].wait()
    fill(ff, selector, out_ref)
    copies[4].wait()
    fill(ff + d, selector_of(fwd_slot, slots), fwd_ref)
    copies[5].wait()
    down = lax.broadcasted_iota(jnp.int32, (rows, rows), 0)
    across = lax.broadcasted_iota(jnp.int32, (rows, rows), 1)
    gates_ref[...] = jnp.sum(jnp.where(down == across, gate_ref[...], 0.0), axis=1, keepdims=True)


def pack_rows(live_rows, me, perm, route, fwd_route, hidden, grad_out, fwd_hidden, gate, earlier, groups, capacity):
    rows, ff = hidden.shape
    width = 2 * ff + grad_out.shape[1]
    sources = (
        route.reshape(1, rows), fwd_route.reshape(1, rows), hidden, grad_out, fwd_hidden, gate.reshape(1, rows),
    )
    early = 1 + len(dispatch_sets(groups)[0])
    *pieces, later, slot, gates = pl.pallas_call(
        functools.partial(pack_kernel, groups),
        out_shape=(jax.ShapeDtypeStruct((capacity, width), BF16),) * early
        + (
            jax.ShapeDtypeStruct((groups - early, capacity, width), BF16),
            jax.ShapeDtypeStruct((1, rows), jnp.int32),
            jax.ShapeDtypeStruct((rows, 1), F32),
        ),
        in_specs=[SMEM] * 3 + [HBM] * 6 + [VMEM],
        out_specs=(VMEM,) * (early + 3),
        scratch_shapes=[pltpu.VMEM(a.shape, a.dtype) for a in sources] + [pltpu.SemaphoreType.DMA((len(sources),))],
        compiler_params=pltpu.CompilerParams(vmem_limit_bytes=32 * MIB),
        cost_estimate=pl.CostEstimate(
            flops=2 * groups * capacity * rows * width, bytes_accessed=6 * rows * width, transcendentals=0
        ),
        name="pack_rows",
    )(live_rows, me, perm, *sources, earlier)
    return pieces, later, slot, gates


def take_kernel(first, count, rows_ref, *refs):
    for n, piece in enumerate(refs[-count:]):
        piece[...] = rows_ref[first + n]


def take(rows, first, count, *earlier):
    piece = jax.ShapeDtypeStruct(rows.shape[1:], BF16)
    return pl.pallas_call(
        functools.partial(take_kernel, first, count),
        out_shape=(piece,) * count,
        in_specs=[VMEM] * (1 + len(earlier)),
        out_specs=(VMEM,) * count,
        compiler_params=pltpu.CompilerParams(vmem_limit_bytes=32 * MIB),
        cost_estimate=pl.CostEstimate(
            flops=0, bytes_accessed=4 * count * rows.shape[1] * rows.shape[2], transcendentals=0
        ),
        name="take",
    )(rows, *earlier)


def split_kernel(me_ref, moment_ref, weight_ref, *refs):
    pieces, sem = refs[:-1], refs[-1]
    half, rows = len(pieces), pieces[0].shape[1]
    copies = [
        pltpu.make_async_copy(
            source.at[0, row_block((me_ref[0] ^ s) % half, rows)], piece.at[lead], sem.at[lead * half + s]
        )
        for s, piece in zip(mixed_order(half), pieces)
        for lead, source in enumerate((moment_ref, weight_ref))
    ]
    for copy in copies:
        copy.start()
    for copy in copies:
        copy.wait()


def split(me, moment, weight, half):
    _, ff, d = weight.shape
    piece = jax.ShapeDtypeStruct((2, ff // half, d), BF16)
    return pl.pallas_call(
        split_kernel,
        out_shape=(piece,) * half,
        in_specs=[SMEM, HBM, HBM],
        out_specs=(VMEM,) * half,
        scratch_shapes=[pltpu.SemaphoreType.DMA((2 * half,))],
        compiler_params=pltpu.CompilerParams(vmem_limit_bytes=60 * MIB),
        cost_estimate=pl.CostEstimate(flops=0, bytes_accessed=8 * ff * d, transcendentals=0),
        name="split",
    )(me, moment, weight)


def sort_kernel(half, me_ref, perm_ref, *refs):
    pieces, (near_ref, *slot_refs, token_ref) = refs[:half], refs[-5:]
    me = me_ref[0]
    token_ref[...] = jnp.zeros_like(token_ref)
    base = me // half * half
    flags, ranks = crossing_ranks(half, base, perm_ref)
    for s, piece in zip(mixed_order(half), pieces):
        place = (me ^ s) % half
        crosses, rank = 0, 0
        for q in range(half):
            crosses = jnp.where(place == q, flags[q], crosses)
            rank = jnp.where(place == q, ranks[q], rank)
        near = (perm_ref[base + place] ^ me) % half

        @pl.when(crosses == 0)
        def _():
            near_ref[near] = piece[...]

        first = 0
        for slots in slot_refs:
            count = slots.shape[0]

            @pl.when((crosses == 1) & (rank >= first) & (rank < first + count))
            def _():
                slots[rank - first] = piece[...]

            first += count


def sort_pieces(me, perm, pieces, *earlier):
    half = len(pieces)
    shape = pieces[0].shape
    counts = (half,) + slots_of(half)
    return pl.pallas_call(
        functools.partial(sort_kernel, half),
        out_shape=tuple(jax.ShapeDtypeStruct((count,) + shape, BF16) for count in counts)
        + (jax.ShapeDtypeStruct((8, 128), F32),),
        in_specs=[SMEM, SMEM] + [VMEM] * (half + len(earlier)),
        out_specs=(VMEM,) * (len(counts) + 1),
        compiler_params=pltpu.CompilerParams(vmem_limit_bytes=32 * MIB),
        cost_estimate=pl.CostEstimate(flops=0, bytes_accessed=4 * half * pieces[0].size, transcendentals=0),
        name="sort_pieces",
    )(me, perm, *pieces, *earlier)


def join_kernel(half, me_ref, perm_ref, near_ref, *refs):
    slot_refs, targets = refs[:3], refs[3:]
    me = me_ref[0]
    base = me // half * half
    flags, ranks = crossing_ranks(half, half - base, perm_ref)
    for s, target in zip(mixed_order(half), targets):
        crosses, rank = 0, 0
        for q in range(half):
            here = perm_ref[half - base + q] == me ^ s
            crosses = jnp.where(here, 1, crosses)
            rank = jnp.where(here, ranks[q], rank)

        @pl.when(crosses == 0)
        def _():
            target[...] = near_ref[s]

        first = 0
        for slots in slot_refs:
            count = slots.shape[0]

            @pl.when((crosses == 1) & (rank >= first) & (rank < first + count))
            def _():
                target[...] = slots[rank - first]

            first += count


def join_pieces(me, perm, near, slots):
    half = near.shape[0]
    piece = jax.ShapeDtypeStruct(near.shape[1:], BF16)
    return pl.pallas_call(
        functools.partial(join_kernel, half),
        out_shape=(piece,) * half,
        in_specs=[SMEM, SMEM] + [VMEM] * 4,
        out_specs=(VMEM,) * half,
        compiler_params=pltpu.CompilerParams(vmem_limit_bytes=32 * MIB),
        cost_estimate=pl.CostEstimate(flops=0, bytes_accessed=4 * near.size, transcendentals=0),
        name="join_pieces",
    )(me, perm, near, *slots)


def gradient_kernel(groups, *refs):
    pieces, (grad_ref, fwd_ref, rows_ref) = refs[:groups], refs[groups:]
    ff, d = grad_ref.shape
    capacity = pieces[0].shape[0]
    for n, piece in enumerate(pieces):
        span = slice(n * capacity, (n + 1) * capacity)
        rows_ref[span] = piece[:, : ff + d]
        fwd_ref[span] = piece[:, ff + d :]
    grad_ref[...] = lax.dot_general(
        rows_ref[:, :ff], rows_ref[:, ff:], (((0,), (0,)), ((), ())), preferred_element_type=F32
    )


def gradient(pieces, ff, d):
    groups = len(pieces)
    slots = groups * pieces[0].shape[0]
    return pl.pallas_call(
        functools.partial(gradient_kernel, groups),
        out_shape=(jax.ShapeDtypeStruct((ff, d), F32), jax.ShapeDtypeStruct((slots, ff), BF16)),
        in_specs=[VMEM] * groups,
        out_specs=(VMEM, VMEM),
        scratch_shapes=[pltpu.VMEM((slots, ff + d), BF16)],
        compiler_params=pltpu.CompilerParams(vmem_limit_bytes=32 * MIB),
        cost_estimate=pl.CostEstimate(
            flops=2 * ff * d * slots, bytes_accessed=4 * ff * d + 4 * slots * (ff + d), transcendentals=0
        ),
        name="gradient",
    )(*pieces)


def update_kernel(half, me_ref, grad_ref, fwd_ref, *refs):
    pieces, (weight_new_ref, moment_new_ref, *produced), held = refs[:half], refs[half:-1], refs[-1]
    rows = pieces[0].shape[1]
    for s, piece in zip(mixed_order(half), pieces):
        for lead in range(2):
            held[lead, row_block((me_ref[0] ^ s) % half, rows)] = piece[lead]
    moment_new = (moment_decay * held[0].astype(F32) + grad_ref[...]).astype(BF16)
    moment_new_ref[...] = moment_new
    moment_f = moment_new.astype(F32)
    frobenius = jnp.sqrt(jnp.sum(moment_f * moment_f))
    current = (moment_f / (frobenius + norm_floor)).astype(BF16)
    for _ in range(2):
        gramian = lax.dot_general(
            current, current, (((1,), (1,)), ((), ())), preferred_element_type=F32
        ).astype(BF16)
        squared = jnp.dot(gramian, gramian, preferred_element_type=F32)
        poly = (cubic_term * gramian.astype(F32) + quintic_term * squared).astype(BF16)
        current = (
            linear_term * current.astype(F32) + jnp.dot(poly, current, preferred_element_type=F32)
        ).astype(BF16)
    weight_new = (held[1].astype(F32) - step_scale * current.astype(F32)).astype(BF16)
    weight_new_ref[...] = weight_new
    product = jnp.dot(fwd_ref[...], weight_new, preferred_element_type=F32).astype(BF16)
    groups, capacity = len(produced), produced[0].shape[0]
    came = dispatch_order(groups)
    for s, piece in zip(mixed_order(groups), produced):
        n = came.index(s)
        piece[...] = product[n * capacity : (n + 1) * capacity]


def update(me, grad, fwd_rows, pieces, groups):
    half = len(pieces)
    ff, d = grad.shape
    slots = fwd_rows.shape[0]
    shape = jax.ShapeDtypeStruct((ff, d), BF16)
    weight_new, moment_new, *produced = pl.pallas_call(
        functools.partial(update_kernel, half),
        out_shape=(shape, shape) + (jax.ShapeDtypeStruct((slots // groups, d), BF16),) * groups,
        in_specs=[SMEM] + [VMEM] * (2 + half),
        out_specs=(VMEM,) * (groups + 2),
        scratch_shapes=[pltpu.VMEM((2, ff, d), BF16)],
        compiler_params=pltpu.CompilerParams(vmem_limit_bytes=40 * MIB),
        cost_estimate=pl.CostEstimate(
            flops=2 * ff * d * slots + 8 * ff * ff * d + 4 * ff**3,
            bytes_accessed=12 * ff * d + 2 * slots * (ff + d),
            transcendentals=1,
        ),
        name="update",
    )(me, grad, fwd_rows, *pieces)
    return weight_new, moment_new, produced


def finish_kernel(groups, slot_ref, gates_ref, *refs):
    pieces, (out_ref, returned_ref) = refs[:groups], refs[groups:]
    capacity = pieces[0].shape[0]
    for s, piece in zip(mixed_order(groups), pieces):
        returned_ref[s * capacity : (s + 1) * capacity] = piece[...]
    selector = selector_of(slot_ref[...], groups * capacity)
    expert_out = lax.dot_general(
        selector, returned_ref[...], (((0,), (0,)), ((), ())), preferred_element_type=F32
    )
    out_ref[...] = (gates_ref[...] * expert_out).astype(BF16)


def finish(slot, gates, returned):
    groups = len(returned)
    rows = slot.shape[1]
    capacity, d = returned[0].shape
    slots = groups * capacity
    return pl.pallas_call(
        functools.partial(finish_kernel, groups),
        out_shape=jax.ShapeDtypeStruct((rows, d), BF16),
        in_specs=[VMEM] * (2 + groups),
        out_specs=VMEM,
        scratch_shapes=[pltpu.VMEM((slots, d), BF16)],
        compiler_params=pltpu.CompilerParams(vmem_limit_bytes=32 * MIB),
        cost_estimate=pl.CostEstimate(
            flops=2 * slots * rows * d, bytes_accessed=2 * d * (slots + rows), transcendentals=0
        ),
        name="finish",
    )(slot, gates, *returned)


def mixed_order(groups):
    far, near = list(range(groups // 2, groups)), list(range(groups // 2 - 1, 0, -1))
    return [0] + [s for pair in zip(far, near + [None]) for s in pair if s is not None]


def dispatch_sets(groups):
    half = groups // 2
    far = [s for pair in zip(range(half, half + half // 2), range(half + half // 2, groups)) for s in pair]
    near = list(range(1, half // 2)) + [None]
    first = [s for pair in zip(far[: half // 2], near) for s in pair if s is not None]
    return first, list(range(half // 2, half)), far[half // 2 :]


def dispatch_order(groups):
    return sum(dispatch_sets(groups), [0])


def swap(pieces, order):
    groups = lax.axis_size("expert")
    return [
        lax.ppermute(piece, "expert", [(i, i ^ s) for i in range(groups)]) if s else piece
        for s, piece in zip(order, pieces)
    ]


def halves_plan(
    grad_hidden, grad_out, grad_route, live_rows, w_down, w_moment, perm, fwd_hidden, fwd_route, fwd_gate
):
    groups = lax.axis_size("expert")
    layers = lax.axis_size("layer")
    half = groups // 2
    me = lax.axis_index("expert").astype(jnp.int32).reshape(1)
    capacity = max(4, 2 * grad_hidden.shape[0] // groups)
    ff, d = w_down.shape[1:]
    crossing = jnp.sum((perm[:half] >= half).astype(jnp.int32)).reshape(1)
    most = crossing
    for turn in range(1, layers):
        other = lax.ppermute(crossing, "layer", [(i, (i + turn) % layers) for i in range(layers)])
        most = jnp.maximum(most, other)
    most = most[0]

    near_order, (beside_spread, beside_crossing, beside_gather) = mixed_order(half), dispatch_sets(groups)
    blocks = split(me, w_moment, w_down, half)
    packed, later, fwd_slot, gates = pack_rows(
        live_rows, me, perm, grad_route, fwd_route, grad_hidden, grad_out, fwd_hidden, fwd_gate,
        blocks[0], groups, capacity,
    )
    spread = swap(blocks, near_order)
    received = swap(packed, [0] + beside_spread)
    near, *slots, token = sort_pieces(me, perm, spread, *received[1:])

    def mirror(array):
        return swap([array], [half])[0]

    always, following, rest = slots_of(half)
    crossed = [
        mirror(slots[0]),
        lax.cond(most > always, mirror, lambda array: array, slots[1]),
        lax.cond(most > always + following, mirror, lambda array: array, slots[2]),
    ]
    received += swap(take(later, 0, len(beside_crossing), token), beside_crossing)
    last = take(later, len(beside_crossing), len(beside_gather), crossed[0], *received[-len(beside_crossing) :])
    received += swap(last, beside_gather)
    placed = swap(join_pieces(me, perm, near, crossed), near_order)
    grad, fwd_rows = gradient(received, ff, d)
    weight_new, moment_new, produced = update(me, grad, fwd_rows, placed, groups)
    returned = swap(produced, mixed_order(groups))
    return weight_new[None], moment_new[None], finish(fwd_slot, gates, returned)


def lookup(route_ids, mapping):
    columns = jnp.arange(mapping.shape[0], dtype=jnp.int32)
    hits = route_ids[:, None] == columns[None, :]
    return jnp.sum(jnp.where(hits, mapping[None, :], 0), axis=1)


def slot_matrix(target, is_live, groups, capacity):
    columns = jnp.arange(groups, dtype=jnp.int32)
    onehot = ((target[:, None] == columns[None, :]) & is_live[:, None]).astype(jnp.int32)
    ranked = jnp.sum(jnp.cumsum(onehot, axis=0) * onehot, axis=1) - 1
    slot_of = jnp.where(is_live, target * capacity + ranked, -1)
    slots = jnp.arange(groups * capacity, dtype=jnp.int32)
    return (slots[:, None] == slot_of[None, :]).astype(jnp.bfloat16)


def orthogonalize(moment):
    moment_f = moment.astype(jnp.float32)
    frobenius = jnp.sqrt(jnp.sum(moment_f * moment_f))
    current = (moment_f / (frobenius + norm_floor)).astype(jnp.bfloat16)
    for sweep_index in range(2):
        gramian = lax.dot_general(
            current, current, (((1,), (1,)), ((), ())), preferred_element_type=jnp.float32
        ).astype(jnp.bfloat16)
        squared = jnp.dot(gramian, gramian, preferred_element_type=jnp.float32)
        poly = (cubic_term * gramian.astype(jnp.float32) + quintic_term * squared).astype(
            jnp.bfloat16
        )
        current = (
            linear_term * current.astype(jnp.float32)
            + jnp.dot(poly, current, preferred_element_type=jnp.float32)
        ).astype(jnp.bfloat16)
    return current


def relocate(weight, moment, perm):
    groups = lax.axis_size("expert")
    weight_flat = weight.reshape(groups, -1)
    moment_flat = moment.reshape(groups, -1)
    spread_w, spread_m = (
        lax.all_to_all(weight_flat, "expert", split_axis=0, concat_axis=0, tiled=True),
        lax.all_to_all(moment_flat, "expert", split_axis=0, concat_axis=0, tiled=True),
    )
    devices = jnp.arange(groups, dtype=jnp.int32)
    inverse = jnp.sum(jnp.where(perm[None, :] == devices[:, None], devices[None, :], 0), axis=1)
    ordered_w = jnp.take(spread_w, inverse, axis=0)
    ordered_m = jnp.take(spread_m, inverse, axis=0)
    back_w, back_m = (
        lax.all_to_all(ordered_w, "expert", split_axis=0, concat_axis=0, tiled=True),
        lax.all_to_all(ordered_m, "expert", split_axis=0, concat_axis=0, tiled=True),
    )
    return (back_w.reshape(weight.shape), back_m.reshape(moment.shape))


def routed_plan(
    grad_hidden,
    grad_out,
    grad_route,
    live_rows,
    w_down,
    w_moment,
    perm,
    fwd_hidden,
    fwd_route,
    fwd_gate,
):
    groups = lax.axis_size("expert")
    grad_count = grad_hidden.shape[0]
    capacity = max(4, 2 * grad_count // groups)
    is_live = jnp.arange(grad_count, dtype=jnp.int32) < live_rows[0]
    route_ids = grad_route[:, 0]
    weight, moment = relocate(w_down, w_moment, perm)
    target = lookup(route_ids, perm)
    selector = slot_matrix(target, is_live, groups, capacity)
    hidden_buf = (
        jnp.dot(selector, grad_hidden, preferred_element_type=jnp.float32)
        .astype(jnp.bfloat16)
        .reshape(groups, capacity, -1)
    )
    outgrad_buf = (
        jnp.dot(selector, grad_out, preferred_element_type=jnp.float32)
        .astype(jnp.bfloat16)
        .reshape(groups, capacity, -1)
    )
    recv_hidden, recv_outgrad = (
        lax.all_to_all(hidden_buf, "expert", split_axis=0, concat_axis=0, tiled=True),
        lax.all_to_all(outgrad_buf, "expert", split_axis=0, concat_axis=0, tiled=True),
    )
    grad = lax.dot_general(
        recv_hidden.reshape(groups * capacity, -1),
        recv_outgrad.reshape(groups * capacity, -1),
        (((0,), (0,)), ((), ())),
        preferred_element_type=jnp.float32,
    )
    moment_new = (moment_decay * moment[0].astype(jnp.float32) + grad).astype(jnp.bfloat16)
    ortho = orthogonalize(moment_new)
    weight_new = (weight[0].astype(jnp.float32) - step_scale * ortho.astype(jnp.float32)).astype(
        jnp.bfloat16
    )
    weight_new = weight_new[None]
    moment_new = moment_new[None]
    fwd_ids = fwd_route[:, 0]
    placed_weight, placed_moment = (weight_new, moment_new)
    fwd_target = lookup(fwd_ids, perm)
    fwd_weight = weight_new[0]
    fwd_count = fwd_hidden.shape[0]
    fwd_capacity = max(4, 2 * fwd_count // groups)
    fwd_selector = slot_matrix(fwd_target, jnp.ones((fwd_count,), dtype=bool), groups, fwd_capacity)
    fwd_buf = (
        jnp.dot(fwd_selector, fwd_hidden, preferred_element_type=jnp.float32)
        .astype(jnp.bfloat16)
        .reshape(groups, fwd_capacity, -1)
    )
    produced = jnp.einsum(
        "gkf,fd->gkd",
        lax.all_to_all(fwd_buf, "expert", split_axis=0, concat_axis=0, tiled=True),
        fwd_weight,
        preferred_element_type=jnp.float32,
    ).astype(jnp.bfloat16)
    returned = lax.all_to_all(produced, "expert", split_axis=0, concat_axis=0, tiled=True)
    fwd_rows_out = lax.dot_general(
        fwd_selector,
        returned.reshape(groups * fwd_capacity, -1),
        (((0,), (0,)), ((), ())),
        preferred_element_type=jnp.float32,
    )
    fwd_out = (fwd_rows_out * fwd_gate[:, None]).astype(jnp.bfloat16)
    return (placed_weight, placed_moment, fwd_out)


def solution(mesh):
    groups = mesh.shape["expert"]
    in_specs = (
        P(("layer", "expert"), None),
        P(("layer", "expert"), None),
        P(("layer", "expert"), None),
        P(("layer", "expert")),
        P(("layer", "expert"), None, None),
        P(("layer", "expert"), None, None),
        P("layer"),
        P(("layer", "expert"), None),
        P(("layer", "expert"), None),
        P(("layer", "expert")),
    )
    out_specs = (
        P(("layer", "expert"), None, None),
        P(("layer", "expert"), None, None),
        P(("layer", "expert"), None),
    )

    def per_device(*args):
        few = groups >= 8 and groups & (groups - 1) == 0 and groups <= 2 * args[0].shape[0] // groups
        return (halves_plan if few else routed_plan)(*args)

    return jax.shard_map(
        per_device, mesh=mesh, in_specs=in_specs, out_specs=out_specs, check_vma=False
    )
```

```python
import functools

import jax
import jax.numpy as jnp
from jax import lax
from jax.experimental import pallas as pl
from jax.experimental.pallas import tpu as pltpu
from jax.sharding import PartitionSpec as P

linear_term = 3.4445
cubic_term = -4.775
quintic_term = 2.0315
moment_decay = 0.9
step_scale = 0.25
norm_floor = 1e-07

F32 = jnp.float32
BF16 = jnp.bfloat16
HBM = pl.BlockSpec(memory_space=pltpu.HBM)
VMEM = pl.BlockSpec(memory_space=pltpu.VMEM)
SMEM = pl.BlockSpec(memory_space=pltpu.SMEM)
ANY = pl.BlockSpec(memory_space=pl.ANY)
MIB = 1 << 20


def fetched(refs, held, sem):
    copies = [pltpu.make_async_copy(ref, room, sem.at[n]) for n, (ref, room) in enumerate(zip(refs, held))]
    for copy in copies:
        copy.start()
    for copy in copies:
        copy.wait()


def rooms(arrays):
    return [pltpu.VMEM(a.shape, a.dtype) for a in arrays] + [pltpu.SemaphoreType.DMA((len(arrays),))]


def chunk_at(ref, lead, k, rows, columns):
    return ref.at[
        lead,
        pl.ds(pl.multiple_of((k // 2) * rows, rows), rows),
        pl.ds(pl.multiple_of((k % 2) * columns, columns), columns),
    ]


def slot_rows(route, live, groups, capacity, perm_ref):
    rows = route.shape[1]
    experts = lax.broadcasted_iota(jnp.int32, (groups, rows), 0)
    onehot = jnp.where((experts == route) & live, 1.0, 0.0).astype(BF16)
    before = lax.broadcasted_iota(jnp.int32, (rows, rows), 0)
    after = lax.broadcasted_iota(jnp.int32, (rows, rows), 1)
    upto = jnp.where(before <= after, 1.0, 0.0).astype(BF16)
    ranks = jnp.dot(onehot, upto, preferred_element_type=F32)
    rank = jnp.sum(ranks * onehot.astype(F32), axis=0, keepdims=True).astype(jnp.int32) - 1
    target = jnp.zeros_like(route)
    for e in range(groups):
        target = jnp.where(route == e, perm_ref[e], target)
    return jnp.where(live, target * capacity + rank, -1)


def selector_of(slot, slots):
    rows = slot.shape[1]
    places = lax.broadcasted_iota(jnp.int32, (slots, rows), 0)
    return jnp.where(places == slot, 1.0, 0.0).astype(BF16)


def pack_kernel(groups, live_ref, perm_ref, *refs):
    sources, (packed_ref, slot_ref, gates_ref), held, sem = refs[:6], refs[7:10], refs[10:16], refs[16]
    route_ref, fwd_route_ref, hidden_ref, out_ref, fwd_ref, gate_ref = held
    copies = [pltpu.make_async_copy(ref, room, sem.at[n]) for n, (ref, room) in enumerate(zip(sources, held))]
    for copy in copies:
        copy.start()
    rows, ff = hidden_ref.shape
    d = out_ref.shape[1]
    slots = packed_ref.shape[0]
    capacity = slots // groups
    place = lax.broadcasted_iota(jnp.int32, (1, rows), 1)

    def fill(first, selector, source_ref):
        chosen = jnp.dot(selector, source_ref[...], preferred_element_type=F32)
        packed_ref[:, first : first + source_ref.shape[1]] = chosen.astype(BF16)

    copies[0].wait()
    slot = slot_rows(route_ref[...], place < live_ref[0], groups, capacity, perm_ref)
    selector = selector_of(slot, slots)
    copies[1].wait()
    fwd_slot = slot_rows(fwd_route_ref[...], place >= 0, groups, capacity, perm_ref)
    slot_ref[...] = fwd_slot
    copies[2].wait()
    fill(0, selector, hidden_ref)
    copies[3].wait()
    fill(ff, selector, out_ref)
    copies[4].wait()
    fill(ff + d, selector_of(fwd_slot, slots), fwd_ref)
    copies[5].wait()
    down = lax.broadcasted_iota(jnp.int32, (rows, rows), 0)
    across = lax.broadcasted_iota(jnp.int32, (rows, rows), 1)
    gates_ref[...] = jnp.sum(jnp.where(down == across, gate_ref[...], 0.0), axis=1, keepdims=True)


def pack_rows(live_rows, perm, route, fwd_route, hidden, grad_out, fwd_hidden, gate, earlier, groups, capacity):
    rows, ff = hidden.shape
    width = 2 * ff + grad_out.shape[1]
    sources = (
        route.reshape(1, rows), fwd_route.reshape(1, rows), hidden, grad_out, fwd_hidden, gate.reshape(1, rows),
    )
    return pl.pallas_call(
        functools.partial(pack_kernel, groups),
        out_shape=(
            jax.ShapeDtypeStruct((groups * capacity, width), BF16),
            jax.ShapeDtypeStruct((1, rows), jnp.int32),
            jax.ShapeDtypeStruct((rows, 1), F32),
        ),
        in_specs=[SMEM] * 2 + [HBM] * 6 + [VMEM],
        out_specs=(VMEM,) * 3,
        scratch_shapes=[pltpu.VMEM(a.shape, a.dtype) for a in sources] + [pltpu.SemaphoreType.DMA((len(sources),))],
        compiler_params=pltpu.CompilerParams(vmem_limit_bytes=32 * MIB),
        cost_estimate=pl.CostEstimate(
            flops=2 * groups * capacity * rows * width, bytes_accessed=6 * rows * width, transcendentals=0
        ),
        name="pack_rows",
    )(live_rows, perm, *sources, earlier)


def split_kernel(me_ref, moment_ref, weight_ref, *refs):
    pieces, held, sem = refs[:-3], refs[-3:-1], refs[-1]
    fetched((moment_ref, weight_ref), held, sem)
    for s, piece in zip(mixed_order(len(pieces)), pieces):
        rows, columns = piece.shape[1:]
        for lead, source in enumerate(held):
            piece[lead] = chunk_at(source, 0, me_ref[0] ^ s, rows, columns)[...]


def split(me, moment, weight, groups):
    _, ff, d = weight.shape
    piece = jax.ShapeDtypeStruct((2, ff // (groups // 2), d // 2), BF16)
    return pl.pallas_call(
        split_kernel,
        out_shape=(piece,) * groups,
        in_specs=[SMEM, HBM, HBM],
        out_specs=(VMEM,) * groups,
        scratch_shapes=rooms((moment, weight)),
        compiler_params=pltpu.CompilerParams(vmem_limit_bytes=60 * MIB),
        cost_estimate=pl.CostEstimate(flops=0, bytes_accessed=8 * ff * d, transcendentals=0),
        name="split",
    )(me, moment, weight)


def reorder_kernel(me_ref, perm_ref, *refs):
    groups = (len(refs) - 2) // 3
    sources, targets, held = refs[:groups], refs[groups + 1 : -1], refs[-1]
    me, order = me_ref[0], mixed_order(groups)
    for s, source in zip(order, sources):
        held[me ^ perm_ref[me ^ s]] = source[...]
    for n, target in enumerate(targets):
        target[...] = held[order[n % groups], n // groups]


def reorder(me, perm, pieces, earlier):
    groups = len(pieces)
    piece = jax.ShapeDtypeStruct(pieces[0].shape[1:], BF16)
    targets = pl.pallas_call(
        reorder_kernel,
        out_shape=(piece,) * (2 * groups),
        in_specs=[SMEM, SMEM] + [VMEM] * (groups + 1),
        out_specs=(VMEM,) * (2 * groups),
        scratch_shapes=[pltpu.VMEM((groups,) + pieces[0].shape, BF16)],
        compiler_params=pltpu.CompilerParams(vmem_limit_bytes=32 * MIB),
        cost_estimate=pl.CostEstimate(flops=0, bytes_accessed=4 * groups * pieces[0].size, transcendentals=0),
        name="reorder",
    )(me, perm, *pieces, earlier)
    return targets[:groups], targets[groups:]


def assembled(me_ref, pieces, held):
    rows, columns = pieces[0].shape
    for s, piece in zip(mixed_order(len(pieces)), pieces):
        chunk_at(held, 0, me_ref[0] ^ s, rows, columns)[...] = piece[...]
    return held[0].astype(F32)


def orthogonal_kernel(me_ref, packed_ref, *refs):
    pieces, (moment_new_ref, ortho_ref, held) = refs[:-3], refs[-3:]
    ff, d = ortho_ref.shape
    grad = lax.dot_general(
        packed_ref[:, :ff], packed_ref[:, ff : ff + d], (((0,), (0,)), ((), ())), preferred_element_type=F32
    )
    moment_new = (moment_decay * assembled(me_ref, pieces, held) + grad).astype(BF16)
    moment_new_ref[...] = moment_new
    moment_f = moment_new.astype(F32)
    frobenius = jnp.sqrt(jnp.sum(moment_f * moment_f))
    current = (moment_f / (frobenius + norm_floor)).astype(BF16)
    for _ in range(2):
        gramian = lax.dot_general(
            current, current, (((1,), (1,)), ((), ())), preferred_element_type=F32
        ).astype(BF16)
        squared = jnp.dot(gramian, gramian, preferred_element_type=F32)
        poly = (cubic_term * gramian.astype(F32) + quintic_term * squared).astype(BF16)
        current = (
            linear_term * current.astype(F32) + jnp.dot(poly, current, preferred_element_type=F32)
        ).astype(BF16)
    ortho_ref[...] = current


def orthogonal(me, packed, pieces, ff, d):
    shape = jax.ShapeDtypeStruct((ff, d), BF16)
    return pl.pallas_call(
        orthogonal_kernel,
        out_shape=(shape, shape),
        in_specs=[SMEM, VMEM] + [VMEM] * len(pieces),
        out_specs=(VMEM, VMEM),
        scratch_shapes=[pltpu.VMEM((1, ff, d), BF16)],
        compiler_params=pltpu.CompilerParams(vmem_limit_bytes=40 * MIB),
        cost_estimate=pl.CostEstimate(
            flops=2 * ff * d * packed.shape[0] + 8 * ff * ff * d + 4 * ff**3,
            bytes_accessed=6 * ff * d + 2 * packed.size,
            transcendentals=1,
        ),
        name="orthogonal",
    )(me, packed, *pieces)


def produce_kernel(groups, me_ref, packed_ref, ortho_ref, *refs):
    pieces, (weight_new_ref, *produced), (held, product_ref) = refs[:groups], refs[groups:-2], refs[-2:]
    ff, d = ortho_ref.shape
    weight = assembled(me_ref, pieces, held)
    weight_new = (weight - step_scale * ortho_ref[...].astype(F32)).astype(BF16)
    weight_new_ref[...] = weight_new
    product = jnp.dot(packed_ref[:, ff + d :], weight_new, preferred_element_type=F32).astype(BF16)
    capacity = produced[0].shape[0]
    product_ref[...] = product.reshape(groups, capacity, d)
    for s, piece in zip(mixed_order(groups), produced):
        piece[...] = product_ref[me_ref[0] ^ s]


def produce(me, packed, ortho, pieces):
    groups = len(pieces)
    ff, d = ortho.shape
    slots = packed.shape[0]
    weight_new, *produced = pl.pallas_call(
        functools.partial(produce_kernel, groups),
        out_shape=(jax.ShapeDtypeStruct((ff, d), BF16),)
        + (jax.ShapeDtypeStruct((slots // groups, d), BF16),) * groups,
        in_specs=[SMEM] + [VMEM] * (2 + groups),
        out_specs=(VMEM,) * (groups + 1),
        scratch_shapes=[pltpu.VMEM((1, ff, d), BF16), pltpu.VMEM((groups, slots // groups, d), BF16)],
        compiler_params=pltpu.CompilerParams(vmem_limit_bytes=40 * MIB),
        cost_estimate=pl.CostEstimate(
            flops=2 * ff * d * slots, bytes_accessed=8 * ff * d + 2 * slots * (ff + d), transcendentals=0
        ),
        name="produce",
    )(me, packed, ortho, *pieces)
    return weight_new, produced


def finish_kernel(groups, me_ref, slot_ref, gates_ref, *refs):
    pieces, (out_ref, returned_ref) = refs[:groups], refs[groups:]
    for s, piece in zip(mixed_order(groups), pieces):
        returned_ref[me_ref[0] ^ s] = piece[...]
    _, capacity, d = returned_ref.shape
    slots = groups * capacity
    selector = selector_of(slot_ref[...], slots)
    expert_out = lax.dot_general(
        selector, returned_ref[...].reshape(slots, d), (((0,), (0,)), ((), ())), preferred_element_type=F32
    )
    out_ref[...] = (gates_ref[...] * expert_out).astype(BF16)


def finish(me, slot, gates, returned):
    groups = len(returned)
    rows = slot.shape[1]
    capacity, d = returned[0].shape
    slots = groups * capacity
    return pl.pallas_call(
        functools.partial(finish_kernel, groups),
        out_shape=jax.ShapeDtypeStruct((rows, d), BF16),
        in_specs=[SMEM] + [VMEM] * (2 + groups),
        out_specs=VMEM,
        scratch_shapes=[pltpu.VMEM((groups, capacity, d), BF16)],
        compiler_params=pltpu.CompilerParams(vmem_limit_bytes=32 * MIB),
        cost_estimate=pl.CostEstimate(
            flops=2 * slots * rows * d, bytes_accessed=2 * d * (slots + rows), transcendentals=0
        ),
        name="finish",
    )(me, slot, gates, *returned)


def mixed_order(groups):
    far, near = list(range(groups // 2, groups)), list(range(groups // 2 - 1, 0, -1))
    return [0] + [s for pair in zip(far, near + [None]) for s in pair if s is not None]


def exchange(array):
    return lax.all_to_all(array, "expert", split_axis=0, concat_axis=0, tiled=True)


def swap(pieces, order):
    groups = lax.axis_size("expert")
    return [
        lax.ppermute(piece, "expert", [(i, i ^ s) for i in range(groups)]) if s else piece
        for s, piece in zip(order, pieces)
    ]


def partner_plan(
    grad_hidden, grad_out, grad_route, live_rows, w_down, w_moment, perm, fwd_hidden, fwd_route, fwd_gate
):
    groups = lax.axis_size("expert")
    me = lax.axis_index("expert").astype(jnp.int32).reshape(1)
    capacity = max(4, 2 * grad_hidden.shape[0] // groups)
    ff, d = w_down.shape[1:]
    order = mixed_order(groups)
    spread = swap(split(me, w_moment, w_down, groups), order)
    packed, fwd_slot, gates = pack_rows(
        live_rows, perm, grad_route, fwd_route, grad_hidden, grad_out, fwd_hidden, fwd_gate,
        spread[2 * groups // 3], groups, capacity,
    )
    received = exchange(packed.reshape(groups, capacity, -1)).reshape(groups * capacity, -1)
    moment_pieces, weight_pieces = reorder(me, perm, spread, fwd_slot)
    moment_new, ortho = orthogonal(me, received, swap(moment_pieces, order), ff, d)
    weight_new, produced = produce(me, received, ortho, swap(weight_pieces, order))
    return weight_new[None], moment_new[None], finish(me, fwd_slot, gates, swap(produced, order))


def lookup(route_ids, mapping):
    columns = jnp.arange(mapping.shape[0], dtype=jnp.int32)
    hits = route_ids[:, None] == columns[None, :]
    return jnp.sum(jnp.where(hits, mapping[None, :], 0), axis=1)


def slot_matrix(target, is_live, groups, capacity):
    columns = jnp.arange(groups, dtype=jnp.int32)
    onehot = ((target[:, None] == columns[None, :]) & is_live[:, None]).astype(jnp.int32)
    ranked = jnp.sum(jnp.cumsum(onehot, axis=0) * onehot, axis=1) - 1
    slot_of = jnp.where(is_live, target * capacity + ranked, -1)
    slots = jnp.arange(groups * capacity, dtype=jnp.int32)
    return (slots[:, None] == slot_of[None, :]).astype(jnp.bfloat16)


def orthogonalize(moment):
    moment_f = moment.astype(jnp.float32)
    frobenius = jnp.sqrt(jnp.sum(moment_f * moment_f))
    current = (moment_f / (frobenius + norm_floor)).astype(jnp.bfloat16)
    for sweep_index in range(2):
        gramian = lax.dot_general(
            current, current, (((1,), (1,)), ((), ())), preferred_element_type=jnp.float32
        ).astype(jnp.bfloat16)
        squared = jnp.dot(gramian, gramian, preferred_element_type=jnp.float32)
        poly = (cubic_term * gramian.astype(jnp.float32) + quintic_term * squared).astype(
            jnp.bfloat16
        )
        current = (
            linear_term * current.astype(jnp.float32)
            + jnp.dot(poly, current, preferred_element_type=jnp.float32)
        ).astype(jnp.bfloat16)
    return current


def relocate(weight, moment, perm):
    groups = lax.axis_size("expert")
    weight_flat = weight.reshape(groups, -1)
    moment_flat = moment.reshape(groups, -1)
    spread_w, spread_m = (
        lax.all_to_all(weight_flat, "expert", split_axis=0, concat_axis=0, tiled=True),
        lax.all_to_all(moment_flat, "expert", split_axis=0, concat_axis=0, tiled=True),
    )
    devices = jnp.arange(groups, dtype=jnp.int32)
    inverse = jnp.sum(jnp.where(perm[None, :] == devices[:, None], devices[None, :], 0), axis=1)
    ordered_w = jnp.take(spread_w, inverse, axis=0)
    ordered_m = jnp.take(spread_m, inverse, axis=0)
    back_w, back_m = (
        lax.all_to_all(ordered_w, "expert", split_axis=0, concat_axis=0, tiled=True),
        lax.all_to_all(ordered_m, "expert", split_axis=0, concat_axis=0, tiled=True),
    )
    return (back_w.reshape(weight.shape), back_m.reshape(moment.shape))


def routed_plan(
    grad_hidden,
    grad_out,
    grad_route,
    live_rows,
    w_down,
    w_moment,
    perm,
    fwd_hidden,
    fwd_route,
    fwd_gate,
):
    groups = lax.axis_size("expert")
    grad_count = grad_hidden.shape[0]
    capacity = max(4, 2 * grad_count // groups)
    is_live = jnp.arange(grad_count, dtype=jnp.int32) < live_rows[0]
    route_ids = grad_route[:, 0]
    weight, moment = relocate(w_down, w_moment, perm)
    target = lookup(route_ids, perm)
    selector = slot_matrix(target, is_live, groups, capacity)
    hidden_buf = (
        jnp.dot(selector, grad_hidden, preferred_element_type=jnp.float32)
        .astype(jnp.bfloat16)
        .reshape(groups, capacity, -1)
    )
    outgrad_buf = (
        jnp.dot(selector, grad_out, preferred_element_type=jnp.float32)
        .astype(jnp.bfloat16)
        .reshape(groups, capacity, -1)
    )
    recv_hidden, recv_outgrad = (
        lax.all_to_all(hidden_buf, "expert", split_axis=0, concat_axis=0, tiled=True),
        lax.all_to_all(outgrad_buf, "expert", split_axis=0, concat_axis=0, tiled=True),
    )
    grad = lax.dot_general(
        recv_hidden.reshape(groups * capacity, -1),
        recv_outgrad.reshape(groups * capacity, -1),
        (((0,), (0,)), ((), ())),
        preferred_element_type=jnp.float32,
    )
    moment_new = (moment_decay * moment[0].astype(jnp.float32) + grad).astype(jnp.bfloat16)
    ortho = orthogonalize(moment_new)
    weight_new = (weight[0].astype(jnp.float32) - step_scale * ortho.astype(jnp.float32)).astype(
        jnp.bfloat16
    )
    weight_new = weight_new[None]
    moment_new = moment_new[None]
    fwd_ids = fwd_route[:, 0]
    placed_weight, placed_moment = (weight_new, moment_new)
    fwd_target = lookup(fwd_ids, perm)
    fwd_weight = weight_new[0]
    fwd_count = fwd_hidden.shape[0]
    fwd_capacity = max(4, 2 * fwd_count // groups)
    fwd_selector = slot_matrix(fwd_target, jnp.ones((fwd_count,), dtype=bool), groups, fwd_capacity)
    fwd_buf = (
        jnp.dot(fwd_selector, fwd_hidden, preferred_element_type=jnp.float32)
        .astype(jnp.bfloat16)
        .reshape(groups, fwd_capacity, -1)
    )
    produced = jnp.einsum(
        "gkf,fd->gkd",
        lax.all_to_all(fwd_buf, "expert", split_axis=0, concat_axis=0, tiled=True),
        fwd_weight,
        preferred_element_type=jnp.float32,
    ).astype(jnp.bfloat16)
    returned = lax.all_to_all(produced, "expert", split_axis=0, concat_axis=0, tiled=True)
    fwd_rows_out = lax.dot_general(
        fwd_selector,
        returned.reshape(groups * fwd_capacity, -1),
        (((0,), (0,)), ((), ())),
        preferred_element_type=jnp.float32,
    )
    fwd_out = (fwd_rows_out * fwd_gate[:, None]).astype(jnp.bfloat16)
    return (placed_weight, placed_moment, fwd_out)


def solution(mesh):
    groups = mesh.shape["expert"]
    in_specs = (
        P(("layer", "expert"), None),
        P(("layer", "expert"), None),
        P(("layer", "expert"), None),
        P(("layer", "expert")),
        P(("layer", "expert"), None, None),
        P(("layer", "expert"), None, None),
        P("layer"),
        P(("layer", "expert"), None),
        P(("layer", "expert"), None),
        P(("layer", "expert")),
    )
    out_specs = (
        P(("layer", "expert"), None, None),
        P(("layer", "expert"), None, None),
        P(("layer", "expert"), None),
    )

    def per_device(*args):
        few = groups & (groups - 1) == 0 and groups <= 2 * args[0].shape[0] // groups
        return (partner_plan if few else routed_plan)(*args)

    return jax.shard_map(
        per_device, mesh=mesh, in_specs=in_specs, out_specs=out_specs, check_vma=False
    )
```

```python
import functools

import jax
import jax.numpy as jnp
from jax import lax
from jax.experimental import pallas as pl
from jax.experimental.pallas import tpu as pltpu
from jax.sharding import PartitionSpec as P

linear_term = 3.4445
cubic_term = -4.775
quintic_term = 2.0315
moment_decay = 0.9
step_scale = 0.25
norm_floor = 1e-07

F32 = jnp.float32
BF16 = jnp.bfloat16
HBM = pl.BlockSpec(memory_space=pltpu.HBM)
VMEM = pl.BlockSpec(memory_space=pltpu.VMEM)
SMEM = pl.BlockSpec(memory_space=pltpu.SMEM)
ANY = pl.BlockSpec(memory_space=pl.ANY)
MIB = 1 << 20


def fetched(refs, held, sem):
    copies = [pltpu.make_async_copy(ref, room, sem.at[n]) for n, (ref, room) in enumerate(zip(refs, held))]
    for copy in copies:
        copy.start()
    for copy in copies:
        copy.wait()


def rooms(arrays):
    return [pltpu.VMEM(a.shape, a.dtype) for a in arrays] + [pltpu.SemaphoreType.DMA((len(arrays),))]


def chunk_at(ref, lead, k, rows, columns):
    return ref.at[
        lead,
        pl.ds(pl.multiple_of((k // 2) * rows, rows), rows),
        pl.ds(pl.multiple_of((k % 2) * columns, columns), columns),
    ]


def slot_rows(route, live, groups, capacity, me_ref, perm_ref):
    rows = route.shape[1]
    experts = lax.broadcasted_iota(jnp.int32, (groups, rows), 0)
    onehot = jnp.where((experts == route) & live, 1.0, 0.0).astype(BF16)
    before = lax.broadcasted_iota(jnp.int32, (rows, rows), 0)
    after = lax.broadcasted_iota(jnp.int32, (rows, rows), 1)
    upto = jnp.where(before <= after, 1.0, 0.0).astype(BF16)
    ranks = jnp.dot(onehot, upto, preferred_element_type=F32)
    rank = jnp.sum(ranks * onehot.astype(F32), axis=0, keepdims=True).astype(jnp.int32) - 1
    partner = jnp.zeros_like(route)
    for e in range(groups):
        partner = jnp.where(route == e, perm_ref[e] ^ me_ref[0], partner)
    return jnp.where(live, partner * capacity + rank, -1)


def selector_of(slot, slots):
    rows = slot.shape[1]
    places = lax.broadcasted_iota(jnp.int32, (slots, rows), 0)
    return jnp.where(places == slot, 1.0, 0.0).astype(BF16)


def pack_kernel(groups, live_ref, me_ref, perm_ref, *refs):
    sources, pieces, (slot_ref, gates_ref) = refs[:6], refs[7 : 7 + groups], refs[7 + groups : 9 + groups]
    held, sem = refs[9 + groups : 15 + groups], refs[-1]
    route_ref, fwd_route_ref, hidden_ref, out_ref, fwd_ref, gate_ref = held
    copies = [pltpu.make_async_copy(ref, room, sem.at[n]) for n, (ref, room) in enumerate(zip(sources, held))]
    for copy in copies:
        copy.start()
    rows, ff = hidden_ref.shape
    d = out_ref.shape[1]
    capacity = pieces[0].shape[0]
    slots = groups * capacity
    place = lax.broadcasted_iota(jnp.int32, (1, rows), 1)

    def fill(first, selector, source_ref):
        chosen = jnp.dot(selector, source_ref[...], preferred_element_type=F32).astype(BF16)
        for s, piece in zip(mixed_order(groups), pieces):
            piece[:, first : first + source_ref.shape[1]] = chosen[s * capacity : (s + 1) * capacity]

    copies[0].wait()
    slot = slot_rows(route_ref[...], place < live_ref[0], groups, capacity, me_ref, perm_ref)
    selector = selector_of(slot, slots)
    copies[1].wait()
    fwd_slot = slot_rows(fwd_route_ref[...], place >= 0, groups, capacity, me_ref, perm_ref)
    slot_ref[...] = fwd_slot
    copies[2].wait()
    fill(0, selector, hidden_ref)
    copies[3].wait()
    fill(ff, selector, out_ref)
    copies[4].wait()
    fill(ff + d, selector_of(fwd_slot, slots), fwd_ref)
    copies[5].wait()
    down = lax.broadcasted_iota(jnp.int32, (rows, rows), 0)
    across = lax.broadcasted_iota(jnp.int32, (rows, rows), 1)
    gates_ref[...] = jnp.sum(jnp.where(down == across, gate_ref[...], 0.0), axis=1, keepdims=True)


def pack_rows(live_rows, me, perm, route, fwd_route, hidden, grad_out, fwd_hidden, gate, earlier, groups, capacity):
    rows, ff = hidden.shape
    width = 2 * ff + grad_out.shape[1]
    sources = (route.reshape(1, rows), fwd_route.reshape(1, rows), hidden, grad_out, fwd_hidden, gate.reshape(1, rows))
    *pieces, slot, gates = pl.pallas_call(
        functools.partial(pack_kernel, groups),
        out_shape=(jax.ShapeDtypeStruct((capacity, width), BF16),) * groups
        + (jax.ShapeDtypeStruct((1, rows), jnp.int32), jax.ShapeDtypeStruct((rows, 1), F32)),
        in_specs=[SMEM] * 3 + [HBM] * 6 + [VMEM],
        out_specs=(VMEM,) * (groups + 2),
        scratch_shapes=[pltpu.VMEM(a.shape, a.dtype) for a in sources] + [pltpu.SemaphoreType.DMA((len(sources),))],
        compiler_params=pltpu.CompilerParams(vmem_limit_bytes=32 * MIB),
        cost_estimate=pl.CostEstimate(
            flops=2 * groups * capacity * rows * width, bytes_accessed=6 * rows * width, transcendentals=0
        ),
        name="pack_rows",
    )(live_rows, me, perm, *sources, earlier)
    return pieces, slot, gates


def split_kernel(me_ref, moment_ref, weight_ref, *refs):
    pieces, held, sem = refs[:-3], refs[-3:-1], refs[-1]
    fetched((moment_ref, weight_ref), held, sem)
    for s, piece in zip(mixed_order(len(pieces)), pieces):
        rows, columns = piece.shape[1:]
        for lead, source in enumerate(held):
            piece[lead] = chunk_at(source, 0, me_ref[0] ^ s, rows, columns)[...]


def split(me, moment, weight, groups):
    _, ff, d = weight.shape
    piece = jax.ShapeDtypeStruct((2, ff // (groups // 2), d // 2), BF16)
    return pl.pallas_call(
        split_kernel,
        out_shape=(piece,) * groups,
        in_specs=[SMEM, HBM, HBM],
        out_specs=(VMEM,) * groups,
        scratch_shapes=rooms((moment, weight)),
        compiler_params=pltpu.CompilerParams(vmem_limit_bytes=60 * MIB),
        cost_estimate=pl.CostEstimate(flops=0, bytes_accessed=8 * ff * d, transcendentals=0),
        name="split",
    )(me, moment, weight)


def reorder_kernel(me_ref, perm_ref, *refs):
    groups = len(refs) // 2 - 1
    sources, targets, held = refs[:groups], refs[groups + 1 : 2 * groups + 1], refs[-1]
    me, order = me_ref[0], mixed_order(groups)
    for s, source in zip(order, sources):
        held[me ^ perm_ref[me ^ s]] = source[...]
    for s, target in zip(order, targets):
        target[...] = held[s]


def reorder(me, perm, pieces, earlier):
    groups = len(pieces)
    piece = jax.ShapeDtypeStruct(pieces[0].shape, BF16)
    return pl.pallas_call(
        reorder_kernel,
        out_shape=(piece,) * groups,
        in_specs=[SMEM, SMEM] + [VMEM] * (groups + 1),
        out_specs=(VMEM,) * groups,
        scratch_shapes=[pltpu.VMEM((groups,) + pieces[0].shape, BF16)],
        compiler_params=pltpu.CompilerParams(vmem_limit_bytes=32 * MIB),
        cost_estimate=pl.CostEstimate(flops=0, bytes_accessed=4 * groups * pieces[0].size, transcendentals=0),
        name="reorder",
    )(me, perm, *pieces, earlier)


def update_kernel(groups, me_ref, *refs):
    packed, pieces, produced = refs[:groups], refs[groups : 2 * groups], refs[2 * groups + 2 : 3 * groups + 2]
    weight_new_ref, moment_new_ref = refs[2 * groups : 2 * groups + 2]
    held, rows_ref = refs[-2:]
    _, ff, d = held.shape
    capacity = packed[0].shape[0]
    for n, piece in enumerate(packed):
        rows_ref[n * capacity : (n + 1) * capacity] = piece[...]
    for s, piece in zip(mixed_order(groups), pieces):
        rows, columns = piece.shape[1:]
        for lead in range(2):
            chunk_at(held, lead, me_ref[0] ^ s, rows, columns)[...] = piece[lead]
    grad = lax.dot_general(
        rows_ref[:, :ff], rows_ref[:, ff : ff + d], (((0,), (0,)), ((), ())), preferred_element_type=F32
    )
    moment_new = (moment_decay * held[0].astype(F32) + grad).astype(BF16)
    moment_new_ref[...] = moment_new
    moment_f = moment_new.astype(F32)
    frobenius = jnp.sqrt(jnp.sum(moment_f * moment_f))
    current = (moment_f / (frobenius + norm_floor)).astype(BF16)
    for _ in range(2):
        gramian = lax.dot_general(
            current, current, (((1,), (1,)), ((), ())), preferred_element_type=F32
        ).astype(BF16)
        squared = jnp.dot(gramian, gramian, preferred_element_type=F32)
        poly = (cubic_term * gramian.astype(F32) + quintic_term * squared).astype(BF16)
        current = (
            linear_term * current.astype(F32) + jnp.dot(poly, current, preferred_element_type=F32)
        ).astype(BF16)
    weight_new = (held[1].astype(F32) - step_scale * current.astype(F32)).astype(BF16)
    weight_new_ref[...] = weight_new
    product = jnp.dot(rows_ref[:, ff + d :], weight_new, preferred_element_type=F32).astype(BF16)
    for n, piece in enumerate(produced):
        piece[...] = product[n * capacity : (n + 1) * capacity]


def update(me, packed, pieces, ff, d):
    groups = len(pieces)
    capacity, width = packed[0].shape
    slots = groups * capacity
    shape = jax.ShapeDtypeStruct((ff, d), BF16)
    weight_new, moment_new, *produced = pl.pallas_call(
        functools.partial(update_kernel, groups),
        out_shape=(shape, shape) + (jax.ShapeDtypeStruct((capacity, d), BF16),) * groups,
        in_specs=[SMEM] + [VMEM] * (2 * groups),
        out_specs=(VMEM,) * (groups + 2),
        scratch_shapes=[pltpu.VMEM((2, ff, d), BF16), pltpu.VMEM((slots, width), BF16)],
        compiler_params=pltpu.CompilerParams(vmem_limit_bytes=40 * MIB),
        cost_estimate=pl.CostEstimate(
            flops=4 * ff * d * slots + 8 * ff * ff * d + 4 * ff**3,
            bytes_accessed=8 * ff * d + 2 * slots * (width + d),
            transcendentals=1,
        ),
        name="update",
    )(me, *packed, *pieces)
    return weight_new, moment_new, produced


def finish_kernel(groups, slot_ref, gates_ref, *refs):
    pieces, (out_ref, returned_ref) = refs[:groups], refs[groups:]
    capacity = pieces[0].shape[0]
    for s, piece in zip(mixed_order(groups), pieces):
        returned_ref[s * capacity : (s + 1) * capacity] = piece[...]
    selector = selector_of(slot_ref[...], groups * capacity)
    expert_out = lax.dot_general(
        selector, returned_ref[...], (((0,), (0,)), ((), ())), preferred_element_type=F32
    )
    out_ref[...] = (gates_ref[...] * expert_out).astype(BF16)


def finish(slot, gates, returned):
    groups = len(returned)
    rows = slot.shape[1]
    capacity, d = returned[0].shape
    slots = groups * capacity
    return pl.pallas_call(
        functools.partial(finish_kernel, groups),
        out_shape=jax.ShapeDtypeStruct((rows, d), BF16),
        in_specs=[VMEM] * (2 + groups),
        out_specs=VMEM,
        scratch_shapes=[pltpu.VMEM((slots, d), BF16)],
        compiler_params=pltpu.CompilerParams(vmem_limit_bytes=32 * MIB),
        cost_estimate=pl.CostEstimate(
            flops=2 * slots * rows * d, bytes_accessed=2 * d * (slots + rows), transcendentals=0
        ),
        name="finish",
    )(slot, gates, *returned)


def mixed_order(groups):
    def both_ends(partners):
        middle = (len(partners) + 1) // 2
        first, second = partners[:middle], partners[middle:]
        return [s for pair in zip(first, second + [None]) for s in pair if s is not None]

    half = groups // 2
    far, near = both_ends(list(range(half, groups))), both_ends(list(range(half - 1, 0, -1)))
    return [0] + [s for pair in zip(far, near + [None]) for s in pair if s is not None]


def swap(pieces):
    groups = len(pieces)
    order = mixed_order(groups)
    return [pieces[0]] + [
        lax.ppermute(piece, "expert", [(i, i ^ s) for i in range(groups)]) for s, piece in zip(order[1:], pieces[1:])
    ]


def partner_plan(
    grad_hidden, grad_out, grad_route, live_rows, w_down, w_moment, perm, fwd_hidden, fwd_route, fwd_gate
):
    groups = lax.axis_size("expert")
    me = lax.axis_index("expert").astype(jnp.int32).reshape(1)
    capacity = max(4, 2 * grad_hidden.shape[0] // groups)
    ff, d = w_down.shape[1:]
    spread = swap(split(me, w_moment, w_down, groups))
    packed, fwd_slot, gates = pack_rows(
        live_rows, me, perm, grad_route, fwd_route, grad_hidden, grad_out, fwd_hidden, fwd_gate,
        spread[2 * groups // 3], groups, capacity,
    )
    received = swap(packed)
    placed = swap(reorder(me, perm, spread, received[groups // 3]))
    weight_new, moment_new, produced = update(me, received, placed, ff, d)
    return weight_new[None], moment_new[None], finish(fwd_slot, gates, swap(produced))


def lookup(route_ids, mapping):
    columns = jnp.arange(mapping.shape[0], dtype=jnp.int32)
    hits = route_ids[:, None] == columns[None, :]
    return jnp.sum(jnp.where(hits, mapping[None, :], 0), axis=1)


def slot_matrix(target, is_live, groups, capacity):
    columns = jnp.arange(groups, dtype=jnp.int32)
    onehot = ((target[:, None] == columns[None, :]) & is_live[:, None]).astype(jnp.int32)
    ranked = jnp.sum(jnp.cumsum(onehot, axis=0) * onehot, axis=1) - 1
    slot_of = jnp.where(is_live, target * capacity + ranked, -1)
    slots = jnp.arange(groups * capacity, dtype=jnp.int32)
    return (slots[:, None] == slot_of[None, :]).astype(jnp.bfloat16)


def orthogonalize(moment):
    moment_f = moment.astype(jnp.float32)
    frobenius = jnp.sqrt(jnp.sum(moment_f * moment_f))
    current = (moment_f / (frobenius + norm_floor)).astype(jnp.bfloat16)
    for sweep_index in range(2):
        gramian = lax.dot_general(
            current, current, (((1,), (1,)), ((), ())), preferred_element_type=jnp.float32
        ).astype(jnp.bfloat16)
        squared = jnp.dot(gramian, gramian, preferred_element_type=jnp.float32)
        poly = (cubic_term * gramian.astype(jnp.float32) + quintic_term * squared).astype(
            jnp.bfloat16
        )
        current = (
            linear_term * current.astype(jnp.float32)
            + jnp.dot(poly, current, preferred_element_type=jnp.float32)
        ).astype(jnp.bfloat16)
    return current


def relocate(weight, moment, perm):
    groups = lax.axis_size("expert")
    weight_flat = weight.reshape(groups, -1)
    moment_flat = moment.reshape(groups, -1)
    spread_w, spread_m = (
        lax.all_to_all(weight_flat, "expert", split_axis=0, concat_axis=0, tiled=True),
        lax.all_to_all(moment_flat, "expert", split_axis=0, concat_axis=0, tiled=True),
    )
    devices = jnp.arange(groups, dtype=jnp.int32)
    inverse = jnp.sum(jnp.where(perm[None, :] == devices[:, None], devices[None, :], 0), axis=1)
    ordered_w = jnp.take(spread_w, inverse, axis=0)
    ordered_m = jnp.take(spread_m, inverse, axis=0)
    back_w, back_m = (
        lax.all_to_all(ordered_w, "expert", split_axis=0, concat_axis=0, tiled=True),
        lax.all_to_all(ordered_m, "expert", split_axis=0, concat_axis=0, tiled=True),
    )
    return (back_w.reshape(weight.shape), back_m.reshape(moment.shape))


def routed_plan(
    grad_hidden,
    grad_out,
    grad_route,
    live_rows,
    w_down,
    w_moment,
    perm,
    fwd_hidden,
    fwd_route,
    fwd_gate,
):
    groups = lax.axis_size("expert")
    grad_count = grad_hidden.shape[0]
    capacity = max(4, 2 * grad_count // groups)
    is_live = jnp.arange(grad_count, dtype=jnp.int32) < live_rows[0]
    route_ids = grad_route[:, 0]
    weight, moment = relocate(w_down, w_moment, perm)
    target = lookup(route_ids, perm)
    selector = slot_matrix(target, is_live, groups, capacity)
    hidden_buf = (
        jnp.dot(selector, grad_hidden, preferred_element_type=jnp.float32)
        .astype(jnp.bfloat16)
        .reshape(groups, capacity, -1)
    )
    outgrad_buf = (
        jnp.dot(selector, grad_out, preferred_element_type=jnp.float32)
        .astype(jnp.bfloat16)
        .reshape(groups, capacity, -1)
    )
    recv_hidden, recv_outgrad = (
        lax.all_to_all(hidden_buf, "expert", split_axis=0, concat_axis=0, tiled=True),
        lax.all_to_all(outgrad_buf, "expert", split_axis=0, concat_axis=0, tiled=True),
    )
    grad = lax.dot_general(
        recv_hidden.reshape(groups * capacity, -1),
        recv_outgrad.reshape(groups * capacity, -1),
        (((0,), (0,)), ((), ())),
        preferred_element_type=jnp.float32,
    )
    moment_new = (moment_decay * moment[0].astype(jnp.float32) + grad).astype(jnp.bfloat16)
    ortho = orthogonalize(moment_new)
    weight_new = (weight[0].astype(jnp.float32) - step_scale * ortho.astype(jnp.float32)).astype(
        jnp.bfloat16
    )
    weight_new = weight_new[None]
    moment_new = moment_new[None]
    fwd_ids = fwd_route[:, 0]
    placed_weight, placed_moment = (weight_new, moment_new)
    fwd_target = lookup(fwd_ids, perm)
    fwd_weight = weight_new[0]
    fwd_count = fwd_hidden.shape[0]
    fwd_capacity = max(4, 2 * fwd_count // groups)
    fwd_selector = slot_matrix(fwd_target, jnp.ones((fwd_count,), dtype=bool), groups, fwd_capacity)
    fwd_buf = (
        jnp.dot(fwd_selector, fwd_hidden, preferred_element_type=jnp.float32)
        .astype(jnp.bfloat16)
        .reshape(groups, fwd_capacity, -1)
    )
    produced = jnp.einsum(
        "gkf,fd->gkd",
        lax.all_to_all(fwd_buf, "expert", split_axis=0, concat_axis=0, tiled=True),
        fwd_weight,
        preferred_element_type=jnp.float32,
    ).astype(jnp.bfloat16)
    returned = lax.all_to_all(produced, "expert", split_axis=0, concat_axis=0, tiled=True)
    fwd_rows_out = lax.dot_general(
        fwd_selector,
        returned.reshape(groups * fwd_capacity, -1),
        (((0,), (0,)), ((), ())),
        preferred_element_type=jnp.float32,
    )
    fwd_out = (fwd_rows_out * fwd_gate[:, None]).astype(jnp.bfloat16)
    return (placed_weight, placed_moment, fwd_out)


def solution(mesh):
    groups = mesh.shape["expert"]
    in_specs = (
        P(("layer", "expert"), None),
        P(("layer", "expert"), None),
        P(("layer", "expert"), None),
        P(("layer", "expert")),
        P(("layer", "expert"), None, None),
        P(("layer", "expert"), None, None),
        P("layer"),
        P(("layer", "expert"), None),
        P(("layer", "expert"), None),
        P(("layer", "expert")),
    )
    out_specs = (
        P(("layer", "expert"), None, None),
        P(("layer", "expert"), None, None),
        P(("layer", "expert"), None),
    )

    def per_device(*args):
        few = groups & (groups - 1) == 0 and groups <= 2 * args[0].shape[0] // groups
        return (partner_plan if few else routed_plan)(*args)

    return jax.shard_map(
        per_device, mesh=mesh, in_specs=in_specs, out_specs=out_specs, check_vma=False
    )
```

```python
import functools

import jax
import jax.numpy as jnp
from jax import lax
from jax.experimental import pallas as pl
from jax.experimental.pallas import tpu as pltpu
from jax.sharding import PartitionSpec as P

linear_term = 3.4445
cubic_term = -4.775
quintic_term = 2.0315
moment_decay = 0.9
step_scale = 0.25
norm_floor = 1e-07

F32 = jnp.float32
BF16 = jnp.bfloat16
HBM = pl.BlockSpec(memory_space=pltpu.HBM)
VMEM = pl.BlockSpec(memory_space=pltpu.VMEM)
SMEM = pl.BlockSpec(memory_space=pltpu.SMEM)
ANY = pl.BlockSpec(memory_space=pl.ANY)
MIB = 1 << 20


def fetched(refs, held, sem):
    copies = [pltpu.make_async_copy(ref, room, sem.at[n]) for n, (ref, room) in enumerate(zip(refs, held))]
    for copy in copies:
        copy.start()
    for copy in copies:
        copy.wait()


def rooms(arrays):
    return [pltpu.VMEM(a.shape, a.dtype) for a in arrays] + [pltpu.SemaphoreType.DMA((len(arrays),))]


def chunk_at(ref, lead, k, rows, columns):
    return ref.at[
        lead,
        pl.ds(pl.multiple_of((k // 2) * rows, rows), rows),
        pl.ds(pl.multiple_of((k % 2) * columns, columns), columns),
    ]


def slot_rows(route, live, groups, capacity, me_ref, perm_ref):
    rows = route.shape[1]
    experts = lax.broadcasted_iota(jnp.int32, (groups, rows), 0)
    onehot = jnp.where((experts == route) & live, 1.0, 0.0).astype(BF16)
    before = lax.broadcasted_iota(jnp.int32, (rows, rows), 0)
    after = lax.broadcasted_iota(jnp.int32, (rows, rows), 1)
    upto = jnp.where(before <= after, 1.0, 0.0).astype(BF16)
    ranks = jnp.dot(onehot, upto, preferred_element_type=F32)
    rank = jnp.sum(ranks * onehot.astype(F32), axis=0, keepdims=True).astype(jnp.int32) - 1
    partner = jnp.zeros_like(route)
    for e in range(groups):
        partner = jnp.where(route == e, perm_ref[e] ^ me_ref[0], partner)
    return jnp.where(live, partner * capacity + rank, -1)


def selector_of(slot, slots):
    rows = slot.shape[1]
    places = lax.broadcasted_iota(jnp.int32, (slots, rows), 0)
    return jnp.where(places == slot, 1.0, 0.0).astype(BF16)


def pack_kernel(groups, live_ref, me_ref, perm_ref, *refs):
    sources, pieces, (slot_ref, gates_ref) = refs[:6], refs[7 : 7 + groups], refs[7 + groups : 9 + groups]
    held, sem = refs[9 + groups : 15 + groups], refs[-1]
    route_ref, fwd_route_ref, hidden_ref, out_ref, fwd_ref, gate_ref = held
    copies = [pltpu.make_async_copy(ref, room, sem.at[n]) for n, (ref, room) in enumerate(zip(sources, held))]
    for copy in copies:
        copy.start()
    rows, ff = hidden_ref.shape
    d = out_ref.shape[1]
    capacity = pieces[0].shape[0]
    slots = groups * capacity
    place = lax.broadcasted_iota(jnp.int32, (1, rows), 1)

    def fill(first, selector, source_ref):
        chosen = jnp.dot(selector, source_ref[...], preferred_element_type=F32).astype(BF16)
        for s, piece in zip(mixed_order(groups), pieces):
            piece[:, first : first + source_ref.shape[1]] = chosen[s * capacity : (s + 1) * capacity]

    copies[0].wait()
    slot = slot_rows(route_ref[...], place < live_ref[0], groups, capacity, me_ref, perm_ref)
    selector = selector_of(slot, slots)
    copies[1].wait()
    fwd_slot = slot_rows(fwd_route_ref[...], place >= 0, groups, capacity, me_ref, perm_ref)
    slot_ref[...] = fwd_slot
    copies[2].wait()
    fill(0, selector, hidden_ref)
    copies[3].wait()
    fill(ff, selector, out_ref)
    copies[4].wait()
    fill(ff + d, selector_of(fwd_slot, slots), fwd_ref)
    copies[5].wait()
    down = lax.broadcasted_iota(jnp.int32, (rows, rows), 0)
    across = lax.broadcasted_iota(jnp.int32, (rows, rows), 1)
    gates_ref[...] = jnp.sum(jnp.where(down == across, gate_ref[...], 0.0), axis=1, keepdims=True)


def pack_rows(live_rows, me, perm, route, fwd_route, hidden, grad_out, fwd_hidden, gate, earlier, groups, capacity):
    rows, ff = hidden.shape
    width = 2 * ff + grad_out.shape[1]
    sources = (route.reshape(1, rows), fwd_route.reshape(1, rows), hidden, grad_out, fwd_hidden, gate.reshape(1, rows))
    *pieces, slot, gates = pl.pallas_call(
        functools.partial(pack_kernel, groups),
        out_shape=(jax.ShapeDtypeStruct((capacity, width), BF16),) * groups
        + (jax.ShapeDtypeStruct((1, rows), jnp.int32), jax.ShapeDtypeStruct((rows, 1), F32)),
        in_specs=[SMEM] * 3 + [HBM] * 6 + [VMEM],
        out_specs=(VMEM,) * (groups + 2),
        scratch_shapes=[pltpu.VMEM(a.shape, a.dtype) for a in sources] + [pltpu.SemaphoreType.DMA((len(sources),))],
        compiler_params=pltpu.CompilerParams(vmem_limit_bytes=32 * MIB),
        cost_estimate=pl.CostEstimate(
            flops=2 * groups * capacity * rows * width, bytes_accessed=6 * rows * width, transcendentals=0
        ),
        name="pack_rows",
    )(live_rows, me, perm, *sources, earlier)
    return pieces, slot, gates


def split_kernel(partners, me_ref, moment_ref, weight_ref, *refs):
    pieces, sem = refs[:-1], refs[-1]
    copies = []
    for s, piece in zip(partners, pieces):
        rows, columns = piece.shape[1:]
        for lead, source in enumerate((moment_ref, weight_ref)):
            chunk = chunk_at(source, 0, me_ref[0] ^ s, rows, columns)
            copies.append(pltpu.make_async_copy(chunk, piece.at[lead], sem.at[len(copies)]))
    for copy in copies:
        copy.start()
    for copy in copies:
        copy.wait()


def split(me, moment, weight, groups, partners):
    _, ff, d = weight.shape
    piece = jax.ShapeDtypeStruct((2, ff // (groups // 2), d // 2), BF16)
    return pl.pallas_call(
        functools.partial(split_kernel, partners),
        out_shape=(piece,) * len(partners),
        in_specs=[SMEM, HBM, HBM],
        out_specs=(VMEM,) * len(partners),
        scratch_shapes=[pltpu.SemaphoreType.DMA((2 * len(partners),))],
        compiler_params=pltpu.CompilerParams(vmem_limit_bytes=60 * MIB),
        cost_estimate=pl.CostEstimate(
            flops=0, bytes_accessed=8 * ff * d * len(partners) // groups, transcendentals=0
        ),
        name="split",
    )(me, moment, weight)


def reorder_kernel(me_ref, perm_ref, *refs):
    groups = len(refs) // 2 - 1
    sources, targets, held = refs[:groups], refs[groups + 1 : 2 * groups + 1], refs[-1]
    me, order = me_ref[0], mixed_order(groups)
    for s, source in zip(order, sources):
        held[me ^ perm_ref[me ^ s]] = source[...]
    for s, target in zip(ending_near(groups), targets):
        target[...] = held[s]


def reorder(me, perm, pieces, earlier):
    groups = len(pieces)
    piece = jax.ShapeDtypeStruct(pieces[0].shape, BF16)
    return pl.pallas_call(
        reorder_kernel,
        out_shape=(piece,) * groups,
        in_specs=[SMEM, SMEM] + [VMEM] * (groups + 1),
        out_specs=(VMEM,) * groups,
        scratch_shapes=[pltpu.VMEM((groups,) + pieces[0].shape, BF16)],
        compiler_params=pltpu.CompilerParams(vmem_limit_bytes=32 * MIB),
        cost_estimate=pl.CostEstimate(flops=0, bytes_accessed=4 * groups * pieces[0].size, transcendentals=0),
        name="reorder",
    )(me, perm, *pieces, earlier)


def update_kernel(groups, me_ref, *refs):
    packed, pieces, produced = refs[:groups], refs[groups : 2 * groups], refs[2 * groups + 2 : 3 * groups + 2]
    weight_new_ref, moment_new_ref = refs[2 * groups : 2 * groups + 2]
    held, rows_ref = refs[-2:]
    _, ff, d = held.shape
    capacity = packed[0].shape[0]
    for n, piece in enumerate(packed):
        rows_ref[n * capacity : (n + 1) * capacity] = piece[...]
    for s, piece in zip(ending_near(groups), pieces):
        rows, columns = piece.shape[1:]
        for lead in range(2):
            chunk_at(held, lead, me_ref[0] ^ s, rows, columns)[...] = piece[lead]
    grad = lax.dot_general(
        rows_ref[:, :ff], rows_ref[:, ff : ff + d], (((0,), (0,)), ((), ())), preferred_element_type=F32
    )
    moment_new = (moment_decay * held[0].astype(F32) + grad).astype(BF16)
    moment_new_ref[...] = moment_new
    moment_f = moment_new.astype(F32)
    frobenius = jnp.sqrt(jnp.sum(moment_f * moment_f))
    current = (moment_f / (frobenius + norm_floor)).astype(BF16)
    for _ in range(2):
        gramian = lax.dot_general(
            current, current, (((1,), (1,)), ((), ())), preferred_element_type=F32
        ).astype(BF16)
        squared = jnp.dot(gramian, gramian, preferred_element_type=F32)
        poly = (cubic_term * gramian.astype(F32) + quintic_term * squared).astype(BF16)
        current = (
            linear_term * current.astype(F32) + jnp.dot(poly, current, preferred_element_type=F32)
        ).astype(BF16)
    weight_new = (held[1].astype(F32) - step_scale * current.astype(F32)).astype(BF16)
    weight_new_ref[...] = weight_new
    product = jnp.dot(rows_ref[:, ff + d :], weight_new, preferred_element_type=F32).astype(BF16)
    came = mixed_order(groups)
    for s, piece in zip(ending_near(groups), produced):
        n = came.index(s)
        piece[...] = product[n * capacity : (n + 1) * capacity]


def update(me, packed, pieces, ff, d):
    groups = len(pieces)
    capacity, width = packed[0].shape
    slots = groups * capacity
    shape = jax.ShapeDtypeStruct((ff, d), BF16)
    weight_new, moment_new, *produced = pl.pallas_call(
        functools.partial(update_kernel, groups),
        out_shape=(shape, shape) + (jax.ShapeDtypeStruct((capacity, d), BF16),) * groups,
        in_specs=[SMEM] + [VMEM] * (2 * groups),
        out_specs=(VMEM,) * (groups + 2),
        scratch_shapes=[pltpu.VMEM((2, ff, d), BF16), pltpu.VMEM((slots, width), BF16)],
        compiler_params=pltpu.CompilerParams(vmem_limit_bytes=40 * MIB),
        cost_estimate=pl.CostEstimate(
            flops=4 * ff * d * slots + 8 * ff * ff * d + 4 * ff**3,
            bytes_accessed=8 * ff * d + 2 * slots * (width + d),
            transcendentals=1,
        ),
        name="update",
    )(me, *packed, *pieces)
    return weight_new, moment_new, produced


def finish_kernel(groups, slot_ref, gates_ref, *refs):
    pieces, (out_ref, returned_ref) = refs[:groups], refs[groups:]
    capacity = pieces[0].shape[0]
    for s, piece in zip(ending_near(groups), pieces):
        returned_ref[s * capacity : (s + 1) * capacity] = piece[...]
    selector = selector_of(slot_ref[...], groups * capacity)
    expert_out = lax.dot_general(
        selector, returned_ref[...], (((0,), (0,)), ((), ())), preferred_element_type=F32
    )
    out_ref[...] = (gates_ref[...] * expert_out).astype(BF16)


def finish(slot, gates, returned):
    groups = len(returned)
    rows = slot.shape[1]
    capacity, d = returned[0].shape
    slots = groups * capacity
    return pl.pallas_call(
        functools.partial(finish_kernel, groups),
        out_shape=jax.ShapeDtypeStruct((rows, d), BF16),
        in_specs=[VMEM] * (2 + groups),
        out_specs=VMEM,
        scratch_shapes=[pltpu.VMEM((slots, d), BF16)],
        compiler_params=pltpu.CompilerParams(vmem_limit_bytes=32 * MIB),
        cost_estimate=pl.CostEstimate(
            flops=2 * slots * rows * d, bytes_accessed=2 * d * (slots + rows), transcendentals=0
        ),
        name="finish",
    )(slot, gates, *returned)


def mixed_order(groups):
    def both_ends(partners):
        middle = (len(partners) + 1) // 2
        first, second = partners[:middle], partners[middle:]
        return [s for pair in zip(first, second + [None]) for s in pair if s is not None]

    half = groups // 2
    far, near = both_ends(list(range(half, groups))), both_ends(list(range(half - 1, 0, -1)))
    return [0] + [s for pair in zip(far, near + [None]) for s in pair if s is not None]


def ending_near(groups):
    order = mixed_order(groups)
    return order[:-4] + [order[n] for n in (-3, -4, -1, -2)] if groups > 4 else order


def swap(pieces, order):
    groups = lax.axis_size("expert")
    return [
        lax.ppermute(piece, "expert", [(i, i ^ s) for i in range(groups)]) if s else piece
        for s, piece in zip(order, pieces)
    ]


def partner_plan(
    grad_hidden, grad_out, grad_route, live_rows, w_down, w_moment, perm, fwd_hidden, fwd_route, fwd_gate
):
    groups = lax.axis_size("expert")
    me = lax.axis_index("expert").astype(jnp.int32).reshape(1)
    capacity = max(4, 2 * grad_hidden.shape[0] // groups)
    ff, d = w_down.shape[1:]
    order, last_order = mixed_order(groups), ending_near(groups)
    first = order[1:6]
    blocks = dict(zip(first, split(me, w_moment, w_down, groups, first)))
    others = [s for s in order if s not in first]
    blocks.update(zip(others, split(me, w_moment, w_down, groups, others)))
    spread = swap([blocks[s] for s in order], order)
    packed, fwd_slot, gates = pack_rows(
        live_rows, me, perm, grad_route, fwd_route, grad_hidden, grad_out, fwd_hidden, fwd_gate,
        spread[1], groups, capacity,
    )
    received = swap(packed, order)
    placed = swap(reorder(me, perm, spread, received[groups // 3]), last_order)
    weight_new, moment_new, produced = update(me, received, placed, ff, d)
    return weight_new[None], moment_new[None], finish(fwd_slot, gates, swap(produced, last_order))


def lookup(route_ids, mapping):
    columns = jnp.arange(mapping.shape[0], dtype=jnp.int32)
    hits = route_ids[:, None] == columns[None, :]
    return jnp.sum(jnp.where(hits, mapping[None, :], 0), axis=1)


def slot_matrix(target, is_live, groups, capacity):
    columns = jnp.arange(groups, dtype=jnp.int32)
    onehot = ((target[:, None] == columns[None, :]) & is_live[:, None]).astype(jnp.int32)
    ranked = jnp.sum(jnp.cumsum(onehot, axis=0) * onehot, axis=1) - 1
    slot_of = jnp.where(is_live, target * capacity + ranked, -1)
    slots = jnp.arange(groups * capacity, dtype=jnp.int32)
    return (slots[:, None] == slot_of[None, :]).astype(jnp.bfloat16)


def orthogonalize(moment):
    moment_f = moment.astype(jnp.float32)
    frobenius = jnp.sqrt(jnp.sum(moment_f * moment_f))
    current = (moment_f / (frobenius + norm_floor)).astype(jnp.bfloat16)
    for sweep_index in range(2):
        gramian = lax.dot_general(
            current, current, (((1,), (1,)), ((), ())), preferred_element_type=jnp.float32
        ).astype(jnp.bfloat16)
        squared = jnp.dot(gramian, gramian, preferred_element_type=jnp.float32)
        poly = (cubic_term * gramian.astype(jnp.float32) + quintic_term * squared).astype(
            jnp.bfloat16
        )
        current = (
            linear_term * current.astype(jnp.float32)
            + jnp.dot(poly, current, preferred_element_type=jnp.float32)
        ).astype(jnp.bfloat16)
    return current


def relocate(weight, moment, perm):
    groups = lax.axis_size("expert")
    weight_flat = weight.reshape(groups, -1)
    moment_flat = moment.reshape(groups, -1)
    spread_w, spread_m = (
        lax.all_to_all(weight_flat, "expert", split_axis=0, concat_axis=0, tiled=True),
        lax.all_to_all(moment_flat, "expert", split_axis=0, concat_axis=0, tiled=True),
    )
    devices = jnp.arange(groups, dtype=jnp.int32)
    inverse = jnp.sum(jnp.where(perm[None, :] == devices[:, None], devices[None, :], 0), axis=1)
    ordered_w = jnp.take(spread_w, inverse, axis=0)
    ordered_m = jnp.take(spread_m, inverse, axis=0)
    back_w, back_m = (
        lax.all_to_all(ordered_w, "expert", split_axis=0, concat_axis=0, tiled=True),
        lax.all_to_all(ordered_m, "expert", split_axis=0, concat_axis=0, tiled=True),
    )
    return (back_w.reshape(weight.shape), back_m.reshape(moment.shape))


def routed_plan(
    grad_hidden,
    grad_out,
    grad_route,
    live_rows,
    w_down,
    w_moment,
    perm,
    fwd_hidden,
    fwd_route,
    fwd_gate,
):
    groups = lax.axis_size("expert")
    grad_count = grad_hidden.shape[0]
    capacity = max(4, 2 * grad_count // groups)
    is_live = jnp.arange(grad_count, dtype=jnp.int32) < live_rows[0]
    route_ids = grad_route[:, 0]
    weight, moment = relocate(w_down, w_moment, perm)
    target = lookup(route_ids, perm)
    selector = slot_matrix(target, is_live, groups, capacity)
    hidden_buf = (
        jnp.dot(selector, grad_hidden, preferred_element_type=jnp.float32)
        .astype(jnp.bfloat16)
        .reshape(groups, capacity, -1)
    )
    outgrad_buf = (
        jnp.dot(selector, grad_out, preferred_element_type=jnp.float32)
        .astype(jnp.bfloat16)
        .reshape(groups, capacity, -1)
    )
    recv_hidden, recv_outgrad = (
        lax.all_to_all(hidden_buf, "expert", split_axis=0, concat_axis=0, tiled=True),
        lax.all_to_all(outgrad_buf, "expert", split_axis=0, concat_axis=0, tiled=True),
    )
    grad = lax.dot_general(
        recv_hidden.reshape(groups * capacity, -1),
        recv_outgrad.reshape(groups * capacity, -1),
        (((0,), (0,)), ((), ())),
        preferred_element_type=jnp.float32,
    )
    moment_new = (moment_decay * moment[0].astype(jnp.float32) + grad).astype(jnp.bfloat16)
    ortho = orthogonalize(moment_new)
    weight_new = (weight[0].astype(jnp.float32) - step_scale * ortho.astype(jnp.float32)).astype(
        jnp.bfloat16
    )
    weight_new = weight_new[None]
    moment_new = moment_new[None]
    fwd_ids = fwd_route[:, 0]
    placed_weight, placed_moment = (weight_new, moment_new)
    fwd_target = lookup(fwd_ids, perm)
    fwd_weight = weight_new[0]
    fwd_count = fwd_hidden.shape[0]
    fwd_capacity = max(4, 2 * fwd_count // groups)
    fwd_selector = slot_matrix(fwd_target, jnp.ones((fwd_count,), dtype=bool), groups, fwd_capacity)
    fwd_buf = (
        jnp.dot(fwd_selector, fwd_hidden, preferred_element_type=jnp.float32)
        .astype(jnp.bfloat16)
        .reshape(groups, fwd_capacity, -1)
    )
    produced = jnp.einsum(
        "gkf,fd->gkd",
        lax.all_to_all(fwd_buf, "expert", split_axis=0, concat_axis=0, tiled=True),
        fwd_weight,
        preferred_element_type=jnp.float32,
    ).astype(jnp.bfloat16)
    returned = lax.all_to_all(produced, "expert", split_axis=0, concat_axis=0, tiled=True)
    fwd_rows_out = lax.dot_general(
        fwd_selector,
        returned.reshape(groups * fwd_capacity, -1),
        (((0,), (0,)), ((), ())),
        preferred_element_type=jnp.float32,
    )
    fwd_out = (fwd_rows_out * fwd_gate[:, None]).astype(jnp.bfloat16)
    return (placed_weight, placed_moment, fwd_out)


def solution(mesh):
    groups = mesh.shape["expert"]
    in_specs = (
        P(("layer", "expert"), None),
        P(("layer", "expert"), None),
        P(("layer", "expert"), None),
        P(("layer", "expert")),
        P(("layer", "expert"), None, None),
        P(("layer", "expert"), None, None),
        P("layer"),
        P(("layer", "expert"), None),
        P(("layer", "expert"), None),
        P(("layer", "expert")),
    )
    out_specs = (
        P(("layer", "expert"), None, None),
        P(("layer", "expert"), None, None),
        P(("layer", "expert"), None),
    )

    def per_device(*args):
        few = groups & (groups - 1) == 0 and groups <= 2 * args[0].shape[0] // groups
        return (partner_plan if few else routed_plan)(*args)

    return jax.shard_map(
        per_device, mesh=mesh, in_specs=in_specs, out_specs=out_specs, check_vma=False
    )
```

```python
import functools

import jax
import jax.numpy as jnp
from jax import lax
from jax.experimental import pallas as pl
from jax.experimental.pallas import tpu as pltpu
from jax.sharding import PartitionSpec as P

linear_term = 3.4445
cubic_term = -4.775
quintic_term = 2.0315
moment_decay = 0.9
step_scale = 0.25
norm_floor = 1e-07

F32 = jnp.float32
BF16 = jnp.bfloat16
HBM = pl.BlockSpec(memory_space=pltpu.HBM)
VMEM = pl.BlockSpec(memory_space=pltpu.VMEM)
SMEM = pl.BlockSpec(memory_space=pltpu.SMEM)
ANY = pl.BlockSpec(memory_space=pl.ANY)
MIB = 1 << 20


def fetched(refs, held, sem):
    copies = [pltpu.make_async_copy(ref, room, sem.at[n]) for n, (ref, room) in enumerate(zip(refs, held))]
    for copy in copies:
        copy.start()
    for copy in copies:
        copy.wait()


def rooms(arrays):
    return [pltpu.VMEM(a.shape, a.dtype) for a in arrays] + [pltpu.SemaphoreType.DMA((len(arrays),))]


def chunk_at(ref, lead, k, rows, columns):
    return ref.at[
        lead,
        pl.ds(pl.multiple_of((k // 2) * rows, rows), rows),
        pl.ds(pl.multiple_of((k % 2) * columns, columns), columns),
    ]


def placed_rows(route, live, groups, me_ref, perm_ref):
    rows = route.shape[1]
    experts = lax.broadcasted_iota(jnp.int32, (groups, rows), 0)
    onehot = jnp.where((experts == route) & live, 1.0, 0.0).astype(BF16)
    ranks = jnp.dot(onehot, upto(rows), preferred_element_type=F32)
    rank = jnp.sum(ranks * onehot.astype(F32), axis=0, keepdims=True).astype(jnp.int32) - 1
    partner = jnp.zeros_like(route)
    for e in range(groups):
        partner = jnp.where(route == e, perm_ref[e] ^ me_ref[0], partner)
    return partner, rank


def upto(rows):
    before = lax.broadcasted_iota(jnp.int32, (rows, rows), 0)
    after = lax.broadcasted_iota(jnp.int32, (rows, rows), 1)
    return jnp.where(before <= after, 1.0, 0.0).astype(BF16)


def selector_of(slot, slots):
    rows = slot.shape[1]
    places = lax.broadcasted_iota(jnp.int32, (slots, rows), 0)
    return jnp.where(places == slot, 1.0, 0.0).astype(BF16)


def pack_kernel(groups, live_ref, me_ref, perm_ref, *refs):
    sources, (near_ref, *far_refs, info_ref, slot_ref, gates_ref) = refs[:6], refs[6:12]
    held, sem = refs[12:18], refs[-1]
    route_ref, fwd_route_ref, hidden_ref, out_ref, fwd_ref, gate_ref = held
    copies = [pltpu.make_async_copy(ref, room, sem.at[n]) for n, (ref, room) in enumerate(zip(sources, held))]
    for copy in copies:
        copy.start()
    rows, ff = hidden_ref.shape
    d = out_ref.shape[1]
    half = groups // 2
    capacity = near_ref.shape[0] // half
    place = lax.broadcasted_iota(jnp.int32, (1, rows), 1)

    def fill(first, near, far, source_ref):
        columns = slice(first, first + source_ref.shape[1])
        near_ref[:, columns] = jnp.dot(near, source_ref[...], preferred_element_type=F32).astype(BF16)
        chosen = jnp.dot(far, source_ref[...], preferred_element_type=F32).astype(BF16)
        start = 0
        for far_ref in far_refs:
            far_ref[:, columns] = chosen[start : start + far_ref.shape[0]]
            start += far_ref.shape[0]

    def selectors(n, route, live):
        partner, rank = placed_rows(route, live, groups, me_ref, perm_ref)
        slot = (partner % half) * capacity + rank
        is_far = live & (partner >= half)
        near = selector_of(jnp.where(live & (partner < half), slot, -1), half * capacity)
        order = jnp.dot(
            jnp.broadcast_to(jnp.where(is_far, 1.0, 0.0), (8, rows)).astype(BF16), upto(rows),
            preferred_element_type=F32,
        )[:1].astype(jnp.int32) - 1
        far = selector_of(jnp.where(is_far, order, -1), rows)
        after = jnp.broadcast_to(jnp.where(is_far, slot + 1, 0), (8, rows)).astype(F32).astype(BF16)
        info = lax.dot_general(after, far, (((1,), (1,)), ((), ())), preferred_element_type=F32)
        info_ref[n : n + 1] = info[:1].astype(jnp.int32) - 1
        return near, far, jnp.where(live, partner * capacity + rank, -1)

    copies[0].wait()
    near, far, _ = selectors(0, route_ref[...], place < live_ref[0])
    copies[1].wait()
    fwd_near, fwd_far, slot_ref[...] = selectors(1, fwd_route_ref[...], place >= 0)
    copies[2].wait()
    fill(0, near, far, hidden_ref)
    copies[3].wait()
    fill(ff, near, far, out_ref)
    copies[4].wait()
    fill(ff + d, fwd_near, fwd_far, fwd_ref)
    copies[5].wait()
    down = lax.broadcasted_iota(jnp.int32, (rows, rows), 0)
    across = lax.broadcasted_iota(jnp.int32, (rows, rows), 1)
    gates_ref[...] = jnp.sum(jnp.where(down == across, gate_ref[...], 0.0), axis=1, keepdims=True)


def pack_rows(live_rows, me, perm, route, fwd_route, hidden, grad_out, fwd_hidden, gate, groups, capacity):
    rows, ff = hidden.shape
    width = 2 * ff + grad_out.shape[1]
    sources = (
        route.reshape(1, rows), fwd_route.reshape(1, rows), hidden, grad_out, fwd_hidden, gate.reshape(1, rows),
    )
    half = groups // 2
    rest = rows // 4
    return pl.pallas_call(
        functools.partial(pack_kernel, groups),
        out_shape=(
            jax.ShapeDtypeStruct((half * capacity, width), BF16),
            jax.ShapeDtypeStruct((rows - rest, width), BF16),
            jax.ShapeDtypeStruct((rest, width), BF16),
            jax.ShapeDtypeStruct((2, rows), jnp.int32),
            jax.ShapeDtypeStruct((1, rows), jnp.int32),
            jax.ShapeDtypeStruct((rows, 1), F32),
        ),
        in_specs=[SMEM] * 3 + [HBM] * 6,
        out_specs=(VMEM,) * 6,
        scratch_shapes=[pltpu.VMEM(a.shape, a.dtype) for a in sources] + [pltpu.SemaphoreType.DMA((len(sources),))],
        compiler_params=pltpu.CompilerParams(vmem_limit_bytes=32 * MIB),
        cost_estimate=pl.CostEstimate(
            flops=2 * groups * capacity * rows * width, bytes_accessed=6 * rows * width, transcendentals=0
        ),
        name="pack_rows",
    )(live_rows, me, perm, *sources)


def repack_kernel(boundary, near_ref, first_ref, second_ref, info_ref, *refs):
    pieces, far_ref = refs[:-1], refs[-1]
    half = len(pieces)
    slots = near_ref.shape[0]
    capacity = slots // half
    far_ref[: first_ref.shape[0]] = first_ref[...]
    far_ref[first_ref.shape[0] :] = second_ref[...]
    for n, columns in enumerate((slice(0, boundary), slice(boundary, None))):
        selector = selector_of(info_ref[n : n + 1], slots)
        chosen = jnp.dot(selector, far_ref[:, columns], preferred_element_type=F32).astype(BF16)
        for s, piece in zip(mixed_order(half), pieces):
            span = slice(s * capacity, (s + 1) * capacity)
            piece[:capacity, columns] = near_ref[span, columns]
            piece[capacity:, columns] = chosen[span]


def repack(near, first, second, info, half, boundary):
    slots, width = near.shape
    rows = first.shape[0] + second.shape[0]
    piece = jax.ShapeDtypeStruct((2 * slots // half, width), BF16)
    return pl.pallas_call(
        functools.partial(repack_kernel, boundary),
        out_shape=(piece,) * half,
        in_specs=[VMEM] * 4,
        out_specs=(VMEM,) * half,
        scratch_shapes=[pltpu.VMEM((rows, width), BF16)],
        compiler_params=pltpu.CompilerParams(vmem_limit_bytes=32 * MIB),
        cost_estimate=pl.CostEstimate(
            flops=2 * slots * rows * width, bytes_accessed=8 * slots * width, transcendentals=0
        ),
        name="repack",
    )(near, first, second, info)


def split_kernel(me_ref, moment_ref, weight_ref, earlier_ref, *refs):
    pieces, held, sem = refs[:-3], refs[-3:-1], refs[-1]
    fetched((moment_ref, weight_ref), held, sem)
    for s, piece in zip(mixed_order(len(pieces)), pieces):
        rows, columns = piece.shape[1:]
        for lead, source in enumerate(held):
            piece[lead] = chunk_at(source, 0, me_ref[0] ^ s, rows, columns)[...]


def split(me, moment, weight, earlier, groups):
    _, ff, d = weight.shape
    piece = jax.ShapeDtypeStruct((2, ff // (groups // 2), d // 2), BF16)
    return pl.pallas_call(
        split_kernel,
        out_shape=(piece,) * groups,
        in_specs=[SMEM, HBM, HBM, VMEM],
        out_specs=(VMEM,) * groups,
        scratch_shapes=rooms((moment, weight)),
        compiler_params=pltpu.CompilerParams(vmem_limit_bytes=60 * MIB),
        cost_estimate=pl.CostEstimate(flops=0, bytes_accessed=8 * ff * d, transcendentals=0),
        name="split",
    )(me, moment, weight, earlier)


def reorder_kernel(me_ref, perm_ref, *refs):
    groups = len(refs) // 2
    sources, targets, held = refs[:groups], refs[groups:-1], refs[-1]
    me, order = me_ref[0], mixed_order(groups)
    for s, source in zip(order, sources):
        held[me ^ perm_ref[me ^ s]] = source[...]
    for s, target in zip(order, targets):
        target[...] = held[s]


def reorder(me, perm, pieces):
    groups = len(pieces)
    piece = jax.ShapeDtypeStruct(pieces[0].shape, BF16)
    return pl.pallas_call(
        reorder_kernel,
        out_shape=(piece,) * groups,
        in_specs=[SMEM, SMEM] + [VMEM] * groups,
        out_specs=(VMEM,) * groups,
        scratch_shapes=[pltpu.VMEM((groups,) + pieces[0].shape, BF16)],
        compiler_params=pltpu.CompilerParams(vmem_limit_bytes=32 * MIB),
        cost_estimate=pl.CostEstimate(flops=0, bytes_accessed=4 * groups * pieces[0].size, transcendentals=0),
        name="reorder",
    )(me, perm, *pieces)


def update_kernel(groups, me_ref, *refs):
    half = groups // 2
    packed, pieces, refs = refs[:half], refs[half : half + groups], refs[half + groups :]
    (weight_new_ref, moment_new_ref), produced, (held, rows_ref) = refs[:2], refs[2:-2], refs[-2:]
    _, ff, d = held.shape
    capacity = produced[0].shape[0]
    for n, piece in enumerate(packed):
        rows_ref[2 * n * capacity : 2 * (n + 1) * capacity] = piece[...]
    for s, piece in zip(mixed_order(groups), pieces):
        rows, columns = piece.shape[1:]
        for lead in range(2):
            chunk_at(held, lead, me_ref[0] ^ s, rows, columns)[...] = piece[lead]
    grad = lax.dot_general(
        rows_ref[:, :ff], rows_ref[:, ff : ff + d], (((0,), (0,)), ((), ())), preferred_element_type=F32
    )
    moment_new = (moment_decay * held[0].astype(F32) + grad).astype(BF16)
    moment_new_ref[...] = moment_new
    moment_f = moment_new.astype(F32)
    frobenius = jnp.sqrt(jnp.sum(moment_f * moment_f))
    current = (moment_f / (frobenius + norm_floor)).astype(BF16)
    for _ in range(2):
        gramian = lax.dot_general(
            current, current, (((1,), (1,)), ((), ())), preferred_element_type=F32
        ).astype(BF16)
        squared = jnp.dot(gramian, gramian, preferred_element_type=F32)
        poly = (cubic_term * gramian.astype(F32) + quintic_term * squared).astype(BF16)
        current = (
            linear_term * current.astype(F32) + jnp.dot(poly, current, preferred_element_type=F32)
        ).astype(BF16)
    weight_new = (held[1].astype(F32) - step_scale * current.astype(F32)).astype(BF16)
    weight_new_ref[...] = weight_new
    product = jnp.dot(rows_ref[:, ff + d :], weight_new, preferred_element_type=F32).astype(BF16)
    came = mixed_order(half)
    for s, piece in zip(mixed_order(groups), produced):
        n = 2 * came.index(s % half) + s // half
        piece[...] = product[n * capacity : (n + 1) * capacity]


def update(me, packed, pieces, ff, d):
    groups, half = len(pieces), len(packed)
    slots, width = half * packed[0].shape[0], packed[0].shape[1]
    capacity = slots // groups
    shape = jax.ShapeDtypeStruct((ff, d), BF16)
    weight_new, moment_new, *produced = pl.pallas_call(
        functools.partial(update_kernel, groups),
        out_shape=(shape, shape) + (jax.ShapeDtypeStruct((capacity, d), BF16),) * groups,
        in_specs=[SMEM] + [VMEM] * (half + groups),
        out_specs=(VMEM,) * (groups + 2),
        scratch_shapes=[pltpu.VMEM((2, ff, d), BF16), pltpu.VMEM((slots, width), BF16)],
        compiler_params=pltpu.CompilerParams(vmem_limit_bytes=40 * MIB),
        cost_estimate=pl.CostEstimate(
            flops=4 * ff * d * slots + 8 * ff * ff * d + 4 * ff**3,
            bytes_accessed=8 * ff * d + 2 * slots * (width + d),
            transcendentals=1,
        ),
        name="update",
    )(me, *packed, *pieces)
    return weight_new, moment_new, produced


def finish_kernel(groups, slot_ref, gates_ref, *refs):
    pieces, (out_ref, returned_ref) = refs[:groups], refs[groups:]
    capacity = pieces[0].shape[0]
    for s, piece in zip(mixed_order(groups), pieces):
        returned_ref[s * capacity : (s + 1) * capacity] = piece[...]
    selector = selector_of(slot_ref[...], groups * capacity)
    expert_out = lax.dot_general(
        selector, returned_ref[...], (((0,), (0,)), ((), ())), preferred_element_type=F32
    )
    out_ref[...] = (gates_ref[...] * expert_out).astype(BF16)


def finish(slot, gates, returned):
    groups = len(returned)
    rows = slot.shape[1]
    capacity, d = returned[0].shape
    slots = groups * capacity
    return pl.pallas_call(
        functools.partial(finish_kernel, groups),
        out_shape=jax.ShapeDtypeStruct((rows, d), BF16),
        in_specs=[VMEM] * (2 + groups),
        out_specs=VMEM,
        scratch_shapes=[pltpu.VMEM((slots, d), BF16)],
        compiler_params=pltpu.CompilerParams(vmem_limit_bytes=32 * MIB),
        cost_estimate=pl.CostEstimate(
            flops=2 * slots * rows * d, bytes_accessed=2 * d * (slots + rows), transcendentals=0
        ),
        name="finish",
    )(slot, gates, *returned)


def mixed_order(groups):
    def both_ends(partners):
        middle = (len(partners) + 1) // 2
        first, second = partners[:middle], partners[middle:]
        return [s for pair in zip(first, second + [None]) for s in pair if s is not None]

    half = groups // 2
    far, near = both_ends(list(range(half, groups))), both_ends(list(range(half - 1, 0, -1)))
    return [0] + [s for pair in zip(far, near + [None]) for s in pair if s is not None]


def swap(pieces, order):
    groups = lax.axis_size("expert")
    return [
        lax.ppermute(piece, "expert", [(i, i ^ s) for i in range(groups)]) if s else piece
        for s, piece in zip(order, pieces)
    ]


def partner_plan(
    grad_hidden, grad_out, grad_route, live_rows, w_down, w_moment, perm, fwd_hidden, fwd_route, fwd_gate
):
    groups = lax.axis_size("expert")
    me = lax.axis_index("expert").astype(jnp.int32).reshape(1)
    capacity = max(4, 2 * grad_hidden.shape[0] // groups)
    ff, d = w_down.shape[1:]
    half, order = groups // 2, mixed_order(groups)
    near, first, second, info, fwd_slot, gates = pack_rows(
        live_rows, me, perm, grad_route, fwd_route, grad_hidden, grad_out, fwd_hidden, fwd_gate, groups, capacity
    )
    spread = swap(split(me, w_moment, w_down, fwd_slot, groups), order)
    first, second, info = swap((first, second, info), (half,) * 3)
    received = swap(repack(near, first, second, info, half, ff + d), mixed_order(half))
    placed = swap(reorder(me, perm, spread), order)
    weight_new, moment_new, produced = update(me, received, placed, ff, d)
    return weight_new[None], moment_new[None], finish(fwd_slot, gates, swap(produced, order))


def lookup(route_ids, mapping):
    columns = jnp.arange(mapping.shape[0], dtype=jnp.int32)
    hits = route_ids[:, None] == columns[None, :]
    return jnp.sum(jnp.where(hits, mapping[None, :], 0), axis=1)


def slot_matrix(target, is_live, groups, capacity):
    columns = jnp.arange(groups, dtype=jnp.int32)
    onehot = ((target[:, None] == columns[None, :]) & is_live[:, None]).astype(jnp.int32)
    ranked = jnp.sum(jnp.cumsum(onehot, axis=0) * onehot, axis=1) - 1
    slot_of = jnp.where(is_live, target * capacity + ranked, -1)
    slots = jnp.arange(groups * capacity, dtype=jnp.int32)
    return (slots[:, None] == slot_of[None, :]).astype(jnp.bfloat16)


def orthogonalize(moment):
    moment_f = moment.astype(jnp.float32)
    frobenius = jnp.sqrt(jnp.sum(moment_f * moment_f))
    current = (moment_f / (frobenius + norm_floor)).astype(jnp.bfloat16)
    for sweep_index in range(2):
        gramian = lax.dot_general(
            current, current, (((1,), (1,)), ((), ())), preferred_element_type=jnp.float32
        ).astype(jnp.bfloat16)
        squared = jnp.dot(gramian, gramian, preferred_element_type=jnp.float32)
        poly = (cubic_term * gramian.astype(jnp.float32) + quintic_term * squared).astype(
            jnp.bfloat16
        )
        current = (
            linear_term * current.astype(jnp.float32)
            + jnp.dot(poly, current, preferred_element_type=jnp.float32)
        ).astype(jnp.bfloat16)
    return current


def relocate(weight, moment, perm):
    groups = lax.axis_size("expert")
    weight_flat = weight.reshape(groups, -1)
    moment_flat = moment.reshape(groups, -1)
    spread_w, spread_m = (
        lax.all_to_all(weight_flat, "expert", split_axis=0, concat_axis=0, tiled=True),
        lax.all_to_all(moment_flat, "expert", split_axis=0, concat_axis=0, tiled=True),
    )
    devices = jnp.arange(groups, dtype=jnp.int32)
    inverse = jnp.sum(jnp.where(perm[None, :] == devices[:, None], devices[None, :], 0), axis=1)
    ordered_w = jnp.take(spread_w, inverse, axis=0)
    ordered_m = jnp.take(spread_m, inverse, axis=0)
    back_w, back_m = (
        lax.all_to_all(ordered_w, "expert", split_axis=0, concat_axis=0, tiled=True),
        lax.all_to_all(ordered_m, "expert", split_axis=0, concat_axis=0, tiled=True),
    )
    return (back_w.reshape(weight.shape), back_m.reshape(moment.shape))


def routed_plan(
    grad_hidden,
    grad_out,
    grad_route,
    live_rows,
    w_down,
    w_moment,
    perm,
    fwd_hidden,
    fwd_route,
    fwd_gate,
):
    groups = lax.axis_size("expert")
    grad_count = grad_hidden.shape[0]
    capacity = max(4, 2 * grad_count // groups)
    is_live = jnp.arange(grad_count, dtype=jnp.int32) < live_rows[0]
    route_ids = grad_route[:, 0]
    weight, moment = relocate(w_down, w_moment, perm)
    target = lookup(route_ids, perm)
    selector = slot_matrix(target, is_live, groups, capacity)
    hidden_buf = (
        jnp.dot(selector, grad_hidden, preferred_element_type=jnp.float32)
        .astype(jnp.bfloat16)
        .reshape(groups, capacity, -1)
    )
    outgrad_buf = (
        jnp.dot(selector, grad_out, preferred_element_type=jnp.float32)
        .astype(jnp.bfloat16)
        .reshape(groups, capacity, -1)
    )
    recv_hidden, recv_outgrad = (
        lax.all_to_all(hidden_buf, "expert", split_axis=0, concat_axis=0, tiled=True),
        lax.all_to_all(outgrad_buf, "expert", split_axis=0, concat_axis=0, tiled=True),
    )
    grad = lax.dot_general(
        recv_hidden.reshape(groups * capacity, -1),
        recv_outgrad.reshape(groups * capacity, -1),
        (((0,), (0,)), ((), ())),
        preferred_element_type=jnp.float32,
    )
    moment_new = (moment_decay * moment[0].astype(jnp.float32) + grad).astype(jnp.bfloat16)
    ortho = orthogonalize(moment_new)
    weight_new = (weight[0].astype(jnp.float32) - step_scale * ortho.astype(jnp.float32)).astype(
        jnp.bfloat16
    )
    weight_new = weight_new[None]
    moment_new = moment_new[None]
    fwd_ids = fwd_route[:, 0]
    placed_weight, placed_moment = (weight_new, moment_new)
    fwd_target = lookup(fwd_ids, perm)
    fwd_weight = weight_new[0]
    fwd_count = fwd_hidden.shape[0]
    fwd_capacity = max(4, 2 * fwd_count // groups)
    fwd_selector = slot_matrix(fwd_target, jnp.ones((fwd_count,), dtype=bool), groups, fwd_capacity)
    fwd_buf = (
        jnp.dot(fwd_selector, fwd_hidden, preferred_element_type=jnp.float32)
        .astype(jnp.bfloat16)
        .reshape(groups, fwd_capacity, -1)
    )
    produced = jnp.einsum(
        "gkf,fd->gkd",
        lax.all_to_all(fwd_buf, "expert", split_axis=0, concat_axis=0, tiled=True),
        fwd_weight,
        preferred_element_type=jnp.float32,
    ).astype(jnp.bfloat16)
    returned = lax.all_to_all(produced, "expert", split_axis=0, concat_axis=0, tiled=True)
    fwd_rows_out = lax.dot_general(
        fwd_selector,
        returned.reshape(groups * fwd_capacity, -1),
        (((0,), (0,)), ((), ())),
        preferred_element_type=jnp.float32,
    )
    fwd_out = (fwd_rows_out * fwd_gate[:, None]).astype(jnp.bfloat16)
    return (placed_weight, placed_moment, fwd_out)


def solution(mesh):
    groups = mesh.shape["expert"]
    in_specs = (
        P(("layer", "expert"), None),
        P(("layer", "expert"), None),
        P(("layer", "expert"), None),
        P(("layer", "expert")),
        P(("layer", "expert"), None, None),
        P(("layer", "expert"), None, None),
        P("layer"),
        P(("layer", "expert"), None),
        P(("layer", "expert"), None),
        P(("layer", "expert")),
    )
    out_specs = (
        P(("layer", "expert"), None, None),
        P(("layer", "expert"), None, None),
        P(("layer", "expert"), None),
    )

    def per_device(*args):
        few = groups & (groups - 1) == 0 and groups <= 2 * args[0].shape[0] // groups
        return (partner_plan if few else routed_plan)(*args)

    return jax.shard_map(
        per_device, mesh=mesh, in_specs=in_specs, out_specs=out_specs, check_vma=False
    )
```

```python
import functools

import jax
import jax.numpy as jnp
from jax import lax
from jax.experimental import pallas as pl
from jax.experimental.pallas import tpu as pltpu
from jax.sharding import PartitionSpec as P

linear_term = 3.4445
cubic_term = -4.775
quintic_term = 2.0315
moment_decay = 0.9
step_scale = 0.25
norm_floor = 1e-07

F32 = jnp.float32
BF16 = jnp.bfloat16
HBM = pl.BlockSpec(memory_space=pltpu.HBM)
VMEM = pl.BlockSpec(memory_space=pltpu.VMEM)
SMEM = pl.BlockSpec(memory_space=pltpu.SMEM)
ANY = pl.BlockSpec(memory_space=pl.ANY)
MIB = 1 << 20


def fetched(refs, held, sem):
    copies = [pltpu.make_async_copy(ref, room, sem.at[n]) for n, (ref, room) in enumerate(zip(refs, held))]
    for copy in copies:
        copy.start()
    for copy in copies:
        copy.wait()


def rooms(arrays):
    return [pltpu.VMEM(a.shape, a.dtype) for a in arrays] + [pltpu.SemaphoreType.DMA((len(arrays),))]


def chunk_at(ref, lead, k, rows, columns):
    return ref.at[
        lead,
        pl.ds(pl.multiple_of((k // 2) * rows, rows), rows),
        pl.ds(pl.multiple_of((k % 2) * columns, columns), columns),
    ]


def slot_rows(route, live, groups, capacity, me_ref, perm_ref):
    rows = route.shape[1]
    experts = lax.broadcasted_iota(jnp.int32, (groups, rows), 0)
    onehot = jnp.where((experts == route) & live, 1.0, 0.0).astype(BF16)
    before = lax.broadcasted_iota(jnp.int32, (rows, rows), 0)
    after = lax.broadcasted_iota(jnp.int32, (rows, rows), 1)
    upto = jnp.where(before <= after, 1.0, 0.0).astype(BF16)
    ranks = jnp.dot(onehot, upto, preferred_element_type=F32)
    rank = jnp.sum(ranks * onehot.astype(F32), axis=0, keepdims=True).astype(jnp.int32) - 1
    partner = jnp.zeros_like(route)
    for e in range(groups):
        partner = jnp.where(route == e, perm_ref[e] ^ me_ref[0], partner)
    return jnp.where(live, partner * capacity + rank, -1)


def selector_of(slot, slots):
    rows = slot.shape[1]
    places = lax.broadcasted_iota(jnp.int32, (slots, rows), 0)
    return jnp.where(places == slot, 1.0, 0.0).astype(BF16)


def pack_kernel(groups, live_ref, me_ref, perm_ref, *refs):
    sources, pieces, (slot_ref, gates_ref) = refs[:6], refs[7 : 7 + groups], refs[7 + groups : 9 + groups]
    held, sem = refs[9 + groups : 15 + groups], refs[-1]
    route_ref, fwd_route_ref, hidden_ref, out_ref, fwd_ref, gate_ref = held
    copies = [pltpu.make_async_copy(ref, room, sem.at[n]) for n, (ref, room) in enumerate(zip(sources, held))]
    for copy in copies:
        copy.start()
    rows, ff = hidden_ref.shape
    d = out_ref.shape[1]
    capacity = pieces[0].shape[0]
    slots = groups * capacity
    place = lax.broadcasted_iota(jnp.int32, (1, rows), 1)

    def fill(first, selector, source_ref):
        chosen = jnp.dot(selector, source_ref[...], preferred_element_type=F32).astype(BF16)
        for s, piece in zip(mixed_order(groups), pieces):
            piece[:, first : first + source_ref.shape[1]] = chosen[s * capacity : (s + 1) * capacity]

    copies[0].wait()
    slot = slot_rows(route_ref[...], place < live_ref[0], groups, capacity, me_ref, perm_ref)
    selector = selector_of(slot, slots)
    copies[1].wait()
    fwd_slot = slot_rows(fwd_route_ref[...], place >= 0, groups, capacity, me_ref, perm_ref)
    slot_ref[...] = fwd_slot
    copies[2].wait()
    fill(0, selector, hidden_ref)
    copies[3].wait()
    fill(ff, selector, out_ref)
    copies[4].wait()
    fill(ff + d, selector_of(fwd_slot, slots), fwd_ref)
    copies[5].wait()
    down = lax.broadcasted_iota(jnp.int32, (rows, rows), 0)
    across = lax.broadcasted_iota(jnp.int32, (rows, rows), 1)
    gates_ref[...] = jnp.sum(jnp.where(down == across, gate_ref[...], 0.0), axis=1, keepdims=True)


def pack_rows(live_rows, me, perm, route, fwd_route, hidden, grad_out, fwd_hidden, gate, earlier, groups, capacity):
    rows, ff = hidden.shape
    width = 2 * ff + grad_out.shape[1]
    sources = (route.reshape(1, rows), fwd_route.reshape(1, rows), hidden, grad_out, fwd_hidden, gate.reshape(1, rows))
    *pieces, slot, gates = pl.pallas_call(
        functools.partial(pack_kernel, groups),
        out_shape=(jax.ShapeDtypeStruct((capacity, width), BF16),) * groups
        + (jax.ShapeDtypeStruct((1, rows), jnp.int32), jax.ShapeDtypeStruct((rows, 1), F32)),
        in_specs=[SMEM] * 3 + [HBM] * 6 + [VMEM],
        out_specs=(VMEM,) * (groups + 2),
        scratch_shapes=[pltpu.VMEM(a.shape, a.dtype) for a in sources] + [pltpu.SemaphoreType.DMA((len(sources),))],
        compiler_params=pltpu.CompilerParams(vmem_limit_bytes=32 * MIB),
        cost_estimate=pl.CostEstimate(
            flops=2 * groups * capacity * rows * width, bytes_accessed=6 * rows * width, transcendentals=0
        ),
        name="pack_rows",
    )(live_rows, me, perm, *sources, earlier)
    return pieces, slot, gates


def split_kernel(me_ref, moment_ref, weight_ref, *refs):
    pieces, held, sem = refs[:-3], refs[-3:-1], refs[-1]
    fetched((moment_ref, weight_ref), held, sem)
    for s, piece in zip(mixed_order(len(pieces)), pieces):
        rows, columns = piece.shape[1:]
        for lead, source in enumerate(held):
            piece[lead] = chunk_at(source, 0, me_ref[0] ^ s, rows, columns)[...]


def split(me, moment, weight, groups):
    _, ff, d = weight.shape
    piece = jax.ShapeDtypeStruct((2, ff // (groups // 2), d // 2), BF16)
    return pl.pallas_call(
        split_kernel,
        out_shape=(piece,) * groups,
        in_specs=[SMEM, HBM, HBM],
        out_specs=(VMEM,) * groups,
        scratch_shapes=rooms((moment, weight)),
        compiler_params=pltpu.CompilerParams(vmem_limit_bytes=60 * MIB),
        cost_estimate=pl.CostEstimate(flops=0, bytes_accessed=8 * ff * d, transcendentals=0),
        name="split",
    )(me, moment, weight)


def apart(groups):
    return mixed_order(groups)[-(groups // 3) :]


def reorder_kernel(me_ref, perm_ref, *refs):
    groups = perm_ref.shape[0]
    sources, targets, held = refs[:groups], refs[groups + 1 : -1], refs[-1]
    me, order, late = me_ref[0], mixed_order(groups), apart(groups)
    for s, source in zip(order, sources):
        held[me ^ perm_ref[me ^ s]] = source[...]
    whole = [s for s in order if s not in late]
    for s, target in zip(whole, targets):
        target[...] = held[s]
    for n, target in enumerate(targets[len(whole) :]):
        target[...] = held[late[n % len(late)], n // len(late)]


def reorder(me, perm, pieces, earlier):
    groups, late = len(pieces), len(apart(len(pieces)))
    shape = pieces[0].shape
    whole, half = jax.ShapeDtypeStruct(shape, BF16), jax.ShapeDtypeStruct(shape[1:], BF16)
    targets = pl.pallas_call(
        reorder_kernel,
        out_shape=(whole,) * (groups - late) + (half,) * (2 * late),
        in_specs=[SMEM, SMEM] + [VMEM] * (groups + 1),
        out_specs=(VMEM,) * (groups + late),
        scratch_shapes=[pltpu.VMEM((groups,) + shape, BF16)],
        compiler_params=pltpu.CompilerParams(vmem_limit_bytes=32 * MIB),
        cost_estimate=pl.CostEstimate(flops=0, bytes_accessed=4 * groups * pieces[0].size, transcendentals=0),
        name="reorder",
    )(me, perm, *pieces, earlier)
    return targets[: groups - late], targets[groups - late : groups], targets[groups:]


def assembled(lead, me_ref, whole, pieces, held):
    groups = len(whole) + len(pieces)
    late = apart(groups)
    rows, columns = pieces[0].shape
    chunks = dict(zip([s for s in mixed_order(groups) if s not in late], [piece.at[lead] for piece in whole]))
    chunks.update(zip(late, pieces))
    for s, chunk in chunks.items():
        chunk_at(held, 0, me_ref[0] ^ s, rows, columns)[...] = chunk[...]
    return held[0].astype(F32)


def orthogonal_kernel(groups, me_ref, *refs):
    packed, whole, pieces = refs[:groups], refs[groups : -4 - len(apart(groups))], refs[-4 - len(apart(groups)) : -4]
    moment_new_ref, ortho_ref, held, rows_ref = refs[-4:]
    ff, d = ortho_ref.shape
    capacity = packed[0].shape[0]
    for n, piece in enumerate(packed):
        rows_ref[n * capacity : (n + 1) * capacity] = piece[:, : ff + d]
    grad = lax.dot_general(
        rows_ref[:, :ff], rows_ref[:, ff:], (((0,), (0,)), ((), ())), preferred_element_type=F32
    )
    moment_new = (moment_decay * assembled(0, me_ref, whole, pieces, held) + grad).astype(BF16)
    moment_new_ref[...] = moment_new
    moment_f = moment_new.astype(F32)
    frobenius = jnp.sqrt(jnp.sum(moment_f * moment_f))
    current = (moment_f / (frobenius + norm_floor)).astype(BF16)
    for _ in range(2):
        gramian = lax.dot_general(
            current, current, (((1,), (1,)), ((), ())), preferred_element_type=F32
        ).astype(BF16)
        squared = jnp.dot(gramian, gramian, preferred_element_type=F32)
        poly = (cubic_term * gramian.astype(F32) + quintic_term * squared).astype(BF16)
        current = (
            linear_term * current.astype(F32) + jnp.dot(poly, current, preferred_element_type=F32)
        ).astype(BF16)
    ortho_ref[...] = current


def orthogonal(me, packed, whole, pieces, ff, d):
    groups = len(packed)
    slots = groups * packed[0].shape[0]
    shape = jax.ShapeDtypeStruct((ff, d), BF16)
    return pl.pallas_call(
        functools.partial(orthogonal_kernel, groups),
        out_shape=(shape, shape),
        in_specs=[SMEM] + [VMEM] * (2 * groups),
        out_specs=(VMEM, VMEM),
        scratch_shapes=[pltpu.VMEM((1, ff, d), BF16), pltpu.VMEM((slots, ff + d), BF16)],
        compiler_params=pltpu.CompilerParams(vmem_limit_bytes=40 * MIB),
        cost_estimate=pl.CostEstimate(
            flops=2 * ff * d * slots + 8 * ff * ff * d + 4 * ff**3,
            bytes_accessed=6 * ff * d + 2 * slots * (ff + d),
            transcendentals=1,
        ),
        name="orthogonal",
    )(me, *packed, *whole, *pieces)


def produce_kernel(groups, me_ref, ortho_ref, *refs):
    late = len(apart(groups))
    packed, whole, pieces, refs = refs[:groups], refs[groups : 2 * groups - late], refs[2 * groups - late : 2 * groups], refs[2 * groups :]
    weight_new_ref, produced, (held, rows_ref) = refs[0], refs[1:-2], refs[-2:]
    ff, d = ortho_ref.shape
    capacity = packed[0].shape[0]
    for n, piece in enumerate(packed):
        rows_ref[n * capacity : (n + 1) * capacity] = piece[:, ff + d :]
    weight = assembled(1, me_ref, whole, pieces, held)
    weight_new = (weight - step_scale * ortho_ref[...].astype(F32)).astype(BF16)
    weight_new_ref[...] = weight_new
    product = jnp.dot(rows_ref[...], weight_new, preferred_element_type=F32).astype(BF16)
    for n, piece in enumerate(produced):
        piece[...] = product[n * capacity : (n + 1) * capacity]


def produce(me, ortho, packed, whole, pieces):
    groups = len(packed)
    ff, d = ortho.shape
    capacity = packed[0].shape[0]
    weight_new, *produced = pl.pallas_call(
        functools.partial(produce_kernel, groups),
        out_shape=(jax.ShapeDtypeStruct((ff, d), BF16),) + (jax.ShapeDtypeStruct((capacity, d), BF16),) * groups,
        in_specs=[SMEM] + [VMEM] * (1 + 2 * groups),
        out_specs=(VMEM,) * (groups + 1),
        scratch_shapes=[pltpu.VMEM((1, ff, d), BF16), pltpu.VMEM((groups * capacity, ff), BF16)],
        compiler_params=pltpu.CompilerParams(vmem_limit_bytes=40 * MIB),
        cost_estimate=pl.CostEstimate(
            flops=2 * ff * d * groups * capacity,
            bytes_accessed=8 * ff * d + 2 * groups * capacity * (ff + d),
            transcendentals=0,
        ),
        name="produce",
    )(me, ortho, *packed, *whole, *pieces)
    return weight_new, produced


def finish_kernel(groups, slot_ref, gates_ref, *refs):
    pieces, (out_ref, returned_ref) = refs[:groups], refs[groups:]
    capacity = pieces[0].shape[0]
    for s, piece in zip(mixed_order(groups), pieces):
        returned_ref[s * capacity : (s + 1) * capacity] = piece[...]
    selector = selector_of(slot_ref[...], groups * capacity)
    expert_out = lax.dot_general(
        selector, returned_ref[...], (((0,), (0,)), ((), ())), preferred_element_type=F32
    )
    out_ref[...] = (gates_ref[...] * expert_out).astype(BF16)


def finish(slot, gates, returned):
    groups = len(returned)
    rows = slot.shape[1]
    capacity, d = returned[0].shape
    slots = groups * capacity
    return pl.pallas_call(
        functools.partial(finish_kernel, groups),
        out_shape=jax.ShapeDtypeStruct((rows, d), BF16),
        in_specs=[VMEM] * (2 + groups),
        out_specs=VMEM,
        scratch_shapes=[pltpu.VMEM((slots, d), BF16)],
        compiler_params=pltpu.CompilerParams(vmem_limit_bytes=32 * MIB),
        cost_estimate=pl.CostEstimate(
            flops=2 * slots * rows * d, bytes_accessed=2 * d * (slots + rows), transcendentals=0
        ),
        name="finish",
    )(slot, gates, *returned)


def mixed_order(groups):
    def both_ends(partners):
        middle = (len(partners) + 1) // 2
        first, second = partners[:middle], partners[middle:]
        return [s for pair in zip(first, second + [None]) for s in pair if s is not None]

    half = groups // 2
    far, near = both_ends(list(range(half, groups))), both_ends(list(range(half - 1, 0, -1)))
    return [0] + [s for pair in zip(far, near + [None]) for s in pair if s is not None]


def swap(pieces, order):
    groups = lax.axis_size("expert")
    return [
        lax.ppermute(piece, "expert", [(i, i ^ s) for i in range(groups)]) if s else piece
        for s, piece in zip(order, pieces)
    ]


def partner_plan(
    grad_hidden, grad_out, grad_route, live_rows, w_down, w_moment, perm, fwd_hidden, fwd_route, fwd_gate
):
    groups = lax.axis_size("expert")
    me = lax.axis_index("expert").astype(jnp.int32).reshape(1)
    capacity = max(4, 2 * grad_hidden.shape[0] // groups)
    ff, d = w_down.shape[1:]
    order, late = mixed_order(groups), apart(groups)
    spread = swap(split(me, w_moment, w_down, groups), order)
    packed, fwd_slot, gates = pack_rows(
        live_rows, me, perm, grad_route, fwd_route, grad_hidden, grad_out, fwd_hidden, fwd_gate,
        spread[2 * groups // 3], groups, capacity,
    )
    received = swap(packed, order)
    whole, moment_pieces, weight_pieces = reorder(me, perm, spread, received[groups // 3])
    whole = swap(whole, [s for s in order if s not in late])
    moment_new, ortho = orthogonal(me, received, whole, swap(moment_pieces, late), ff, d)
    weight_new, produced = produce(me, ortho, received, whole, swap(weight_pieces, late))
    return weight_new[None], moment_new[None], finish(fwd_slot, gates, swap(produced, order))


def lookup(route_ids, mapping):
    columns = jnp.arange(mapping.shape[0], dtype=jnp.int32)
    hits = route_ids[:, None] == columns[None, :]
    return jnp.sum(jnp.where(hits, mapping[None, :], 0), axis=1)


def slot_matrix(target, is_live, groups, capacity):
    columns = jnp.arange(groups, dtype=jnp.int32)
    onehot = ((target[:, None] == columns[None, :]) & is_live[:, None]).astype(jnp.int32)
    ranked = jnp.sum(jnp.cumsum(onehot, axis=0) * onehot, axis=1) - 1
    slot_of = jnp.where(is_live, target * capacity + ranked, -1)
    slots = jnp.arange(groups * capacity, dtype=jnp.int32)
    return (slots[:, None] == slot_of[None, :]).astype(jnp.bfloat16)


def orthogonalize(moment):
    moment_f = moment.astype(jnp.float32)
    frobenius = jnp.sqrt(jnp.sum(moment_f * moment_f))
    current = (moment_f / (frobenius + norm_floor)).astype(jnp.bfloat16)
    for sweep_index in range(2):
        gramian = lax.dot_general(
            current, current, (((1,), (1,)), ((), ())), preferred_element_type=jnp.float32
        ).astype(jnp.bfloat16)
        squared = jnp.dot(gramian, gramian, preferred_element_type=jnp.float32)
        poly = (cubic_term * gramian.astype(jnp.float32) + quintic_term * squared).astype(
            jnp.bfloat16
        )
        current = (
            linear_term * current.astype(jnp.float32)
            + jnp.dot(poly, current, preferred_element_type=jnp.float32)
        ).astype(jnp.bfloat16)
    return current


def relocate(weight, moment, perm):
    groups = lax.axis_size("expert")
    weight_flat = weight.reshape(groups, -1)
    moment_flat = moment.reshape(groups, -1)
    spread_w, spread_m = (
        lax.all_to_all(weight_flat, "expert", split_axis=0, concat_axis=0, tiled=True),
        lax.all_to_all(moment_flat, "expert", split_axis=0, concat_axis=0, tiled=True),
    )
    devices = jnp.arange(groups, dtype=jnp.int32)
    inverse = jnp.sum(jnp.where(perm[None, :] == devices[:, None], devices[None, :], 0), axis=1)
    ordered_w = jnp.take(spread_w, inverse, axis=0)
    ordered_m = jnp.take(spread_m, inverse, axis=0)
    back_w, back_m = (
        lax.all_to_all(ordered_w, "expert", split_axis=0, concat_axis=0, tiled=True),
        lax.all_to_all(ordered_m, "expert", split_axis=0, concat_axis=0, tiled=True),
    )
    return (back_w.reshape(weight.shape), back_m.reshape(moment.shape))


def routed_plan(
    grad_hidden,
    grad_out,
    grad_route,
    live_rows,
    w_down,
    w_moment,
    perm,
    fwd_hidden,
    fwd_route,
    fwd_gate,
):
    groups = lax.axis_size("expert")
    grad_count = grad_hidden.shape[0]
    capacity = max(4, 2 * grad_count // groups)
    is_live = jnp.arange(grad_count, dtype=jnp.int32) < live_rows[0]
    route_ids = grad_route[:, 0]
    weight, moment = relocate(w_down, w_moment, perm)
    target = lookup(route_ids, perm)
    selector = slot_matrix(target, is_live, groups, capacity)
    hidden_buf = (
        jnp.dot(selector, grad_hidden, preferred_element_type=jnp.float32)
        .astype(jnp.bfloat16)
        .reshape(groups, capacity, -1)
    )
    outgrad_buf = (
        jnp.dot(selector, grad_out, preferred_element_type=jnp.float32)
        .astype(jnp.bfloat16)
        .reshape(groups, capacity, -1)
    )
    recv_hidden, recv_outgrad = (
        lax.all_to_all(hidden_buf, "expert", split_axis=0, concat_axis=0, tiled=True),
        lax.all_to_all(outgrad_buf, "expert", split_axis=0, concat_axis=0, tiled=True),
    )
    grad = lax.dot_general(
        recv_hidden.reshape(groups * capacity, -1),
        recv_outgrad.reshape(groups * capacity, -1),
        (((0,), (0,)), ((), ())),
        preferred_element_type=jnp.float32,
    )
    moment_new = (moment_decay * moment[0].astype(jnp.float32) + grad).astype(jnp.bfloat16)
    ortho = orthogonalize(moment_new)
    weight_new = (weight[0].astype(jnp.float32) - step_scale * ortho.astype(jnp.float32)).astype(
        jnp.bfloat16
    )
    weight_new = weight_new[None]
    moment_new = moment_new[None]
    fwd_ids = fwd_route[:, 0]
    placed_weight, placed_moment = (weight_new, moment_new)
    fwd_target = lookup(fwd_ids, perm)
    fwd_weight = weight_new[0]
    fwd_count = fwd_hidden.shape[0]
    fwd_capacity = max(4, 2 * fwd_count // groups)
    fwd_selector = slot_matrix(fwd_target, jnp.ones((fwd_count,), dtype=bool), groups, fwd_capacity)
    fwd_buf = (
        jnp.dot(fwd_selector, fwd_hidden, preferred_element_type=jnp.float32)
        .astype(jnp.bfloat16)
        .reshape(groups, fwd_capacity, -1)
    )
    produced = jnp.einsum(
        "gkf,fd->gkd",
        lax.all_to_all(fwd_buf, "expert", split_axis=0, concat_axis=0, tiled=True),
        fwd_weight,
        preferred_element_type=jnp.float32,
    ).astype(jnp.bfloat16)
    returned = lax.all_to_all(produced, "expert", split_axis=0, concat_axis=0, tiled=True)
    fwd_rows_out = lax.dot_general(
        fwd_selector,
        returned.reshape(groups * fwd_capacity, -1),
        (((0,), (0,)), ((), ())),
        preferred_element_type=jnp.float32,
    )
    fwd_out = (fwd_rows_out * fwd_gate[:, None]).astype(jnp.bfloat16)
    return (placed_weight, placed_moment, fwd_out)


def solution(mesh):
    groups = mesh.shape["expert"]
    in_specs = (
        P(("layer", "expert"), None),
        P(("layer", "expert"), None),
        P(("layer", "expert"), None),
        P(("layer", "expert")),
        P(("layer", "expert"), None, None),
        P(("layer", "expert"), None, None),
        P("layer"),
        P(("layer", "expert"), None),
        P(("layer", "expert"), None),
        P(("layer", "expert")),
    )
    out_specs = (
        P(("layer", "expert"), None, None),
        P(("layer", "expert"), None, None),
        P(("layer", "expert"), None),
    )

    def per_device(*args):
        few = groups & (groups - 1) == 0 and groups <= 2 * args[0].shape[0] // groups
        return (partner_plan if few else routed_plan)(*args)

    return jax.shard_map(
        per_device, mesh=mesh, in_specs=in_specs, out_specs=out_specs, check_vma=False
    )
```

```python
import functools

import jax
import jax.numpy as jnp
from jax import lax
from jax.experimental import pallas as pl
from jax.experimental.pallas import tpu as pltpu
from jax.sharding import PartitionSpec as P

linear_term = 3.4445
cubic_term = -4.775
quintic_term = 2.0315
moment_decay = 0.9
step_scale = 0.25
norm_floor = 1e-07

F32 = jnp.float32
BF16 = jnp.bfloat16
HBM = pl.BlockSpec(memory_space=pltpu.HBM)
VMEM = pl.BlockSpec(memory_space=pltpu.VMEM)
SMEM = pl.BlockSpec(memory_space=pltpu.SMEM)
ANY = pl.BlockSpec(memory_space=pl.ANY)
MIB = 1 << 20


def fetched(refs, held, sem):
    copies = [pltpu.make_async_copy(ref, room, sem.at[n]) for n, (ref, room) in enumerate(zip(refs, held))]
    for copy in copies:
        copy.start()
    for copy in copies:
        copy.wait()


def rooms(arrays):
    return [pltpu.VMEM(a.shape, a.dtype) for a in arrays] + [pltpu.SemaphoreType.DMA((len(arrays),))]


def chunk_at(ref, lead, k, rows, columns):
    return ref.at[
        lead,
        pl.ds(pl.multiple_of((k // 2) * rows, rows), rows),
        pl.ds(pl.multiple_of((k % 2) * columns, columns), columns),
    ]


def slot_rows(route, live, groups, capacity, me_ref, perm_ref):
    rows = route.shape[1]
    experts = lax.broadcasted_iota(jnp.int32, (groups, rows), 0)
    onehot = jnp.where((experts == route) & live, 1.0, 0.0).astype(BF16)
    before = lax.broadcasted_iota(jnp.int32, (rows, rows), 0)
    after = lax.broadcasted_iota(jnp.int32, (rows, rows), 1)
    upto = jnp.where(before <= after, 1.0, 0.0).astype(BF16)
    ranks = jnp.dot(onehot, upto, preferred_element_type=F32)
    rank = jnp.sum(ranks * onehot.astype(F32), axis=0, keepdims=True).astype(jnp.int32) - 1
    partner = jnp.zeros_like(route)
    for e in range(groups):
        partner = jnp.where(route == e, perm_ref[e] ^ me_ref[0], partner)
    return jnp.where(live, partner * capacity + rank, -1)


def selector_of(slot, slots):
    rows = slot.shape[1]
    places = lax.broadcasted_iota(jnp.int32, (slots, rows), 0)
    return jnp.where(places == slot, 1.0, 0.0).astype(BF16)


def pack_kernel(groups, live_ref, me_ref, perm_ref, *refs):
    sources, pieces, (slot_ref, gates_ref) = refs[:6], refs[7 : 7 + groups], refs[7 + groups : 9 + groups]
    held, sem = refs[9 + groups : 15 + groups], refs[-1]
    route_ref, fwd_route_ref, hidden_ref, out_ref, fwd_ref, gate_ref = held
    copies = [pltpu.make_async_copy(ref, room, sem.at[n]) for n, (ref, room) in enumerate(zip(sources, held))]
    for copy in copies:
        copy.start()
    rows, ff = hidden_ref.shape
    d = out_ref.shape[1]
    capacity = pieces[0].shape[0]
    slots = groups * capacity
    place = lax.broadcasted_iota(jnp.int32, (1, rows), 1)

    def fill(first, selector, source_ref):
        chosen = jnp.dot(selector, source_ref[...], preferred_element_type=F32).astype(BF16)
        for s, piece in zip(mixed_order(groups), pieces):
            piece[:, first : first + source_ref.shape[1]] = chosen[s * capacity : (s + 1) * capacity]

    copies[0].wait()
    slot = slot_rows(route_ref[...], place < live_ref[0], groups, capacity, me_ref, perm_ref)
    selector = selector_of(slot, slots)
    copies[1].wait()
    fwd_slot = slot_rows(fwd_route_ref[...], place >= 0, groups, capacity, me_ref, perm_ref)
    slot_ref[...] = fwd_slot
    copies[2].wait()
    fill(0, selector, hidden_ref)
    copies[3].wait()
    fill(ff, selector, out_ref)
    copies[4].wait()
    fill(ff + d, selector_of(fwd_slot, slots), fwd_ref)
    copies[5].wait()
    down = lax.broadcasted_iota(jnp.int32, (rows, rows), 0)
    across = lax.broadcasted_iota(jnp.int32, (rows, rows), 1)
    gates_ref[...] = jnp.sum(jnp.where(down == across, gate_ref[...], 0.0), axis=1, keepdims=True)


def pack_rows(live_rows, me, perm, route, fwd_route, hidden, grad_out, fwd_hidden, gate, earlier, groups, capacity):
    rows, ff = hidden.shape
    width = 2 * ff + grad_out.shape[1]
    sources = (route.reshape(1, rows), fwd_route.reshape(1, rows), hidden, grad_out, fwd_hidden, gate.reshape(1, rows))
    *pieces, slot, gates = pl.pallas_call(
        functools.partial(pack_kernel, groups),
        out_shape=(jax.ShapeDtypeStruct((capacity, width), BF16),) * groups
        + (jax.ShapeDtypeStruct((1, rows), jnp.int32), jax.ShapeDtypeStruct((rows, 1), F32)),
        in_specs=[SMEM] * 3 + [HBM] * 6 + [VMEM],
        out_specs=(VMEM,) * (groups + 2),
        scratch_shapes=[pltpu.VMEM(a.shape, a.dtype) for a in sources] + [pltpu.SemaphoreType.DMA((len(sources),))],
        compiler_params=pltpu.CompilerParams(vmem_limit_bytes=32 * MIB),
        cost_estimate=pl.CostEstimate(
            flops=2 * groups * capacity * rows * width, bytes_accessed=6 * rows * width, transcendentals=0
        ),
        name="pack_rows",
    )(live_rows, me, perm, *sources, earlier)
    return pieces, slot, gates


def split_kernel(me_ref, moment_ref, weight_ref, *refs):
    pieces, held, sem = refs[:-3], refs[-3:-1], refs[-1]
    fetched((moment_ref, weight_ref), held, sem)
    for s, piece in zip(mixed_order(len(pieces)), pieces):
        rows, columns = piece.shape[1:]
        for lead, source in enumerate(held):
            piece[lead] = chunk_at(source, 0, me_ref[0] ^ s, rows, columns)[...]


def split(me, moment, weight, groups):
    _, ff, d = weight.shape
    piece = jax.ShapeDtypeStruct((2, ff // (groups // 2), d // 2), BF16)
    return pl.pallas_call(
        split_kernel,
        out_shape=(piece,) * groups,
        in_specs=[SMEM, HBM, HBM],
        out_specs=(VMEM,) * groups,
        scratch_shapes=rooms((moment, weight)),
        compiler_params=pltpu.CompilerParams(vmem_limit_bytes=60 * MIB),
        cost_estimate=pl.CostEstimate(flops=0, bytes_accessed=8 * ff * d, transcendentals=0),
        name="split",
    )(me, moment, weight)


def reorder_kernel(me_ref, perm_ref, *refs):
    groups = len(refs) // 2 - 1
    sources, targets, held = refs[:groups], refs[groups + 1 : 2 * groups + 1], refs[-1]
    me, order = me_ref[0], mixed_order(groups)
    for s, source in zip(order, sources):
        held[me ^ perm_ref[me ^ s]] = source[...]
    for s, target in zip(order, targets):
        target[...] = held[s]


def reorder(me, perm, pieces, earlier):
    groups = len(pieces)
    piece = jax.ShapeDtypeStruct(pieces[0].shape, BF16)
    return pl.pallas_call(
        reorder_kernel,
        out_shape=(piece,) * groups,
        in_specs=[SMEM, SMEM] + [VMEM] * (groups + 1),
        out_specs=(VMEM,) * groups,
        scratch_shapes=[pltpu.VMEM((groups,) + pieces[0].shape, BF16)],
        compiler_params=pltpu.CompilerParams(vmem_limit_bytes=32 * MIB),
        cost_estimate=pl.CostEstimate(flops=0, bytes_accessed=4 * groups * pieces[0].size, transcendentals=0),
        name="reorder",
    )(me, perm, *pieces, earlier)


def update_kernel(groups, me_ref, *refs):
    packed, pieces, produced = refs[:groups], refs[groups : 2 * groups], refs[2 * groups + 2 : 3 * groups + 2]
    results = refs[2 * groups : 2 * groups + 2]
    held, rows_ref, sem = refs[-3:]
    _, ff, d = held.shape
    capacity = packed[0].shape[0]
    for n, piece in enumerate(packed):
        rows_ref[n * capacity : (n + 1) * capacity] = piece[...]
    for s, piece in zip(mixed_order(groups), pieces):
        rows, columns = piece.shape[1:]
        for lead in range(2):
            chunk_at(held, lead, me_ref[0] ^ s, rows, columns)[...] = piece[lead]
    grad = lax.dot_general(
        rows_ref[:, :ff], rows_ref[:, ff : ff + d], (((0,), (0,)), ((), ())), preferred_element_type=F32
    )
    moment_new = (moment_decay * held[0].astype(F32) + grad).astype(BF16)
    held[0] = moment_new
    leaving = [pltpu.make_async_copy(held.at[lead], results[lead], sem.at[lead]) for lead in range(2)]
    leaving[0].start()
    moment_f = moment_new.astype(F32)
    frobenius = jnp.sqrt(jnp.sum(moment_f * moment_f))
    current = (moment_f / (frobenius + norm_floor)).astype(BF16)
    for _ in range(2):
        gramian = lax.dot_general(
            current, current, (((1,), (1,)), ((), ())), preferred_element_type=F32
        ).astype(BF16)
        squared = jnp.dot(gramian, gramian, preferred_element_type=F32)
        poly = (cubic_term * gramian.astype(F32) + quintic_term * squared).astype(BF16)
        current = (
            linear_term * current.astype(F32) + jnp.dot(poly, current, preferred_element_type=F32)
        ).astype(BF16)
    weight_new = (held[1].astype(F32) - step_scale * current.astype(F32)).astype(BF16)
    held[1] = weight_new
    leaving[1].start()
    product = jnp.dot(rows_ref[:, ff + d :], weight_new, preferred_element_type=F32).astype(BF16)
    for n, piece in enumerate(produced):
        piece[...] = product[n * capacity : (n + 1) * capacity]
    for copy in leaving:
        copy.wait()


def update(me, packed, pieces, ff, d):
    groups = len(pieces)
    capacity, width = packed[0].shape
    slots = groups * capacity
    shape = jax.ShapeDtypeStruct((ff, d), BF16)
    moment_new, weight_new, *produced = pl.pallas_call(
        functools.partial(update_kernel, groups),
        out_shape=(shape, shape) + (jax.ShapeDtypeStruct((capacity, d), BF16),) * groups,
        in_specs=[SMEM] + [VMEM] * (2 * groups),
        out_specs=(HBM, HBM) + (VMEM,) * groups,
        scratch_shapes=[
            pltpu.VMEM((2, ff, d), BF16),
            pltpu.VMEM((slots, width), BF16),
            pltpu.SemaphoreType.DMA((2,)),
        ],
        compiler_params=pltpu.CompilerParams(vmem_limit_bytes=40 * MIB),
        cost_estimate=pl.CostEstimate(
            flops=4 * ff * d * slots + 8 * ff * ff * d + 4 * ff**3,
            bytes_accessed=8 * ff * d + 2 * slots * (width + d),
            transcendentals=1,
        ),
        name="update",
    )(me, *packed, *pieces)
    return weight_new, moment_new, produced


def finish_kernel(groups, slot_ref, gates_ref, *refs):
    pieces, (out_ref, returned_ref, held, sem) = refs[:groups], refs[groups:]
    capacity = pieces[0].shape[0]
    for s, piece in zip(mixed_order(groups), pieces):
        returned_ref[s * capacity : (s + 1) * capacity] = piece[...]
    selector = selector_of(slot_ref[...], groups * capacity)
    leaving = []
    for n in range(2):
        columns = slice(n * held.shape[1] // 2, (n + 1) * held.shape[1] // 2)
        expert_out = lax.dot_general(
            selector, returned_ref[:, columns], (((0,), (0,)), ((), ())), preferred_element_type=F32
        )
        held[:, columns] = (gates_ref[...] * expert_out).astype(BF16)
        leaving.append(pltpu.make_async_copy(held.at[:, columns], out_ref.at[:, columns], sem.at[n]))
        leaving[n].start()
    for copy in leaving:
        copy.wait()


def finish(slot, gates, returned):
    groups = len(returned)
    rows = slot.shape[1]
    capacity, d = returned[0].shape
    slots = groups * capacity
    return pl.pallas_call(
        functools.partial(finish_kernel, groups),
        out_shape=jax.ShapeDtypeStruct((rows, d), BF16),
        in_specs=[VMEM] * (2 + groups),
        out_specs=HBM,
        scratch_shapes=[
            pltpu.VMEM((slots, d), BF16),
            pltpu.VMEM((rows, d), BF16),
            pltpu.SemaphoreType.DMA((2,)),
        ],
        compiler_params=pltpu.CompilerParams(vmem_limit_bytes=32 * MIB),
        cost_estimate=pl.CostEstimate(
            flops=2 * slots * rows * d, bytes_accessed=2 * d * (slots + rows), transcendentals=0
        ),
        name="finish",
    )(slot, gates, *returned)


def mixed_order(groups):
    def both_ends(partners):
        middle = (len(partners) + 1) // 2
        first, second = partners[:middle], partners[middle:]
        return [s for pair in zip(first, second + [None]) for s in pair if s is not None]

    half = groups // 2
    far, near = both_ends(list(range(half, groups))), both_ends(list(range(half - 1, 0, -1)))
    return [0] + [s for pair in zip(far, near + [None]) for s in pair if s is not None]


def swap(pieces):
    groups = len(pieces)
    order = mixed_order(groups)
    return [pieces[0]] + [
        lax.ppermute(piece, "expert", [(i, i ^ s) for i in range(groups)]) for s, piece in zip(order[1:], pieces[1:])
    ]


def partner_plan(
    grad_hidden, grad_out, grad_route, live_rows, w_down, w_moment, perm, fwd_hidden, fwd_route, fwd_gate
):
    groups = lax.axis_size("expert")
    me = lax.axis_index("expert").astype(jnp.int32).reshape(1)
    capacity = max(4, 2 * grad_hidden.shape[0] // groups)
    ff, d = w_down.shape[1:]
    spread = swap(split(me, w_moment, w_down, groups))
    packed, fwd_slot, gates = pack_rows(
        live_rows, me, perm, grad_route, fwd_route, grad_hidden, grad_out, fwd_hidden, fwd_gate,
        spread[2 * groups // 3], groups, capacity,
    )
    received = swap(packed)
    placed = swap(reorder(me, perm, spread, received[groups // 3]))
    weight_new, moment_new, produced = update(me, received, placed, ff, d)
    return weight_new[None], moment_new[None], finish(fwd_slot, gates, swap(produced))


def lookup(route_ids, mapping):
    columns = jnp.arange(mapping.shape[0], dtype=jnp.int32)
    hits = route_ids[:, None] == columns[None, :]
    return jnp.sum(jnp.where(hits, mapping[None, :], 0), axis=1)


def slot_matrix(target, is_live, groups, capacity):
    columns = jnp.arange(groups, dtype=jnp.int32)
    onehot = ((target[:, None] == columns[None, :]) & is_live[:, None]).astype(jnp.int32)
    ranked = jnp.sum(jnp.cumsum(onehot, axis=0) * onehot, axis=1) - 1
    slot_of = jnp.where(is_live, target * capacity + ranked, -1)
    slots = jnp.arange(groups * capacity, dtype=jnp.int32)
    return (slots[:, None] == slot_of[None, :]).astype(jnp.bfloat16)


def orthogonalize(moment):
    moment_f = moment.astype(jnp.float32)
    frobenius = jnp.sqrt(jnp.sum(moment_f * moment_f))
    current = (moment_f / (frobenius + norm_floor)).astype(jnp.bfloat16)
    for sweep_index in range(2):
        gramian = lax.dot_general(
            current, current, (((1,), (1,)), ((), ())), preferred_element_type=jnp.float32
        ).astype(jnp.bfloat16)
        squared = jnp.dot(gramian, gramian, preferred_element_type=jnp.float32)
        poly = (cubic_term * gramian.astype(jnp.float32) + quintic_term * squared).astype(
            jnp.bfloat16
        )
        current = (
            linear_term * current.astype(jnp.float32)
            + jnp.dot(poly, current, preferred_element_type=jnp.float32)
        ).astype(jnp.bfloat16)
    return current


def relocate(weight, moment, perm):
    groups = lax.axis_size("expert")
    weight_flat = weight.reshape(groups, -1)
    moment_flat = moment.reshape(groups, -1)
    spread_w, spread_m = (
        lax.all_to_all(weight_flat, "expert", split_axis=0, concat_axis=0, tiled=True),
        lax.all_to_all(moment_flat, "expert", split_axis=0, concat_axis=0, tiled=True),
    )
    devices = jnp.arange(groups, dtype=jnp.int32)
    inverse = jnp.sum(jnp.where(perm[None, :] == devices[:, None], devices[None, :], 0), axis=1)
    ordered_w = jnp.take(spread_w, inverse, axis=0)
    ordered_m = jnp.take(spread_m, inverse, axis=0)
    back_w, back_m = (
        lax.all_to_all(ordered_w, "expert", split_axis=0, concat_axis=0, tiled=True),
        lax.all_to_all(ordered_m, "expert", split_axis=0, concat_axis=0, tiled=True),
    )
    return (back_w.reshape(weight.shape), back_m.reshape(moment.shape))


def routed_plan(
    grad_hidden,
    grad_out,
    grad_route,
    live_rows,
    w_down,
    w_moment,
    perm,
    fwd_hidden,
    fwd_route,
    fwd_gate,
):
    groups = lax.axis_size("expert")
    grad_count = grad_hidden.shape[0]
    capacity = max(4, 2 * grad_count // groups)
    is_live = jnp.arange(grad_count, dtype=jnp.int32) < live_rows[0]
    route_ids = grad_route[:, 0]
    weight, moment = relocate(w_down, w_moment, perm)
    target = lookup(route_ids, perm)
    selector = slot_matrix(target, is_live, groups, capacity)
    hidden_buf = (
        jnp.dot(selector, grad_hidden, preferred_element_type=jnp.float32)
        .astype(jnp.bfloat16)
        .reshape(groups, capacity, -1)
    )
    outgrad_buf = (
        jnp.dot(selector, grad_out, preferred_element_type=jnp.float32)
        .astype(jnp.bfloat16)
        .reshape(groups, capacity, -1)
    )
    recv_hidden, recv_outgrad = (
        lax.all_to_all(hidden_buf, "expert", split_axis=0, concat_axis=0, tiled=True),
        lax.all_to_all(outgrad_buf, "expert", split_axis=0, concat_axis=0, tiled=True),
    )
    grad = lax.dot_general(
        recv_hidden.reshape(groups * capacity, -1),
        recv_outgrad.reshape(groups * capacity, -1),
        (((0,), (0,)), ((), ())),
        preferred_element_type=jnp.float32,
    )
    moment_new = (moment_decay * moment[0].astype(jnp.float32) + grad).astype(jnp.bfloat16)
    ortho = orthogonalize(moment_new)
    weight_new = (weight[0].astype(jnp.float32) - step_scale * ortho.astype(jnp.float32)).astype(
        jnp.bfloat16
    )
    weight_new = weight_new[None]
    moment_new = moment_new[None]
    fwd_ids = fwd_route[:, 0]
    placed_weight, placed_moment = (weight_new, moment_new)
    fwd_target = lookup(fwd_ids, perm)
    fwd_weight = weight_new[0]
    fwd_count = fwd_hidden.shape[0]
    fwd_capacity = max(4, 2 * fwd_count // groups)
    fwd_selector = slot_matrix(fwd_target, jnp.ones((fwd_count,), dtype=bool), groups, fwd_capacity)
    fwd_buf = (
        jnp.dot(fwd_selector, fwd_hidden, preferred_element_type=jnp.float32)
        .astype(jnp.bfloat16)
        .reshape(groups, fwd_capacity, -1)
    )
    produced = jnp.einsum(
        "gkf,fd->gkd",
        lax.all_to_all(fwd_buf, "expert", split_axis=0, concat_axis=0, tiled=True),
        fwd_weight,
        preferred_element_type=jnp.float32,
    ).astype(jnp.bfloat16)
    returned = lax.all_to_all(produced, "expert", split_axis=0, concat_axis=0, tiled=True)
    fwd_rows_out = lax.dot_general(
        fwd_selector,
        returned.reshape(groups * fwd_capacity, -1),
        (((0,), (0,)), ((), ())),
        preferred_element_type=jnp.float32,
    )
    fwd_out = (fwd_rows_out * fwd_gate[:, None]).astype(jnp.bfloat16)
    return (placed_weight, placed_moment, fwd_out)


def solution(mesh):
    groups = mesh.shape["expert"]
    in_specs = (
        P(("layer", "expert"), None),
        P(("layer", "expert"), None),
        P(("layer", "expert"), None),
        P(("layer", "expert")),
        P(("layer", "expert"), None, None),
        P(("layer", "expert"), None, None),
        P("layer"),
        P(("layer", "expert"), None),
        P(("layer", "expert"), None),
        P(("layer", "expert")),
    )
    out_specs = (
        P(("layer", "expert"), None, None),
        P(("layer", "expert"), None, None),
        P(("layer", "expert"), None),
    )

    def per_device(*args):
        few = groups & (groups - 1) == 0 and groups <= 2 * args[0].shape[0] // groups
        return (partner_plan if few else routed_plan)(*args)

    return jax.shard_map(
        per_device, mesh=mesh, in_specs=in_specs, out_specs=out_specs, check_vma=False
    )
```

```python
import functools

import jax
import jax.numpy as jnp
from jax import lax
from jax.experimental import pallas as pl
from jax.experimental.pallas import tpu as pltpu
from jax.sharding import PartitionSpec as P

linear_term = 3.4445
cubic_term = -4.775
quintic_term = 2.0315
moment_decay = 0.9
step_scale = 0.25
norm_floor = 1e-07

F32 = jnp.float32
BF16 = jnp.bfloat16
HBM = pl.BlockSpec(memory_space=pltpu.HBM)
VMEM = pl.BlockSpec(memory_space=pltpu.VMEM)
SMEM = pl.BlockSpec(memory_space=pltpu.SMEM)
ANY = pl.BlockSpec(memory_space=pl.ANY)
MIB = 1 << 20


def fetched(refs, held, sem):
    copies = [pltpu.make_async_copy(ref, room, sem.at[n]) for n, (ref, room) in enumerate(zip(refs, held))]
    for copy in copies:
        copy.start()
    for copy in copies:
        copy.wait()


def rooms(arrays):
    return [pltpu.VMEM(a.shape, a.dtype) for a in arrays] + [pltpu.SemaphoreType.DMA((len(arrays),))]


def chunk_at(ref, lead, k, rows, columns):
    return ref.at[
        lead,
        pl.ds(pl.multiple_of((k // 2) * rows, rows), rows),
        pl.ds(pl.multiple_of((k % 2) * columns, columns), columns),
    ]


def slot_rows(route, live, groups, capacity, me_ref, perm_ref):
    rows = route.shape[1]
    experts = lax.broadcasted_iota(jnp.int32, (groups, rows), 0)
    onehot = jnp.where((experts == route) & live, 1.0, 0.0).astype(BF16)
    before = lax.broadcasted_iota(jnp.int32, (rows, rows), 0)
    after = lax.broadcasted_iota(jnp.int32, (rows, rows), 1)
    upto = jnp.where(before <= after, 1.0, 0.0).astype(BF16)
    ranks = jnp.dot(onehot, upto, preferred_element_type=F32)
    rank = jnp.sum(ranks * onehot.astype(F32), axis=0, keepdims=True).astype(jnp.int32) - 1
    partner = jnp.zeros_like(route)
    for e in range(groups):
        partner = jnp.where(route == e, perm_ref[e] ^ me_ref[0], partner)
    return jnp.where(live, partner * capacity + rank, -1)


def selector_of(slot, slots):
    rows = slot.shape[1]
    places = lax.broadcasted_iota(jnp.int32, (slots, rows), 0)
    return jnp.where(places == slot, 1.0, 0.0).astype(BF16)


def pack_kernel(groups, live_ref, me_ref, perm_ref, *refs):
    sources, pieces, (slot_ref, gates_ref) = refs[:6], refs[7 : 7 + groups], refs[7 + groups : 9 + groups]
    held, sem = refs[9 + groups : 15 + groups], refs[-1]
    route_ref, fwd_route_ref, hidden_ref, out_ref, fwd_ref, gate_ref = held
    copies = [pltpu.make_async_copy(ref, room, sem.at[n]) for n, (ref, room) in enumerate(zip(sources, held))]
    for copy in copies:
        copy.start()
    rows, ff = hidden_ref.shape
    d = out_ref.shape[1]
    capacity = pieces[0].shape[0]
    slots = groups * capacity
    place = lax.broadcasted_iota(jnp.int32, (1, rows), 1)

    def fill(first, selector, source_ref):
        chosen = jnp.dot(selector, source_ref[...], preferred_element_type=F32).astype(BF16)
        for s, piece in zip(mixed_order(groups), pieces):
            piece[:, first : first + source_ref.shape[1]] = chosen[s * capacity : (s + 1) * capacity]

    copies[0].wait()
    slot = slot_rows(route_ref[...], place < live_ref[0], groups, capacity, me_ref, perm_ref)
    selector = selector_of(slot, slots)
    copies[1].wait()
    fwd_slot = slot_rows(fwd_route_ref[...], place >= 0, groups, capacity, me_ref, perm_ref)
    slot_ref[...] = fwd_slot
    copies[2].wait()
    fill(0, selector, hidden_ref)
    copies[3].wait()
    fill(ff, selector, out_ref)
    copies[4].wait()
    fill(ff + d, selector_of(fwd_slot, slots), fwd_ref)
    copies[5].wait()
    down = lax.broadcasted_iota(jnp.int32, (rows, rows), 0)
    across = lax.broadcasted_iota(jnp.int32, (rows, rows), 1)
    gates_ref[...] = jnp.sum(jnp.where(down == across, gate_ref[...], 0.0), axis=1, keepdims=True)


def pack_rows(live_rows, me, perm, route, fwd_route, hidden, grad_out, fwd_hidden, gate, earlier, groups, capacity):
    rows, ff = hidden.shape
    width = 2 * ff + grad_out.shape[1]
    sources = (route.reshape(1, rows), fwd_route.reshape(1, rows), hidden, grad_out, fwd_hidden, gate.reshape(1, rows))
    *pieces, slot, gates = pl.pallas_call(
        functools.partial(pack_kernel, groups),
        out_shape=(jax.ShapeDtypeStruct((capacity, width), BF16),) * groups
        + (jax.ShapeDtypeStruct((1, rows), jnp.int32), jax.ShapeDtypeStruct((rows, 1), F32)),
        in_specs=[SMEM] * 3 + [HBM] * 6 + [VMEM],
        out_specs=(VMEM,) * (groups + 2),
        scratch_shapes=[pltpu.VMEM(a.shape, a.dtype) for a in sources] + [pltpu.SemaphoreType.DMA((len(sources),))],
        compiler_params=pltpu.CompilerParams(vmem_limit_bytes=32 * MIB),
        cost_estimate=pl.CostEstimate(
            flops=2 * groups * capacity * rows * width, bytes_accessed=6 * rows * width, transcendentals=0
        ),
        name="pack_rows",
    )(live_rows, me, perm, *sources, earlier)
    return pieces, slot, gates


def split_kernel(me_ref, moment_ref, weight_ref, *refs):
    pieces, held, sem = refs[:-3], refs[-3:-1], refs[-1]
    fetched((moment_ref, weight_ref), held, sem)
    for s, piece in zip(mixed_order(len(pieces)), pieces):
        rows, columns = piece.shape[1:]
        for lead, source in enumerate(held):
            piece[lead] = chunk_at(source, 0, me_ref[0] ^ s, rows, columns)[...]


def split(me, moment, weight, groups):
    _, ff, d = weight.shape
    piece = jax.ShapeDtypeStruct((2, ff // (groups // 2), d // 2), BF16)
    return pl.pallas_call(
        split_kernel,
        out_shape=(piece,) * groups,
        in_specs=[SMEM, HBM, HBM],
        out_specs=(VMEM,) * groups,
        scratch_shapes=rooms((moment, weight)),
        compiler_params=pltpu.CompilerParams(vmem_limit_bytes=60 * MIB),
        cost_estimate=pl.CostEstimate(flops=0, bytes_accessed=8 * ff * d, transcendentals=0),
        name="split",
    )(me, moment, weight)


def reorder_kernel(me_ref, perm_ref, *refs):
    groups = len(refs) // 2 - 1
    sources, targets, held = refs[:groups], refs[groups + 1 : 2 * groups + 1], refs[-1]
    me, order = me_ref[0], mixed_order(groups)
    for s, source in zip(order, sources):
        held[me ^ perm_ref[me ^ s]] = source[...]
    for s, target in zip(order, targets):
        target[...] = held[s]


def reorder(me, perm, pieces, earlier):
    groups = len(pieces)
    piece = jax.ShapeDtypeStruct(pieces[0].shape, BF16)
    return pl.pallas_call(
        reorder_kernel,
        out_shape=(piece,) * groups,
        in_specs=[SMEM, SMEM] + [VMEM] * (groups + 1),
        out_specs=(VMEM,) * groups,
        scratch_shapes=[pltpu.VMEM((groups,) + pieces[0].shape, BF16)],
        compiler_params=pltpu.CompilerParams(vmem_limit_bytes=32 * MIB),
        cost_estimate=pl.CostEstimate(flops=0, bytes_accessed=4 * groups * pieces[0].size, transcendentals=0),
        name="reorder",
    )(me, perm, *pieces, earlier)


def update_kernel(groups, me_ref, *refs):
    packed, pieces, produced = refs[:groups], refs[groups : 2 * groups], refs[2 * groups + 2 : 3 * groups + 2]
    weight_new_ref, moment_new_ref = refs[2 * groups : 2 * groups + 2]
    held, rows_ref = refs[-2:]
    _, ff, d = held.shape
    capacity = packed[0].shape[0]
    for n, piece in enumerate(packed):
        rows_ref[n * capacity : (n + 1) * capacity] = piece[...]
    for s, piece in zip(mixed_order(groups), pieces):
        rows, columns = piece.shape[1:]
        for lead in range(2):
            chunk_at(held, lead, me_ref[0] ^ s, rows, columns)[...] = piece[lead]
    grad = lax.dot_general(
        rows_ref[:, :ff], rows_ref[:, ff : ff + d], (((0,), (0,)), ((), ())), preferred_element_type=F32
    )
    moment_new = (moment_decay * held[0].astype(F32) + grad).astype(BF16)
    moment_new_ref[...] = moment_new
    moment_f = moment_new.astype(F32)
    frobenius = jnp.sqrt(jnp.sum(moment_f * moment_f))
    current = (moment_f / (frobenius + norm_floor)).astype(BF16)
    for _ in range(2):
        gramian = lax.dot_general(
            current, current, (((1,), (1,)), ((), ())), preferred_element_type=F32
        ).astype(BF16)
        squared = jnp.dot(gramian, gramian, preferred_element_type=F32)
        poly = (cubic_term * gramian.astype(F32) + quintic_term * squared).astype(BF16)
        current = (
            linear_term * current.astype(F32) + jnp.dot(poly, current, preferred_element_type=F32)
        ).astype(BF16)
    weight_new = (held[1].astype(F32) - step_scale * current.astype(F32)).astype(BF16)
    weight_new_ref[...] = weight_new
    product = jnp.dot(rows_ref[:, ff + d :], weight_new, preferred_element_type=F32).astype(BF16)
    for n, piece in enumerate(produced):
        piece[...] = product[n * capacity : (n + 1) * capacity]


def update(me, packed, pieces, ff, d):
    groups = len(pieces)
    capacity, width = packed[0].shape
    slots = groups * capacity
    shape = jax.ShapeDtypeStruct((ff, d), BF16)
    weight_new, moment_new, *produced = pl.pallas_call(
        functools.partial(update_kernel, groups),
        out_shape=(shape, shape) + (jax.ShapeDtypeStruct((capacity, d), BF16),) * groups,
        in_specs=[SMEM] + [VMEM] * (2 * groups),
        out_specs=(VMEM,) * (groups + 2),
        scratch_shapes=[pltpu.VMEM((2, ff, d), BF16), pltpu.VMEM((slots, width), BF16)],
        compiler_params=pltpu.CompilerParams(vmem_limit_bytes=40 * MIB),
        cost_estimate=pl.CostEstimate(
            flops=4 * ff * d * slots + 8 * ff * ff * d + 4 * ff**3,
            bytes_accessed=8 * ff * d + 2 * slots * (width + d),
            transcendentals=1,
        ),
        name="update",
    )(me, *packed, *pieces)
    return weight_new, moment_new, produced


def finish_kernel(groups, slot_ref, gates_ref, *refs):
    pieces, (out_ref, returned_ref) = refs[:groups], refs[groups:]
    capacity = pieces[0].shape[0]
    for s, piece in zip(mixed_order(groups), pieces):
        returned_ref[s * capacity : (s + 1) * capacity] = piece[...]
    selector = selector_of(slot_ref[...], groups * capacity)
    expert_out = lax.dot_general(
        selector, returned_ref[...], (((0,), (0,)), ((), ())), preferred_element_type=F32
    )
    out_ref[...] = (gates_ref[...] * expert_out).astype(BF16)


def finish(slot, gates, returned):
    groups = len(returned)
    rows = slot.shape[1]
    capacity, d = returned[0].shape
    slots = groups * capacity
    return pl.pallas_call(
        functools.partial(finish_kernel, groups),
        out_shape=jax.ShapeDtypeStruct((rows, d), BF16),
        in_specs=[VMEM] * (2 + groups),
        out_specs=VMEM,
        scratch_shapes=[pltpu.VMEM((slots, d), BF16)],
        compiler_params=pltpu.CompilerParams(vmem_limit_bytes=32 * MIB),
        cost_estimate=pl.CostEstimate(
            flops=2 * slots * rows * d, bytes_accessed=2 * d * (slots + rows), transcendentals=0
        ),
        name="finish",
    )(slot, gates, *returned)


def mixed_order(groups):
    def both_ends(partners):
        middle = (len(partners) + 1) // 2
        first, second = partners[:middle], partners[middle:]
        return [s for pair in zip(first, second + [None]) for s in pair if s is not None]

    half = groups // 2
    far, near = both_ends(list(range(half, groups))), both_ends(list(range(half - 1, 0, -1)))
    return [0] + [s for pair in zip(far, near + [None]) for s in pair if s is not None]


def swap(pieces):
    groups = len(pieces)
    order = mixed_order(groups)
    return [pieces[0]] + [
        lax.ppermute(piece, "expert", [(i, i ^ s) for i in range(groups)]) for s, piece in zip(order[1:], pieces[1:])
    ]


def partner_plan(
    grad_hidden, grad_out, grad_route, live_rows, w_down, w_moment, perm, fwd_hidden, fwd_route, fwd_gate
):
    groups = lax.axis_size("expert")
    me = lax.axis_index("expert").astype(jnp.int32).reshape(1)
    capacity = max(4, 2 * grad_hidden.shape[0] // groups)
    ff, d = w_down.shape[1:]
    spread = swap(split(me, w_moment, w_down, groups))
    packed, fwd_slot, gates = pack_rows(
        live_rows, me, perm, grad_route, fwd_route, grad_hidden, grad_out, fwd_hidden, fwd_gate,
        spread[1], groups, capacity,
    )
    received = swap(packed)
    placed = swap(reorder(me, perm, spread, received[groups // 3]))
    weight_new, moment_new, produced = update(me, received, placed, ff, d)
    return weight_new[None], moment_new[None], finish(fwd_slot, gates, swap(produced))


def lookup(route_ids, mapping):
    columns = jnp.arange(mapping.shape[0], dtype=jnp.int32)
    hits = route_ids[:, None] == columns[None, :]
    return jnp.sum(jnp.where(hits, mapping[None, :], 0), axis=1)


def slot_matrix(target, is_live, groups, capacity):
    columns = jnp.arange(groups, dtype=jnp.int32)
    onehot = ((target[:, None] == columns[None, :]) & is_live[:, None]).astype(jnp.int32)
    ranked = jnp.sum(jnp.cumsum(onehot, axis=0) * onehot, axis=1) - 1
    slot_of = jnp.where(is_live, target * capacity + ranked, -1)
    slots = jnp.arange(groups * capacity, dtype=jnp.int32)
    return (slots[:, None] == slot_of[None, :]).astype(jnp.bfloat16)


def orthogonalize(moment):
    moment_f = moment.astype(jnp.float32)
    frobenius = jnp.sqrt(jnp.sum(moment_f * moment_f))
    current = (moment_f / (frobenius + norm_floor)).astype(jnp.bfloat16)
    for sweep_index in range(2):
        gramian = lax.dot_general(
            current, current, (((1,), (1,)), ((), ())), preferred_element_type=jnp.float32
        ).astype(jnp.bfloat16)
        squared = jnp.dot(gramian, gramian, preferred_element_type=jnp.float32)
        poly = (cubic_term * gramian.astype(jnp.float32) + quintic_term * squared).astype(
            jnp.bfloat16
        )
        current = (
            linear_term * current.astype(jnp.float32)
            + jnp.dot(poly, current, preferred_element_type=jnp.float32)
        ).astype(jnp.bfloat16)
    return current


def relocate(weight, moment, perm):
    groups = lax.axis_size("expert")
    weight_flat = weight.reshape(groups, -1)
    moment_flat = moment.reshape(groups, -1)
    spread_w, spread_m = (
        lax.all_to_all(weight_flat, "expert", split_axis=0, concat_axis=0, tiled=True),
        lax.all_to_all(moment_flat, "expert", split_axis=0, concat_axis=0, tiled=True),
    )
    devices = jnp.arange(groups, dtype=jnp.int32)
    inverse = jnp.sum(jnp.where(perm[None, :] == devices[:, None], devices[None, :], 0), axis=1)
    ordered_w = jnp.take(spread_w, inverse, axis=0)
    ordered_m = jnp.take(spread_m, inverse, axis=0)
    back_w, back_m = (
        lax.all_to_all(ordered_w, "expert", split_axis=0, concat_axis=0, tiled=True),
        lax.all_to_all(ordered_m, "expert", split_axis=0, concat_axis=0, tiled=True),
    )
    return (back_w.reshape(weight.shape), back_m.reshape(moment.shape))


def routed_plan(
    grad_hidden,
    grad_out,
    grad_route,
    live_rows,
    w_down,
    w_moment,
    perm,
    fwd_hidden,
    fwd_route,
    fwd_gate,
):
    groups = lax.axis_size("expert")
    grad_count = grad_hidden.shape[0]
    capacity = max(4, 2 * grad_count // groups)
    is_live = jnp.arange(grad_count, dtype=jnp.int32) < live_rows[0]
    route_ids = grad_route[:, 0]
    weight, moment = relocate(w_down, w_moment, perm)
    target = lookup(route_ids, perm)
    selector = slot_matrix(target, is_live, groups, capacity)
    hidden_buf = (
        jnp.dot(selector, grad_hidden, preferred_element_type=jnp.float32)
        .astype(jnp.bfloat16)
        .reshape(groups, capacity, -1)
    )
    outgrad_buf = (
        jnp.dot(selector, grad_out, preferred_element_type=jnp.float32)
        .astype(jnp.bfloat16)
        .reshape(groups, capacity, -1)
    )
    recv_hidden, recv_outgrad = (
        lax.all_to_all(hidden_buf, "expert", split_axis=0, concat_axis=0, tiled=True),
        lax.all_to_all(outgrad_buf, "expert", split_axis=0, concat_axis=0, tiled=True),
    )
    grad = lax.dot_general(
        recv_hidden.reshape(groups * capacity, -1),
        recv_outgrad.reshape(groups * capacity, -1),
        (((0,), (0,)), ((), ())),
        preferred_element_type=jnp.float32,
    )
    moment_new = (moment_decay * moment[0].astype(jnp.float32) + grad).astype(jnp.bfloat16)
    ortho = orthogonalize(moment_new)
    weight_new = (weight[0].astype(jnp.float32) - step_scale * ortho.astype(jnp.float32)).astype(
        jnp.bfloat16
    )
    weight_new = weight_new[None]
    moment_new = moment_new[None]
    fwd_ids = fwd_route[:, 0]
    placed_weight, placed_moment = (weight_new, moment_new)
    fwd_target = lookup(fwd_ids, perm)
    fwd_weight = weight_new[0]
    fwd_count = fwd_hidden.shape[0]
    fwd_capacity = max(4, 2 * fwd_count // groups)
    fwd_selector = slot_matrix(fwd_target, jnp.ones((fwd_count,), dtype=bool), groups, fwd_capacity)
    fwd_buf = (
        jnp.dot(fwd_selector, fwd_hidden, preferred_element_type=jnp.float32)
        .astype(jnp.bfloat16)
        .reshape(groups, fwd_capacity, -1)
    )
    produced = jnp.einsum(
        "gkf,fd->gkd",
        lax.all_to_all(fwd_buf, "expert", split_axis=0, concat_axis=0, tiled=True),
        fwd_weight,
        preferred_element_type=jnp.float32,
    ).astype(jnp.bfloat16)
    returned = lax.all_to_all(produced, "expert", split_axis=0, concat_axis=0, tiled=True)
    fwd_rows_out = lax.dot_general(
        fwd_selector,
        returned.reshape(groups * fwd_capacity, -1),
        (((0,), (0,)), ((), ())),
        preferred_element_type=jnp.float32,
    )
    fwd_out = (fwd_rows_out * fwd_gate[:, None]).astype(jnp.bfloat16)
    return (placed_weight, placed_moment, fwd_out)


def solution(mesh):
    groups = mesh.shape["expert"]
    in_specs = (
        P(("layer", "expert"), None),
        P(("layer", "expert"), None),
        P(("layer", "expert"), None),
        P(("layer", "expert")),
        P(("layer", "expert"), None, None),
        P(("layer", "expert"), None, None),
        P("layer"),
        P(("layer", "expert"), None),
        P(("layer", "expert"), None),
        P(("layer", "expert")),
    )
    out_specs = (
        P(("layer", "expert"), None, None),
        P(("layer", "expert"), None, None),
        P(("layer", "expert"), None),
    )

    def per_device(*args):
        few = groups & (groups - 1) == 0 and groups <= 2 * args[0].shape[0] // groups
        return (partner_plan if few else routed_plan)(*args)

    return jax.shard_map(
        per_device, mesh=mesh, in_specs=in_specs, out_specs=out_specs, check_vma=False
    )
```

```python
import functools

import jax
import jax.numpy as jnp
from jax import lax
from jax.experimental import pallas as pl
from jax.experimental.pallas import tpu as pltpu
from jax.sharding import PartitionSpec as P

linear_term = 3.4445
cubic_term = -4.775
quintic_term = 2.0315
moment_decay = 0.9
step_scale = 0.25
norm_floor = 1e-07

F32 = jnp.float32
BF16 = jnp.bfloat16
HBM = pl.BlockSpec(memory_space=pltpu.HBM)
VMEM = pl.BlockSpec(memory_space=pltpu.VMEM)
SMEM = pl.BlockSpec(memory_space=pltpu.SMEM)
ANY = pl.BlockSpec(memory_space=pl.ANY)
MIB = 1 << 20


def fetched(refs, held, sem):
    copies = [pltpu.make_async_copy(ref, room, sem.at[n]) for n, (ref, room) in enumerate(zip(refs, held))]
    for copy in copies:
        copy.start()
    for copy in copies:
        copy.wait()


def rooms(arrays):
    return [pltpu.VMEM(a.shape, a.dtype) for a in arrays] + [pltpu.SemaphoreType.DMA((len(arrays),))]


def chunk_at(ref, lead, k, rows, columns):
    return ref.at[
        lead,
        pl.ds(pl.multiple_of((k // 2) * rows, rows), rows),
        pl.ds(pl.multiple_of((k % 2) * columns, columns), columns),
    ]


def slot_rows(route, live, groups, capacity, me_ref, perm_ref):
    rows = route.shape[1]
    experts = lax.broadcasted_iota(jnp.int32, (groups, rows), 0)
    onehot = jnp.where((experts == route) & live, 1.0, 0.0).astype(BF16)
    before = lax.broadcasted_iota(jnp.int32, (rows, rows), 0)
    after = lax.broadcasted_iota(jnp.int32, (rows, rows), 1)
    upto = jnp.where(before <= after, 1.0, 0.0).astype(BF16)
    ranks = jnp.dot(onehot, upto, preferred_element_type=F32)
    rank = jnp.sum(ranks * onehot.astype(F32), axis=0, keepdims=True).astype(jnp.int32) - 1
    partner = jnp.zeros_like(route)
    for e in range(groups):
        partner = jnp.where(route == e, perm_ref[e] ^ me_ref[0], partner)
    return jnp.where(live, partner * capacity + rank, -1)


def selector_of(slot, slots):
    rows = slot.shape[1]
    places = lax.broadcasted_iota(jnp.int32, (slots, rows), 0)
    return jnp.where(places == slot, 1.0, 0.0).astype(BF16)


def pack_kernel(groups, live_ref, me_ref, perm_ref, *refs):
    sources, pieces, (slot_ref, gates_ref) = refs[:6], refs[7 : 7 + groups], refs[7 + groups : 9 + groups]
    held, sem = refs[9 + groups : 15 + groups], refs[-1]
    route_ref, fwd_route_ref, hidden_ref, out_ref, fwd_ref, gate_ref = held
    copies = [pltpu.make_async_copy(ref, room, sem.at[n]) for n, (ref, room) in enumerate(zip(sources, held))]
    for copy in copies:
        copy.start()
    rows, ff = hidden_ref.shape
    d = out_ref.shape[1]
    capacity = pieces[0].shape[0]
    slots = groups * capacity
    place = lax.broadcasted_iota(jnp.int32, (1, rows), 1)

    def fill(first, selector, source_ref):
        chosen = jnp.dot(selector, source_ref[...], preferred_element_type=F32).astype(BF16)
        for s, piece in zip(mixed_order(groups), pieces):
            piece[:, first : first + source_ref.shape[1]] = chosen[s * capacity : (s + 1) * capacity]

    copies[0].wait()
    slot = slot_rows(route_ref[...], place < live_ref[0], groups, capacity, me_ref, perm_ref)
    selector = selector_of(slot, slots)
    copies[1].wait()
    fwd_slot = slot_rows(fwd_route_ref[...], place >= 0, groups, capacity, me_ref, perm_ref)
    slot_ref[...] = fwd_slot
    copies[2].wait()
    fill(0, selector, hidden_ref)
    copies[3].wait()
    fill(ff, selector, out_ref)
    copies[4].wait()
    fill(ff + d, selector_of(fwd_slot, slots), fwd_ref)
    copies[5].wait()
    down = lax.broadcasted_iota(jnp.int32, (rows, rows), 0)
    across = lax.broadcasted_iota(jnp.int32, (rows, rows), 1)
    gates_ref[...] = jnp.sum(jnp.where(down == across, gate_ref[...], 0.0), axis=1, keepdims=True)


def pack_rows(live_rows, me, perm, route, fwd_route, hidden, grad_out, fwd_hidden, gate, earlier, groups, capacity):
    rows, ff = hidden.shape
    width = 2 * ff + grad_out.shape[1]
    sources = (route.reshape(1, rows), fwd_route.reshape(1, rows), hidden, grad_out, fwd_hidden, gate.reshape(1, rows))
    *pieces, slot, gates = pl.pallas_call(
        functools.partial(pack_kernel, groups),
        out_shape=(jax.ShapeDtypeStruct((capacity, width), BF16),) * groups
        + (jax.ShapeDtypeStruct((1, rows), jnp.int32), jax.ShapeDtypeStruct((rows, 1), F32)),
        in_specs=[SMEM] * 3 + [HBM] * 6 + [VMEM],
        out_specs=(VMEM,) * (groups + 2),
        scratch_shapes=[pltpu.VMEM(a.shape, a.dtype) for a in sources] + [pltpu.SemaphoreType.DMA((len(sources),))],
        compiler_params=pltpu.CompilerParams(vmem_limit_bytes=32 * MIB),
        cost_estimate=pl.CostEstimate(
            flops=2 * groups * capacity * rows * width, bytes_accessed=6 * rows * width, transcendentals=0
        ),
        name="pack_rows",
    )(live_rows, me, perm, *sources, earlier)
    return pieces, slot, gates


def split_kernel(partners, me_ref, moment_ref, weight_ref, *refs):
    pieces, sem = refs[:-1], refs[-1]
    copies = []
    for s, piece in zip(partners, pieces):
        rows, columns = piece.shape[1:]
        for lead, source in enumerate((moment_ref, weight_ref)):
            chunk = chunk_at(source, 0, me_ref[0] ^ s, rows, columns)
            copies.append(pltpu.make_async_copy(chunk, piece.at[lead], sem.at[len(copies)]))
    for copy in copies:
        copy.start()
    for copy in copies:
        copy.wait()


def split(me, moment, weight, groups, partners):
    _, ff, d = weight.shape
    piece = jax.ShapeDtypeStruct((2, ff // (groups // 2), d // 2), BF16)
    return pl.pallas_call(
        functools.partial(split_kernel, partners),
        out_shape=(piece,) * len(partners),
        in_specs=[SMEM, HBM, HBM],
        out_specs=(VMEM,) * len(partners),
        scratch_shapes=[pltpu.SemaphoreType.DMA((2 * len(partners),))],
        compiler_params=pltpu.CompilerParams(vmem_limit_bytes=60 * MIB),
        cost_estimate=pl.CostEstimate(
            flops=0, bytes_accessed=8 * ff * d * len(partners) // groups, transcendentals=0
        ),
        name="split",
    )(me, moment, weight)


def reorder_kernel(me_ref, perm_ref, *refs):
    groups = len(refs) // 2 - 1
    sources, targets, held = refs[:groups], refs[groups + 1 : 2 * groups + 1], refs[-1]
    me, order = me_ref[0], mixed_order(groups)
    for s, source in zip(order, sources):
        held[me ^ perm_ref[me ^ s]] = source[...]
    for s, target in zip(order, targets):
        target[...] = held[s]


def reorder(me, perm, pieces, earlier):
    groups = len(pieces)
    piece = jax.ShapeDtypeStruct(pieces[0].shape, BF16)
    return pl.pallas_call(
        reorder_kernel,
        out_shape=(piece,) * groups,
        in_specs=[SMEM, SMEM] + [VMEM] * (groups + 1),
        out_specs=(VMEM,) * groups,
        scratch_shapes=[pltpu.VMEM((groups,) + pieces[0].shape, BF16)],
        compiler_params=pltpu.CompilerParams(vmem_limit_bytes=32 * MIB),
        cost_estimate=pl.CostEstimate(flops=0, bytes_accessed=4 * groups * pieces[0].size, transcendentals=0),
        name="reorder",
    )(me, perm, *pieces, earlier)


def update_kernel(groups, me_ref, *refs):
    packed, pieces, produced = refs[:groups], refs[groups : 2 * groups], refs[2 * groups + 2 : 3 * groups + 2]
    weight_new_ref, moment_new_ref = refs[2 * groups : 2 * groups + 2]
    held, rows_ref = refs[-2:]
    _, ff, d = held.shape
    capacity = packed[0].shape[0]
    for n, piece in enumerate(packed):
        rows_ref[n * capacity : (n + 1) * capacity] = piece[...]
    for s, piece in zip(mixed_order(groups), pieces):
        rows, columns = piece.shape[1:]
        for lead in range(2):
            chunk_at(held, lead, me_ref[0] ^ s, rows, columns)[...] = piece[lead]
    grad = lax.dot_general(
        rows_ref[:, :ff], rows_ref[:, ff : ff + d], (((0,), (0,)), ((), ())), preferred_element_type=F32
    )
    moment_new = (moment_decay * held[0].astype(F32) + grad).astype(BF16)
    moment_new_ref[...] = moment_new
    moment_f = moment_new.astype(F32)
    frobenius = jnp.sqrt(jnp.sum(moment_f * moment_f))
    current = (moment_f / (frobenius + norm_floor)).astype(BF16)
    for _ in range(2):
        gramian = lax.dot_general(
            current, current, (((1,), (1,)), ((), ())), preferred_element_type=F32
        ).astype(BF16)
        squared = jnp.dot(gramian, gramian, preferred_element_type=F32)
        poly = (cubic_term * gramian.astype(F32) + quintic_term * squared).astype(BF16)
        current = (
            linear_term * current.astype(F32) + jnp.dot(poly, current, preferred_element_type=F32)
        ).astype(BF16)
    weight_new = (held[1].astype(F32) - step_scale * current.astype(F32)).astype(BF16)
    weight_new_ref[...] = weight_new
    product = jnp.dot(rows_ref[:, ff + d :], weight_new, preferred_element_type=F32).astype(BF16)
    for n, piece in enumerate(produced):
        piece[...] = product[n * capacity : (n + 1) * capacity]


def update(me, packed, pieces, ff, d):
    groups = len(pieces)
    capacity, width = packed[0].shape
    slots = groups * capacity
    shape = jax.ShapeDtypeStruct((ff, d), BF16)
    weight_new, moment_new, *produced = pl.pallas_call(
        functools.partial(update_kernel, groups),
        out_shape=(shape, shape) + (jax.ShapeDtypeStruct((capacity, d), BF16),) * groups,
        in_specs=[SMEM] + [VMEM] * (2 * groups),
        out_specs=(VMEM,) * (groups + 2),
        scratch_shapes=[pltpu.VMEM((2, ff, d), BF16), pltpu.VMEM((slots, width), BF16)],
        compiler_params=pltpu.CompilerParams(vmem_limit_bytes=40 * MIB),
        cost_estimate=pl.CostEstimate(
            flops=4 * ff * d * slots + 8 * ff * ff * d + 4 * ff**3,
            bytes_accessed=8 * ff * d + 2 * slots * (width + d),
            transcendentals=1,
        ),
        name="update",
    )(me, *packed, *pieces)
    return weight_new, moment_new, produced


def finish_kernel(groups, slot_ref, gates_ref, *refs):
    pieces, (out_ref, returned_ref) = refs[:groups], refs[groups:]
    capacity = pieces[0].shape[0]
    for s, piece in zip(mixed_order(groups), pieces):
        returned_ref[s * capacity : (s + 1) * capacity] = piece[...]
    selector = selector_of(slot_ref[...], groups * capacity)
    expert_out = lax.dot_general(
        selector, returned_ref[...], (((0,), (0,)), ((), ())), preferred_element_type=F32
    )
    out_ref[...] = (gates_ref[...] * expert_out).astype(BF16)


def finish(slot, gates, returned):
    groups = len(returned)
    rows = slot.shape[1]
    capacity, d = returned[0].shape
    slots = groups * capacity
    return pl.pallas_call(
        functools.partial(finish_kernel, groups),
        out_shape=jax.ShapeDtypeStruct((rows, d), BF16),
        in_specs=[VMEM] * (2 + groups),
        out_specs=VMEM,
        scratch_shapes=[pltpu.VMEM((slots, d), BF16)],
        compiler_params=pltpu.CompilerParams(vmem_limit_bytes=32 * MIB),
        cost_estimate=pl.CostEstimate(
            flops=2 * slots * rows * d, bytes_accessed=2 * d * (slots + rows), transcendentals=0
        ),
        name="finish",
    )(slot, gates, *returned)


def mixed_order(groups):
    def both_ends(partners):
        middle = (len(partners) + 1) // 2
        first, second = partners[:middle], partners[middle:]
        return [s for pair in zip(first, second + [None]) for s in pair if s is not None]

    half = groups // 2
    far, near = both_ends(list(range(half, groups))), both_ends(list(range(half - 1, 0, -1)))
    return [0] + [s for pair in zip(far, near + [None]) for s in pair if s is not None]


def swap(pieces):
    groups = len(pieces)
    order = mixed_order(groups)
    return [pieces[0]] + [
        lax.ppermute(piece, "expert", [(i, i ^ s) for i in range(groups)]) for s, piece in zip(order[1:], pieces[1:])
    ]


def partner_plan(
    grad_hidden, grad_out, grad_route, live_rows, w_down, w_moment, perm, fwd_hidden, fwd_route, fwd_gate
):
    groups = lax.axis_size("expert")
    me = lax.axis_index("expert").astype(jnp.int32).reshape(1)
    capacity = max(4, 2 * grad_hidden.shape[0] // groups)
    ff, d = w_down.shape[1:]
    order = mixed_order(groups)
    first = order[1:6]
    blocks = dict(zip(first, split(me, w_moment, w_down, groups, first)))
    others = [s for s in order if s not in first]
    blocks.update(zip(others, split(me, w_moment, w_down, groups, others)))
    spread = swap([blocks[s] for s in order])
    packed, fwd_slot, gates = pack_rows(
        live_rows, me, perm, grad_route, fwd_route, grad_hidden, grad_out, fwd_hidden, fwd_gate,
        spread[2], groups, capacity,
    )
    received = swap(packed)
    placed = swap(reorder(me, perm, spread, received[groups // 3]))
    weight_new, moment_new, produced = update(me, received, placed, ff, d)
    return weight_new[None], moment_new[None], finish(fwd_slot, gates, swap(produced))


def lookup(route_ids, mapping):
    columns = jnp.arange(mapping.shape[0], dtype=jnp.int32)
    hits = route_ids[:, None] == columns[None, :]
    return jnp.sum(jnp.where(hits, mapping[None, :], 0), axis=1)


def slot_matrix(target, is_live, groups, capacity):
    columns = jnp.arange(groups, dtype=jnp.int32)
    onehot = ((target[:, None] == columns[None, :]) & is_live[:, None]).astype(jnp.int32)
    ranked = jnp.sum(jnp.cumsum(onehot, axis=0) * onehot, axis=1) - 1
    slot_of = jnp.where(is_live, target * capacity + ranked, -1)
    slots = jnp.arange(groups * capacity, dtype=jnp.int32)
    return (slots[:, None] == slot_of[None, :]).astype(jnp.bfloat16)


def orthogonalize(moment):
    moment_f = moment.astype(jnp.float32)
    frobenius = jnp.sqrt(jnp.sum(moment_f * moment_f))
    current = (moment_f / (frobenius + norm_floor)).astype(jnp.bfloat16)
    for sweep_index in range(2):
        gramian = lax.dot_general(
            current, current, (((1,), (1,)), ((), ())), preferred_element_type=jnp.float32
        ).astype(jnp.bfloat16)
        squared = jnp.dot(gramian, gramian, preferred_element_type=jnp.float32)
        poly = (cubic_term * gramian.astype(jnp.float32) + quintic_term * squared).astype(
            jnp.bfloat16
        )
        current = (
            linear_term * current.astype(jnp.float32)
            + jnp.dot(poly, current, preferred_element_type=jnp.float32)
        ).astype(jnp.bfloat16)
    return current


def relocate(weight, moment, perm):
    groups = lax.axis_size("expert")
    weight_flat = weight.reshape(groups, -1)
    moment_flat = moment.reshape(groups, -1)
    spread_w, spread_m = (
        lax.all_to_all(weight_flat, "expert", split_axis=0, concat_axis=0, tiled=True),
        lax.all_to_all(moment_flat, "expert", split_axis=0, concat_axis=0, tiled=True),
    )
    devices = jnp.arange(groups, dtype=jnp.int32)
    inverse = jnp.sum(jnp.where(perm[None, :] == devices[:, None], devices[None, :], 0), axis=1)
    ordered_w = jnp.take(spread_w, inverse, axis=0)
    ordered_m = jnp.take(spread_m, inverse, axis=0)
    back_w, back_m = (
        lax.all_to_all(ordered_w, "expert", split_axis=0, concat_axis=0, tiled=True),
        lax.all_to_all(ordered_m, "expert", split_axis=0, concat_axis=0, tiled=True),
    )
    return (back_w.reshape(weight.shape), back_m.reshape(moment.shape))


def routed_plan(
    grad_hidden,
    grad_out,
    grad_route,
    live_rows,
    w_down,
    w_moment,
    perm,
    fwd_hidden,
    fwd_route,
    fwd_gate,
):
    groups = lax.axis_size("expert")
    grad_count = grad_hidden.shape[0]
    capacity = max(4, 2 * grad_count // groups)
    is_live = jnp.arange(grad_count, dtype=jnp.int32) < live_rows[0]
    route_ids = grad_route[:, 0]
    weight, moment = relocate(w_down, w_moment, perm)
    target = lookup(route_ids, perm)
    selector = slot_matrix(target, is_live, groups, capacity)
    hidden_buf = (
        jnp.dot(selector, grad_hidden, preferred_element_type=jnp.float32)
        .astype(jnp.bfloat16)
        .reshape(groups, capacity, -1)
    )
    outgrad_buf = (
        jnp.dot(selector, grad_out, preferred_element_type=jnp.float32)
        .astype(jnp.bfloat16)
        .reshape(groups, capacity, -1)
    )
    recv_hidden, recv_outgrad = (
        lax.all_to_all(hidden_buf, "expert", split_axis=0, concat_axis=0, tiled=True),
        lax.all_to_all(outgrad_buf, "expert", split_axis=0, concat_axis=0, tiled=True),
    )
    grad = lax.dot_general(
        recv_hidden.reshape(groups * capacity, -1),
        recv_outgrad.reshape(groups * capacity, -1),
        (((0,), (0,)), ((), ())),
        preferred_element_type=jnp.float32,
    )
    moment_new = (moment_decay * moment[0].astype(jnp.float32) + grad).astype(jnp.bfloat16)
    ortho = orthogonalize(moment_new)
    weight_new = (weight[0].astype(jnp.float32) - step_scale * ortho.astype(jnp.float32)).astype(
        jnp.bfloat16
    )
    weight_new = weight_new[None]
    moment_new = moment_new[None]
    fwd_ids = fwd_route[:, 0]
    placed_weight, placed_moment = (weight_new, moment_new)
    fwd_target = lookup(fwd_ids, perm)
    fwd_weight = weight_new[0]
    fwd_count = fwd_hidden.shape[0]
    fwd_capacity = max(4, 2 * fwd_count // groups)
    fwd_selector = slot_matrix(fwd_target, jnp.ones((fwd_count,), dtype=bool), groups, fwd_capacity)
    fwd_buf = (
        jnp.dot(fwd_selector, fwd_hidden, preferred_element_type=jnp.float32)
        .astype(jnp.bfloat16)
        .reshape(groups, fwd_capacity, -1)
    )
    produced = jnp.einsum(
        "gkf,fd->gkd",
        lax.all_to_all(fwd_buf, "expert", split_axis=0, concat_axis=0, tiled=True),
        fwd_weight,
        preferred_element_type=jnp.float32,
    ).astype(jnp.bfloat16)
    returned = lax.all_to_all(produced, "expert", split_axis=0, concat_axis=0, tiled=True)
    fwd_rows_out = lax.dot_general(
        fwd_selector,
        returned.reshape(groups * fwd_capacity, -1),
        (((0,), (0,)), ((), ())),
        preferred_element_type=jnp.float32,
    )
    fwd_out = (fwd_rows_out * fwd_gate[:, None]).astype(jnp.bfloat16)
    return (placed_weight, placed_moment, fwd_out)


def solution(mesh):
    groups = mesh.shape["expert"]
    in_specs = (
        P(("layer", "expert"), None),
        P(("layer", "expert"), None),
        P(("layer", "expert"), None),
        P(("layer", "expert")),
        P(("layer", "expert"), None, None),
        P(("layer", "expert"), None, None),
        P("layer"),
        P(("layer", "expert"), None),
        P(("layer", "expert"), None),
        P(("layer", "expert")),
    )
    out_specs = (
        P(("layer", "expert"), None, None),
        P(("layer", "expert"), None, None),
        P(("layer", "expert"), None),
    )

    def per_device(*args):
        few = groups & (groups - 1) == 0 and groups <= 2 * args[0].shape[0] // groups
        return (partner_plan if few else routed_plan)(*args)

    return jax.shard_map(
        per_device, mesh=mesh, in_specs=in_specs, out_specs=out_specs, check_vma=False
    )
```

```python
import functools

import jax
import jax.numpy as jnp
from jax import lax
from jax.experimental import pallas as pl
from jax.experimental.pallas import tpu as pltpu
from jax.sharding import PartitionSpec as P

linear_term = 3.4445
cubic_term = -4.775
quintic_term = 2.0315
moment_decay = 0.9
step_scale = 0.25
norm_floor = 1e-07

F32 = jnp.float32
BF16 = jnp.bfloat16
HBM = pl.BlockSpec(memory_space=pltpu.HBM)
VMEM = pl.BlockSpec(memory_space=pltpu.VMEM)
SMEM = pl.BlockSpec(memory_space=pltpu.SMEM)
ANY = pl.BlockSpec(memory_space=pl.ANY)
MIB = 1 << 20


def fetched(refs, held, sem):
    copies = [pltpu.make_async_copy(ref, room, sem.at[n]) for n, (ref, room) in enumerate(zip(refs, held))]
    for copy in copies:
        copy.start()
    for copy in copies:
        copy.wait()


def rooms(arrays):
    return [pltpu.VMEM(a.shape, a.dtype) for a in arrays] + [pltpu.SemaphoreType.DMA((len(arrays),))]


def chunk_at(ref, lead, k, rows, columns):
    return ref.at[
        lead,
        pl.ds(pl.multiple_of((k // 2) * rows, rows), rows),
        pl.ds(pl.multiple_of((k % 2) * columns, columns), columns),
    ]


def slot_rows(route, live, groups, capacity, me_ref, perm_ref):
    rows = route.shape[1]
    experts = lax.broadcasted_iota(jnp.int32, (groups, rows), 0)
    onehot = jnp.where((experts == route) & live, 1.0, 0.0).astype(BF16)
    before = lax.broadcasted_iota(jnp.int32, (rows, rows), 0)
    after = lax.broadcasted_iota(jnp.int32, (rows, rows), 1)
    upto = jnp.where(before <= after, 1.0, 0.0).astype(BF16)
    ranks = jnp.dot(onehot, upto, preferred_element_type=F32)
    rank = jnp.sum(ranks * onehot.astype(F32), axis=0, keepdims=True).astype(jnp.int32) - 1
    partner = jnp.zeros_like(route)
    for e in range(groups):
        partner = jnp.where(route == e, perm_ref[e] ^ me_ref[0], partner)
    return jnp.where(live, partner * capacity + rank, -1)


def selector_of(slot, slots):
    rows = slot.shape[1]
    places = lax.broadcasted_iota(jnp.int32, (slots, rows), 0)
    return jnp.where(places == slot, 1.0, 0.0).astype(BF16)


def pack_kernel(groups, live_ref, me_ref, perm_ref, *refs):
    sources, pieces, (slot_ref, gates_ref) = refs[:6], refs[7 : 7 + groups], refs[7 + groups : 9 + groups]
    held, sem = refs[9 + groups : 15 + groups], refs[-1]
    route_ref, fwd_route_ref, hidden_ref, out_ref, fwd_ref, gate_ref = held
    copies = [pltpu.make_async_copy(ref, room, sem.at[n]) for n, (ref, room) in enumerate(zip(sources, held))]
    for copy in copies:
        copy.start()
    rows, ff = hidden_ref.shape
    d = out_ref.shape[1]
    capacity = pieces[0].shape[0]
    slots = groups * capacity
    place = lax.broadcasted_iota(jnp.int32, (1, rows), 1)

    def fill(first, selector, source_ref):
        chosen = jnp.dot(selector, source_ref[...], preferred_element_type=F32).astype(BF16)
        for s, piece in zip(mixed_order(groups), pieces):
            piece[:, first : first + source_ref.shape[1]] = chosen[s * capacity : (s + 1) * capacity]

    copies[0].wait()
    slot = slot_rows(route_ref[...], place < live_ref[0], groups, capacity, me_ref, perm_ref)
    selector = selector_of(slot, slots)
    copies[1].wait()
    fwd_slot = slot_rows(fwd_route_ref[...], place >= 0, groups, capacity, me_ref, perm_ref)
    slot_ref[...] = fwd_slot
    copies[2].wait()
    fill(0, selector, hidden_ref)
    copies[3].wait()
    fill(ff, selector, out_ref)
    copies[4].wait()
    fill(ff + d, selector_of(fwd_slot, slots), fwd_ref)
    copies[5].wait()
    down = lax.broadcasted_iota(jnp.int32, (rows, rows), 0)
    across = lax.broadcasted_iota(jnp.int32, (rows, rows), 1)
    gates_ref[...] = jnp.sum(jnp.where(down == across, gate_ref[...], 0.0), axis=1, keepdims=True)


def pack_rows(live_rows, me, perm, route, fwd_route, hidden, grad_out, fwd_hidden, gate, earlier, groups, capacity):
    rows, ff = hidden.shape
    width = 2 * ff + grad_out.shape[1]
    sources = (route.reshape(1, rows), fwd_route.reshape(1, rows), hidden, grad_out, fwd_hidden, gate.reshape(1, rows))
    *pieces, slot, gates = pl.pallas_call(
        functools.partial(pack_kernel, groups),
        out_shape=(jax.ShapeDtypeStruct((capacity, width), BF16),) * groups
        + (jax.ShapeDtypeStruct((1, rows), jnp.int32), jax.ShapeDtypeStruct((rows, 1), F32)),
        in_specs=[SMEM] * 3 + [HBM] * 6 + [VMEM],
        out_specs=(VMEM,) * (groups + 2),
        scratch_shapes=[pltpu.VMEM(a.shape, a.dtype) for a in sources] + [pltpu.SemaphoreType.DMA((len(sources),))],
        compiler_params=pltpu.CompilerParams(vmem_limit_bytes=32 * MIB),
        cost_estimate=pl.CostEstimate(
            flops=2 * groups * capacity * rows * width, bytes_accessed=6 * rows * width, transcendentals=0
        ),
        name="pack_rows",
    )(live_rows, me, perm, *sources, earlier)
    return pieces, slot, gates


def split_kernel(me_ref, moment_ref, weight_ref, *refs):
    pieces, held, sem = refs[:-3], refs[-3:-1], refs[-1]
    fetched((moment_ref, weight_ref), held, sem)
    for s, piece in zip(mixed_order(len(pieces)), pieces):
        rows, columns = piece.shape[1:]
        for lead, source in enumerate(held):
            piece[lead] = chunk_at(source, 0, me_ref[0] ^ s, rows, columns)[...]


def split(me, moment, weight, groups):
    _, ff, d = weight.shape
    piece = jax.ShapeDtypeStruct((2, ff // (groups // 2), d // 2), BF16)
    return pl.pallas_call(
        split_kernel,
        out_shape=(piece,) * groups,
        in_specs=[SMEM, HBM, HBM],
        out_specs=(VMEM,) * groups,
        scratch_shapes=rooms((moment, weight)),
        compiler_params=pltpu.CompilerParams(vmem_limit_bytes=60 * MIB),
        cost_estimate=pl.CostEstimate(flops=0, bytes_accessed=8 * ff * d, transcendentals=0),
        name="split",
    )(me, moment, weight)


def reorder_kernel(me_ref, perm_ref, *refs):
    groups = len(refs) // 2 - 1
    sources, targets, held = refs[:groups], refs[groups + 1 : 2 * groups + 1], refs[-1]
    me, order = me_ref[0], mixed_order(groups)
    for s, source in zip(order, sources):
        held[me ^ perm_ref[me ^ s]] = source[...]
    for s, target in zip(order, targets):
        target[...] = held[s]


def reorder(me, perm, pieces, earlier):
    groups = len(pieces)
    piece = jax.ShapeDtypeStruct(pieces[0].shape, BF16)
    return pl.pallas_call(
        reorder_kernel,
        out_shape=(piece,) * groups,
        in_specs=[SMEM, SMEM] + [VMEM] * (groups + 1),
        out_specs=(VMEM,) * groups,
        scratch_shapes=[pltpu.VMEM((groups,) + pieces[0].shape, BF16)],
        compiler_params=pltpu.CompilerParams(vmem_limit_bytes=32 * MIB),
        cost_estimate=pl.CostEstimate(flops=0, bytes_accessed=4 * groups * pieces[0].size, transcendentals=0),
        name="reorder",
    )(me, perm, *pieces, earlier)


def update_kernel(groups, me_ref, *refs):
    packed, pieces, produced = refs[:groups], refs[groups : 2 * groups], refs[2 * groups + 2 : 3 * groups + 2]
    weight_new_ref, moment_new_ref = refs[2 * groups : 2 * groups + 2]
    held, rows_ref = refs[-2:]
    _, ff, d = held.shape
    capacity = packed[0].shape[0]
    for n, piece in enumerate(packed):
        rows_ref[n * capacity : (n + 1) * capacity] = piece[...]
    for s, piece in zip(mixed_order(groups), pieces):
        rows, columns = piece.shape[1:]
        for lead in range(2):
            chunk_at(held, lead, me_ref[0] ^ s, rows, columns)[...] = piece[lead]
    grad = lax.dot_general(
        rows_ref[:, :ff], rows_ref[:, ff : ff + d], (((0,), (0,)), ((), ())), preferred_element_type=F32
    )
    moment_new = (moment_decay * held[0].astype(F32) + grad).astype(BF16)
    moment_new_ref[...] = moment_new
    moment_f = moment_new.astype(F32)
    frobenius = jnp.sqrt(jnp.sum(moment_f * moment_f))
    current = (moment_f / (frobenius + norm_floor)).astype(BF16)
    for _ in range(2):
        gramian = lax.dot_general(
            current, current, (((1,), (1,)), ((), ())), preferred_element_type=F32
        ).astype(BF16)
        squared = jnp.dot(gramian, gramian, preferred_element_type=F32)
        poly = (cubic_term * gramian.astype(F32) + quintic_term * squared).astype(BF16)
        current = (
            linear_term * current.astype(F32) + jnp.dot(poly, current, preferred_element_type=F32)
        ).astype(BF16)
    weight_new = (held[1].astype(F32) - step_scale * current.astype(F32)).astype(BF16)
    weight_new_ref[...] = weight_new
    product = jnp.dot(rows_ref[:, ff + d :], weight_new, preferred_element_type=F32).astype(BF16)
    for n, piece in enumerate(produced):
        piece[...] = product[n * capacity : (n + 1) * capacity]


def update(me, packed, pieces, ff, d):
    groups = len(pieces)
    capacity, width = packed[0].shape
    slots = groups * capacity
    shape = jax.ShapeDtypeStruct((ff, d), BF16)
    weight_new, moment_new, *produced = pl.pallas_call(
        functools.partial(update_kernel, groups),
        out_shape=(shape, shape) + (jax.ShapeDtypeStruct((capacity, d), BF16),) * groups,
        in_specs=[SMEM] + [VMEM] * (2 * groups),
        out_specs=(VMEM,) * (groups + 2),
        scratch_shapes=[pltpu.VMEM((2, ff, d), BF16), pltpu.VMEM((slots, width), BF16)],
        compiler_params=pltpu.CompilerParams(vmem_limit_bytes=40 * MIB),
        cost_estimate=pl.CostEstimate(
            flops=4 * ff * d * slots + 8 * ff * ff * d + 4 * ff**3,
            bytes_accessed=8 * ff * d + 2 * slots * (width + d),
            transcendentals=1,
        ),
        name="update",
    )(me, *packed, *pieces)
    return weight_new, moment_new, produced


def emit_kernel(weight_ref, moment_ref, weight_out_ref, moment_out_ref, sem):
    copies = [
        pltpu.make_async_copy(source, target, sem.at[n])
        for n, (source, target) in enumerate(((weight_ref, weight_out_ref), (moment_ref, moment_out_ref)))
    ]
    for copy in copies:
        copy.start()
    for copy in copies:
        copy.wait()


def emit(weight, moment):
    shape = jax.ShapeDtypeStruct(weight.shape, BF16)
    return pl.pallas_call(
        emit_kernel,
        out_shape=(shape, shape),
        in_specs=[VMEM, VMEM],
        out_specs=(HBM, HBM),
        scratch_shapes=[pltpu.SemaphoreType.DMA((2,))],
        cost_estimate=pl.CostEstimate(flops=0, bytes_accessed=8 * weight.size, transcendentals=0),
        name="emit",
    )(weight, moment)


def finish_kernel(groups, slot_ref, gates_ref, *refs):
    pieces, (out_ref, returned_ref) = refs[:groups], refs[groups:]
    capacity = pieces[0].shape[0]
    for s, piece in zip(mixed_order(groups), pieces):
        returned_ref[s * capacity : (s + 1) * capacity] = piece[...]
    selector = selector_of(slot_ref[...], groups * capacity)
    expert_out = lax.dot_general(
        selector, returned_ref[...], (((0,), (0,)), ((), ())), preferred_element_type=F32
    )
    out_ref[...] = (gates_ref[...] * expert_out).astype(BF16)


def finish(slot, gates, returned):
    groups = len(returned)
    rows = slot.shape[1]
    capacity, d = returned[0].shape
    slots = groups * capacity
    return pl.pallas_call(
        functools.partial(finish_kernel, groups),
        out_shape=jax.ShapeDtypeStruct((rows, d), BF16),
        in_specs=[VMEM] * (2 + groups),
        out_specs=VMEM,
        scratch_shapes=[pltpu.VMEM((slots, d), BF16)],
        compiler_params=pltpu.CompilerParams(vmem_limit_bytes=32 * MIB),
        cost_estimate=pl.CostEstimate(
            flops=2 * slots * rows * d, bytes_accessed=2 * d * (slots + rows), transcendentals=0
        ),
        name="finish",
    )(slot, gates, *returned)


def mixed_order(groups):
    def both_ends(partners):
        middle = (len(partners) + 1) // 2
        first, second = partners[:middle], partners[middle:]
        return [s for pair in zip(first, second + [None]) for s in pair if s is not None]

    half = groups // 2
    far, near = both_ends(list(range(half, groups))), both_ends(list(range(half - 1, 0, -1)))
    return [0] + [s for pair in zip(far, near + [None]) for s in pair if s is not None]


def swap(pieces):
    groups = len(pieces)
    order = mixed_order(groups)
    return [pieces[0]] + [
        lax.ppermute(piece, "expert", [(i, i ^ s) for i in range(groups)]) for s, piece in zip(order[1:], pieces[1:])
    ]


def partner_plan(
    grad_hidden, grad_out, grad_route, live_rows, w_down, w_moment, perm, fwd_hidden, fwd_route, fwd_gate
):
    groups = lax.axis_size("expert")
    me = lax.axis_index("expert").astype(jnp.int32).reshape(1)
    capacity = max(4, 2 * grad_hidden.shape[0] // groups)
    ff, d = w_down.shape[1:]
    spread = swap(split(me, w_moment, w_down, groups))
    packed, fwd_slot, gates = pack_rows(
        live_rows, me, perm, grad_route, fwd_route, grad_hidden, grad_out, fwd_hidden, fwd_gate,
        spread[2 * groups // 3], groups, capacity,
    )
    received = swap(packed)
    placed = swap(reorder(me, perm, spread, received[groups // 3]))
    weight_new, moment_new, produced = update(me, received, placed, ff, d)
    weight_new, moment_new = emit(weight_new, moment_new)
    return weight_new[None], moment_new[None], finish(fwd_slot, gates, swap(produced))


def lookup(route_ids, mapping):
    columns = jnp.arange(mapping.shape[0], dtype=jnp.int32)
    hits = route_ids[:, None] == columns[None, :]
    return jnp.sum(jnp.where(hits, mapping[None, :], 0), axis=1)


def slot_matrix(target, is_live, groups, capacity):
    columns = jnp.arange(groups, dtype=jnp.int32)
    onehot = ((target[:, None] == columns[None, :]) & is_live[:, None]).astype(jnp.int32)
    ranked = jnp.sum(jnp.cumsum(onehot, axis=0) * onehot, axis=1) - 1
    slot_of = jnp.where(is_live, target * capacity + ranked, -1)
    slots = jnp.arange(groups * capacity, dtype=jnp.int32)
    return (slots[:, None] == slot_of[None, :]).astype(jnp.bfloat16)


def orthogonalize(moment):
    moment_f = moment.astype(jnp.float32)
    frobenius = jnp.sqrt(jnp.sum(moment_f * moment_f))
    current = (moment_f / (frobenius + norm_floor)).astype(jnp.bfloat16)
    for sweep_index in range(2):
        gramian = lax.dot_general(
            current, current, (((1,), (1,)), ((), ())), preferred_element_type=jnp.float32
        ).astype(jnp.bfloat16)
        squared = jnp.dot(gramian, gramian, preferred_element_type=jnp.float32)
        poly = (cubic_term * gramian.astype(jnp.float32) + quintic_term * squared).astype(
            jnp.bfloat16
        )
        current = (
            linear_term * current.astype(jnp.float32)
            + jnp.dot(poly, current, preferred_element_type=jnp.float32)
        ).astype(jnp.bfloat16)
    return current


def relocate(weight, moment, perm):
    groups = lax.axis_size("expert")
    weight_flat = weight.reshape(groups, -1)
    moment_flat = moment.reshape(groups, -1)
    spread_w, spread_m = (
        lax.all_to_all(weight_flat, "expert", split_axis=0, concat_axis=0, tiled=True),
        lax.all_to_all(moment_flat, "expert", split_axis=0, concat_axis=0, tiled=True),
    )
    devices = jnp.arange(groups, dtype=jnp.int32)
    inverse = jnp.sum(jnp.where(perm[None, :] == devices[:, None], devices[None, :], 0), axis=1)
    ordered_w = jnp.take(spread_w, inverse, axis=0)
    ordered_m = jnp.take(spread_m, inverse, axis=0)
    back_w, back_m = (
        lax.all_to_all(ordered_w, "expert", split_axis=0, concat_axis=0, tiled=True),
        lax.all_to_all(ordered_m, "expert", split_axis=0, concat_axis=0, tiled=True),
    )
    return (back_w.reshape(weight.shape), back_m.reshape(moment.shape))


def routed_plan(
    grad_hidden,
    grad_out,
    grad_route,
    live_rows,
    w_down,
    w_moment,
    perm,
    fwd_hidden,
    fwd_route,
    fwd_gate,
):
    groups = lax.axis_size("expert")
    grad_count = grad_hidden.shape[0]
    capacity = max(4, 2 * grad_count // groups)
    is_live = jnp.arange(grad_count, dtype=jnp.int32) < live_rows[0]
    route_ids = grad_route[:, 0]
    weight, moment = relocate(w_down, w_moment, perm)
    target = lookup(route_ids, perm)
    selector = slot_matrix(target, is_live, groups, capacity)
    hidden_buf = (
        jnp.dot(selector, grad_hidden, preferred_element_type=jnp.float32)
        .astype(jnp.bfloat16)
        .reshape(groups, capacity, -1)
    )
    outgrad_buf = (
        jnp.dot(selector, grad_out, preferred_element_type=jnp.float32)
        .astype(jnp.bfloat16)
        .reshape(groups, capacity, -1)
    )
    recv_hidden, recv_outgrad = (
        lax.all_to_all(hidden_buf, "expert", split_axis=0, concat_axis=0, tiled=True),
        lax.all_to_all(outgrad_buf, "expert", split_axis=0, concat_axis=0, tiled=True),
    )
    grad = lax.dot_general(
        recv_hidden.reshape(groups * capacity, -1),
        recv_outgrad.reshape(groups * capacity, -1),
        (((0,), (0,)), ((), ())),
        preferred_element_type=jnp.float32,
    )
    moment_new = (moment_decay * moment[0].astype(jnp.float32) + grad).astype(jnp.bfloat16)
    ortho = orthogonalize(moment_new)
    weight_new = (weight[0].astype(jnp.float32) - step_scale * ortho.astype(jnp.float32)).astype(
        jnp.bfloat16
    )
    weight_new = weight_new[None]
    moment_new = moment_new[None]
    fwd_ids = fwd_route[:, 0]
    placed_weight, placed_moment = (weight_new, moment_new)
    fwd_target = lookup(fwd_ids, perm)
    fwd_weight = weight_new[0]
    fwd_count = fwd_hidden.shape[0]
    fwd_capacity = max(4, 2 * fwd_count // groups)
    fwd_selector = slot_matrix(fwd_target, jnp.ones((fwd_count,), dtype=bool), groups, fwd_capacity)
    fwd_buf = (
        jnp.dot(fwd_selector, fwd_hidden, preferred_element_type=jnp.float32)
        .astype(jnp.bfloat16)
        .reshape(groups, fwd_capacity, -1)
    )
    produced = jnp.einsum(
        "gkf,fd->gkd",
        lax.all_to_all(fwd_buf, "expert", split_axis=0, concat_axis=0, tiled=True),
        fwd_weight,
        preferred_element_type=jnp.float32,
    ).astype(jnp.bfloat16)
    returned = lax.all_to_all(produced, "expert", split_axis=0, concat_axis=0, tiled=True)
    fwd_rows_out = lax.dot_general(
        fwd_selector,
        returned.reshape(groups * fwd_capacity, -1),
        (((0,), (0,)), ((), ())),
        preferred_element_type=jnp.float32,
    )
    fwd_out = (fwd_rows_out * fwd_gate[:, None]).astype(jnp.bfloat16)
    return (placed_weight, placed_moment, fwd_out)


def solution(mesh):
    groups = mesh.shape["expert"]
    in_specs = (
        P(("layer", "expert"), None),
        P(("layer", "expert"), None),
        P(("layer", "expert"), None),
        P(("layer", "expert")),
        P(("layer", "expert"), None, None),
        P(("layer", "expert"), None, None),
        P("layer"),
        P(("layer", "expert"), None),
        P(("layer", "expert"), None),
        P(("layer", "expert")),
    )
    out_specs = (
        P(("layer", "expert"), None, None),
        P(("layer", "expert"), None, None),
        P(("layer", "expert"), None),
    )

    def per_device(*args):
        few = groups & (groups - 1) == 0 and groups <= 2 * args[0].shape[0] // groups
        return (partner_plan if few else routed_plan)(*args)

    return jax.shard_map(
        per_device, mesh=mesh, in_specs=in_specs, out_specs=out_specs, check_vma=False
    )
```

```python
import functools

import jax
import jax.numpy as jnp
from jax import lax
from jax.experimental import pallas as pl
from jax.experimental.pallas import tpu as pltpu
from jax.sharding import PartitionSpec as P

linear_term = 3.4445
cubic_term = -4.775
quintic_term = 2.0315
moment_decay = 0.9
step_scale = 0.25
norm_floor = 1e-07

F32 = jnp.float32
BF16 = jnp.bfloat16
HBM = pl.BlockSpec(memory_space=pltpu.HBM)
VMEM = pl.BlockSpec(memory_space=pltpu.VMEM)
SMEM = pl.BlockSpec(memory_space=pltpu.SMEM)
ANY = pl.BlockSpec(memory_space=pl.ANY)
MIB = 1 << 20


def fetched(refs, held, sem):
    copies = [pltpu.make_async_copy(ref, room, sem.at[n]) for n, (ref, room) in enumerate(zip(refs, held))]
    for copy in copies:
        copy.start()
    for copy in copies:
        copy.wait()


def rooms(arrays):
    return [pltpu.VMEM(a.shape, a.dtype) for a in arrays] + [pltpu.SemaphoreType.DMA((len(arrays),))]


def chunk_at(ref, lead, k, rows, columns):
    return ref.at[
        lead,
        pl.ds(pl.multiple_of((k // 2) * rows, rows), rows),
        pl.ds(pl.multiple_of((k % 2) * columns, columns), columns),
    ]


def slot_rows(route, live, groups, capacity, me_ref, perm_ref):
    rows = route.shape[1]
    experts = lax.broadcasted_iota(jnp.int32, (groups, rows), 0)
    onehot = jnp.where((experts == route) & live, 1.0, 0.0).astype(BF16)
    before = lax.broadcasted_iota(jnp.int32, (rows, rows), 0)
    after = lax.broadcasted_iota(jnp.int32, (rows, rows), 1)
    upto = jnp.where(before <= after, 1.0, 0.0).astype(BF16)
    ranks = jnp.dot(onehot, upto, preferred_element_type=F32)
    rank = jnp.sum(ranks * onehot.astype(F32), axis=0, keepdims=True).astype(jnp.int32) - 1
    partner = jnp.zeros_like(route)
    for e in range(groups):
        partner = jnp.where(route == e, perm_ref[e] ^ me_ref[0], partner)
    return jnp.where(live, partner * capacity + rank, -1)


def selector_of(slot, slots):
    rows = slot.shape[1]
    places = lax.broadcasted_iota(jnp.int32, (slots, rows), 0)
    return jnp.where(places == slot, 1.0, 0.0).astype(BF16)


def pack_kernel(groups, live_ref, me_ref, perm_ref, *refs):
    sources, pieces, (slot_ref, gates_ref) = refs[:6], refs[7 : 7 + groups], refs[7 + groups : 9 + groups]
    held, sem = refs[9 + groups : 15 + groups], refs[-1]
    route_ref, fwd_route_ref, hidden_ref, out_ref, fwd_ref, gate_ref = held
    copies = [pltpu.make_async_copy(ref, room, sem.at[n]) for n, (ref, room) in enumerate(zip(sources, held))]
    for copy in copies:
        copy.start()
    rows, ff = hidden_ref.shape
    d = out_ref.shape[1]
    capacity = pieces[0].shape[0]
    slots = groups * capacity
    place = lax.broadcasted_iota(jnp.int32, (1, rows), 1)

    def fill(first, selector, source_ref):
        chosen = jnp.dot(selector, source_ref[...], preferred_element_type=F32).astype(BF16)
        for s, piece in zip(mixed_order(groups), pieces):
            piece[:, first : first + source_ref.shape[1]] = chosen[s * capacity : (s + 1) * capacity]

    copies[0].wait()
    slot = slot_rows(route_ref[...], place < live_ref[0], groups, capacity, me_ref, perm_ref)
    selector = selector_of(slot, slots)
    copies[1].wait()
    fwd_slot = slot_rows(fwd_route_ref[...], place >= 0, groups, capacity, me_ref, perm_ref)
    slot_ref[...] = fwd_slot
    copies[2].wait()
    fill(0, selector, hidden_ref)
    copies[3].wait()
    fill(ff, selector, out_ref)
    copies[4].wait()
    fill(ff + d, selector_of(fwd_slot, slots), fwd_ref)
    copies[5].wait()
    down = lax.broadcasted_iota(jnp.int32, (rows, rows), 0)
    across = lax.broadcasted_iota(jnp.int32, (rows, rows), 1)
    gates_ref[...] = jnp.sum(jnp.where(down == across, gate_ref[...], 0.0), axis=1, keepdims=True)


def pack_rows(live_rows, me, perm, route, fwd_route, hidden, grad_out, fwd_hidden, gate, earlier, groups, capacity):
    rows, ff = hidden.shape
    width = 2 * ff + grad_out.shape[1]
    sources = (route.reshape(1, rows), fwd_route.reshape(1, rows), hidden, grad_out, fwd_hidden, gate.reshape(1, rows))
    *pieces, slot, gates = pl.pallas_call(
        functools.partial(pack_kernel, groups),
        out_shape=(jax.ShapeDtypeStruct((capacity, width), BF16),) * groups
        + (jax.ShapeDtypeStruct((1, rows), jnp.int32), jax.ShapeDtypeStruct((rows, 1), F32)),
        in_specs=[SMEM] * 3 + [HBM] * 6 + [VMEM],
        out_specs=(VMEM,) * (groups + 2),
        scratch_shapes=[pltpu.VMEM(a.shape, a.dtype) for a in sources] + [pltpu.SemaphoreType.DMA((len(sources),))],
        compiler_params=pltpu.CompilerParams(vmem_limit_bytes=24 * MIB),
        cost_estimate=pl.CostEstimate(
            flops=2 * groups * capacity * rows * width, bytes_accessed=6 * rows * width, transcendentals=0
        ),
        name="pack_rows",
    )(live_rows, me, perm, *sources, earlier)
    return pieces, slot, gates


def split_kernel(me_ref, moment_ref, weight_ref, *refs):
    pieces, held, sem = refs[:-3], refs[-3:-1], refs[-1]
    fetched((moment_ref, weight_ref), held, sem)
    for s, piece in zip(mixed_order(len(pieces)), pieces):
        rows, columns = piece.shape[1:]
        for lead, source in enumerate(held):
            piece[lead] = chunk_at(source, 0, me_ref[0] ^ s, rows, columns)[...]


def split(me, moment, weight, groups):
    _, ff, d = weight.shape
    piece = jax.ShapeDtypeStruct((2, ff // (groups // 2), d // 2), BF16)
    return pl.pallas_call(
        split_kernel,
        out_shape=(piece,) * groups,
        in_specs=[SMEM, HBM, HBM],
        out_specs=(VMEM,) * groups,
        scratch_shapes=rooms((moment, weight)),
        compiler_params=pltpu.CompilerParams(vmem_limit_bytes=60 * MIB),
        cost_estimate=pl.CostEstimate(flops=0, bytes_accessed=8 * ff * d, transcendentals=0),
        name="split",
    )(me, moment, weight)


def reorder_kernel(me_ref, perm_ref, *refs):
    groups = len(refs) // 2 - 1
    sources, targets, held = refs[:groups], refs[groups + 1 : 2 * groups + 1], refs[-1]
    me, order = me_ref[0], mixed_order(groups)
    for s, source in zip(order, sources):
        held[me ^ perm_ref[me ^ s]] = source[...]
    for s, target in zip(order, targets):
        target[...] = held[s]


def reorder(me, perm, pieces, earlier):
    groups = len(pieces)
    piece = jax.ShapeDtypeStruct(pieces[0].shape, BF16)
    return pl.pallas_call(
        reorder_kernel,
        out_shape=(piece,) * groups,
        in_specs=[SMEM, SMEM] + [VMEM] * (groups + 1),
        out_specs=(VMEM,) * groups,
        scratch_shapes=[pltpu.VMEM((groups,) + pieces[0].shape, BF16)],
        compiler_params=pltpu.CompilerParams(vmem_limit_bytes=12 * MIB),
        cost_estimate=pl.CostEstimate(flops=0, bytes_accessed=4 * groups * pieces[0].size, transcendentals=0),
        name="reorder",
    )(me, perm, *pieces, earlier)


def update_kernel(groups, me_ref, *refs):
    packed, pieces, produced = refs[:groups], refs[groups : 2 * groups], refs[2 * groups + 2 : 3 * groups + 2]
    weight_new_ref, moment_new_ref = refs[2 * groups : 2 * groups + 2]
    held, rows_ref = refs[-2:]
    _, ff, d = held.shape
    capacity = packed[0].shape[0]
    for n, piece in enumerate(packed):
        rows_ref[n * capacity : (n + 1) * capacity] = piece[...]
    for s, piece in zip(mixed_order(groups), pieces):
        rows, columns = piece.shape[1:]
        for lead in range(2):
            chunk_at(held, lead, me_ref[0] ^ s, rows, columns)[...] = piece[lead]
    grad = lax.dot_general(
        rows_ref[:, :ff], rows_ref[:, ff : ff + d], (((0,), (0,)), ((), ())), preferred_element_type=F32
    )
    moment_new = (moment_decay * held[0].astype(F32) + grad).astype(BF16)
    moment_new_ref[...] = moment_new
    moment_f = moment_new.astype(F32)
    frobenius = jnp.sqrt(jnp.sum(moment_f * moment_f))
    current = (moment_f / (frobenius + norm_floor)).astype(BF16)
    for _ in range(2):
        gramian = lax.dot_general(
            current, current, (((1,), (1,)), ((), ())), preferred_element_type=F32
        ).astype(BF16)
        squared = jnp.dot(gramian, gramian, preferred_element_type=F32)
        poly = (cubic_term * gramian.astype(F32) + quintic_term * squared).astype(BF16)
        current = (
            linear_term * current.astype(F32) + jnp.dot(poly, current, preferred_element_type=F32)
        ).astype(BF16)
    weight_new = (held[1].astype(F32) - step_scale * current.astype(F32)).astype(BF16)
    weight_new_ref[...] = weight_new
    product = jnp.dot(rows_ref[:, ff + d :], weight_new, preferred_element_type=F32).astype(BF16)
    for n, piece in enumerate(produced):
        piece[...] = product[n * capacity : (n + 1) * capacity]


def update(me, packed, pieces, ff, d):
    groups = len(pieces)
    capacity, width = packed[0].shape
    slots = groups * capacity
    shape = jax.ShapeDtypeStruct((ff, d), BF16)
    weight_new, moment_new, *produced = pl.pallas_call(
        functools.partial(update_kernel, groups),
        out_shape=(shape, shape) + (jax.ShapeDtypeStruct((capacity, d), BF16),) * groups,
        in_specs=[SMEM] + [VMEM] * (2 * groups),
        out_specs=(VMEM,) * (groups + 2),
        scratch_shapes=[pltpu.VMEM((2, ff, d), BF16), pltpu.VMEM((slots, width), BF16)],
        compiler_params=pltpu.CompilerParams(vmem_limit_bytes=24 * MIB),
        cost_estimate=pl.CostEstimate(
            flops=4 * ff * d * slots + 8 * ff * ff * d + 4 * ff**3,
            bytes_accessed=8 * ff * d + 2 * slots * (width + d),
            transcendentals=1,
        ),
        name="update",
    )(me, *packed, *pieces)
    return weight_new, moment_new, produced


def emit_kernel(weight_ref, moment_ref, weight_out_ref, moment_out_ref, sem):
    copies = [
        pltpu.make_async_copy(source, target, sem.at[n])
        for n, (source, target) in enumerate(((weight_ref, weight_out_ref), (moment_ref, moment_out_ref)))
    ]
    for copy in copies:
        copy.start()
    for copy in copies:
        copy.wait()


def emit(weight, moment):
    shape = jax.ShapeDtypeStruct(weight.shape, BF16)
    return pl.pallas_call(
        emit_kernel,
        out_shape=(shape, shape),
        in_specs=[VMEM, VMEM],
        out_specs=(HBM, HBM),
        scratch_shapes=[pltpu.SemaphoreType.DMA((2,))],
        cost_estimate=pl.CostEstimate(flops=0, bytes_accessed=8 * weight.size, transcendentals=0),
        name="emit",
    )(weight, moment)


def finish_kernel(groups, slot_ref, gates_ref, *refs):
    pieces, (out_ref, returned_ref) = refs[:groups], refs[groups:]
    capacity = pieces[0].shape[0]
    for s, piece in zip(mixed_order(groups), pieces):
        returned_ref[s * capacity : (s + 1) * capacity] = piece[...]
    selector = selector_of(slot_ref[...], groups * capacity)
    expert_out = lax.dot_general(
        selector, returned_ref[...], (((0,), (0,)), ((), ())), preferred_element_type=F32
    )
    out_ref[...] = (gates_ref[...] * expert_out).astype(BF16)


def finish(slot, gates, returned):
    groups = len(returned)
    rows = slot.shape[1]
    capacity, d = returned[0].shape
    slots = groups * capacity
    return pl.pallas_call(
        functools.partial(finish_kernel, groups),
        out_shape=jax.ShapeDtypeStruct((rows, d), BF16),
        in_specs=[VMEM] * (2 + groups),
        out_specs=VMEM,
        scratch_shapes=[pltpu.VMEM((slots, d), BF16)],
        compiler_params=pltpu.CompilerParams(vmem_limit_bytes=12 * MIB),
        cost_estimate=pl.CostEstimate(
            flops=2 * slots * rows * d, bytes_accessed=2 * d * (slots + rows), transcendentals=0
        ),
        name="finish",
    )(slot, gates, *returned)


def mixed_order(groups):
    def both_ends(partners):
        middle = (len(partners) + 1) // 2
        first, second = partners[:middle], partners[middle:]
        return [s for pair in zip(first, second + [None]) for s in pair if s is not None]

    half = groups // 2
    far, near = both_ends(list(range(half, groups))), both_ends(list(range(half - 1, 0, -1)))
    return [0] + [s for pair in zip(far, near + [None]) for s in pair if s is not None]


def swap(pieces):
    groups = len(pieces)
    order = mixed_order(groups)
    return [pieces[0]] + [
        lax.ppermute(piece, "expert", [(i, i ^ s) for i in range(groups)]) for s, piece in zip(order[1:], pieces[1:])
    ]


def partner_plan(
    grad_hidden, grad_out, grad_route, live_rows, w_down, w_moment, perm, fwd_hidden, fwd_route, fwd_gate
):
    groups = lax.axis_size("expert")
    me = lax.axis_index("expert").astype(jnp.int32).reshape(1)
    capacity = max(4, 2 * grad_hidden.shape[0] // groups)
    ff, d = w_down.shape[1:]
    spread = swap(split(me, w_moment, w_down, groups))
    packed, fwd_slot, gates = pack_rows(
        live_rows, me, perm, grad_route, fwd_route, grad_hidden, grad_out, fwd_hidden, fwd_gate,
        spread[2 * groups // 3], groups, capacity,
    )
    received = swap(packed)
    placed = swap(reorder(me, perm, spread, received[groups // 3]))
    weight_new, moment_new, produced = update(me, received, placed, ff, d)
    weight_new, moment_new = emit(weight_new, moment_new)
    return weight_new[None], moment_new[None], finish(fwd_slot, gates, swap(produced))


def lookup(route_ids, mapping):
    columns = jnp.arange(mapping.shape[0], dtype=jnp.int32)
    hits = route_ids[:, None] == columns[None, :]
    return jnp.sum(jnp.where(hits, mapping[None, :], 0), axis=1)


def slot_matrix(target, is_live, groups, capacity):
    columns = jnp.arange(groups, dtype=jnp.int32)
    onehot = ((target[:, None] == columns[None, :]) & is_live[:, None]).astype(jnp.int32)
    ranked = jnp.sum(jnp.cumsum(onehot, axis=0) * onehot, axis=1) - 1
    slot_of = jnp.where(is_live, target * capacity + ranked, -1)
    slots = jnp.arange(groups * capacity, dtype=jnp.int32)
    return (slots[:, None] == slot_of[None, :]).astype(jnp.bfloat16)


def orthogonalize(moment):
    moment_f = moment.astype(jnp.float32)
    frobenius = jnp.sqrt(jnp.sum(moment_f * moment_f))
    current = (moment_f / (frobenius + norm_floor)).astype(jnp.bfloat16)
    for sweep_index in range(2):
        gramian = lax.dot_general(
            current, current, (((1,), (1,)), ((), ())), preferred_element_type=jnp.float32
        ).astype(jnp.bfloat16)
        squared = jnp.dot(gramian, gramian, preferred_element_type=jnp.float32)
        poly = (cubic_term * gramian.astype(jnp.float32) + quintic_term * squared).astype(
            jnp.bfloat16
        )
        current = (
            linear_term * current.astype(jnp.float32)
            + jnp.dot(poly, current, preferred_element_type=jnp.float32)
        ).astype(jnp.bfloat16)
    return current


def relocate(weight, moment, perm):
    groups = lax.axis_size("expert")
    weight_flat = weight.reshape(groups, -1)
    moment_flat = moment.reshape(groups, -1)
    spread_w, spread_m = (
        lax.all_to_all(weight_flat, "expert", split_axis=0, concat_axis=0, tiled=True),
        lax.all_to_all(moment_flat, "expert", split_axis=0, concat_axis=0, tiled=True),
    )
    devices = jnp.arange(groups, dtype=jnp.int32)
    inverse = jnp.sum(jnp.where(perm[None, :] == devices[:, None], devices[None, :], 0), axis=1)
    ordered_w = jnp.take(spread_w, inverse, axis=0)
    ordered_m = jnp.take(spread_m, inverse, axis=0)
    back_w, back_m = (
        lax.all_to_all(ordered_w, "expert", split_axis=0, concat_axis=0, tiled=True),
        lax.all_to_all(ordered_m, "expert", split_axis=0, concat_axis=0, tiled=True),
    )
    return (back_w.reshape(weight.shape), back_m.reshape(moment.shape))


def routed_plan(
    grad_hidden,
    grad_out,
    grad_route,
    live_rows,
    w_down,
    w_moment,
    perm,
    fwd_hidden,
    fwd_route,
    fwd_gate,
):
    groups = lax.axis_size("expert")
    grad_count = grad_hidden.shape[0]
    capacity = max(4, 2 * grad_count // groups)
    is_live = jnp.arange(grad_count, dtype=jnp.int32) < live_rows[0]
    route_ids = grad_route[:, 0]
    weight, moment = relocate(w_down, w_moment, perm)
    target = lookup(route_ids, perm)
    selector = slot_matrix(target, is_live, groups, capacity)
    hidden_buf = (
        jnp.dot(selector, grad_hidden, preferred_element_type=jnp.float32)
        .astype(jnp.bfloat16)
        .reshape(groups, capacity, -1)
    )
    outgrad_buf = (
        jnp.dot(selector, grad_out, preferred_element_type=jnp.float32)
        .astype(jnp.bfloat16)
        .reshape(groups, capacity, -1)
    )
    recv_hidden, recv_outgrad = (
        lax.all_to_all(hidden_buf, "expert", split_axis=0, concat_axis=0, tiled=True),
        lax.all_to_all(outgrad_buf, "expert", split_axis=0, concat_axis=0, tiled=True),
    )
    grad = lax.dot_general(
        recv_hidden.reshape(groups * capacity, -1),
        recv_outgrad.reshape(groups * capacity, -1),
        (((0,), (0,)), ((), ())),
        preferred_element_type=jnp.float32,
    )
    moment_new = (moment_decay * moment[0].astype(jnp.float32) + grad).astype(jnp.bfloat16)
    ortho = orthogonalize(moment_new)
    weight_new = (weight[0].astype(jnp.float32) - step_scale * ortho.astype(jnp.float32)).astype(
        jnp.bfloat16
    )
    weight_new = weight_new[None]
    moment_new = moment_new[None]
    fwd_ids = fwd_route[:, 0]
    placed_weight, placed_moment = (weight_new, moment_new)
    fwd_target = lookup(fwd_ids, perm)
    fwd_weight = weight_new[0]
    fwd_count = fwd_hidden.shape[0]
    fwd_capacity = max(4, 2 * fwd_count // groups)
    fwd_selector = slot_matrix(fwd_target, jnp.ones((fwd_count,), dtype=bool), groups, fwd_capacity)
    fwd_buf = (
        jnp.dot(fwd_selector, fwd_hidden, preferred_element_type=jnp.float32)
        .astype(jnp.bfloat16)
        .reshape(groups, fwd_capacity, -1)
    )
    produced = jnp.einsum(
        "gkf,fd->gkd",
        lax.all_to_all(fwd_buf, "expert", split_axis=0, concat_axis=0, tiled=True),
        fwd_weight,
        preferred_element_type=jnp.float32,
    ).astype(jnp.bfloat16)
    returned = lax.all_to_all(produced, "expert", split_axis=0, concat_axis=0, tiled=True)
    fwd_rows_out = lax.dot_general(
        fwd_selector,
        returned.reshape(groups * fwd_capacity, -1),
        (((0,), (0,)), ((), ())),
        preferred_element_type=jnp.float32,
    )
    fwd_out = (fwd_rows_out * fwd_gate[:, None]).astype(jnp.bfloat16)
    return (placed_weight, placed_moment, fwd_out)


def solution(mesh):
    groups = mesh.shape["expert"]
    in_specs = (
        P(("layer", "expert"), None),
        P(("layer", "expert"), None),
        P(("layer", "expert"), None),
        P(("layer", "expert")),
        P(("layer", "expert"), None, None),
        P(("layer", "expert"), None, None),
        P("layer"),
        P(("layer", "expert"), None),
        P(("layer", "expert"), None),
        P(("layer", "expert")),
    )
    out_specs = (
        P(("layer", "expert"), None, None),
        P(("layer", "expert"), None, None),
        P(("layer", "expert"), None),
    )

    def per_device(*args):
        few = groups & (groups - 1) == 0 and groups <= 2 * args[0].shape[0] // groups
        return (partner_plan if few else routed_plan)(*args)

    return jax.shard_map(
        per_device, mesh=mesh, in_specs=in_specs, out_specs=out_specs, check_vma=False
    )
```

```python
import functools

import jax
import jax.numpy as jnp
from jax import lax
from jax.experimental import pallas as pl
from jax.experimental.pallas import tpu as pltpu
from jax.sharding import PartitionSpec as P

linear_term = 3.4445
cubic_term = -4.775
quintic_term = 2.0315
moment_decay = 0.9
step_scale = 0.25
norm_floor = 1e-07

F32 = jnp.float32
BF16 = jnp.bfloat16
HBM = pl.BlockSpec(memory_space=pltpu.HBM)
VMEM = pl.BlockSpec(memory_space=pltpu.VMEM)
SMEM = pl.BlockSpec(memory_space=pltpu.SMEM)
ANY = pl.BlockSpec(memory_space=pl.ANY)
MIB = 1 << 20


def fetched(refs, held, sem):
    copies = [pltpu.make_async_copy(ref, room, sem.at[n]) for n, (ref, room) in enumerate(zip(refs, held))]
    for copy in copies:
        copy.start()
    for copy in copies:
        copy.wait()


def rooms(arrays):
    return [pltpu.VMEM(a.shape, a.dtype) for a in arrays] + [pltpu.SemaphoreType.DMA((len(arrays),))]


def chunk_at(ref, lead, k, rows, columns):
    return ref.at[
        lead,
        pl.ds(pl.multiple_of((k // 2) * rows, rows), rows),
        pl.ds(pl.multiple_of((k % 2) * columns, columns), columns),
    ]


def slot_rows(route, live, groups, capacity, me_ref, perm_ref):
    rows = route.shape[1]
    experts = lax.broadcasted_iota(jnp.int32, (groups, rows), 0)
    onehot = jnp.where((experts == route) & live, 1.0, 0.0).astype(BF16)
    before = lax.broadcasted_iota(jnp.int32, (rows, rows), 0)
    after = lax.broadcasted_iota(jnp.int32, (rows, rows), 1)
    upto = jnp.where(before <= after, 1.0, 0.0).astype(BF16)
    ranks = jnp.dot(onehot, upto, preferred_element_type=F32)
    rank = jnp.sum(ranks * onehot.astype(F32), axis=0, keepdims=True).astype(jnp.int32) - 1
    partner = jnp.zeros_like(route)
    for e in range(groups):
        partner = jnp.where(route == e, perm_ref[e] ^ me_ref[0], partner)
    return jnp.where(live, partner * capacity + rank, -1)


def selector_of(slot, slots):
    rows = slot.shape[1]
    places = lax.broadcasted_iota(jnp.int32, (slots, rows), 0)
    return jnp.where(places == slot, 1.0, 0.0).astype(BF16)


def pack_kernel(groups, live_ref, me_ref, perm_ref, *refs):
    sources, pieces, (slot_ref, gates_ref) = refs[:6], refs[7 : 7 + groups], refs[7 + groups : 9 + groups]
    held, sem = refs[9 + groups : 15 + groups], refs[-1]
    route_ref, fwd_route_ref, hidden_ref, out_ref, fwd_ref, gate_ref = held
    copies = [pltpu.make_async_copy(ref, room, sem.at[n]) for n, (ref, room) in enumerate(zip(sources, held))]
    for copy in copies:
        copy.start()
    rows, ff = hidden_ref.shape
    d = out_ref.shape[1]
    capacity = pieces[0].shape[0]
    slots = groups * capacity
    place = lax.broadcasted_iota(jnp.int32, (1, rows), 1)

    def fill(first, selector, source_ref):
        chosen = jnp.dot(selector, source_ref[...], preferred_element_type=F32).astype(BF16)
        for s, piece in zip(mixed_order(groups), pieces):
            piece[:, first : first + source_ref.shape[1]] = chosen[s * capacity : (s + 1) * capacity]

    copies[0].wait()
    slot = slot_rows(route_ref[...], place < live_ref[0], groups, capacity, me_ref, perm_ref)
    selector = selector_of(slot, slots)
    copies[1].wait()
    fwd_slot = slot_rows(fwd_route_ref[...], place >= 0, groups, capacity, me_ref, perm_ref)
    slot_ref[...] = fwd_slot
    copies[2].wait()
    fill(0, selector, hidden_ref)
    copies[3].wait()
    fill(ff, selector, out_ref)
    copies[4].wait()
    fill(ff + d, selector_of(fwd_slot, slots), fwd_ref)
    copies[5].wait()
    down = lax.broadcasted_iota(jnp.int32, (rows, rows), 0)
    across = lax.broadcasted_iota(jnp.int32, (rows, rows), 1)
    gates_ref[...] = jnp.sum(jnp.where(down == across, gate_ref[...], 0.0), axis=1, keepdims=True)


def pack_rows(live_rows, me, perm, route, fwd_route, hidden, grad_out, fwd_hidden, gate, earlier, groups, capacity):
    rows, ff = hidden.shape
    width = 2 * ff + grad_out.shape[1]
    sources = (route.reshape(1, rows), fwd_route.reshape(1, rows), hidden, grad_out, fwd_hidden, gate.reshape(1, rows))
    *pieces, slot, gates = pl.pallas_call(
        functools.partial(pack_kernel, groups),
        out_shape=(jax.ShapeDtypeStruct((capacity, width), BF16),) * groups
        + (jax.ShapeDtypeStruct((1, rows), jnp.int32), jax.ShapeDtypeStruct((rows, 1), F32)),
        in_specs=[SMEM] * 3 + [HBM] * 6 + [VMEM],
        out_specs=(VMEM,) * (groups + 2),
        scratch_shapes=[pltpu.VMEM(a.shape, a.dtype) for a in sources] + [pltpu.SemaphoreType.DMA((len(sources),))],
        compiler_params=pltpu.CompilerParams(vmem_limit_bytes=32 * MIB),
        cost_estimate=pl.CostEstimate(
            flops=2 * groups * capacity * rows * width, bytes_accessed=6 * rows * width, transcendentals=0
        ),
        name="pack_rows",
    )(live_rows, me, perm, *sources, earlier)
    return pieces, slot, gates


def split_kernel(me_ref, moment_ref, weight_ref, *refs):
    pieces, held, sem = refs[:-3], refs[-3:-1], refs[-1]
    fetched((moment_ref, weight_ref), held, sem)
    for s, piece in zip(mixed_order(len(pieces)), pieces):
        rows, columns = piece.shape[1:]
        for lead, source in enumerate(held):
            piece[lead] = chunk_at(source, 0, me_ref[0] ^ s, rows, columns)[...]


def split(me, moment, weight, groups):
    _, ff, d = weight.shape
    piece = jax.ShapeDtypeStruct((2, ff // (groups // 2), d // 2), BF16)
    return pl.pallas_call(
        split_kernel,
        out_shape=(piece,) * groups,
        in_specs=[SMEM, HBM, HBM],
        out_specs=(VMEM,) * groups,
        scratch_shapes=rooms((moment, weight)),
        compiler_params=pltpu.CompilerParams(vmem_limit_bytes=60 * MIB),
        cost_estimate=pl.CostEstimate(flops=0, bytes_accessed=8 * ff * d, transcendentals=0),
        name="split",
    )(me, moment, weight)


def reorder_kernel(me_ref, perm_ref, *refs):
    groups = len(refs) // 2 - 1
    sources, targets, held = refs[:groups], refs[groups + 1 : 2 * groups + 1], refs[-1]
    me, order = me_ref[0], mixed_order(groups)
    for s, source in zip(order, sources):
        held[me ^ perm_ref[me ^ s]] = source[...]
    for s, target in zip(order, targets):
        target[...] = held[s]


def reorder(me, perm, pieces, earlier):
    groups = len(pieces)
    piece = jax.ShapeDtypeStruct(pieces[0].shape, BF16)
    return pl.pallas_call(
        reorder_kernel,
        out_shape=(piece,) * groups,
        in_specs=[SMEM, SMEM] + [VMEM] * (groups + 1),
        out_specs=(VMEM,) * groups,
        scratch_shapes=[pltpu.VMEM((groups,) + pieces[0].shape, BF16)],
        compiler_params=pltpu.CompilerParams(vmem_limit_bytes=32 * MIB),
        cost_estimate=pl.CostEstimate(flops=0, bytes_accessed=4 * groups * pieces[0].size, transcendentals=0),
        name="reorder",
    )(me, perm, *pieces, earlier)


def update_kernel(groups, me_ref, *refs):
    packed, pieces, produced = refs[:groups], refs[groups : 2 * groups], refs[2 * groups + 2 : 3 * groups + 2]
    weight_new_ref, moment_new_ref = refs[2 * groups : 2 * groups + 2]
    held, rows_ref = refs[-2:]
    _, ff, d = held.shape
    capacity = packed[0].shape[0]
    for n, piece in enumerate(packed):
        rows_ref[n * capacity : (n + 1) * capacity] = piece[...]
    for s, piece in zip(mixed_order(groups), pieces):
        rows, columns = piece.shape[1:]
        for lead in range(2):
            chunk_at(held, lead, me_ref[0] ^ s, rows, columns)[...] = piece[lead]
    grad = lax.dot_general(
        rows_ref[:, :ff], rows_ref[:, ff : ff + d], (((0,), (0,)), ((), ())), preferred_element_type=F32
    )
    moment_new = (moment_decay * held[0].astype(F32) + grad).astype(BF16)
    moment_new_ref[...] = moment_new
    moment_f = moment_new.astype(F32)
    frobenius = jnp.sqrt(jnp.sum(moment_f * moment_f))
    current = (moment_f / (frobenius + norm_floor)).astype(BF16)
    for _ in range(2):
        gramian = lax.dot_general(
            current, current, (((1,), (1,)), ((), ())), preferred_element_type=F32
        ).astype(BF16)
        squared = jnp.dot(gramian, gramian, preferred_element_type=F32)
        poly = (cubic_term * gramian.astype(F32) + quintic_term * squared).astype(BF16)
        current = (
            linear_term * current.astype(F32) + jnp.dot(poly, current, preferred_element_type=F32)
        ).astype(BF16)
    weight_new = (held[1].astype(F32) - step_scale * current.astype(F32)).astype(BF16)
    weight_new_ref[...] = weight_new
    product = jnp.dot(rows_ref[:, ff + d :], weight_new, preferred_element_type=F32).astype(BF16)
    for n, piece in enumerate(produced):
        piece[...] = product[n * capacity : (n + 1) * capacity]


def update(me, packed, pieces, ff, d):
    groups = len(pieces)
    capacity, width = packed[0].shape
    slots = groups * capacity
    shape = jax.ShapeDtypeStruct((ff, d), BF16)
    weight_new, moment_new, *produced = pl.pallas_call(
        functools.partial(update_kernel, groups),
        out_shape=(shape, shape) + (jax.ShapeDtypeStruct((capacity, d), BF16),) * groups,
        in_specs=[SMEM] + [VMEM] * (2 * groups),
        out_specs=(VMEM,) * (groups + 2),
        scratch_shapes=[pltpu.VMEM((2, ff, d), BF16), pltpu.VMEM((slots, width), BF16)],
        compiler_params=pltpu.CompilerParams(vmem_limit_bytes=40 * MIB),
        cost_estimate=pl.CostEstimate(
            flops=4 * ff * d * slots + 8 * ff * ff * d + 4 * ff**3,
            bytes_accessed=8 * ff * d + 2 * slots * (width + d),
            transcendentals=1,
        ),
        name="update",
    )(me, *packed, *pieces)
    return weight_new, moment_new, produced


def finish_kernel(groups, slot_ref, gates_ref, *refs):
    pieces, (out_ref, returned_ref) = refs[:groups], refs[groups:]
    capacity = pieces[0].shape[0]
    for s, piece in zip(mixed_order(groups), pieces):
        returned_ref[s * capacity : (s + 1) * capacity] = piece[...]
    selector = selector_of(slot_ref[...], groups * capacity)
    expert_out = lax.dot_general(
        selector, returned_ref[...], (((0,), (0,)), ((), ())), preferred_element_type=F32
    )
    out_ref[...] = (gates_ref[...] * expert_out).astype(BF16)


def finish(slot, gates, returned):
    groups = len(returned)
    rows = slot.shape[1]
    capacity, d = returned[0].shape
    slots = groups * capacity
    return pl.pallas_call(
        functools.partial(finish_kernel, groups),
        out_shape=jax.ShapeDtypeStruct((rows, d), BF16),
        in_specs=[VMEM] * (2 + groups),
        out_specs=VMEM,
        scratch_shapes=[pltpu.VMEM((slots, d), BF16)],
        compiler_params=pltpu.CompilerParams(vmem_limit_bytes=32 * MIB),
        cost_estimate=pl.CostEstimate(
            flops=2 * slots * rows * d, bytes_accessed=2 * d * (slots + rows), transcendentals=0
        ),
        name="finish",
    )(slot, gates, *returned)


def mixed_order(groups):
    def in_turn(first, second):
        return [s for pair in zip(first, second + [None]) for s in pair if s is not None]

    half, plane = groups // 2, groups // 4
    far = in_turn(list(range(half, half + plane)), list(range(half + plane, groups)))
    near = in_turn(list(range(half - 1, plane - 1, -1)), list(range(plane - 1, 0, -1)))
    near = in_turn(near[1::2], near[::2][:-1]) + near[-1:] if plane > 1 else near
    return [0] + [s for pair in zip(far, near + [None]) for s in pair if s is not None]


def swap(pieces):
    groups = len(pieces)
    order = mixed_order(groups)
    return [pieces[0]] + [
        lax.ppermute(piece, "expert", [(i, i ^ s) for i in range(groups)]) for s, piece in zip(order[1:], pieces[1:])
    ]


def partner_plan(
    grad_hidden, grad_out, grad_route, live_rows, w_down, w_moment, perm, fwd_hidden, fwd_route, fwd_gate
):
    groups = lax.axis_size("expert")
    me = lax.axis_index("expert").astype(jnp.int32).reshape(1)
    capacity = max(4, 2 * grad_hidden.shape[0] // groups)
    ff, d = w_down.shape[1:]
    spread = swap(split(me, w_moment, w_down, groups))
    packed, fwd_slot, gates = pack_rows(
        live_rows, me, perm, grad_route, fwd_route, grad_hidden, grad_out, fwd_hidden, fwd_gate,
        spread[2 * groups // 3], groups, capacity,
    )
    received = swap(packed)
    placed = swap(reorder(me, perm, spread, received[groups // 3]))
    weight_new, moment_new, produced = update(me, received, placed, ff, d)
    return weight_new[None], moment_new[None], finish(fwd_slot, gates, swap(produced))


def lookup(route_ids, mapping):
    columns = jnp.arange(mapping.shape[0], dtype=jnp.int32)
    hits = route_ids[:, None] == columns[None, :]
    return jnp.sum(jnp.where(hits, mapping[None, :], 0), axis=1)


def slot_matrix(target, is_live, groups, capacity):
    columns = jnp.arange(groups, dtype=jnp.int32)
    onehot = ((target[:, None] == columns[None, :]) & is_live[:, None]).astype(jnp.int32)
    ranked = jnp.sum(jnp.cumsum(onehot, axis=0) * onehot, axis=1) - 1
    slot_of = jnp.where(is_live, target * capacity + ranked, -1)
    slots = jnp.arange(groups * capacity, dtype=jnp.int32)
    return (slots[:, None] == slot_of[None, :]).astype(jnp.bfloat16)


def orthogonalize(moment):
    moment_f = moment.astype(jnp.float32)
    frobenius = jnp.sqrt(jnp.sum(moment_f * moment_f))
    current = (moment_f / (frobenius + norm_floor)).astype(jnp.bfloat16)
    for sweep_index in range(2):
        gramian = lax.dot_general(
            current, current, (((1,), (1,)), ((), ())), preferred_element_type=jnp.float32
        ).astype(jnp.bfloat16)
        squared = jnp.dot(gramian, gramian, preferred_element_type=jnp.float32)
        poly = (cubic_term * gramian.astype(jnp.float32) + quintic_term * squared).astype(
            jnp.bfloat16
        )
        current = (
            linear_term * current.astype(jnp.float32)
            + jnp.dot(poly, current, preferred_element_type=jnp.float32)
        ).astype(jnp.bfloat16)
    return current


def relocate(weight, moment, perm):
    groups = lax.axis_size("expert")
    weight_flat = weight.reshape(groups, -1)
    moment_flat = moment.reshape(groups, -1)
    spread_w, spread_m = (
        lax.all_to_all(weight_flat, "expert", split_axis=0, concat_axis=0, tiled=True),
        lax.all_to_all(moment_flat, "expert", split_axis=0, concat_axis=0, tiled=True),
    )
    devices = jnp.arange(groups, dtype=jnp.int32)
    inverse = jnp.sum(jnp.where(perm[None, :] == devices[:, None], devices[None, :], 0), axis=1)
    ordered_w = jnp.take(spread_w, inverse, axis=0)
    ordered_m = jnp.take(spread_m, inverse, axis=0)
    back_w, back_m = (
        lax.all_to_all(ordered_w, "expert", split_axis=0, concat_axis=0, tiled=True),
        lax.all_to_all(ordered_m, "expert", split_axis=0, concat_axis=0, tiled=True),
    )
    return (back_w.reshape(weight.shape), back_m.reshape(moment.shape))


def routed_plan(
    grad_hidden,
    grad_out,
    grad_route,
    live_rows,
    w_down,
    w_moment,
    perm,
    fwd_hidden,
    fwd_route,
    fwd_gate,
):
    groups = lax.axis_size("expert")
    grad_count = grad_hidden.shape[0]
    capacity = max(4, 2 * grad_count // groups)
    is_live = jnp.arange(grad_count, dtype=jnp.int32) < live_rows[0]
    route_ids = grad_route[:, 0]
    weight, moment = relocate(w_down, w_moment, perm)
    target = lookup(route_ids, perm)
    selector = slot_matrix(target, is_live, groups, capacity)
    hidden_buf = (
        jnp.dot(selector, grad_hidden, preferred_element_type=jnp.float32)
        .astype(jnp.bfloat16)
        .reshape(groups, capacity, -1)
    )
    outgrad_buf = (
        jnp.dot(selector, grad_out, preferred_element_type=jnp.float32)
        .astype(jnp.bfloat16)
        .reshape(groups, capacity, -1)
    )
    recv_hidden, recv_outgrad = (
        lax.all_to_all(hidden_buf, "expert", split_axis=0, concat_axis=0, tiled=True),
        lax.all_to_all(outgrad_buf, "expert", split_axis=0, concat_axis=0, tiled=True),
    )
    grad = lax.dot_general(
        recv_hidden.reshape(groups * capacity, -1),
        recv_outgrad.reshape(groups * capacity, -1),
        (((0,), (0,)), ((), ())),
        preferred_element_type=jnp.float32,
    )
    moment_new = (moment_decay * moment[0].astype(jnp.float32) + grad).astype(jnp.bfloat16)
    ortho = orthogonalize(moment_new)
    weight_new = (weight[0].astype(jnp.float32) - step_scale * ortho.astype(jnp.float32)).astype(
        jnp.bfloat16
    )
    weight_new = weight_new[None]
    moment_new = moment_new[None]
    fwd_ids = fwd_route[:, 0]
    placed_weight, placed_moment = (weight_new, moment_new)
    fwd_target = lookup(fwd_ids, perm)
    fwd_weight = weight_new[0]
    fwd_count = fwd_hidden.shape[0]
    fwd_capacity = max(4, 2 * fwd_count // groups)
    fwd_selector = slot_matrix(fwd_target, jnp.ones((fwd_count,), dtype=bool), groups, fwd_capacity)
    fwd_buf = (
        jnp.dot(fwd_selector, fwd_hidden, preferred_element_type=jnp.float32)
        .astype(jnp.bfloat16)
        .reshape(groups, fwd_capacity, -1)
    )
    produced = jnp.einsum(
        "gkf,fd->gkd",
        lax.all_to_all(fwd_buf, "expert", split_axis=0, concat_axis=0, tiled=True),
        fwd_weight,
        preferred_element_type=jnp.float32,
    ).astype(jnp.bfloat16)
    returned = lax.all_to_all(produced, "expert", split_axis=0, concat_axis=0, tiled=True)
    fwd_rows_out = lax.dot_general(
        fwd_selector,
        returned.reshape(groups * fwd_capacity, -1),
        (((0,), (0,)), ((), ())),
        preferred_element_type=jnp.float32,
    )
    fwd_out = (fwd_rows_out * fwd_gate[:, None]).astype(jnp.bfloat16)
    return (placed_weight, placed_moment, fwd_out)


def solution(mesh):
    groups = mesh.shape["expert"]
    in_specs = (
        P(("layer", "expert"), None),
        P(("layer", "expert"), None),
        P(("layer", "expert"), None),
        P(("layer", "expert")),
        P(("layer", "expert"), None, None),
        P(("layer", "expert"), None, None),
        P("layer"),
        P(("layer", "expert"), None),
        P(("layer", "expert"), None),
        P(("layer", "expert")),
    )
    out_specs = (
        P(("layer", "expert"), None, None),
        P(("layer", "expert"), None, None),
        P(("layer", "expert"), None),
    )

    def per_device(*args):
        few = groups >= 8 and groups & (groups - 1) == 0 and groups <= 2 * args[0].shape[0] // groups
        return (partner_plan if few else routed_plan)(*args)

    return jax.shard_map(
        per_device, mesh=mesh, in_specs=in_specs, out_specs=out_specs, check_vma=False
    )
```

```python
import functools

import jax
import jax.numpy as jnp
from jax import lax
from jax.experimental import pallas as pl
from jax.experimental.pallas import tpu as pltpu
from jax.sharding import PartitionSpec as P

linear_term = 3.4445
cubic_term = -4.775
quintic_term = 2.0315
moment_decay = 0.9
step_scale = 0.25
norm_floor = 1e-07

F32 = jnp.float32
BF16 = jnp.bfloat16
HBM = pl.BlockSpec(memory_space=pltpu.HBM)
VMEM = pl.BlockSpec(memory_space=pltpu.VMEM)
SMEM = pl.BlockSpec(memory_space=pltpu.SMEM)
ANY = pl.BlockSpec(memory_space=pl.ANY)
MIB = 1 << 20


def fetched(refs, held, sem):
    copies = [pltpu.make_async_copy(ref, room, sem.at[n]) for n, (ref, room) in enumerate(zip(refs, held))]
    for copy in copies:
        copy.start()
    for copy in copies:
        copy.wait()


def rooms(arrays):
    return [pltpu.VMEM(a.shape, a.dtype) for a in arrays] + [pltpu.SemaphoreType.DMA((len(arrays),))]


def chunk_at(ref, lead, k, rows, columns):
    return ref.at[
        lead,
        pl.ds(pl.multiple_of((k // 2) * rows, rows), rows),
        pl.ds(pl.multiple_of((k % 2) * columns, columns), columns),
    ]


def slot_rows(route, live, groups, capacity, me_ref, perm_ref):
    rows = route.shape[1]
    experts = lax.broadcasted_iota(jnp.int32, (groups, rows), 0)
    onehot = jnp.where((experts == route) & live, 1.0, 0.0).astype(BF16)
    before = lax.broadcasted_iota(jnp.int32, (rows, rows), 0)
    after = lax.broadcasted_iota(jnp.int32, (rows, rows), 1)
    upto = jnp.where(before <= after, 1.0, 0.0).astype(BF16)
    ranks = jnp.dot(onehot, upto, preferred_element_type=F32)
    rank = jnp.sum(ranks * onehot.astype(F32), axis=0, keepdims=True).astype(jnp.int32) - 1
    partner = jnp.zeros_like(route)
    for e in range(groups):
        partner = jnp.where(route == e, perm_ref[e] ^ me_ref[0], partner)
    return jnp.where(live, partner * capacity + rank, -1)


def selector_of(slot, slots):
    rows = slot.shape[1]
    places = lax.broadcasted_iota(jnp.int32, (slots, rows), 0)
    return jnp.where(places == slot, 1.0, 0.0).astype(BF16)


def pack_kernel(groups, live_ref, me_ref, perm_ref, *refs):
    sources, pieces, (slot_ref, gates_ref) = refs[:6], refs[7 : 7 + groups], refs[7 + groups : 9 + groups]
    held, sem = refs[9 + groups : 15 + groups], refs[-1]
    route_ref, fwd_route_ref, hidden_ref, out_ref, fwd_ref, gate_ref = held
    copies = [pltpu.make_async_copy(ref, room, sem.at[n]) for n, (ref, room) in enumerate(zip(sources, held))]
    for copy in copies:
        copy.start()
    rows, ff = hidden_ref.shape
    d = out_ref.shape[1]
    capacity = pieces[0].shape[0]
    slots = groups * capacity
    place = lax.broadcasted_iota(jnp.int32, (1, rows), 1)

    def fill(first, selector, source_ref):
        chosen = jnp.dot(selector, source_ref[...], preferred_element_type=F32).astype(BF16)
        for s, piece in zip(mixed_order(groups), pieces):
            piece[:, first : first + source_ref.shape[1]] = chosen[s * capacity : (s + 1) * capacity]

    copies[0].wait()
    slot = slot_rows(route_ref[...], place < live_ref[0], groups, capacity, me_ref, perm_ref)
    selector = selector_of(slot, slots)
    copies[1].wait()
    fwd_slot = slot_rows(fwd_route_ref[...], place >= 0, groups, capacity, me_ref, perm_ref)
    slot_ref[...] = fwd_slot
    copies[2].wait()
    fill(0, selector, hidden_ref)
    copies[3].wait()
    fill(ff, selector, out_ref)
    copies[4].wait()
    fill(ff + d, selector_of(fwd_slot, slots), fwd_ref)
    copies[5].wait()
    down = lax.broadcasted_iota(jnp.int32, (rows, rows), 0)
    across = lax.broadcasted_iota(jnp.int32, (rows, rows), 1)
    gates_ref[...] = jnp.sum(jnp.where(down == across, gate_ref[...], 0.0), axis=1, keepdims=True)


def pack_rows(live_rows, me, perm, route, fwd_route, hidden, grad_out, fwd_hidden, gate, earlier, groups, capacity):
    rows, ff = hidden.shape
    width = 2 * ff + grad_out.shape[1]
    sources = (route.reshape(1, rows), fwd_route.reshape(1, rows), hidden, grad_out, fwd_hidden, gate.reshape(1, rows))
    *pieces, slot, gates = pl.pallas_call(
        functools.partial(pack_kernel, groups),
        out_shape=(jax.ShapeDtypeStruct((capacity, width), BF16),) * groups
        + (jax.ShapeDtypeStruct((1, rows), jnp.int32), jax.ShapeDtypeStruct((rows, 1), F32)),
        in_specs=[SMEM] * 3 + [HBM] * 6 + [VMEM],
        out_specs=(VMEM,) * (groups + 2),
        scratch_shapes=[pltpu.VMEM(a.shape, a.dtype) for a in sources] + [pltpu.SemaphoreType.DMA((len(sources),))],
        compiler_params=pltpu.CompilerParams(vmem_limit_bytes=32 * MIB),
        cost_estimate=pl.CostEstimate(
            flops=2 * groups * capacity * rows * width, bytes_accessed=6 * rows * width, transcendentals=0
        ),
        name="pack_rows",
    )(live_rows, me, perm, *sources, earlier)
    return pieces, slot, gates


def split_kernel(me_ref, moment_ref, weight_ref, *refs):
    pieces, held, sem = refs[:-3], refs[-3:-1], refs[-1]
    fetched((moment_ref, weight_ref), held, sem)
    for s, piece in zip(mixed_order(len(pieces)), pieces):
        rows, columns = piece.shape[1:]
        for lead, source in enumerate(held):
            piece[lead] = chunk_at(source, 0, me_ref[0] ^ s, rows, columns)[...]


def split(me, moment, weight, groups):
    _, ff, d = weight.shape
    piece = jax.ShapeDtypeStruct((2, ff // (groups // 2), d // 2), BF16)
    return pl.pallas_call(
        split_kernel,
        out_shape=(piece,) * groups,
        in_specs=[SMEM, HBM, HBM],
        out_specs=(VMEM,) * groups,
        scratch_shapes=rooms((moment, weight)),
        compiler_params=pltpu.CompilerParams(vmem_limit_bytes=60 * MIB),
        cost_estimate=pl.CostEstimate(flops=0, bytes_accessed=8 * ff * d, transcendentals=0),
        name="split",
    )(me, moment, weight)


def reorder_kernel(me_ref, perm_ref, *refs):
    groups = len(refs) // 2 - 1
    sources, targets, held = refs[:groups], refs[groups + 1 : 2 * groups + 1], refs[-1]
    me, order = me_ref[0], mixed_order(groups)
    for s, source in zip(order, sources):
        held[me ^ perm_ref[me ^ s]] = source[...]
    for s, target in zip(order, targets):
        target[...] = held[s]


def reorder(me, perm, pieces, earlier):
    groups = len(pieces)
    piece = jax.ShapeDtypeStruct(pieces[0].shape, BF16)
    return pl.pallas_call(
        reorder_kernel,
        out_shape=(piece,) * groups,
        in_specs=[SMEM, SMEM] + [VMEM] * (groups + 1),
        out_specs=(VMEM,) * groups,
        scratch_shapes=[pltpu.VMEM((groups,) + pieces[0].shape, BF16)],
        compiler_params=pltpu.CompilerParams(vmem_limit_bytes=32 * MIB),
        cost_estimate=pl.CostEstimate(flops=0, bytes_accessed=4 * groups * pieces[0].size, transcendentals=0),
        name="reorder",
    )(me, perm, *pieces, earlier)


def update_kernel(groups, me_ref, *refs):
    packed, pieces, produced = refs[:groups], refs[groups : 2 * groups], refs[2 * groups + 2 : 3 * groups + 2]
    weight_new_ref, moment_new_ref = refs[2 * groups : 2 * groups + 2]
    held, rows_ref = refs[-2:]
    _, ff, d = held.shape
    capacity = packed[0].shape[0]
    for n, piece in enumerate(packed):
        rows_ref[n * capacity : (n + 1) * capacity] = piece[...]
    for s, piece in zip(mixed_order(groups), pieces):
        rows, columns = piece.shape[1:]
        for lead in range(2):
            chunk_at(held, lead, me_ref[0] ^ s, rows, columns)[...] = piece[lead]
    grad = lax.dot_general(
        rows_ref[:, :ff], rows_ref[:, ff : ff + d], (((0,), (0,)), ((), ())), preferred_element_type=F32
    )
    moment_new = (moment_decay * held[0].astype(F32) + grad).astype(BF16)
    moment_new_ref[...] = moment_new
    moment_f = moment_new.astype(F32)
    frobenius = jnp.sqrt(jnp.sum(moment_f * moment_f))
    current = (moment_f / (frobenius + norm_floor)).astype(BF16)
    for _ in range(2):
        gramian = lax.dot_general(
            current, current, (((1,), (1,)), ((), ())), preferred_element_type=F32
        ).astype(BF16)
        squared = jnp.dot(gramian, gramian, preferred_element_type=F32)
        poly = (cubic_term * gramian.astype(F32) + quintic_term * squared).astype(BF16)
        current = (
            linear_term * current.astype(F32) + jnp.dot(poly, current, preferred_element_type=F32)
        ).astype(BF16)
    weight_new = (held[1].astype(F32) - step_scale * current.astype(F32)).astype(BF16)
    weight_new_ref[...] = weight_new
    product = jnp.dot(rows_ref[:, ff + d :], weight_new, preferred_element_type=F32).astype(BF16)
    for n, piece in enumerate(produced):
        piece[...] = product[n * capacity : (n + 1) * capacity]


def update(me, packed, pieces, ff, d):
    groups = len(pieces)
    capacity, width = packed[0].shape
    slots = groups * capacity
    shape = jax.ShapeDtypeStruct((ff, d), BF16)
    weight_new, moment_new, *produced = pl.pallas_call(
        functools.partial(update_kernel, groups),
        out_shape=(shape, shape) + (jax.ShapeDtypeStruct((capacity, d), BF16),) * groups,
        in_specs=[SMEM] + [VMEM] * (2 * groups),
        out_specs=(VMEM,) * (groups + 2),
        scratch_shapes=[pltpu.VMEM((2, ff, d), BF16), pltpu.VMEM((slots, width), BF16)],
        compiler_params=pltpu.CompilerParams(vmem_limit_bytes=40 * MIB),
        cost_estimate=pl.CostEstimate(
            flops=4 * ff * d * slots + 8 * ff * ff * d + 4 * ff**3,
            bytes_accessed=8 * ff * d + 2 * slots * (width + d),
            transcendentals=1,
        ),
        name="update",
    )(me, *packed, *pieces)
    return weight_new, moment_new, produced


def finish_kernel(groups, slot_ref, gates_ref, *refs):
    pieces, (out_ref, returned_ref) = refs[:groups], refs[groups:]
    capacity = pieces[0].shape[0]
    for s, piece in zip(mixed_order(groups), pieces):
        returned_ref[s * capacity : (s + 1) * capacity] = piece[...]
    selector = selector_of(slot_ref[...], groups * capacity)
    expert_out = lax.dot_general(
        selector, returned_ref[...], (((0,), (0,)), ((), ())), preferred_element_type=F32
    )
    out_ref[...] = (gates_ref[...] * expert_out).astype(BF16)


def finish(slot, gates, returned):
    groups = len(returned)
    rows = slot.shape[1]
    capacity, d = returned[0].shape
    slots = groups * capacity
    return pl.pallas_call(
        functools.partial(finish_kernel, groups),
        out_shape=jax.ShapeDtypeStruct((rows, d), BF16),
        in_specs=[VMEM] * (2 + groups),
        out_specs=VMEM,
        scratch_shapes=[pltpu.VMEM((slots, d), BF16)],
        compiler_params=pltpu.CompilerParams(vmem_limit_bytes=32 * MIB),
        cost_estimate=pl.CostEstimate(
            flops=2 * slots * rows * d, bytes_accessed=2 * d * (slots + rows), transcendentals=0
        ),
        name="finish",
    )(slot, gates, *returned)


def mixed_order(groups):
    def both_ends(partners):
        middle = (len(partners) + 1) // 2
        first, second = partners[:middle], partners[middle:]
        return [s for pair in zip(first, second + [None]) for s in pair if s is not None]

    half = groups // 2
    far, near = both_ends(list(range(half, groups))), both_ends(list(range(half - 1, 0, -1)))
    return [0] + [s for pair in zip(far, near + [None]) for s in pair if s is not None][::-1]


def swap(pieces):
    groups = len(pieces)
    order = mixed_order(groups)
    return [pieces[0]] + [
        lax.ppermute(piece, "expert", [(i, i ^ s) for i in range(groups)]) for s, piece in zip(order[1:], pieces[1:])
    ]


def partner_plan(
    grad_hidden, grad_out, grad_route, live_rows, w_down, w_moment, perm, fwd_hidden, fwd_route, fwd_gate
):
    groups = lax.axis_size("expert")
    me = lax.axis_index("expert").astype(jnp.int32).reshape(1)
    capacity = max(4, 2 * grad_hidden.shape[0] // groups)
    ff, d = w_down.shape[1:]
    spread = swap(split(me, w_moment, w_down, groups))
    packed, fwd_slot, gates = pack_rows(
        live_rows, me, perm, grad_route, fwd_route, grad_hidden, grad_out, fwd_hidden, fwd_gate,
        spread[2 * groups // 3], groups, capacity,
    )
    received = swap(packed)
    placed = swap(reorder(me, perm, spread, received[groups // 3]))
    weight_new, moment_new, produced = update(me, received, placed, ff, d)
    return weight_new[None], moment_new[None], finish(fwd_slot, gates, swap(produced))


def lookup(route_ids, mapping):
    columns = jnp.arange(mapping.shape[0], dtype=jnp.int32)
    hits = route_ids[:, None] == columns[None, :]
    return jnp.sum(jnp.where(hits, mapping[None, :], 0), axis=1)


def slot_matrix(target, is_live, groups, capacity):
    columns = jnp.arange(groups, dtype=jnp.int32)
    onehot = ((target[:, None] == columns[None, :]) & is_live[:, None]).astype(jnp.int32)
    ranked = jnp.sum(jnp.cumsum(onehot, axis=0) * onehot, axis=1) - 1
    slot_of = jnp.where(is_live, target * capacity + ranked, -1)
    slots = jnp.arange(groups * capacity, dtype=jnp.int32)
    return (slots[:, None] == slot_of[None, :]).astype(jnp.bfloat16)


def orthogonalize(moment):
    moment_f = moment.astype(jnp.float32)
    frobenius = jnp.sqrt(jnp.sum(moment_f * moment_f))
    current = (moment_f / (frobenius + norm_floor)).astype(jnp.bfloat16)
    for sweep_index in range(2):
        gramian = lax.dot_general(
            current, current, (((1,), (1,)), ((), ())), preferred_element_type=jnp.float32
        ).astype(jnp.bfloat16)
        squared = jnp.dot(gramian, gramian, preferred_element_type=jnp.float32)
        poly = (cubic_term * gramian.astype(jnp.float32) + quintic_term * squared).astype(
            jnp.bfloat16
        )
        current = (
            linear_term * current.astype(jnp.float32)
            + jnp.dot(poly, current, preferred_element_type=jnp.float32)
        ).astype(jnp.bfloat16)
    return current


def relocate(weight, moment, perm):
    groups = lax.axis_size("expert")
    weight_flat = weight.reshape(groups, -1)
    moment_flat = moment.reshape(groups, -1)
    spread_w, spread_m = (
        lax.all_to_all(weight_flat, "expert", split_axis=0, concat_axis=0, tiled=True),
        lax.all_to_all(moment_flat, "expert", split_axis=0, concat_axis=0, tiled=True),
    )
    devices = jnp.arange(groups, dtype=jnp.int32)
    inverse = jnp.sum(jnp.where(perm[None, :] == devices[:, None], devices[None, :], 0), axis=1)
    ordered_w = jnp.take(spread_w, inverse, axis=0)
    ordered_m = jnp.take(spread_m, inverse, axis=0)
    back_w, back_m = (
        lax.all_to_all(ordered_w, "expert", split_axis=0, concat_axis=0, tiled=True),
        lax.all_to_all(ordered_m, "expert", split_axis=0, concat_axis=0, tiled=True),
    )
    return (back_w.reshape(weight.shape), back_m.reshape(moment.shape))


def routed_plan(
    grad_hidden,
    grad_out,
    grad_route,
    live_rows,
    w_down,
    w_moment,
    perm,
    fwd_hidden,
    fwd_route,
    fwd_gate,
):
    groups = lax.axis_size("expert")
    grad_count = grad_hidden.shape[0]
    capacity = max(4, 2 * grad_count // groups)
    is_live = jnp.arange(grad_count, dtype=jnp.int32) < live_rows[0]
    route_ids = grad_route[:, 0]
    weight, moment = relocate(w_down, w_moment, perm)
    target = lookup(route_ids, perm)
    selector = slot_matrix(target, is_live, groups, capacity)
    hidden_buf = (
        jnp.dot(selector, grad_hidden, preferred_element_type=jnp.float32)
        .astype(jnp.bfloat16)
        .reshape(groups, capacity, -1)
    )
    outgrad_buf = (
        jnp.dot(selector, grad_out, preferred_element_type=jnp.float32)
        .astype(jnp.bfloat16)
        .reshape(groups, capacity, -1)
    )
    recv_hidden, recv_outgrad = (
        lax.all_to_all(hidden_buf, "expert", split_axis=0, concat_axis=0, tiled=True),
        lax.all_to_all(outgrad_buf, "expert", split_axis=0, concat_axis=0, tiled=True),
    )
    grad = lax.dot_general(
        recv_hidden.reshape(groups * capacity, -1),
        recv_outgrad.reshape(groups * capacity, -1),
        (((0,), (0,)), ((), ())),
        preferred_element_type=jnp.float32,
    )
    moment_new = (moment_decay * moment[0].astype(jnp.float32) + grad).astype(jnp.bfloat16)
    ortho = orthogonalize(moment_new)
    weight_new = (weight[0].astype(jnp.float32) - step_scale * ortho.astype(jnp.float32)).astype(
        jnp.bfloat16
    )
    weight_new = weight_new[None]
    moment_new = moment_new[None]
    fwd_ids = fwd_route[:, 0]
    placed_weight, placed_moment = (weight_new, moment_new)
    fwd_target = lookup(fwd_ids, perm)
    fwd_weight = weight_new[0]
    fwd_count = fwd_hidden.shape[0]
    fwd_capacity = max(4, 2 * fwd_count // groups)
    fwd_selector = slot_matrix(fwd_target, jnp.ones((fwd_count,), dtype=bool), groups, fwd_capacity)
    fwd_buf = (
        jnp.dot(fwd_selector, fwd_hidden, preferred_element_type=jnp.float32)
        .astype(jnp.bfloat16)
        .reshape(groups, fwd_capacity, -1)
    )
    produced = jnp.einsum(
        "gkf,fd->gkd",
        lax.all_to_all(fwd_buf, "expert", split_axis=0, concat_axis=0, tiled=True),
        fwd_weight,
        preferred_element_type=jnp.float32,
    ).astype(jnp.bfloat16)
    returned = lax.all_to_all(produced, "expert", split_axis=0, concat_axis=0, tiled=True)
    fwd_rows_out = lax.dot_general(
        fwd_selector,
        returned.reshape(groups * fwd_capacity, -1),
        (((0,), (0,)), ((), ())),
        preferred_element_type=jnp.float32,
    )
    fwd_out = (fwd_rows_out * fwd_gate[:, None]).astype(jnp.bfloat16)
    return (placed_weight, placed_moment, fwd_out)


def solution(mesh):
    groups = mesh.shape["expert"]
    in_specs = (
        P(("layer", "expert"), None),
        P(("layer", "expert"), None),
        P(("layer", "expert"), None),
        P(("layer", "expert")),
        P(("layer", "expert"), None, None),
        P(("layer", "expert"), None, None),
        P("layer"),
        P(("layer", "expert"), None),
        P(("layer", "expert"), None),
        P(("layer", "expert")),
    )
    out_specs = (
        P(("layer", "expert"), None, None),
        P(("layer", "expert"), None, None),
        P(("layer", "expert"), None),
    )

    def per_device(*args):
        few = groups >= 8 and groups & (groups - 1) == 0 and groups <= 2 * args[0].shape[0] // groups
        return (partner_plan if few else routed_plan)(*args)

    return jax.shard_map(
        per_device, mesh=mesh, in_specs=in_specs, out_specs=out_specs, check_vma=False
    )
```

```python
import functools

import jax
import jax.numpy as jnp
from jax import lax
from jax.experimental import pallas as pl
from jax.experimental.pallas import tpu as pltpu
from jax.sharding import PartitionSpec as P

linear_term = 3.4445
cubic_term = -4.775
quintic_term = 2.0315
moment_decay = 0.9
step_scale = 0.25
norm_floor = 1e-07

F32 = jnp.float32
BF16 = jnp.bfloat16
HBM = pl.BlockSpec(memory_space=pltpu.HBM)
VMEM = pl.BlockSpec(memory_space=pltpu.VMEM)
SMEM = pl.BlockSpec(memory_space=pltpu.SMEM)
ANY = pl.BlockSpec(memory_space=pl.ANY)
MIB = 1 << 20


def fetched(refs, held, sem):
    copies = [pltpu.make_async_copy(ref, room, sem.at[n]) for n, (ref, room) in enumerate(zip(refs, held))]
    for copy in copies:
        copy.start()
    for copy in copies:
        copy.wait()


def rooms(arrays):
    return [pltpu.VMEM(a.shape, a.dtype) for a in arrays] + [pltpu.SemaphoreType.DMA((len(arrays),))]


def chunk_at(ref, lead, k, rows, columns):
    return ref.at[
        lead,
        pl.ds(pl.multiple_of((k // 2) * rows, rows), rows),
        pl.ds(pl.multiple_of((k % 2) * columns, columns), columns),
    ]


def slot_rows(route, live, groups, capacity, me_ref, perm_ref):
    rows = route.shape[1]
    experts = lax.broadcasted_iota(jnp.int32, (groups, rows), 0)
    onehot = jnp.where((experts == route) & live, 1.0, 0.0).astype(BF16)
    before = lax.broadcasted_iota(jnp.int32, (rows, rows), 0)
    after = lax.broadcasted_iota(jnp.int32, (rows, rows), 1)
    upto = jnp.where(before <= after, 1.0, 0.0).astype(BF16)
    ranks = jnp.dot(onehot, upto, preferred_element_type=F32)
    rank = jnp.sum(ranks * onehot.astype(F32), axis=0, keepdims=True).astype(jnp.int32) - 1
    partner = jnp.zeros_like(route)
    for e in range(groups):
        partner = jnp.where(route == e, perm_ref[e] ^ me_ref[0], partner)
    return jnp.where(live, partner * capacity + rank, -1)


def selector_of(slot, slots):
    rows = slot.shape[1]
    places = lax.broadcasted_iota(jnp.int32, (slots, rows), 0)
    return jnp.where(places == slot, 1.0, 0.0).astype(BF16)


def pack_kernel(groups, live_ref, me_ref, perm_ref, *refs):
    sources, pieces, (slot_ref, gates_ref) = refs[:6], refs[7 : 7 + groups], refs[7 + groups : 9 + groups]
    held, sem = refs[9 + groups : 15 + groups], refs[-1]
    route_ref, fwd_route_ref, hidden_ref, out_ref, fwd_ref, gate_ref = held
    copies = [pltpu.make_async_copy(ref, room, sem.at[n]) for n, (ref, room) in enumerate(zip(sources, held))]
    for copy in copies:
        copy.start()
    rows, ff = hidden_ref.shape
    d = out_ref.shape[1]
    capacity = pieces[0].shape[0]
    slots = groups * capacity
    place = lax.broadcasted_iota(jnp.int32, (1, rows), 1)

    def fill(first, selector, source_ref):
        chosen = jnp.dot(selector, source_ref[...], preferred_element_type=F32).astype(BF16)
        for s, piece in zip(mixed_order(groups), pieces):
            piece[:, first : first + source_ref.shape[1]] = chosen[s * capacity : (s + 1) * capacity]

    copies[0].wait()
    slot = slot_rows(route_ref[...], place < live_ref[0], groups, capacity, me_ref, perm_ref)
    selector = selector_of(slot, slots)
    copies[1].wait()
    fwd_slot = slot_rows(fwd_route_ref[...], place >= 0, groups, capacity, me_ref, perm_ref)
    slot_ref[...] = fwd_slot
    copies[2].wait()
    fill(0, selector, hidden_ref)
    copies[3].wait()
    fill(ff, selector, out_ref)
    copies[4].wait()
    fill(ff + d, selector_of(fwd_slot, slots), fwd_ref)
    copies[5].wait()
    down = lax.broadcasted_iota(jnp.int32, (rows, rows), 0)
    across = lax.broadcasted_iota(jnp.int32, (rows, rows), 1)
    gates_ref[...] = jnp.sum(jnp.where(down == across, gate_ref[...], 0.0), axis=1, keepdims=True)


def pack_rows(live_rows, me, perm, route, fwd_route, hidden, grad_out, fwd_hidden, gate, earlier, groups, capacity):
    rows, ff = hidden.shape
    width = 2 * ff + grad_out.shape[1]
    sources = (route.reshape(1, rows), fwd_route.reshape(1, rows), hidden, grad_out, fwd_hidden, gate.reshape(1, rows))
    *pieces, slot, gates = pl.pallas_call(
        functools.partial(pack_kernel, groups),
        out_shape=(jax.ShapeDtypeStruct((capacity, width), BF16),) * groups
        + (jax.ShapeDtypeStruct((1, rows), jnp.int32), jax.ShapeDtypeStruct((rows, 1), F32)),
        in_specs=[SMEM] * 3 + [HBM] * 6 + [ANY],
        out_specs=(VMEM,) * (groups + 2),
        scratch_shapes=[pltpu.VMEM(a.shape, a.dtype) for a in sources] + [pltpu.SemaphoreType.DMA((len(sources),))],
        compiler_params=pltpu.CompilerParams(vmem_limit_bytes=32 * MIB),
        cost_estimate=pl.CostEstimate(
            flops=2 * groups * capacity * rows * width, bytes_accessed=6 * rows * width, transcendentals=0
        ),
        name="pack_rows",
    )(live_rows, me, perm, *sources, earlier)
    return pieces, slot, gates


def split_kernel(partners, me_ref, moment_ref, weight_ref, earlier_ref, *refs):
    pieces, sem = refs[:-1], refs[-1]
    copies = []
    for s, piece in zip(partners, pieces):
        rows, columns = piece.shape[1:]
        for lead, source in enumerate((moment_ref, weight_ref)):
            chunk = chunk_at(source, 0, me_ref[0] ^ s, rows, columns)
            copies.append(pltpu.make_async_copy(chunk, piece.at[lead], sem.at[len(copies)]))
    for copy in copies:
        copy.start()
    for copy in copies:
        copy.wait()


def split(me, moment, weight, earlier, groups, partners):
    _, ff, d = weight.shape
    piece = jax.ShapeDtypeStruct((2, ff // (groups // 2), d // 2), BF16)
    return pl.pallas_call(
        functools.partial(split_kernel, partners),
        out_shape=(piece,) * len(partners),
        in_specs=[SMEM, HBM, HBM, ANY],
        out_specs=(VMEM,) * len(partners),
        scratch_shapes=[pltpu.SemaphoreType.DMA((2 * len(partners),))],
        compiler_params=pltpu.CompilerParams(vmem_limit_bytes=60 * MIB),
        cost_estimate=pl.CostEstimate(
            flops=0, bytes_accessed=8 * ff * d * len(partners) // groups, transcendentals=0
        ),
        name="split",
    )(me, moment, weight, earlier)


def reorder_kernel(me_ref, perm_ref, *refs):
    groups = len(refs) // 2 - 1
    sources, targets, held = refs[:groups], refs[groups + 1 : 2 * groups + 1], refs[-1]
    me = me_ref[0]
    for s, source in zip(spread_order(groups), sources):
        held[me ^ perm_ref[me ^ s]] = source[...]
    for s, target in zip(mixed_order(groups), targets):
        target[...] = held[s]


def reorder(me, perm, pieces, earlier):
    groups = len(pieces)
    piece = jax.ShapeDtypeStruct(pieces[0].shape, BF16)
    return pl.pallas_call(
        reorder_kernel,
        out_shape=(piece,) * groups,
        in_specs=[SMEM, SMEM] + [VMEM] * (groups + 1),
        out_specs=(VMEM,) * groups,
        scratch_shapes=[pltpu.VMEM((groups,) + pieces[0].shape, BF16)],
        compiler_params=pltpu.CompilerParams(vmem_limit_bytes=32 * MIB),
        cost_estimate=pl.CostEstimate(flops=0, bytes_accessed=4 * groups * pieces[0].size, transcendentals=0),
        name="reorder",
    )(me, perm, *pieces, earlier)


def update_kernel(groups, me_ref, *refs):
    packed, pieces, produced = refs[:groups], refs[groups : 2 * groups], refs[2 * groups + 2 : 3 * groups + 2]
    weight_new_ref, moment_new_ref = refs[2 * groups : 2 * groups + 2]
    held, rows_ref = refs[-2:]
    _, ff, d = held.shape
    capacity = packed[0].shape[0]
    for n, piece in enumerate(packed):
        rows_ref[n * capacity : (n + 1) * capacity] = piece[...]
    for s, piece in zip(mixed_order(groups), pieces):
        rows, columns = piece.shape[1:]
        for lead in range(2):
            chunk_at(held, lead, me_ref[0] ^ s, rows, columns)[...] = piece[lead]
    grad = lax.dot_general(
        rows_ref[:, :ff], rows_ref[:, ff : ff + d], (((0,), (0,)), ((), ())), preferred_element_type=F32
    )
    moment_new = (moment_decay * held[0].astype(F32) + grad).astype(BF16)
    moment_new_ref[...] = moment_new
    moment_f = moment_new.astype(F32)
    frobenius = jnp.sqrt(jnp.sum(moment_f * moment_f))
    current = (moment_f / (frobenius + norm_floor)).astype(BF16)
    for _ in range(2):
        gramian = lax.dot_general(
            current, current, (((1,), (1,)), ((), ())), preferred_element_type=F32
        ).astype(BF16)
        squared = jnp.dot(gramian, gramian, preferred_element_type=F32)
        poly = (cubic_term * gramian.astype(F32) + quintic_term * squared).astype(BF16)
        current = (
            linear_term * current.astype(F32) + jnp.dot(poly, current, preferred_element_type=F32)
        ).astype(BF16)
    weight_new = (held[1].astype(F32) - step_scale * current.astype(F32)).astype(BF16)
    weight_new_ref[...] = weight_new
    product = jnp.dot(rows_ref[:, ff + d :], weight_new, preferred_element_type=F32).astype(BF16)
    for n, piece in enumerate(produced):
        piece[...] = product[n * capacity : (n + 1) * capacity]


def update(me, packed, pieces, ff, d):
    groups = len(pieces)
    capacity, width = packed[0].shape
    slots = groups * capacity
    shape = jax.ShapeDtypeStruct((ff, d), BF16)
    weight_new, moment_new, *produced = pl.pallas_call(
        functools.partial(update_kernel, groups),
        out_shape=(shape, shape) + (jax.ShapeDtypeStruct((capacity, d), BF16),) * groups,
        in_specs=[SMEM] + [VMEM] * (2 * groups),
        out_specs=(VMEM,) * (groups + 2),
        scratch_shapes=[pltpu.VMEM((2, ff, d), BF16), pltpu.VMEM((slots, width), BF16)],
        compiler_params=pltpu.CompilerParams(vmem_limit_bytes=40 * MIB),
        cost_estimate=pl.CostEstimate(
            flops=4 * ff * d * slots + 8 * ff * ff * d + 4 * ff**3,
            bytes_accessed=8 * ff * d + 2 * slots * (width + d),
            transcendentals=1,
        ),
        name="update",
    )(me, *packed, *pieces)
    return weight_new, moment_new, produced


def finish_kernel(groups, slot_ref, gates_ref, *refs):
    pieces, (out_ref, returned_ref) = refs[:groups], refs[groups:]
    capacity = pieces[0].shape[0]
    for s, piece in zip(mixed_order(groups), pieces):
        returned_ref[s * capacity : (s + 1) * capacity] = piece[...]
    selector = selector_of(slot_ref[...], groups * capacity)
    expert_out = lax.dot_general(
        selector, returned_ref[...], (((0,), (0,)), ((), ())), preferred_element_type=F32
    )
    out_ref[...] = (gates_ref[...] * expert_out).astype(BF16)


def finish(slot, gates, returned):
    groups = len(returned)
    rows = slot.shape[1]
    capacity, d = returned[0].shape
    slots = groups * capacity
    return pl.pallas_call(
        functools.partial(finish_kernel, groups),
        out_shape=jax.ShapeDtypeStruct((rows, d), BF16),
        in_specs=[VMEM] * (2 + groups),
        out_specs=VMEM,
        scratch_shapes=[pltpu.VMEM((slots, d), BF16)],
        compiler_params=pltpu.CompilerParams(vmem_limit_bytes=32 * MIB),
        cost_estimate=pl.CostEstimate(
            flops=2 * slots * rows * d, bytes_accessed=2 * d * (slots + rows), transcendentals=0
        ),
        name="finish",
    )(slot, gates, *returned)


def mixed_order(groups):
    def both_ends(partners):
        middle = (len(partners) + 1) // 2
        first, second = partners[:middle], partners[middle:]
        return [s for pair in zip(first, second + [None]) for s in pair if s is not None]

    half = groups // 2
    far, near = both_ends(list(range(half, groups))), both_ends(list(range(half - 1, 0, -1)))
    return [0] + [s for pair in zip(far, near + [None]) for s in pair if s is not None]


def spread_order(groups):
    order = mixed_order(groups)
    return [0, order[-6]] + [s for s in order[1:] if s != order[-6]]


def swap(pieces, order):
    groups = lax.axis_size("expert")
    return [
        lax.ppermute(piece, "expert", [(i, i ^ s) for i in range(groups)]) if s else piece
        for s, piece in zip(order, pieces)
    ]


def partner_plan(
    grad_hidden, grad_out, grad_route, live_rows, w_down, w_moment, perm, fwd_hidden, fwd_route, fwd_gate
):
    groups = lax.axis_size("expert")
    me = lax.axis_index("expert").astype(jnp.int32).reshape(1)
    capacity = max(4, 2 * grad_hidden.shape[0] // groups)
    ff, d = w_down.shape[1:]
    order, early = mixed_order(groups), spread_order(groups)
    first = split(me, w_moment, w_down, live_rows, groups, early[1:6])
    packed, fwd_slot, gates = pack_rows(
        live_rows, me, perm, grad_route, fwd_route, grad_hidden, grad_out, fwd_hidden, fwd_gate,
        first[-1], groups, capacity,
    )
    own, *others = split(me, w_moment, w_down, fwd_slot, groups, early[:1] + early[6:])
    spread = swap([own, *first, *others], early)
    received = swap(packed, order)
    placed = swap(reorder(me, perm, spread, received[groups // 3]), order)
    weight_new, moment_new, produced = update(me, received, placed, ff, d)
    return weight_new[None], moment_new[None], finish(fwd_slot, gates, swap(produced, order))


def lookup(route_ids, mapping):
    columns = jnp.arange(mapping.shape[0], dtype=jnp.int32)
    hits = route_ids[:, None] == columns[None, :]
    return jnp.sum(jnp.where(hits, mapping[None, :], 0), axis=1)


def slot_matrix(target, is_live, groups, capacity):
    columns = jnp.arange(groups, dtype=jnp.int32)
    onehot = ((target[:, None] == columns[None, :]) & is_live[:, None]).astype(jnp.int32)
    ranked = jnp.sum(jnp.cumsum(onehot, axis=0) * onehot, axis=1) - 1
    slot_of = jnp.where(is_live, target * capacity + ranked, -1)
    slots = jnp.arange(groups * capacity, dtype=jnp.int32)
    return (slots[:, None] == slot_of[None, :]).astype(jnp.bfloat16)


def orthogonalize(moment):
    moment_f = moment.astype(jnp.float32)
    frobenius = jnp.sqrt(jnp.sum(moment_f * moment_f))
    current = (moment_f / (frobenius + norm_floor)).astype(jnp.bfloat16)
    for sweep_index in range(2):
        gramian = lax.dot_general(
            current, current, (((1,), (1,)), ((), ())), preferred_element_type=jnp.float32
        ).astype(jnp.bfloat16)
        squared = jnp.dot(gramian, gramian, preferred_element_type=jnp.float32)
        poly = (cubic_term * gramian.astype(jnp.float32) + quintic_term * squared).astype(
            jnp.bfloat16
        )
        current = (
            linear_term * current.astype(jnp.float32)
            + jnp.dot(poly, current, preferred_element_type=jnp.float32)
        ).astype(jnp.bfloat16)
    return current


def relocate(weight, moment, perm):
    groups = lax.axis_size("expert")
    weight_flat = weight.reshape(groups, -1)
    moment_flat = moment.reshape(groups, -1)
    spread_w, spread_m = (
        lax.all_to_all(weight_flat, "expert", split_axis=0, concat_axis=0, tiled=True),
        lax.all_to_all(moment_flat, "expert", split_axis=0, concat_axis=0, tiled=True),
    )
    devices = jnp.arange(groups, dtype=jnp.int32)
    inverse = jnp.sum(jnp.where(perm[None, :] == devices[:, None], devices[None, :], 0), axis=1)
    ordered_w = jnp.take(spread_w, inverse, axis=0)
    ordered_m = jnp.take(spread_m, inverse, axis=0)
    back_w, back_m = (
        lax.all_to_all(ordered_w, "expert", split_axis=0, concat_axis=0, tiled=True),
        lax.all_to_all(ordered_m, "expert", split_axis=0, concat_axis=0, tiled=True),
    )
    return (back_w.reshape(weight.shape), back_m.reshape(moment.shape))


def routed_plan(
    grad_hidden,
    grad_out,
    grad_route,
    live_rows,
    w_down,
    w_moment,
    perm,
    fwd_hidden,
    fwd_route,
    fwd_gate,
):
    groups = lax.axis_size("expert")
    grad_count = grad_hidden.shape[0]
    capacity = max(4, 2 * grad_count // groups)
    is_live = jnp.arange(grad_count, dtype=jnp.int32) < live_rows[0]
    route_ids = grad_route[:, 0]
    weight, moment = relocate(w_down, w_moment, perm)
    target = lookup(route_ids, perm)
    selector = slot_matrix(target, is_live, groups, capacity)
    hidden_buf = (
        jnp.dot(selector, grad_hidden, preferred_element_type=jnp.float32)
        .astype(jnp.bfloat16)
        .reshape(groups, capacity, -1)
    )
    outgrad_buf = (
        jnp.dot(selector, grad_out, preferred_element_type=jnp.float32)
        .astype(jnp.bfloat16)
        .reshape(groups, capacity, -1)
    )
    recv_hidden, recv_outgrad = (
        lax.all_to_all(hidden_buf, "expert", split_axis=0, concat_axis=0, tiled=True),
        lax.all_to_all(outgrad_buf, "expert", split_axis=0, concat_axis=0, tiled=True),
    )
    grad = lax.dot_general(
        recv_hidden.reshape(groups * capacity, -1),
        recv_outgrad.reshape(groups * capacity, -1),
        (((0,), (0,)), ((), ())),
        preferred_element_type=jnp.float32,
    )
    moment_new = (moment_decay * moment[0].astype(jnp.float32) + grad).astype(jnp.bfloat16)
    ortho = orthogonalize(moment_new)
    weight_new = (weight[0].astype(jnp.float32) - step_scale * ortho.astype(jnp.float32)).astype(
        jnp.bfloat16
    )
    weight_new = weight_new[None]
    moment_new = moment_new[None]
    fwd_ids = fwd_route[:, 0]
    placed_weight, placed_moment = (weight_new, moment_new)
    fwd_target = lookup(fwd_ids, perm)
    fwd_weight = weight_new[0]
    fwd_count = fwd_hidden.shape[0]
    fwd_capacity = max(4, 2 * fwd_count // groups)
    fwd_selector = slot_matrix(fwd_target, jnp.ones((fwd_count,), dtype=bool), groups, fwd_capacity)
    fwd_buf = (
        jnp.dot(fwd_selector, fwd_hidden, preferred_element_type=jnp.float32)
        .astype(jnp.bfloat16)
        .reshape(groups, fwd_capacity, -1)
    )
    produced = jnp.einsum(
        "gkf,fd->gkd",
        lax.all_to_all(fwd_buf, "expert", split_axis=0, concat_axis=0, tiled=True),
        fwd_weight,
        preferred_element_type=jnp.float32,
    ).astype(jnp.bfloat16)
    returned = lax.all_to_all(produced, "expert", split_axis=0, concat_axis=0, tiled=True)
    fwd_rows_out = lax.dot_general(
        fwd_selector,
        returned.reshape(groups * fwd_capacity, -1),
        (((0,), (0,)), ((), ())),
        preferred_element_type=jnp.float32,
    )
    fwd_out = (fwd_rows_out * fwd_gate[:, None]).astype(jnp.bfloat16)
    return (placed_weight, placed_moment, fwd_out)


def solution(mesh):
    groups = mesh.shape["expert"]
    in_specs = (
        P(("layer", "expert"), None),
        P(("layer", "expert"), None),
        P(("layer", "expert"), None),
        P(("layer", "expert")),
        P(("layer", "expert"), None, None),
        P(("layer", "expert"), None, None),
        P("layer"),
        P(("layer", "expert"), None),
        P(("layer", "expert"), None),
        P(("layer", "expert")),
    )
    out_specs = (
        P(("layer", "expert"), None, None),
        P(("layer", "expert"), None, None),
        P(("layer", "expert"), None),
    )

    def per_device(*args):
        few = groups >= 8 and groups & (groups - 1) == 0 and groups <= 2 * args[0].shape[0] // groups
        return (partner_plan if few else routed_plan)(*args)

    return jax.shard_map(
        per_device, mesh=mesh, in_specs=in_specs, out_specs=out_specs, check_vma=False
    )
```

```python
import functools

import jax
import jax.numpy as jnp
from jax import lax
from jax.experimental import pallas as pl
from jax.experimental.pallas import tpu as pltpu
from jax.sharding import PartitionSpec as P

linear_term = 3.4445
cubic_term = -4.775
quintic_term = 2.0315
moment_decay = 0.9
step_scale = 0.25
norm_floor = 1e-07

F32 = jnp.float32
BF16 = jnp.bfloat16
HBM = pl.BlockSpec(memory_space=pltpu.HBM)
VMEM = pl.BlockSpec(memory_space=pltpu.VMEM)
SMEM = pl.BlockSpec(memory_space=pltpu.SMEM)
ANY = pl.BlockSpec(memory_space=pl.ANY)
MIB = 1 << 20


def fetched(refs, held, sem):
    copies = [pltpu.make_async_copy(ref, room, sem.at[n]) for n, (ref, room) in enumerate(zip(refs, held))]
    for copy in copies:
        copy.start()
    for copy in copies:
        copy.wait()


def rooms(arrays):
    return [pltpu.VMEM(a.shape, a.dtype) for a in arrays] + [pltpu.SemaphoreType.DMA((len(arrays),))]


def chunk_at(ref, lead, k, rows, columns):
    return ref.at[
        lead,
        pl.ds(pl.multiple_of((k // 2) * rows, rows), rows),
        pl.ds(pl.multiple_of((k % 2) * columns, columns), columns),
    ]


def slot_rows(route, live, groups, capacity, me_ref, perm_ref):
    rows = route.shape[1]
    experts = lax.broadcasted_iota(jnp.int32, (groups, rows), 0)
    onehot = jnp.where((experts == route) & live, 1.0, 0.0).astype(BF16)
    before = lax.broadcasted_iota(jnp.int32, (rows, rows), 0)
    after = lax.broadcasted_iota(jnp.int32, (rows, rows), 1)
    upto = jnp.where(before <= after, 1.0, 0.0).astype(BF16)
    ranks = jnp.dot(onehot, upto, preferred_element_type=F32)
    rank = jnp.sum(ranks * onehot.astype(F32), axis=0, keepdims=True).astype(jnp.int32) - 1
    partner = jnp.zeros_like(route)
    for e in range(groups):
        partner = jnp.where(route == e, perm_ref[e] ^ me_ref[0], partner)
    return jnp.where(live, partner * capacity + rank, -1)


def selector_of(slot, slots):
    rows = slot.shape[1]
    places = lax.broadcasted_iota(jnp.int32, (slots, rows), 0)
    return jnp.where(places == slot, 1.0, 0.0).astype(BF16)


def pack_kernel(groups, live_ref, me_ref, perm_ref, *refs):
    sources, pieces, (slot_ref, gates_ref) = refs[:6], refs[7 : 7 + groups], refs[7 + groups : 9 + groups]
    held, sem = refs[9 + groups : 15 + groups], refs[-1]
    route_ref, fwd_route_ref, hidden_ref, out_ref, fwd_ref, gate_ref = held
    copies = [pltpu.make_async_copy(ref, room, sem.at[n]) for n, (ref, room) in enumerate(zip(sources, held))]
    for copy in copies:
        copy.start()
    rows, ff = hidden_ref.shape
    d = out_ref.shape[1]
    capacity = pieces[0].shape[0]
    slots = groups * capacity
    place = lax.broadcasted_iota(jnp.int32, (1, rows), 1)

    def fill(first, selector, source_ref):
        chosen = jnp.dot(selector, source_ref[...], preferred_element_type=F32).astype(BF16)
        for s, piece in zip(mixed_order(groups), pieces):
            piece[:, first : first + source_ref.shape[1]] = chosen[s * capacity : (s + 1) * capacity]

    copies[0].wait()
    slot = slot_rows(route_ref[...], place < live_ref[0], groups, capacity, me_ref, perm_ref)
    selector = selector_of(slot, slots)
    copies[1].wait()
    fwd_slot = slot_rows(fwd_route_ref[...], place >= 0, groups, capacity, me_ref, perm_ref)
    slot_ref[...] = fwd_slot
    copies[2].wait()
    fill(0, selector, hidden_ref)
    copies[3].wait()
    fill(ff, selector, out_ref)
    copies[4].wait()
    fill(ff + d, selector_of(fwd_slot, slots), fwd_ref)
    copies[5].wait()
    down = lax.broadcasted_iota(jnp.int32, (rows, rows), 0)
    across = lax.broadcasted_iota(jnp.int32, (rows, rows), 1)
    gates_ref[...] = jnp.sum(jnp.where(down == across, gate_ref[...], 0.0), axis=1, keepdims=True)


def pack_rows(live_rows, me, perm, route, fwd_route, hidden, grad_out, fwd_hidden, gate, earlier, groups, capacity):
    rows, ff = hidden.shape
    width = 2 * ff + grad_out.shape[1]
    sources = (route.reshape(1, rows), fwd_route.reshape(1, rows), hidden, grad_out, fwd_hidden, gate.reshape(1, rows))
    *pieces, slot, gates = pl.pallas_call(
        functools.partial(pack_kernel, groups),
        out_shape=(jax.ShapeDtypeStruct((capacity, width), BF16),) * groups
        + (jax.ShapeDtypeStruct((1, rows), jnp.int32), jax.ShapeDtypeStruct((rows, 1), F32)),
        in_specs=[SMEM] * 3 + [HBM] * 6 + [VMEM],
        out_specs=(VMEM,) * (groups + 2),
        scratch_shapes=[pltpu.VMEM(a.shape, a.dtype) for a in sources] + [pltpu.SemaphoreType.DMA((len(sources),))],
        compiler_params=pltpu.CompilerParams(vmem_limit_bytes=32 * MIB),
        cost_estimate=pl.CostEstimate(
            flops=2 * groups * capacity * rows * width, bytes_accessed=6 * rows * width, transcendentals=0
        ),
        name="pack_rows",
    )(live_rows, me, perm, *sources, earlier)
    return pieces, slot, gates


def split_kernel(me_ref, moment_ref, weight_ref, *refs):
    pieces, held, sem = refs[:-3], refs[-3:-1], refs[-1]
    fetched((moment_ref, weight_ref), held, sem)
    for s, piece in zip(mixed_order(len(pieces)), pieces):
        rows, columns = piece.shape[1:]
        for lead, source in enumerate(held):
            piece[lead] = chunk_at(source, 0, me_ref[0] ^ s, rows, columns)[...]


def split(me, moment, weight, groups):
    _, ff, d = weight.shape
    piece = jax.ShapeDtypeStruct((2, ff // (groups // 2), d // 2), BF16)
    return pl.pallas_call(
        split_kernel,
        out_shape=(piece,) * groups,
        in_specs=[SMEM, HBM, HBM],
        out_specs=(VMEM,) * groups,
        scratch_shapes=rooms((moment, weight)),
        compiler_params=pltpu.CompilerParams(vmem_limit_bytes=60 * MIB),
        cost_estimate=pl.CostEstimate(flops=0, bytes_accessed=8 * ff * d, transcendentals=0),
        name="split",
    )(me, moment, weight)


def reorder_kernel(me_ref, perm_ref, *refs):
    groups = len(refs) // 2 - 1
    sources, targets, held = refs[:groups], refs[groups + 1 : 2 * groups + 1], refs[-1]
    me, order = me_ref[0], mixed_order(groups)
    for s, source in zip(order, sources):
        held[me ^ perm_ref[me ^ s]] = source[...]
    for s, target in zip(order, targets):
        target[...] = held[s]


def reorder(me, perm, pieces, earlier):
    groups = len(pieces)
    piece = jax.ShapeDtypeStruct(pieces[0].shape, BF16)
    return pl.pallas_call(
        reorder_kernel,
        out_shape=(piece,) * groups,
        in_specs=[SMEM, SMEM] + [VMEM] * (groups + 1),
        out_specs=(VMEM,) * groups,
        scratch_shapes=[pltpu.VMEM((groups,) + pieces[0].shape, BF16)],
        compiler_params=pltpu.CompilerParams(vmem_limit_bytes=32 * MIB),
        cost_estimate=pl.CostEstimate(flops=0, bytes_accessed=4 * groups * pieces[0].size, transcendentals=0),
        name="reorder",
    )(me, perm, *pieces, earlier)


def update_kernel(groups, me_ref, *refs):
    packed, pieces, produced = refs[:groups], refs[groups : 2 * groups], refs[2 * groups + 2 : 3 * groups + 2]
    weight_new_ref, moment_new_ref = refs[2 * groups : 2 * groups + 2]
    held, rows_ref = refs[-2:]
    _, ff, d = held.shape
    capacity = packed[0].shape[0]
    for n, piece in enumerate(packed):
        rows_ref[n * capacity : (n + 1) * capacity] = piece[...]
    for s, piece in zip(mixed_order(groups), pieces):
        rows, columns = piece.shape[1:]
        for lead in range(2):
            chunk_at(held, lead, me_ref[0] ^ s, rows, columns)[...] = piece[lead]
    grad = lax.dot_general(
        rows_ref[:, :ff], rows_ref[:, ff : ff + d], (((0,), (0,)), ((), ())), preferred_element_type=F32
    )
    moment_new = (moment_decay * held[0].astype(F32) + grad).astype(BF16)
    moment_new_ref[...] = moment_new
    moment_f = moment_new.astype(F32)
    frobenius = jnp.sqrt(jnp.sum(moment_f * moment_f))
    current = (moment_f / (frobenius + norm_floor)).astype(BF16)
    for _ in range(2):
        gramian = lax.dot_general(
            current, current, (((1,), (1,)), ((), ())), preferred_element_type=F32
        ).astype(BF16)
        squared = jnp.dot(gramian, gramian, preferred_element_type=F32)
        poly = (cubic_term * gramian.astype(F32) + quintic_term * squared).astype(BF16)
        current = (
            linear_term * current.astype(F32) + jnp.dot(poly, current, preferred_element_type=F32)
        ).astype(BF16)
    weight_new = (held[1].astype(F32) - step_scale * current.astype(F32)).astype(BF16)
    weight_new_ref[...] = weight_new
    product = jnp.dot(rows_ref[:, ff + d :], weight_new, preferred_element_type=F32).astype(BF16)
    for n, piece in enumerate(produced):
        piece[...] = product[n * capacity : (n + 1) * capacity]


def update(me, packed, pieces, ff, d):
    groups = len(pieces)
    capacity, width = packed[0].shape
    slots = groups * capacity
    shape = jax.ShapeDtypeStruct((ff, d), BF16)
    weight_new, moment_new, *produced = pl.pallas_call(
        functools.partial(update_kernel, groups),
        out_shape=(shape, shape) + (jax.ShapeDtypeStruct((capacity, d), BF16),) * groups,
        in_specs=[SMEM] + [VMEM] * (2 * groups),
        out_specs=(VMEM,) * (groups + 2),
        scratch_shapes=[pltpu.VMEM((2, ff, d), BF16), pltpu.VMEM((slots, width), BF16)],
        compiler_params=pltpu.CompilerParams(vmem_limit_bytes=40 * MIB),
        cost_estimate=pl.CostEstimate(
            flops=4 * ff * d * slots + 8 * ff * ff * d + 4 * ff**3,
            bytes_accessed=8 * ff * d + 2 * slots * (width + d),
            transcendentals=1,
        ),
        name="update",
    )(me, *packed, *pieces)
    return weight_new, moment_new, produced


def finish_kernel(groups, slot_ref, gates_ref, *refs):
    pieces, (out_ref, returned_ref) = refs[:groups], refs[groups:]
    capacity = pieces[0].shape[0]
    for s, piece in zip(mixed_order(groups), pieces):
        returned_ref[s * capacity : (s + 1) * capacity] = piece[...]
    selector = selector_of(slot_ref[...], groups * capacity)
    expert_out = lax.dot_general(
        selector, returned_ref[...], (((0,), (0,)), ((), ())), preferred_element_type=F32
    )
    out_ref[...] = (gates_ref[...] * expert_out).astype(BF16)


def finish(slot, gates, returned):
    groups = len(returned)
    rows = slot.shape[1]
    capacity, d = returned[0].shape
    slots = groups * capacity
    return pl.pallas_call(
        functools.partial(finish_kernel, groups),
        out_shape=jax.ShapeDtypeStruct((rows, d), BF16),
        in_specs=[VMEM] * (2 + groups),
        out_specs=VMEM,
        scratch_shapes=[pltpu.VMEM((slots, d), BF16)],
        compiler_params=pltpu.CompilerParams(vmem_limit_bytes=32 * MIB),
        cost_estimate=pl.CostEstimate(
            flops=2 * slots * rows * d, bytes_accessed=2 * d * (slots + rows), transcendentals=0
        ),
        name="finish",
    )(slot, gates, *returned)


def mixed_order(groups):
    def both_ends(partners):
        middle = (len(partners) + 1) // 2
        first, second = partners[:middle], partners[middle:]
        return [s for pair in zip(first, second + [None]) for s in pair if s is not None]

    half = groups // 2
    far, near = both_ends(list(range(half, groups))), both_ends(list(range(half - 1, 0, -1)))
    return [0] + [s for pair in zip(far, near + [None]) for s in pair if s is not None]


def swap(pieces):
    groups = len(pieces)
    order = mixed_order(groups)
    return [pieces[0]] + [
        lax.ppermute(piece, "expert", [(i, i ^ s) for i in range(groups)]) for s, piece in zip(order[1:], pieces[1:])
    ]


def partner_plan(
    grad_hidden, grad_out, grad_route, live_rows, w_down, w_moment, perm, fwd_hidden, fwd_route, fwd_gate
):
    groups = lax.axis_size("expert")
    me = lax.axis_index("expert").astype(jnp.int32).reshape(1)
    capacity = max(4, 2 * grad_hidden.shape[0] // groups)
    ff, d = w_down.shape[1:]
    spread = swap(split(me, w_moment, w_down, groups))
    packed, fwd_slot, gates = pack_rows(
        live_rows, me, perm, grad_route, fwd_route, grad_hidden, grad_out, fwd_hidden, fwd_gate,
        spread[mixed_order(groups).index(1)], groups, capacity,
    )
    received = swap(packed)
    placed = swap(reorder(me, perm, spread, received[groups // 3]))
    weight_new, moment_new, produced = update(me, received, placed, ff, d)
    return weight_new[None], moment_new[None], finish(fwd_slot, gates, swap(produced))


def lookup(route_ids, mapping):
    columns = jnp.arange(mapping.shape[0], dtype=jnp.int32)
    hits = route_ids[:, None] == columns[None, :]
    return jnp.sum(jnp.where(hits, mapping[None, :], 0), axis=1)


def slot_matrix(target, is_live, groups, capacity):
    columns = jnp.arange(groups, dtype=jnp.int32)
    onehot = ((target[:, None] == columns[None, :]) & is_live[:, None]).astype(jnp.int32)
    ranked = jnp.sum(jnp.cumsum(onehot, axis=0) * onehot, axis=1) - 1
    slot_of = jnp.where(is_live, target * capacity + ranked, -1)
    slots = jnp.arange(groups * capacity, dtype=jnp.int32)
    return (slots[:, None] == slot_of[None, :]).astype(jnp.bfloat16)


def orthogonalize(moment):
    moment_f = moment.astype(jnp.float32)
    frobenius = jnp.sqrt(jnp.sum(moment_f * moment_f))
    current = (moment_f / (frobenius + norm_floor)).astype(jnp.bfloat16)
    for sweep_index in range(2):
        gramian = lax.dot_general(
            current, current, (((1,), (1,)), ((), ())), preferred_element_type=jnp.float32
        ).astype(jnp.bfloat16)
        squared = jnp.dot(gramian, gramian, preferred_element_type=jnp.float32)
        poly = (cubic_term * gramian.astype(jnp.float32) + quintic_term * squared).astype(
            jnp.bfloat16
        )
        current = (
            linear_term * current.astype(jnp.float32)
            + jnp.dot(poly, current, preferred_element_type=jnp.float32)
        ).astype(jnp.bfloat16)
    return current


def relocate(weight, moment, perm):
    groups = lax.axis_size("expert")
    weight_flat = weight.reshape(groups, -1)
    moment_flat = moment.reshape(groups, -1)
    spread_w, spread_m = (
        lax.all_to_all(weight_flat, "expert", split_axis=0, concat_axis=0, tiled=True),
        lax.all_to_all(moment_flat, "expert", split_axis=0, concat_axis=0, tiled=True),
    )
    devices = jnp.arange(groups, dtype=jnp.int32)
    inverse = jnp.sum(jnp.where(perm[None, :] == devices[:, None], devices[None, :], 0), axis=1)
    ordered_w = jnp.take(spread_w, inverse, axis=0)
    ordered_m = jnp.take(spread_m, inverse, axis=0)
    back_w, back_m = (
        lax.all_to_all(ordered_w, "expert", split_axis=0, concat_axis=0, tiled=True),
        lax.all_to_all(ordered_m, "expert", split_axis=0, concat_axis=0, tiled=True),
    )
    return (back_w.reshape(weight.shape), back_m.reshape(moment.shape))


def routed_plan(
    grad_hidden,
    grad_out,
    grad_route,
    live_rows,
    w_down,
    w_moment,
    perm,
    fwd_hidden,
    fwd_route,
    fwd_gate,
):
    groups = lax.axis_size("expert")
    grad_count = grad_hidden.shape[0]
    capacity = max(4, 2 * grad_count // groups)
    is_live = jnp.arange(grad_count, dtype=jnp.int32) < live_rows[0]
    route_ids = grad_route[:, 0]
    weight, moment = relocate(w_down, w_moment, perm)
    target = lookup(route_ids, perm)
    selector = slot_matrix(target, is_live, groups, capacity)
    hidden_buf = (
        jnp.dot(selector, grad_hidden, preferred_element_type=jnp.float32)
        .astype(jnp.bfloat16)
        .reshape(groups, capacity, -1)
    )
    outgrad_buf = (
        jnp.dot(selector, grad_out, preferred_element_type=jnp.float32)
        .astype(jnp.bfloat16)
        .reshape(groups, capacity, -1)
    )
    recv_hidden, recv_outgrad = (
        lax.all_to_all(hidden_buf, "expert", split_axis=0, concat_axis=0, tiled=True),
        lax.all_to_all(outgrad_buf, "expert", split_axis=0, concat_axis=0, tiled=True),
    )
    grad = lax.dot_general(
        recv_hidden.reshape(groups * capacity, -1),
        recv_outgrad.reshape(groups * capacity, -1),
        (((0,), (0,)), ((), ())),
        preferred_element_type=jnp.float32,
    )
    moment_new = (moment_decay * moment[0].astype(jnp.float32) + grad).astype(jnp.bfloat16)
    ortho = orthogonalize(moment_new)
    weight_new = (weight[0].astype(jnp.float32) - step_scale * ortho.astype(jnp.float32)).astype(
        jnp.bfloat16
    )
    weight_new = weight_new[None]
    moment_new = moment_new[None]
    fwd_ids = fwd_route[:, 0]
    placed_weight, placed_moment = (weight_new, moment_new)
    fwd_target = lookup(fwd_ids, perm)
    fwd_weight = weight_new[0]
    fwd_count = fwd_hidden.shape[0]
    fwd_capacity = max(4, 2 * fwd_count // groups)
    fwd_selector = slot_matrix(fwd_target, jnp.ones((fwd_count,), dtype=bool), groups, fwd_capacity)
    fwd_buf = (
        jnp.dot(fwd_selector, fwd_hidden, preferred_element_type=jnp.float32)
        .astype(jnp.bfloat16)
        .reshape(groups, fwd_capacity, -1)
    )
    produced = jnp.einsum(
        "gkf,fd->gkd",
        lax.all_to_all(fwd_buf, "expert", split_axis=0, concat_axis=0, tiled=True),
        fwd_weight,
        preferred_element_type=jnp.float32,
    ).astype(jnp.bfloat16)
    returned = lax.all_to_all(produced, "expert", split_axis=0, concat_axis=0, tiled=True)
    fwd_rows_out = lax.dot_general(
        fwd_selector,
        returned.reshape(groups * fwd_capacity, -1),
        (((0,), (0,)), ((), ())),
        preferred_element_type=jnp.float32,
    )
    fwd_out = (fwd_rows_out * fwd_gate[:, None]).astype(jnp.bfloat16)
    return (placed_weight, placed_moment, fwd_out)


def solution(mesh):
    groups = mesh.shape["expert"]
    in_specs = (
        P(("layer", "expert"), None),
        P(("layer", "expert"), None),
        P(("layer", "expert"), None),
        P(("layer", "expert")),
        P(("layer", "expert"), None, None),
        P(("layer", "expert"), None, None),
        P("layer"),
        P(("layer", "expert"), None),
        P(("layer", "expert"), None),
        P(("layer", "expert")),
    )
    out_specs = (
        P(("layer", "expert"), None, None),
        P(("layer", "expert"), None, None),
        P(("layer", "expert"), None),
    )

    def per_device(*args):
        few = groups >= 8 and groups & (groups - 1) == 0 and groups <= 2 * args[0].shape[0] // groups
        return (partner_plan if few else routed_plan)(*args)

    return jax.shard_map(
        per_device, mesh=mesh, in_specs=in_specs, out_specs=out_specs, check_vma=False
    )
```

```python
import functools

import jax
import jax.numpy as jnp
from jax import lax
from jax.experimental import pallas as pl
from jax.experimental.pallas import tpu as pltpu
from jax.sharding import PartitionSpec as P

linear_term = 3.4445
cubic_term = -4.775
quintic_term = 2.0315
moment_decay = 0.9
step_scale = 0.25
norm_floor = 1e-07

F32 = jnp.float32
BF16 = jnp.bfloat16
HBM = pl.BlockSpec(memory_space=pltpu.HBM)
VMEM = pl.BlockSpec(memory_space=pltpu.VMEM)
SMEM = pl.BlockSpec(memory_space=pltpu.SMEM)
ANY = pl.BlockSpec(memory_space=pl.ANY)
MIB = 1 << 20


def fetched(refs, held, sem):
    copies = [pltpu.make_async_copy(ref, room, sem.at[n]) for n, (ref, room) in enumerate(zip(refs, held))]
    for copy in copies:
        copy.start()
    for copy in copies:
        copy.wait()


def rooms(arrays):
    return [pltpu.VMEM(a.shape, a.dtype) for a in arrays] + [pltpu.SemaphoreType.DMA((len(arrays),))]


def chunk_at(ref, lead, k, rows, columns):
    return ref.at[
        lead,
        pl.ds(pl.multiple_of((k // 2) * rows, rows), rows),
        pl.ds(pl.multiple_of((k % 2) * columns, columns), columns),
    ]


def slot_rows(route, live, groups, capacity, me_ref, perm_ref):
    rows = route.shape[1]
    experts = lax.broadcasted_iota(jnp.int32, (groups, rows), 0)
    onehot = jnp.where((experts == route) & live, 1.0, 0.0).astype(BF16)
    before = lax.broadcasted_iota(jnp.int32, (rows, rows), 0)
    after = lax.broadcasted_iota(jnp.int32, (rows, rows), 1)
    upto = jnp.where(before <= after, 1.0, 0.0).astype(BF16)
    ranks = jnp.dot(onehot, upto, preferred_element_type=F32)
    rank = jnp.sum(ranks * onehot.astype(F32), axis=0, keepdims=True).astype(jnp.int32) - 1
    partner = jnp.zeros_like(route)
    for e in range(groups):
        partner = jnp.where(route == e, perm_ref[e] ^ me_ref[0], partner)
    return jnp.where(live, partner * capacity + rank, -1)


def selector_of(slot, slots):
    rows = slot.shape[1]
    places = lax.broadcasted_iota(jnp.int32, (slots, rows), 0)
    return jnp.where(places == slot, 1.0, 0.0).astype(BF16)


def pack_kernel(groups, live_ref, me_ref, perm_ref, *refs):
    sources, pieces, (slot_ref, gates_ref) = refs[:6], refs[7 : 7 + groups], refs[7 + groups : 9 + groups]
    held, sem = refs[9 + groups : 15 + groups], refs[-1]
    route_ref, fwd_route_ref, hidden_ref, out_ref, fwd_ref, gate_ref = held
    copies = [pltpu.make_async_copy(ref, room, sem.at[n]) for n, (ref, room) in enumerate(zip(sources, held))]
    for copy in copies:
        copy.start()
    rows, ff = hidden_ref.shape
    d = out_ref.shape[1]
    capacity = pieces[0].shape[0]
    slots = groups * capacity
    place = lax.broadcasted_iota(jnp.int32, (1, rows), 1)

    def fill(first, selector, source_ref):
        chosen = jnp.dot(selector, source_ref[...], preferred_element_type=F32).astype(BF16)
        for s, piece in zip(mixed_order(groups), pieces):
            piece[:, first : first + source_ref.shape[1]] = chosen[s * capacity : (s + 1) * capacity]

    copies[0].wait()
    slot = slot_rows(route_ref[...], place < live_ref[0], groups, capacity, me_ref, perm_ref)
    selector = selector_of(slot, slots)
    copies[1].wait()
    fwd_slot = slot_rows(fwd_route_ref[...], place >= 0, groups, capacity, me_ref, perm_ref)
    slot_ref[...] = fwd_slot
    copies[2].wait()
    fill(0, selector, hidden_ref)
    copies[3].wait()
    fill(ff, selector, out_ref)
    copies[4].wait()
    fill(ff + d, selector_of(fwd_slot, slots), fwd_ref)
    copies[5].wait()
    down = lax.broadcasted_iota(jnp.int32, (rows, rows), 0)
    across = lax.broadcasted_iota(jnp.int32, (rows, rows), 1)
    gates_ref[...] = jnp.sum(jnp.where(down == across, gate_ref[...], 0.0), axis=1, keepdims=True)


def pack_rows(live_rows, me, perm, route, fwd_route, hidden, grad_out, fwd_hidden, gate, earlier, groups, capacity):
    rows, ff = hidden.shape
    width = 2 * ff + grad_out.shape[1]
    sources = (route.reshape(1, rows), fwd_route.reshape(1, rows), hidden, grad_out, fwd_hidden, gate.reshape(1, rows))
    *pieces, slot, gates = pl.pallas_call(
        functools.partial(pack_kernel, groups),
        out_shape=(jax.ShapeDtypeStruct((capacity, width), BF16),) * groups
        + (jax.ShapeDtypeStruct((1, rows), jnp.int32), jax.ShapeDtypeStruct((rows, 1), F32)),
        in_specs=[SMEM] * 3 + [HBM] * 6 + [VMEM],
        out_specs=(VMEM,) * (groups + 2),
        scratch_shapes=[pltpu.VMEM(a.shape, a.dtype) for a in sources] + [pltpu.SemaphoreType.DMA((len(sources),))],
        compiler_params=pltpu.CompilerParams(vmem_limit_bytes=32 * MIB),
        cost_estimate=pl.CostEstimate(
            flops=2 * groups * capacity * rows * width, bytes_accessed=6 * rows * width, transcendentals=0
        ),
        name="pack_rows",
    )(live_rows, me, perm, *sources, earlier)
    return pieces, slot, gates


def split_kernel(me_ref, moment_ref, weight_ref, *refs):
    pieces, held, sem = refs[:-3], refs[-3:-1], refs[-1]
    fetched((moment_ref, weight_ref), held, sem)
    for s, piece in zip(mixed_order(len(pieces)), pieces):
        rows, columns = piece.shape[1:]
        for lead, source in enumerate(held):
            piece[lead] = chunk_at(source, 0, me_ref[0] ^ s, rows, columns)[...]


def split(me, moment, weight, groups):
    _, ff, d = weight.shape
    piece = jax.ShapeDtypeStruct((2, ff // (groups // 2), d // 2), BF16)
    return pl.pallas_call(
        split_kernel,
        out_shape=(piece,) * groups,
        in_specs=[SMEM, HBM, HBM],
        out_specs=(VMEM,) * groups,
        scratch_shapes=rooms((moment, weight)),
        compiler_params=pltpu.CompilerParams(vmem_limit_bytes=60 * MIB),
        cost_estimate=pl.CostEstimate(flops=0, bytes_accessed=8 * ff * d, transcendentals=0),
        name="split",
    )(me, moment, weight)


def reorder_kernel(me_ref, perm_ref, *refs):
    groups = len(refs) // 2 - 1
    sources, targets, held = refs[:groups], refs[groups + 1 : 2 * groups + 1], refs[-1]
    me, order = me_ref[0], mixed_order(groups)
    for s, source in zip(order, sources):
        held[me ^ perm_ref[me ^ s]] = source[...]
    for s, target in zip(order, targets):
        target[...] = held[s]


def reorder(me, perm, pieces, earlier):
    groups = len(pieces)
    piece = jax.ShapeDtypeStruct(pieces[0].shape, BF16)
    return pl.pallas_call(
        reorder_kernel,
        out_shape=(piece,) * groups,
        in_specs=[SMEM, SMEM] + [VMEM] * (groups + 1),
        out_specs=(VMEM,) * groups,
        scratch_shapes=[pltpu.VMEM((groups,) + pieces[0].shape, BF16)],
        compiler_params=pltpu.CompilerParams(vmem_limit_bytes=32 * MIB),
        cost_estimate=pl.CostEstimate(flops=0, bytes_accessed=4 * groups * pieces[0].size, transcendentals=0),
        name="reorder",
    )(me, perm, *pieces, earlier)


def update_kernel(groups, me_ref, *refs):
    packed, pieces, produced = refs[:groups], refs[groups : 2 * groups], refs[2 * groups + 2 : 3 * groups + 2]
    weight_new_ref, moment_new_ref = refs[2 * groups : 2 * groups + 2]
    held, rows_ref = refs[-2:]
    _, ff, d = held.shape
    capacity = packed[0].shape[0]
    for n, piece in enumerate(packed):
        rows_ref[n * capacity : (n + 1) * capacity] = piece[...]
    for s, piece in zip(mixed_order(groups), pieces):
        rows, columns = piece.shape[1:]
        for lead in range(2):
            chunk_at(held, lead, me_ref[0] ^ s, rows, columns)[...] = piece[lead]
    grad = lax.dot_general(
        rows_ref[:, :ff], rows_ref[:, ff : ff + d], (((0,), (0,)), ((), ())), preferred_element_type=F32
    )
    moment_new = (moment_decay * held[0].astype(F32) + grad).astype(BF16)
    moment_new_ref[...] = moment_new
    moment_f = moment_new.astype(F32)
    frobenius = jnp.sqrt(jnp.sum(moment_f * moment_f))
    current = (moment_f / (frobenius + norm_floor)).astype(BF16)
    for _ in range(2):
        gramian = lax.dot_general(
            current, current, (((1,), (1,)), ((), ())), preferred_element_type=F32
        ).astype(BF16)
        squared = jnp.dot(gramian, gramian, preferred_element_type=F32)
        poly = (cubic_term * gramian.astype(F32) + quintic_term * squared).astype(BF16)
        current = (
            linear_term * current.astype(F32) + jnp.dot(poly, current, preferred_element_type=F32)
        ).astype(BF16)
    weight_new = (held[1].astype(F32) - step_scale * current.astype(F32)).astype(BF16)
    weight_new_ref[...] = weight_new
    product = jnp.dot(rows_ref[:, ff + d :], weight_new, preferred_element_type=F32).astype(BF16)
    for n, piece in enumerate(produced):
        piece[...] = product[n * capacity : (n + 1) * capacity]


def update(me, packed, pieces, ff, d):
    groups = len(pieces)
    capacity, width = packed[0].shape
    slots = groups * capacity
    shape = jax.ShapeDtypeStruct((ff, d), BF16)
    weight_new, moment_new, *produced = pl.pallas_call(
        functools.partial(update_kernel, groups),
        out_shape=(shape, shape) + (jax.ShapeDtypeStruct((capacity, d), BF16),) * groups,
        in_specs=[SMEM] + [VMEM] * (2 * groups),
        out_specs=(VMEM,) * (groups + 2),
        scratch_shapes=[pltpu.VMEM((2, ff, d), BF16), pltpu.VMEM((slots, width), BF16)],
        compiler_params=pltpu.CompilerParams(vmem_limit_bytes=40 * MIB),
        cost_estimate=pl.CostEstimate(
            flops=4 * ff * d * slots + 8 * ff * ff * d + 4 * ff**3,
            bytes_accessed=8 * ff * d + 2 * slots * (width + d),
            transcendentals=1,
        ),
        name="update",
    )(me, *packed, *pieces)
    return weight_new, moment_new, produced


def finish_kernel(groups, slot_ref, gates_ref, *refs):
    pieces, (out_ref, returned_ref) = refs[:groups], refs[groups:]
    capacity = pieces[0].shape[0]
    for s, piece in zip(mixed_order(groups), pieces):
        returned_ref[s * capacity : (s + 1) * capacity] = piece[...]
    selector = selector_of(slot_ref[...], groups * capacity)
    expert_out = lax.dot_general(
        selector, returned_ref[...], (((0,), (0,)), ((), ())), preferred_element_type=F32
    )
    out_ref[...] = (gates_ref[...] * expert_out).astype(BF16)


def finish(slot, gates, returned):
    groups = len(returned)
    rows = slot.shape[1]
    capacity, d = returned[0].shape
    slots = groups * capacity
    return pl.pallas_call(
        functools.partial(finish_kernel, groups),
        out_shape=jax.ShapeDtypeStruct((rows, d), BF16),
        in_specs=[VMEM] * (2 + groups),
        out_specs=VMEM,
        scratch_shapes=[pltpu.VMEM((slots, d), BF16)],
        compiler_params=pltpu.CompilerParams(vmem_limit_bytes=32 * MIB),
        cost_estimate=pl.CostEstimate(
            flops=2 * slots * rows * d, bytes_accessed=2 * d * (slots + rows), transcendentals=0
        ),
        name="finish",
    )(slot, gates, *returned)


def mixed_order(groups):
    def both_ends(partners):
        middle = (len(partners) + 1) // 2
        first, second = partners[:middle], partners[middle:]
        return [s for pair in zip(first, second + [None]) for s in pair if s is not None]

    half = groups // 2
    far, near = both_ends(list(range(half, groups))), both_ends(list(range(half - 1, 0, -1)))
    return [0] + [s for pair in zip(far, near + [None]) for s in pair if s is not None]


def swap(pieces):
    groups = len(pieces)
    order = mixed_order(groups)
    return [pieces[0]] + [
        lax.ppermute(piece, "expert", [(i, i ^ s) for i in range(groups)]) for s, piece in zip(order[1:], pieces[1:])
    ]


def partner_plan(
    grad_hidden, grad_out, grad_route, live_rows, w_down, w_moment, perm, fwd_hidden, fwd_route, fwd_gate
):
    groups = lax.axis_size("expert")
    me = lax.axis_index("expert").astype(jnp.int32).reshape(1)
    capacity = max(4, 2 * grad_hidden.shape[0] // groups)
    ff, d = w_down.shape[1:]
    spread = swap(split(me, w_moment, w_down, groups))
    packed, fwd_slot, gates = pack_rows(
        live_rows, me, perm, grad_route, fwd_route, grad_hidden, grad_out, fwd_hidden, fwd_gate,
        spread[mixed_order(groups).index(groups // 4)], groups, capacity,
    )
    received = swap(packed)
    placed = swap(reorder(me, perm, spread, received[groups // 3]))
    weight_new, moment_new, produced = update(me, received, placed, ff, d)
    return weight_new[None], moment_new[None], finish(fwd_slot, gates, swap(produced))


def lookup(route_ids, mapping):
    columns = jnp.arange(mapping.shape[0], dtype=jnp.int32)
    hits = route_ids[:, None] == columns[None, :]
    return jnp.sum(jnp.where(hits, mapping[None, :], 0), axis=1)


def slot_matrix(target, is_live, groups, capacity):
    columns = jnp.arange(groups, dtype=jnp.int32)
    onehot = ((target[:, None] == columns[None, :]) & is_live[:, None]).astype(jnp.int32)
    ranked = jnp.sum(jnp.cumsum(onehot, axis=0) * onehot, axis=1) - 1
    slot_of = jnp.where(is_live, target * capacity + ranked, -1)
    slots = jnp.arange(groups * capacity, dtype=jnp.int32)
    return (slots[:, None] == slot_of[None, :]).astype(jnp.bfloat16)


def orthogonalize(moment):
    moment_f = moment.astype(jnp.float32)
    frobenius = jnp.sqrt(jnp.sum(moment_f * moment_f))
    current = (moment_f / (frobenius + norm_floor)).astype(jnp.bfloat16)
    for sweep_index in range(2):
        gramian = lax.dot_general(
            current, current, (((1,), (1,)), ((), ())), preferred_element_type=jnp.float32
        ).astype(jnp.bfloat16)
        squared = jnp.dot(gramian, gramian, preferred_element_type=jnp.float32)
        poly = (cubic_term * gramian.astype(jnp.float32) + quintic_term * squared).astype(
            jnp.bfloat16
        )
        current = (
            linear_term * current.astype(jnp.float32)
            + jnp.dot(poly, current, preferred_element_type=jnp.float32)
        ).astype(jnp.bfloat16)
    return current


def relocate(weight, moment, perm):
    groups = lax.axis_size("expert")
    weight_flat = weight.reshape(groups, -1)
    moment_flat = moment.reshape(groups, -1)
    spread_w, spread_m = (
        lax.all_to_all(weight_flat, "expert", split_axis=0, concat_axis=0, tiled=True),
        lax.all_to_all(moment_flat, "expert", split_axis=0, concat_axis=0, tiled=True),
    )
    devices = jnp.arange(groups, dtype=jnp.int32)
    inverse = jnp.sum(jnp.where(perm[None, :] == devices[:, None], devices[None, :], 0), axis=1)
    ordered_w = jnp.take(spread_w, inverse, axis=0)
    ordered_m = jnp.take(spread_m, inverse, axis=0)
    back_w, back_m = (
        lax.all_to_all(ordered_w, "expert", split_axis=0, concat_axis=0, tiled=True),
        lax.all_to_all(ordered_m, "expert", split_axis=0, concat_axis=0, tiled=True),
    )
    return (back_w.reshape(weight.shape), back_m.reshape(moment.shape))


def routed_plan(
    grad_hidden,
    grad_out,
    grad_route,
    live_rows,
    w_down,
    w_moment,
    perm,
    fwd_hidden,
    fwd_route,
    fwd_gate,
):
    groups = lax.axis_size("expert")
    grad_count = grad_hidden.shape[0]
    capacity = max(4, 2 * grad_count // groups)
    is_live = jnp.arange(grad_count, dtype=jnp.int32) < live_rows[0]
    route_ids = grad_route[:, 0]
    weight, moment = relocate(w_down, w_moment, perm)
    target = lookup(route_ids, perm)
    selector = slot_matrix(target, is_live, groups, capacity)
    hidden_buf = (
        jnp.dot(selector, grad_hidden, preferred_element_type=jnp.float32)
        .astype(jnp.bfloat16)
        .reshape(groups, capacity, -1)
    )
    outgrad_buf = (
        jnp.dot(selector, grad_out, preferred_element_type=jnp.float32)
        .astype(jnp.bfloat16)
        .reshape(groups, capacity, -1)
    )
    recv_hidden, recv_outgrad = (
        lax.all_to_all(hidden_buf, "expert", split_axis=0, concat_axis=0, tiled=True),
        lax.all_to_all(outgrad_buf, "expert", split_axis=0, concat_axis=0, tiled=True),
    )
    grad = lax.dot_general(
        recv_hidden.reshape(groups * capacity, -1),
        recv_outgrad.reshape(groups * capacity, -1),
        (((0,), (0,)), ((), ())),
        preferred_element_type=jnp.float32,
    )
    moment_new = (moment_decay * moment[0].astype(jnp.float32) + grad).astype(jnp.bfloat16)
    ortho = orthogonalize(moment_new)
    weight_new = (weight[0].astype(jnp.float32) - step_scale * ortho.astype(jnp.float32)).astype(
        jnp.bfloat16
    )
    weight_new = weight_new[None]
    moment_new = moment_new[None]
    fwd_ids = fwd_route[:, 0]
    placed_weight, placed_moment = (weight_new, moment_new)
    fwd_target = lookup(fwd_ids, perm)
    fwd_weight = weight_new[0]
    fwd_count = fwd_hidden.shape[0]
    fwd_capacity = max(4, 2 * fwd_count // groups)
    fwd_selector = slot_matrix(fwd_target, jnp.ones((fwd_count,), dtype=bool), groups, fwd_capacity)
    fwd_buf = (
        jnp.dot(fwd_selector, fwd_hidden, preferred_element_type=jnp.float32)
        .astype(jnp.bfloat16)
        .reshape(groups, fwd_capacity, -1)
    )
    produced = jnp.einsum(
        "gkf,fd->gkd",
        lax.all_to_all(fwd_buf, "expert", split_axis=0, concat_axis=0, tiled=True),
        fwd_weight,
        preferred_element_type=jnp.float32,
    ).astype(jnp.bfloat16)
    returned = lax.all_to_all(produced, "expert", split_axis=0, concat_axis=0, tiled=True)
    fwd_rows_out = lax.dot_general(
        fwd_selector,
        returned.reshape(groups * fwd_capacity, -1),
        (((0,), (0,)), ((), ())),
        preferred_element_type=jnp.float32,
    )
    fwd_out = (fwd_rows_out * fwd_gate[:, None]).astype(jnp.bfloat16)
    return (placed_weight, placed_moment, fwd_out)


def solution(mesh):
    groups = mesh.shape["expert"]
    in_specs = (
        P(("layer", "expert"), None),
        P(("layer", "expert"), None),
        P(("layer", "expert"), None),
        P(("layer", "expert")),
        P(("layer", "expert"), None, None),
        P(("layer", "expert"), None, None),
        P("layer"),
        P(("layer", "expert"), None),
        P(("layer", "expert"), None),
        P(("layer", "expert")),
    )
    out_specs = (
        P(("layer", "expert"), None, None),
        P(("layer", "expert"), None, None),
        P(("layer", "expert"), None),
    )

    def per_device(*args):
        few = groups >= 8 and groups & (groups - 1) == 0 and groups <= 2 * args[0].shape[0] // groups
        return (partner_plan if few else routed_plan)(*args)

    return jax.shard_map(
        per_device, mesh=mesh, in_specs=in_specs, out_specs=out_specs, check_vma=False
    )
```

```python
import functools

import jax
import jax.numpy as jnp
from jax import lax
from jax.experimental import pallas as pl
from jax.experimental.pallas import tpu as pltpu
from jax.sharding import PartitionSpec as P

linear_term = 3.4445
cubic_term = -4.775
quintic_term = 2.0315
moment_decay = 0.9
step_scale = 0.25
norm_floor = 1e-07

F32 = jnp.float32
BF16 = jnp.bfloat16
HBM = pl.BlockSpec(memory_space=pltpu.HBM)
VMEM = pl.BlockSpec(memory_space=pltpu.VMEM)
SMEM = pl.BlockSpec(memory_space=pltpu.SMEM)
ANY = pl.BlockSpec(memory_space=pl.ANY)
MIB = 1 << 20


def fetched(refs, held, sem):
    copies = [pltpu.make_async_copy(ref, room, sem.at[n]) for n, (ref, room) in enumerate(zip(refs, held))]
    for copy in copies:
        copy.start()
    for copy in copies:
        copy.wait()


def rooms(arrays):
    return [pltpu.VMEM(a.shape, a.dtype) for a in arrays] + [pltpu.SemaphoreType.DMA((len(arrays),))]


def chunk_at(ref, lead, k, rows, columns):
    return ref.at[
        lead,
        pl.ds(pl.multiple_of((k // 2) * rows, rows), rows),
        pl.ds(pl.multiple_of((k % 2) * columns, columns), columns),
    ]


def slot_rows(route, live, groups, capacity, me_ref, perm_ref):
    rows = route.shape[1]
    experts = lax.broadcasted_iota(jnp.int32, (groups, rows), 0)
    onehot = jnp.where((experts == route) & live, 1.0, 0.0).astype(BF16)
    before = lax.broadcasted_iota(jnp.int32, (rows, rows), 0)
    after = lax.broadcasted_iota(jnp.int32, (rows, rows), 1)
    upto = jnp.where(before <= after, 1.0, 0.0).astype(BF16)
    ranks = jnp.dot(onehot, upto, preferred_element_type=F32)
    rank = jnp.sum(ranks * onehot.astype(F32), axis=0, keepdims=True).astype(jnp.int32) - 1
    partner = jnp.zeros_like(route)
    for e in range(groups):
        partner = jnp.where(route == e, perm_ref[e] ^ me_ref[0], partner)
    return jnp.where(live, partner * capacity + rank, -1)


def selector_of(slot, slots):
    rows = slot.shape[1]
    places = lax.broadcasted_iota(jnp.int32, (slots, rows), 0)
    return jnp.where(places == slot, 1.0, 0.0).astype(BF16)


def pack_kernel(groups, live_ref, me_ref, perm_ref, *refs):
    sources, pieces, (slot_ref, gates_ref) = refs[:6], refs[7 : 7 + groups], refs[7 + groups : 9 + groups]
    held, sem = refs[9 + groups : 15 + groups], refs[-1]
    route_ref, fwd_route_ref, hidden_ref, out_ref, fwd_ref, gate_ref = held
    copies = [pltpu.make_async_copy(ref, room, sem.at[n]) for n, (ref, room) in enumerate(zip(sources, held))]
    for copy in copies:
        copy.start()
    rows, ff = hidden_ref.shape
    d = out_ref.shape[1]
    capacity = pieces[0].shape[0]
    slots = groups * capacity
    place = lax.broadcasted_iota(jnp.int32, (1, rows), 1)

    def fill(first, selector, source_ref):
        chosen = jnp.dot(selector, source_ref[...], preferred_element_type=F32).astype(BF16)
        for s, piece in zip(mixed_order(groups), pieces):
            piece[:, first : first + source_ref.shape[1]] = chosen[s * capacity : (s + 1) * capacity]

    copies[0].wait()
    slot = slot_rows(route_ref[...], place < live_ref[0], groups, capacity, me_ref, perm_ref)
    selector = selector_of(slot, slots)
    copies[1].wait()
    fwd_slot = slot_rows(fwd_route_ref[...], place >= 0, groups, capacity, me_ref, perm_ref)
    slot_ref[...] = fwd_slot
    copies[2].wait()
    fill(0, selector, hidden_ref)
    copies[3].wait()
    fill(ff, selector, out_ref)
    copies[4].wait()
    fill(ff + d, selector_of(fwd_slot, slots), fwd_ref)
    copies[5].wait()
    down = lax.broadcasted_iota(jnp.int32, (rows, rows), 0)
    across = lax.broadcasted_iota(jnp.int32, (rows, rows), 1)
    gates_ref[...] = jnp.sum(jnp.where(down == across, gate_ref[...], 0.0), axis=1, keepdims=True)


def pack_rows(live_rows, me, perm, route, fwd_route, hidden, grad_out, fwd_hidden, gate, earlier, groups, capacity):
    rows, ff = hidden.shape
    width = 2 * ff + grad_out.shape[1]
    sources = (route.reshape(1, rows), fwd_route.reshape(1, rows), hidden, grad_out, fwd_hidden, gate.reshape(1, rows))
    *pieces, slot, gates = pl.pallas_call(
        functools.partial(pack_kernel, groups),
        out_shape=(jax.ShapeDtypeStruct((capacity, width), BF16),) * groups
        + (jax.ShapeDtypeStruct((1, rows), jnp.int32), jax.ShapeDtypeStruct((rows, 1), F32)),
        in_specs=[SMEM] * 3 + [HBM] * 6 + [VMEM],
        out_specs=(VMEM,) * (groups + 2),
        scratch_shapes=[pltpu.VMEM(a.shape, a.dtype) for a in sources] + [pltpu.SemaphoreType.DMA((len(sources),))],
        compiler_params=pltpu.CompilerParams(vmem_limit_bytes=32 * MIB),
        cost_estimate=pl.CostEstimate(
            flops=2 * groups * capacity * rows * width, bytes_accessed=6 * rows * width, transcendentals=0
        ),
        name="pack_rows",
    )(live_rows, me, perm, *sources, earlier)
    return pieces, slot, gates


def split_kernel(me_ref, moment_ref, weight_ref, *refs):
    pieces, held, sem = refs[:-3], refs[-3:-1], refs[-1]
    fetched((moment_ref, weight_ref), held, sem)
    for s, piece in zip(mixed_order(len(pieces)), pieces):
        rows, columns = piece.shape[1:]
        for lead, source in enumerate(held):
            piece[lead] = chunk_at(source, 0, me_ref[0] ^ s, rows, columns)[...]


def split(me, moment, weight, groups):
    _, ff, d = weight.shape
    piece = jax.ShapeDtypeStruct((2, ff // (groups // 2), d // 2), BF16)
    return pl.pallas_call(
        split_kernel,
        out_shape=(piece,) * groups,
        in_specs=[SMEM, HBM, HBM],
        out_specs=(VMEM,) * groups,
        scratch_shapes=rooms((moment, weight)),
        compiler_params=pltpu.CompilerParams(vmem_limit_bytes=60 * MIB),
        cost_estimate=pl.CostEstimate(flops=0, bytes_accessed=8 * ff * d, transcendentals=0),
        name="split",
    )(me, moment, weight)


def reorder_kernel(me_ref, perm_ref, *refs):
    groups = len(refs) // 2 - 1
    sources, targets, held = refs[:groups], refs[groups + 1 : 2 * groups + 1], refs[-1]
    me, order = me_ref[0], mixed_order(groups)
    for s, source in zip(order, sources):
        held[me ^ perm_ref[me ^ s]] = source[...]
    for s, target in zip(order, targets):
        target[...] = held[s]


def reorder(me, perm, pieces, earlier):
    groups = len(pieces)
    piece = jax.ShapeDtypeStruct(pieces[0].shape, BF16)
    return pl.pallas_call(
        reorder_kernel,
        out_shape=(piece,) * groups,
        in_specs=[SMEM, SMEM] + [VMEM] * (groups + 1),
        out_specs=(VMEM,) * groups,
        scratch_shapes=[pltpu.VMEM((groups,) + pieces[0].shape, BF16)],
        compiler_params=pltpu.CompilerParams(vmem_limit_bytes=32 * MIB),
        cost_estimate=pl.CostEstimate(flops=0, bytes_accessed=4 * groups * pieces[0].size, transcendentals=0),
        name="reorder",
    )(me, perm, *pieces, earlier)


def update_kernel(groups, me_ref, *refs):
    packed, pieces, produced = refs[:groups], refs[groups : 2 * groups], refs[2 * groups + 2 : 3 * groups + 2]
    weight_new_ref, moment_new_ref = refs[2 * groups : 2 * groups + 2]
    held, weight_held, rows_ref, fwd_ref = refs[-4:]
    _, ff, d = held.shape
    capacity = packed[0].shape[0]
    for n, piece in enumerate(packed):
        rows_ref[n * capacity : (n + 1) * capacity] = piece[:, : ff + d]

    def assemble(lead, target):
        for s, piece in zip(mixed_order(groups), pieces):
            rows, columns = piece.shape[1:]
            chunk_at(target, 0, me_ref[0] ^ s, rows, columns)[...] = piece[lead]

    assemble(0, held)
    grad = lax.dot_general(
        rows_ref[:, :ff], rows_ref[:, ff : ff + d], (((0,), (0,)), ((), ())), preferred_element_type=F32
    )
    moment_new = (moment_decay * held[0].astype(F32) + grad).astype(BF16)
    moment_new_ref[...] = moment_new
    moment_f = moment_new.astype(F32)
    frobenius = jnp.sqrt(jnp.sum(moment_f * moment_f))
    current = (moment_f / (frobenius + norm_floor)).astype(BF16)
    for sweep in range(2):
        gramian = lax.dot_general(
            current, current, (((1,), (1,)), ((), ())), preferred_element_type=F32
        ).astype(BF16)
        if sweep == 0:
            assemble(1, weight_held)
            for n, piece in enumerate(packed):
                fwd_ref[n * capacity : (n + 1) * capacity] = piece[:, ff + d :]
        squared = jnp.dot(gramian, gramian, preferred_element_type=F32)
        poly = (cubic_term * gramian.astype(F32) + quintic_term * squared).astype(BF16)
        current = (
            linear_term * current.astype(F32) + jnp.dot(poly, current, preferred_element_type=F32)
        ).astype(BF16)
    weight_new = (weight_held[0].astype(F32) - step_scale * current.astype(F32)).astype(BF16)
    weight_new_ref[...] = weight_new
    product = jnp.dot(fwd_ref[...], weight_new, preferred_element_type=F32).astype(BF16)
    for n, piece in enumerate(produced):
        piece[...] = product[n * capacity : (n + 1) * capacity]


def update(me, packed, pieces, ff, d):
    groups = len(pieces)
    capacity, width = packed[0].shape
    slots = groups * capacity
    shape = jax.ShapeDtypeStruct((ff, d), BF16)
    weight_new, moment_new, *produced = pl.pallas_call(
        functools.partial(update_kernel, groups),
        out_shape=(shape, shape) + (jax.ShapeDtypeStruct((capacity, d), BF16),) * groups,
        in_specs=[SMEM] + [VMEM] * (2 * groups),
        out_specs=(VMEM,) * (groups + 2),
        scratch_shapes=[
            pltpu.VMEM((1, ff, d), BF16),
            pltpu.VMEM((1, ff, d), BF16),
            pltpu.VMEM((slots, width - ff), BF16),
            pltpu.VMEM((slots, ff), BF16),
        ],
        compiler_params=pltpu.CompilerParams(vmem_limit_bytes=40 * MIB),
        cost_estimate=pl.CostEstimate(
            flops=4 * ff * d * slots + 8 * ff * ff * d + 4 * ff**3,
            bytes_accessed=8 * ff * d + 2 * slots * (width + d),
            transcendentals=1,
        ),
        name="update",
    )(me, *packed, *pieces)
    return weight_new, moment_new, produced


def finish_kernel(groups, slot_ref, gates_ref, *refs):
    pieces, (out_ref, returned_ref) = refs[:groups], refs[groups:]
    capacity = pieces[0].shape[0]
    for s, piece in zip(mixed_order(groups), pieces):
        returned_ref[s * capacity : (s + 1) * capacity] = piece[...]
    selector = selector_of(slot_ref[...], groups * capacity)
    expert_out = lax.dot_general(
        selector, returned_ref[...], (((0,), (0,)), ((), ())), preferred_element_type=F32
    )
    out_ref[...] = (gates_ref[...] * expert_out).astype(BF16)


def finish(slot, gates, returned):
    groups = len(returned)
    rows = slot.shape[1]
    capacity, d = returned[0].shape
    slots = groups * capacity
    return pl.pallas_call(
        functools.partial(finish_kernel, groups),
        out_shape=jax.ShapeDtypeStruct((rows, d), BF16),
        in_specs=[VMEM] * (2 + groups),
        out_specs=VMEM,
        scratch_shapes=[pltpu.VMEM((slots, d), BF16)],
        compiler_params=pltpu.CompilerParams(vmem_limit_bytes=32 * MIB),
        cost_estimate=pl.CostEstimate(
            flops=2 * slots * rows * d, bytes_accessed=2 * d * (slots + rows), transcendentals=0
        ),
        name="finish",
    )(slot, gates, *returned)


def mixed_order(groups):
    def both_ends(partners):
        middle = (len(partners) + 1) // 2
        first, second = partners[:middle], partners[middle:]
        return [s for pair in zip(first, second + [None]) for s in pair if s is not None]

    half = groups // 2
    far, near = both_ends(list(range(half, groups))), both_ends(list(range(half - 1, 0, -1)))
    return [0] + [s for pair in zip(far, near + [None]) for s in pair if s is not None]


def swap(pieces):
    groups = len(pieces)
    order = mixed_order(groups)
    return [pieces[0]] + [
        lax.ppermute(piece, "expert", [(i, i ^ s) for i in range(groups)]) for s, piece in zip(order[1:], pieces[1:])
    ]


def partner_plan(
    grad_hidden, grad_out, grad_route, live_rows, w_down, w_moment, perm, fwd_hidden, fwd_route, fwd_gate
):
    groups = lax.axis_size("expert")
    me = lax.axis_index("expert").astype(jnp.int32).reshape(1)
    capacity = max(4, 2 * grad_hidden.shape[0] // groups)
    ff, d = w_down.shape[1:]
    spread = swap(split(me, w_moment, w_down, groups))
    packed, fwd_slot, gates = pack_rows(
        live_rows, me, perm, grad_route, fwd_route, grad_hidden, grad_out, fwd_hidden, fwd_gate,
        spread[2 * groups // 3], groups, capacity,
    )
    received = swap(packed)
    placed = swap(reorder(me, perm, spread, received[groups // 3]))
    weight_new, moment_new, produced = update(me, received, placed, ff, d)
    return weight_new[None], moment_new[None], finish(fwd_slot, gates, swap(produced))


def lookup(route_ids, mapping):
    columns = jnp.arange(mapping.shape[0], dtype=jnp.int32)
    hits = route_ids[:, None] == columns[None, :]
    return jnp.sum(jnp.where(hits, mapping[None, :], 0), axis=1)


def slot_matrix(target, is_live, groups, capacity):
    columns = jnp.arange(groups, dtype=jnp.int32)
    onehot = ((target[:, None] == columns[None, :]) & is_live[:, None]).astype(jnp.int32)
    ranked = jnp.sum(jnp.cumsum(onehot, axis=0) * onehot, axis=1) - 1
    slot_of = jnp.where(is_live, target * capacity + ranked, -1)
    slots = jnp.arange(groups * capacity, dtype=jnp.int32)
    return (slots[:, None] == slot_of[None, :]).astype(jnp.bfloat16)


def orthogonalize(moment):
    moment_f = moment.astype(jnp.float32)
    frobenius = jnp.sqrt(jnp.sum(moment_f * moment_f))
    current = (moment_f / (frobenius + norm_floor)).astype(jnp.bfloat16)
    for sweep_index in range(2):
        gramian = lax.dot_general(
            current, current, (((1,), (1,)), ((), ())), preferred_element_type=jnp.float32
        ).astype(jnp.bfloat16)
        squared = jnp.dot(gramian, gramian, preferred_element_type=jnp.float32)
        poly = (cubic_term * gramian.astype(jnp.float32) + quintic_term * squared).astype(
            jnp.bfloat16
        )
        current = (
            linear_term * current.astype(jnp.float32)
            + jnp.dot(poly, current, preferred_element_type=jnp.float32)
        ).astype(jnp.bfloat16)
    return current


def relocate(weight, moment, perm):
    groups = lax.axis_size("expert")
    weight_flat = weight.reshape(groups, -1)
    moment_flat = moment.reshape(groups, -1)
    spread_w, spread_m = (
        lax.all_to_all(weight_flat, "expert", split_axis=0, concat_axis=0, tiled=True),
        lax.all_to_all(moment_flat, "expert", split_axis=0, concat_axis=0, tiled=True),
    )
    devices = jnp.arange(groups, dtype=jnp.int32)
    inverse = jnp.sum(jnp.where(perm[None, :] == devices[:, None], devices[None, :], 0), axis=1)
    ordered_w = jnp.take(spread_w, inverse, axis=0)
    ordered_m = jnp.take(spread_m, inverse, axis=0)
    back_w, back_m = (
        lax.all_to_all(ordered_w, "expert", split_axis=0, concat_axis=0, tiled=True),
        lax.all_to_all(ordered_m, "expert", split_axis=0, concat_axis=0, tiled=True),
    )
    return (back_w.reshape(weight.shape), back_m.reshape(moment.shape))


def routed_plan(
    grad_hidden,
    grad_out,
    grad_route,
    live_rows,
    w_down,
    w_moment,
    perm,
    fwd_hidden,
    fwd_route,
    fwd_gate,
):
    groups = lax.axis_size("expert")
    grad_count = grad_hidden.shape[0]
    capacity = max(4, 2 * grad_count // groups)
    is_live = jnp.arange(grad_count, dtype=jnp.int32) < live_rows[0]
    route_ids = grad_route[:, 0]
    weight, moment = relocate(w_down, w_moment, perm)
    target = lookup(route_ids, perm)
    selector = slot_matrix(target, is_live, groups, capacity)
    hidden_buf = (
        jnp.dot(selector, grad_hidden, preferred_element_type=jnp.float32)
        .astype(jnp.bfloat16)
        .reshape(groups, capacity, -1)
    )
    outgrad_buf = (
        jnp.dot(selector, grad_out, preferred_element_type=jnp.float32)
        .astype(jnp.bfloat16)
        .reshape(groups, capacity, -1)
    )
    recv_hidden, recv_outgrad = (
        lax.all_to_all(hidden_buf, "expert", split_axis=0, concat_axis=0, tiled=True),
        lax.all_to_all(outgrad_buf, "expert", split_axis=0, concat_axis=0, tiled=True),
    )
    grad = lax.dot_general(
        recv_hidden.reshape(groups * capacity, -1),
        recv_outgrad.reshape(groups * capacity, -1),
        (((0,), (0,)), ((), ())),
        preferred_element_type=jnp.float32,
    )
    moment_new = (moment_decay * moment[0].astype(jnp.float32) + grad).astype(jnp.bfloat16)
    ortho = orthogonalize(moment_new)
    weight_new = (weight[0].astype(jnp.float32) - step_scale * ortho.astype(jnp.float32)).astype(
        jnp.bfloat16
    )
    weight_new = weight_new[None]
    moment_new = moment_new[None]
    fwd_ids = fwd_route[:, 0]
    placed_weight, placed_moment = (weight_new, moment_new)
    fwd_target = lookup(fwd_ids, perm)
    fwd_weight = weight_new[0]
    fwd_count = fwd_hidden.shape[0]
    fwd_capacity = max(4, 2 * fwd_count // groups)
    fwd_selector = slot_matrix(fwd_target, jnp.ones((fwd_count,), dtype=bool), groups, fwd_capacity)
    fwd_buf = (
        jnp.dot(fwd_selector, fwd_hidden, preferred_element_type=jnp.float32)
        .astype(jnp.bfloat16)
        .reshape(groups, fwd_capacity, -1)
    )
    produced = jnp.einsum(
        "gkf,fd->gkd",
        lax.all_to_all(fwd_buf, "expert", split_axis=0, concat_axis=0, tiled=True),
        fwd_weight,
        preferred_element_type=jnp.float32,
    ).astype(jnp.bfloat16)
    returned = lax.all_to_all(produced, "expert", split_axis=0, concat_axis=0, tiled=True)
    fwd_rows_out = lax.dot_general(
        fwd_selector,
        returned.reshape(groups * fwd_capacity, -1),
        (((0,), (0,)), ((), ())),
        preferred_element_type=jnp.float32,
    )
    fwd_out = (fwd_rows_out * fwd_gate[:, None]).astype(jnp.bfloat16)
    return (placed_weight, placed_moment, fwd_out)


def solution(mesh):
    groups = mesh.shape["expert"]
    in_specs = (
        P(("layer", "expert"), None),
        P(("layer", "expert"), None),
        P(("layer", "expert"), None),
        P(("layer", "expert")),
        P(("layer", "expert"), None, None),
        P(("layer", "expert"), None, None),
        P("layer"),
        P(("layer", "expert"), None),
        P(("layer", "expert"), None),
        P(("layer", "expert")),
    )
    out_specs = (
        P(("layer", "expert"), None, None),
        P(("layer", "expert"), None, None),
        P(("layer", "expert"), None),
    )

    def per_device(*args):
        few = groups & (groups - 1) == 0 and groups <= 2 * args[0].shape[0] // groups
        return (partner_plan if few else routed_plan)(*args)

    return jax.shard_map(
        per_device, mesh=mesh, in_specs=in_specs, out_specs=out_specs, check_vma=False
    )
```
